32 devices in a mesh: narrow: 2 (over core), wide: 16 (over z, y, x).
Axes of the slice: x: 2, y: 2, z: 4, core: 2. Of those that a mesh axis runs over, the one named last changes fastest.
Arguments:
- hidden_in: bfloat16 [32768, 768], P(('narrow', 'wide')), may hold values from -6 to 6
- first_gain: bfloat16 [768], replicated, may hold values from 0.5 to 1.5
- w_query: bfloat16 [768, 768], replicated, may hold values from -0.3125 to 0.3125
- w_key: bfloat16 [768, 768], replicated, may hold values from -0.3125 to 0.3125
- w_value: bfloat16 [768, 768], replicated, may hold values from -0.21875 to 0.21875
- w_output: bfloat16 [768, 768], replicated, may hold values from -2.5 to 2.5
- rel_table: bfloat16 [32, 12], replicated, may hold values from -4 to 4
- second_gain: bfloat16 [768], replicated, may hold values from 0.5 to 1.5
- router: bfloat16 [768, 32], replicated, may hold values from -0.109375 to 0.109375
- expert_up: bfloat16 [32, 768, 3072], P(('narrow', 'wide')), may hold values from -0.21875 to 0.21875
- expert_down: bfloat16 [32, 3072, 768], P(('narrow', 'wide')), may hold values from -6 to 6
- routes: int32 [32768, 1], P(('narrow', 'wide')), may hold values from 0 to 31; in each aligned block of 1024 rows (0 to 1023, 1024 to 2047, ...) at most 64 rows name the same one
- capacity_factor: int32 [32], P(('narrow', 'wide')), may hold values from 1 to 2, as said below
- cotangent: bfloat16 [32768, 768], P(('narrow', 'wide')), may hold values from -6 to 6
Outputs:
- block_out: bfloat16 [32768, 768], P(('narrow', 'wide'))
- gradient_hidden: bfloat16 [32768, 768], P(('narrow', 'wide'))
- gradient_first_gain: float32 [768], replicated
- gradient_query: float32 [768, 768], replicated
- gradient_key: float32 [768, 768], replicated
- gradient_value: float32 [768, 768], replicated
- gradient_output: float32 [768, 768], replicated
- gradient_table: float32 [32, 12], replicated
- gradient_second_gain: float32 [768], replicated
- gradient_router: float32 [768, 32], replicated
- gradient_expert_up: float32 [32, 768, 3072], P(('narrow', 'wide'))
- gradient_expert_down: float32 [32, 3072, 768], P(('narrow', 'wide'))
The draws below stay inside these ranges and needn't reach their ends.
Inputs may be any that keep to these rules, and one draw needn't show every extreme that they name: `routes`: in the 1024 rows of one device no expert is named more than 64 times, and in every draw some device names one expert exactly 64 times. `capacity_factor`: both values occur in every draw.
All inputs are finite; a program needn't handle non-finite values.
Results may differ from the reference program's by a relative error of at most 0.019.
Values may be sent and summed in bfloat16 or wider, within the bound.
No kernel may reach another device: no remote copies, remote signals or barrier semaphores. Data moves between devices by JAX's collectives and lax.ppermute only.
A program may use at most 576 MiB of HBM per device.

```python
import math
import jax
import jax.numpy as jnp
import numpy as np
from jax import lax

D = 768
HEADS = 12
HDIM = 64
FF = 3072
BUCKETS = 32
SEQ = 1024
GROUPS = 32
EXPERTS = 32
TOK_DEV = 1024
TOKENS = 32768
CAP_MAX = 64


def draw_capacity_factor(key, part):
    key = jax.random.fold_in(key, 7)
    first, second, third = jax.random.split(key, 3)
    values = jax.random.randint(first, (GROUPS,), 1, 3)
    high_place = jax.random.randint(second, (), 0, GROUPS)
    low_place = (high_place + 1 + jax.random.randint(third, (), 0, GROUPS - 1)) % GROUPS
    values = values.at[high_place].set(2)
    values = values.at[low_place].set(1)
    return values.astype(jnp.int32)


def shard_levels(rng, shape, cuts, low, largest):
    loudness, own = 1.0, jax.random.fold_in(rng, 6)
    for dim, shards_of in cuts:
        heights = jnp.exp(jax.random.uniform(jax.random.fold_in(own, dim), (shards_of,), jnp.float32, low / len(cuts), largest / len(cuts)))
        loudness = loudness * jnp.repeat(heights, shape[dim] // shards_of).reshape([-1 if axis == dim else 1 for axis in range(len(shape))])
    return loudness


def deal_out(stream_key, own, number, rows, count, top, reach, lean):
    sequence = jax.random.permutation(stream_key, count)
    crowded, ordinary = shares(count, rows * top, reach, lean, True), shares(count, rows * top, reach, lean, False)
    places = jnp.arange(count)

    def named(lengths, offset_by):
        used = int((lengths > 0).sum())
        fixed = max(1, used // 4)
        passed = fixed + (places - fixed + offset_by * (used - fixed)) % max(1, count - fixed)
        return jnp.zeros((count,), jnp.int32).at[sequence[jnp.where(places < fixed, places, passed)]].set(jnp.asarray(lengths, jnp.int32))

    lengths = jnp.where(number % 4 == 0, named(crowded, number // 4), named(ordinary, number - number // 4 - 1))
    mixed = jax.random.permutation(jax.random.fold_in(own, 3), count)
    source_of, receiver = mixed[0:count // 2 * 2:2], mixed[1:count // 2 * 2:2]
    slack = jnp.minimum(lengths[source_of] - 1, reach - lengths[receiver]) // 2
    slack = jnp.where((source_of == sequence[0]) | (receiver == sequence[0]) | (lengths[receiver] == 0), 0, jnp.maximum(slack, 0))
    passed = jax.random.randint(jax.random.fold_in(own, 4), (count // 2,), 0, 1 << 20) % (slack + 1)
    lengths = lengths.at[source_of].add(-passed).at[receiver].add(passed)
    members = jnp.searchsorted(jnp.cumsum(lengths), jnp.arange(rows * top), side="right").astype(jnp.int32)
    grid = members.reshape(top, rows).T
    grid = grid[jax.random.permutation(jax.random.fold_in(own, 1), rows)]
    offset_by = jax.random.randint(jax.random.fold_in(own, 2), (rows, 1), 0, top)
    return jnp.take_along_axis(grid, (jnp.arange(top)[None, :] + offset_by) % top, axis=1)


def shares(count, total, reach, skew, full):
    portions = [(1 << 20) // math.isqrt(standing ** skew) + 1 for standing in range(1, count + 1)]
    largest = reach if full else min(reach, max(-(-total // count), total * portions[0] // sum(portions)))
    least = 1 if total - largest >= count - 1 else 0
    given, rest = [largest] + [least] * (count - 1), total - largest - least * (count - 1)
    while rest > 0:
        movable = [i for i in range(1, count) if given[i] < largest] or [i for i in range(1, count) if given[i] < reach]
        mass, left = sum([portions[i] for i in movable]), rest
        for i in movable:
            more = min(reach - given[i], max(1, left * portions[i] // mass), rest)
            given[i] = given[i] + more
            rest = rest - more
    return np.array(given)


def bell_draw(rng, shape, deviation, reach, pieces=(), kind=jnp.bfloat16):
    array = jax.random.normal(rng, shape, jnp.float32) * deviation
    if len(pieces) > 0:
        array = shard_levels(rng, shape, pieces, -0.22, 0.18) * array
    return jnp.clip(array, min=-reach, max=reach).astype(kind)


def setup_inputs(seed: int = 0) -> dict:
    key_list = jax.random.split(jax.random.key(seed), 15)
    hidden_in = bell_draw(key_list[0], (TOKENS, D), 1.0, 6.0, ((0, 32),))
    first_gain = jnp.clip(1.0 + 0.1 * jax.random.normal(key_list[1], (D,), jnp.float32), 0.5, 1.5).astype(jnp.bfloat16)
    w_query = bell_draw(key_list[2], (D, D), (D // 2) ** -0.5, 0.3125)
    w_key = bell_draw(key_list[3], (D, D), (D // 2) ** -0.5, 0.3125)
    w_value = bell_draw(key_list[4], (D, D), D ** -0.5, 0.21875)
    w_output = bell_draw(key_list[5], (D, D), (max(D // 128, 1)) ** -0.5, 2.5)
    rel_table = bell_draw(key_list[6], (BUCKETS, HEADS), 1.0, 4.0)
    second_gain = jnp.clip(1.0 + 0.1 * jax.random.normal(key_list[7], (D,), jnp.float32), 0.5, 1.5).astype(jnp.bfloat16)
    router = bell_draw(key_list[8], (D, EXPERTS), (4 * D) ** -0.5, 0.109375)
    expert_up = bell_draw(key_list[9], (EXPERTS, D, FF), D ** -0.5, 0.21875, ((0, 32),))
    expert_down = bell_draw(key_list[10], (EXPERTS, FF, D), (2.0 * EXPERTS * FF ** -0.5), 6.0, ((0, 32),))
    routes_keys = jax.random.split(jax.random.fold_in(key_list[11], 1), TOKENS // TOK_DEV)
    routes_turns = jax.random.permutation(jax.random.fold_in(key_list[11], 3), TOKENS // TOK_DEV)
    routes = jax.vmap(lambda own, number: deal_out(jax.random.fold_in(key_list[11], 2), own, number, TOK_DEV, EXPERTS, 1, CAP_MAX, 2))(routes_keys, routes_turns).reshape((TOKENS, 1))
    capacity_factor = draw_capacity_factor(jax.random.fold_in(key_list[14], 71), 0)
    cotangent = bell_draw(key_list[13], (TOKENS, D), 1.0, 6.0, ((0, 32),))
    return dict(hidden_in=hidden_in, first_gain=first_gain, w_query=w_query, w_key=w_key, w_value=w_value, w_output=w_output, rel_table=rel_table, second_gain=second_gain, router=router, expert_up=expert_up, expert_down=expert_down, routes=routes, capacity_factor=capacity_factor, cotangent=cotangent)


eps_norm = 1e-06
bucket_edges = (12, 16, 23, 32, 46, 64, 91)

@jax.custom_vjp
def low(v):
    return lax.optimization_barrier(v.astype(jnp.bfloat16)).astype(jnp.float32)

@jax.custom_vjp
def low_back(v):
    return v

def low_keep(v):
    return (low(v), None)

def low_pass(kept, grad):
    return (grad,)

def back_keep(v):
    return (v, None)

def back_low(kept, grad):
    return (low(grad),)
low.defvjp(low_keep, low_pass)
low_back.defvjp(back_keep, back_low)

def bucket_of(offset):
    distance = jnp.abs(offset)
    far_bucket = jnp.full(distance.shape, 8, jnp.int32)
    for edge in bucket_edges:
        far_bucket = far_bucket + (distance >= edge).astype(jnp.int32)
    near_bucket = jnp.where(distance < 8, distance, far_bucket)
    return near_bucket + 16 * (offset > 0).astype(jnp.int32)

def matmul(left, right):
    return jnp.dot(left, right, precision=lax.Precision.HIGHEST, preferred_element_type=jnp.float32)

def rms_scale(rows, gain):
    return rows * lax.rsqrt(lax.optimization_barrier(jnp.mean(rows * rows, axis=-1, keepdims=True)) + eps_norm) * gain

def exact_gelu(values):
    return jax.nn.gelu(values, approximate=False)

def attention_sequence(rows, first_gain, w_query, w_key, w_value, w_output, bias):
    normed = low(rms_scale(rows, first_gain))
    queries = low(low_back(matmul(normed, w_query))).reshape(SEQ, HEADS, HDIM)
    keys = low(low_back(matmul(normed, w_key))).reshape(SEQ, HEADS, HDIM)
    values = low(low_back(matmul(normed, w_value))).reshape(SEQ, HEADS, HDIM)
    scores = jnp.einsum('qhd,khd->hqk', queries, keys, precision=lax.Precision.HIGHEST) * HDIM ** (-0.5) + bias
    scores = low_back(scores)
    weights = low(jax.nn.softmax(scores, axis=-1))
    attended = jnp.einsum('hqk,khd->qhd', weights, values, precision=lax.Precision.HIGHEST).reshape(SEQ, D)
    attended = low(low_back(attended))
    return rows + low_back(matmul(attended, w_output))

def expert_rows(packed):
    rows, upper, lower = packed
    pre_act = low_back(matmul(rows, upper))
    activated = low(exact_gelu(pre_act))
    return low(low_back(matmul(activated, lower)))

def reference(hidden_in, first_gain, w_query, w_key, w_value, w_output, rel_table, second_gain, router, expert_up, expert_down, routes, capacity_factor, cotangent):
    route = routes[:, 0]
    group = jnp.arange(TOKENS, dtype=jnp.int32) // TOK_DEV
    chosen = (route[:, None] == jnp.arange(EXPERTS, dtype=jnp.int32)[None, :]).astype(jnp.int32)
    grouped = chosen.reshape(GROUPS, TOK_DEV, EXPERTS)
    earlier = (jnp.cumsum(grouped, axis=1) - grouped).reshape(TOKENS, EXPERTS)
    slot = lax.optimization_barrier(jnp.sum(earlier * chosen, axis=1))
    capacity = capacity_factor[group] * TOK_DEV // EXPERTS
    kept = slot < capacity
    row_index = group * CAP_MAX + jnp.minimum(slot, CAP_MAX - 1)
    chosen_float = chosen.astype(jnp.float32)
    positions = jnp.arange(SEQ, dtype=jnp.int32)
    buckets = bucket_of(positions[None, :] - positions[:, None])

    def forward(hidden, gain_one, query_w, key_w, value_w, output_w, table, gain_two, router_w, upper_w, lower_w):
        bias = jnp.transpose(table[buckets], (2, 0, 1))

        def one_sequence(rows):
            return attention_sequence(rows, gain_one, query_w, key_w, value_w, output_w, bias)
        mixed = lax.map(jax.checkpoint(one_sequence), hidden.reshape(TOKENS // SEQ, SEQ, D)).reshape(TOKENS, D)
        normed = low(rms_scale(mixed, gain_two))
        logits = low_back(matmul(normed, router_w))
        gate = lax.optimization_barrier(jnp.sum(jax.nn.softmax(logits, axis=-1) * chosen_float, axis=-1))
        placed = jnp.where(kept[:, None], normed, 0.0)
        buffer = jnp.zeros((EXPERTS, GROUPS * CAP_MAX, D), jnp.float32).at[route, row_index].add(placed)
        buffer = low_back(buffer)
        results = lax.map(jax.checkpoint(expert_rows), (buffer, upper_w, lower_w))
        fetched = jnp.where(kept[:, None], results[route, row_index], 0.0)
        return mixed + gate[:, None] * fetched
    floats = (hidden_in.astype(jnp.float32), first_gain.astype(jnp.float32), w_query.astype(jnp.float32), w_key.astype(jnp.float32), w_value.astype(jnp.float32), w_output.astype(jnp.float32), rel_table.astype(jnp.float32), second_gain.astype(jnp.float32), router.astype(jnp.float32), expert_up.astype(jnp.float32), expert_down.astype(jnp.float32))
    result, pullback = jax.vjp(forward, *floats)
    grads = pullback(cotangent.astype(jnp.float32))
    return (result.astype(jnp.bfloat16), grads[0].astype(jnp.bfloat16), grads[1], grads[2], grads[3], grads[4], grads[5], grads[6], grads[7], grads[8], grads[9], grads[10])
```

```python
import jax
import jax.numpy as jnp
from jax import lax
from jax.experimental import pallas as pl
from jax.experimental.pallas import tpu as pltpu
from jax.sharding import PartitionSpec as P

TILE = 128
STRIP = 256
VMEM_CAP = 60 * 1024 * 1024
eps_norm = 1e-06
bucket_edges = (12, 16, 23, 32, 46, 64, 91)


def bucket_of(offset):
    distance = jnp.abs(offset)
    far_bucket = jnp.full(distance.shape, 8, jnp.int32)
    for edge in bucket_edges:
        far_bucket = far_bucket + (distance >= edge).astype(jnp.int32)
    near_bucket = jnp.where(distance < 8, distance, far_bucket)
    return near_bucket + 16 * (offset > 0).astype(jnp.int32)


def band_buckets():
    rows = lax.broadcasted_iota(jnp.int32, (3 * TILE, TILE), 0)
    lanes = lax.broadcasted_iota(jnp.int32, (3 * TILE, TILE), 1)
    return bucket_of(rows - TILE - lanes)


def times_transposed(left, right):
    return lax.dot_general(
        left, right, (((1,), (1,)), ((), ())), preferred_element_type=jnp.float32
    )


def times(left, right):
    return jnp.dot(left, right, preferred_element_type=jnp.float32)


def fill_wide(edge_ref, band_ref, wide):
    length = (wide.shape[1] + TILE) // 2
    pair = pl.program_id(0)
    for side in range(2):
        head = 2 * pair + side
        wide[side, : length - 2 * TILE] = jnp.full(
            (length - 2 * TILE, TILE), edge_ref[head, 0], jnp.float32
        )
        wide[side, length - 2 * TILE : length + TILE] = band_ref[side]
        wide[side, length + TILE :] = jnp.full(
            (length - 2 * TILE, TILE), edge_ref[head, 1], jnp.float32
        )


def strip_bias(wide, side, key_start, keys, query_start):
    length = (wide.shape[1] + TILE) // 2
    parts = []
    for start in range(query_start, query_start + STRIP, TILE):
        first = length - TILE - start + key_start
        parts.append(wide[side, first : first + keys, :])
    return jnp.concatenate(parts, axis=1)


def half_of(rows, side):
    half = rows.shape[1] // 2
    lanes = lax.broadcasted_iota(jnp.int32, rows.shape, 1)
    own = lanes < half if side == 0 else lanes >= half
    return jnp.where(own, rows, jnp.zeros_like(rows))


def attend_kernel(edge_ref, q_ref, k_ref, v_ref, band_ref, out_ref, log_ref, wide):
    length = q_ref.shape[0]
    half = q_ref.shape[1] // 2
    scale = half ** (-0.5)
    fill_wide(edge_ref, band_ref, wide)
    keys = k_ref[...]
    values_t = jnp.transpose(v_ref[...])
    for start in range(0, length, STRIP):
        mixed = []
        for side in range(2):
            query = half_of(q_ref[start : start + STRIP, :] * scale, side)
            scores = times_transposed(keys, query) + strip_bias(wide, side, 0, length, start)
            top = jnp.max(scores, axis=0, keepdims=True)
            powers = jnp.exp(scores - top)
            total = jnp.sum(powers, axis=0, keepdims=True)
            raw = times(values_t[side * half : (side + 1) * half], powers.astype(jnp.bfloat16))
            mixed.append(raw / total)
            log_ref[0, side : side + 1, start : start + STRIP] = top + jnp.log(total)
        both = jnp.concatenate(mixed, axis=0)
        out_ref[start : start + STRIP, :] = jnp.transpose(both).astype(jnp.bfloat16)


def attend(queries, keys, values, band, edges):
    length, width = queries.shape
    heads = edges.shape[0]
    pairs = heads // 2
    columns = width // pairs
    part = pl.BlockSpec((length, columns), lambda pair: (0, pair))
    return pl.pallas_call(
        attend_kernel,
        grid=(pairs,),
        in_specs=[
            pl.BlockSpec(memory_space=pltpu.SMEM),
            part,
            part,
            part,
            pl.BlockSpec((2, 3 * TILE, TILE), lambda pair: (pair, 0, 0)),
        ],
        out_specs=[part, pl.BlockSpec((1, 2, length), lambda pair: (pair, 0, 0))],
        out_shape=[
            jax.ShapeDtypeStruct((length, width), jnp.bfloat16),
            jax.ShapeDtypeStruct((pairs, 2, length), jnp.float32),
        ],
        scratch_shapes=[pltpu.VMEM((2, 2 * length - TILE, TILE), jnp.float32)],
        compiler_params=pltpu.CompilerParams(vmem_limit_bytes=VMEM_CAP),
        cost_estimate=pl.CostEstimate(
            flops=4 * heads * length * length * (width // heads),
            bytes_accessed=8 * length * width,
            transcendentals=heads * length * length,
        ),
        name="attend",
    )(edges, queries, keys, values, band)


def attend_back_kernel(
    edge_ref, q_ref, k_ref, v_ref, grad_ref, out_ref, log_ref, band_ref,
    dq_ref, dk_ref, dv_ref, near_ref, far_ref,
    wide, key_total, value_total,
):
    length = q_ref.shape[0]
    half = q_ref.shape[1] // 2
    scale = half ** (-0.5)
    fill_wide(edge_ref, band_ref, wide)
    keys_t = jnp.transpose(k_ref[...])
    products = jnp.transpose(grad_ref[...].astype(jnp.float32) * out_ref[...].astype(jnp.float32))
    centers = [
        jnp.sum(products[side * half : (side + 1) * half], axis=0, keepdims=True)
        for side in range(2)
    ]
    near_ref[...] = jnp.zeros_like(near_ref)
    far_ref[...] = jnp.zeros_like(far_ref)
    for start in range(0, length, STRIP):
        strip = slice(start, start + STRIP)
        query_parts = []
        for side in range(2):
            query = half_of(q_ref[strip, :] * scale, side)
            grad = half_of(grad_ref[strip, :], side)
            log_total = log_ref[0, side : side + 1, strip]
            center = centers[side][:, strip]
            query_total = None
            for first in range(0, length, STRIP):
                block = slice(first, first + STRIP)
                scores = times_transposed(k_ref[block, :], query) + strip_bias(
                    wide, side, first, STRIP, start
                )
                weights = jnp.exp(scores - log_total)
                weight_grad = times_transposed(v_ref[block, :], grad)
                score_grad = weights * (weight_grad - center)
                score_low = score_grad.astype(jnp.bfloat16)
                value_term = times(weights.astype(jnp.bfloat16), grad)
                key_term = times(score_low, query)
                if start == 0 and side == 0:
                    value_total[block, :] = value_term
                    key_total[block, :] = key_term
                else:
                    value_total[block, :] += value_term
                    key_total[block, :] += key_term
                query_term = times(keys_t[side * half : (side + 1) * half, block], score_low)
                query_total = query_term if query_total is None else query_total + query_term
                for row in range(0, STRIP, TILE):
                    for lane in range(0, STRIP, TILE):
                        piece = score_grad[row : row + TILE, lane : lane + TILE]
                        apart = (first + row - start - lane) // TILE
                        if abs(apart) <= 1:
                            spot = (apart + 1) * TILE
                            near_ref[side, spot : spot + TILE, :] += piece
                        else:
                            far_ref[side, 0 if apart < 0 else 1] += jnp.sum(
                                piece.reshape(TILE // 8, 8, TILE), axis=0
                            )
            query_parts.append(query_total * scale)
        both = jnp.concatenate(query_parts, axis=0)
        dq_ref[strip, :] = jnp.transpose(both).astype(jnp.bfloat16)
    dk_ref[...] = key_total[...].astype(jnp.bfloat16)
    dv_ref[...] = value_total[...].astype(jnp.bfloat16)


def attend_back(queries, keys, values, grads, attended, logs, band, edges):
    length, width = queries.shape
    heads = edges.shape[0]
    pairs = heads // 2
    columns = width // pairs
    part = pl.BlockSpec((length, columns), lambda pair: (0, pair))
    band_spec = pl.BlockSpec((2, 3 * TILE, TILE), lambda pair: (pair, 0, 0))
    rows = jax.ShapeDtypeStruct((length, width), jnp.bfloat16)
    return pl.pallas_call(
        attend_back_kernel,
        grid=(pairs,),
        in_specs=[
            pl.BlockSpec(memory_space=pltpu.SMEM),
            part, part, part, part, part,
            pl.BlockSpec((1, 2, length), lambda pair: (pair, 0, 0)),
            band_spec,
        ],
        out_specs=[
            part, part, part, band_spec,
            pl.BlockSpec((2, 2, 8, TILE), lambda pair: (pair, 0, 0, 0)),
        ],
        out_shape=[
            rows, rows, rows,
            jax.ShapeDtypeStruct((heads, 3 * TILE, TILE), jnp.float32),
            jax.ShapeDtypeStruct((heads, 2, 8, TILE), jnp.float32),
        ],
        scratch_shapes=[
            pltpu.VMEM((2, 2 * length - TILE, TILE), jnp.float32),
            pltpu.VMEM((length, columns), jnp.float32),
            pltpu.VMEM((length, columns), jnp.float32),
        ],
        compiler_params=pltpu.CompilerParams(vmem_limit_bytes=VMEM_CAP),
        cost_estimate=pl.CostEstimate(
            flops=10 * heads * length * length * (width // heads),
            bytes_accessed=16 * length * width,
            transcendentals=heads * length * length,
        ),
        name="attend_back",
    )(edges, queries, keys, values, grads, attended, logs, band)


def bias_band(rel_table):
    buckets, heads = rel_table.shape
    labels = band_buckets().reshape(1, -1)
    onehot = (labels == jnp.arange(buckets, dtype=jnp.int32)[:, None]).astype(jnp.bfloat16)
    band = lax.dot_general(
        rel_table, onehot, (((0,), (0,)), ((), ())), preferred_element_type=jnp.float32
    )
    half = buckets // 2
    edges = jnp.stack([rel_table[half - 1], rel_table[buckets - 1]], axis=1).astype(jnp.float32)
    return band.reshape(heads, 3 * TILE, TILE), edges


def table_gradient(near, far, buckets):
    heads = near.shape[0]
    labels = band_buckets().reshape(-1, 1)
    onehot = (labels == jnp.arange(buckets, dtype=jnp.int32)[None, :]).astype(jnp.float32)
    sums = lax.dot_general(
        near.reshape(heads, -1), onehot, (((1,), (0,)), ((), ())),
        precision=lax.Precision.HIGHEST, preferred_element_type=jnp.float32,
    )
    half = buckets // 2
    sides = jnp.sum(far, axis=(2, 3))
    sums = sums.at[:, half - 1].add(sides[:, 0]).at[:, buckets - 1].add(sides[:, 1])
    return jnp.transpose(sums)


def rms_scale(rows, gain):
    return rows * lax.rsqrt(jnp.mean(rows * rows, axis=-1, keepdims=True) + eps_norm) * gain


def exact_gelu(values):
    return jax.nn.gelu(values, approximate=False)


def inner_rows(left, right):
    return lax.dot_general(
        left, right, (((0,), (0,)), ((), ())), preferred_element_type=jnp.float32
    )


def on_device(
    hidden_in,
    first_gain,
    w_query,
    w_key,
    w_value,
    w_output,
    rel_table,
    second_gain,
    router,
    expert_up,
    expert_down,
    routes,
    capacity_factor,
    cotangent,
):
    tokens, width = hidden_in.shape
    bucket_count, heads = rel_table.shape
    experts_total = router.shape[1]
    local_experts = expert_up.shape[0]
    narrow = lax.axis_size("narrow")
    wide = lax.axis_size("wide")
    groups = narrow * wide
    slots = 2 * tokens // experts_total
    band, edges = bias_band(rel_table)
    hidden_float = hidden_in.astype(jnp.float32)
    first_values, first_pullback = jax.vjp(rms_scale, hidden_float, first_gain.astype(jnp.float32))
    normed_first = first_values.astype(jnp.bfloat16)
    queries = jnp.dot(normed_first, w_query, preferred_element_type=jnp.float32).astype(
        jnp.bfloat16
    )
    keys = jnp.dot(normed_first, w_key, preferred_element_type=jnp.float32).astype(jnp.bfloat16)
    values = jnp.dot(normed_first, w_value, preferred_element_type=jnp.float32).astype(jnp.bfloat16)
    attended, logs = attend(queries, keys, values, band, edges)
    residual = hidden_float + jnp.dot(attended, w_output, preferred_element_type=jnp.float32)
    second_values, second_pullback = jax.vjp(rms_scale, residual, second_gain.astype(jnp.float32))
    normed_second = second_values.astype(jnp.bfloat16)
    logits = jnp.dot(normed_second, router, preferred_element_type=jnp.float32)
    route = routes[:, 0]
    chosen = route[:, None] == jnp.arange(experts_total, dtype=jnp.int32)[None, :]
    chosen_float = chosen.astype(jnp.float32)

    def gate_of(logit_rows):
        return jnp.sum(jax.nn.softmax(logit_rows, axis=-1) * chosen_float, axis=-1)

    gate, gate_pullback = jax.vjp(gate_of, logits)
    chosen_count = chosen.astype(jnp.int32)
    earlier = jnp.cumsum(chosen_count, axis=0) - chosen_count
    slot = jnp.sum(earlier * chosen_count, axis=1)
    capacity = capacity_factor[0] * tokens // experts_total
    kept = slot < capacity
    target = jnp.where(kept, route * slots + slot, experts_total * slots)
    owner = (
        jnp.full((experts_total * slots,), tokens, jnp.int32)
        .at[target]
        .set(jnp.arange(tokens, dtype=jnp.int32), mode="drop")
    )
    send = jnp.take(normed_second, owner, axis=0, mode="fill", fill_value=0).reshape(
        groups, local_experts, slots, width
    )
    received = lax.all_to_all(send, ("narrow", "wide"), split_axis=0, concat_axis=0, tiled=True)
    pre_act = jnp.einsum("glcd,ldf->glcf", received, expert_up, preferred_element_type=jnp.float32)
    activated, gelu_pullback = jax.vjp(exact_gelu, pre_act)
    activated = activated.astype(jnp.bfloat16)
    produced = jnp.einsum(
        "glcf,lfd->glcd", activated, expert_down, preferred_element_type=jnp.float32
    ).astype(jnp.bfloat16)
    returned = lax.all_to_all(produced, ("narrow", "wide"), split_axis=0, concat_axis=0, tiled=True)
    fetched = jnp.take(
        returned.reshape(experts_total * slots, width), target, axis=0, mode="fill", fill_value=0
    ).astype(jnp.float32)
    block_out = (residual + gate[:, None] * fetched).astype(jnp.bfloat16)
    upstream = cotangent.astype(jnp.float32)
    scaled_up = (gate[:, None] * upstream).astype(jnp.bfloat16)
    back_send = jnp.take(scaled_up, owner, axis=0, mode="fill", fill_value=0).reshape(
        groups, local_experts, slots, width
    )
    slot_grad = lax.all_to_all(
        back_send, ("narrow", "wide"), split_axis=0, concat_axis=0, tiled=True
    )
    gate_grad = jnp.sum(upstream * fetched, axis=1)
    act_grad = jnp.einsum(
        "glcd,lfd->glcf", slot_grad, expert_down, preferred_element_type=jnp.float32
    )
    pre_grad = gelu_pullback(act_grad)[0].astype(jnp.bfloat16)
    gradient_expert_down = jnp.einsum(
        "glcf,glcd->lfd", activated, slot_grad, preferred_element_type=jnp.float32
    )
    gradient_expert_up = jnp.einsum(
        "glcd,glcf->ldf", received, pre_grad, preferred_element_type=jnp.float32
    )
    input_grad = jnp.einsum(
        "glcf,ldf->glcd", pre_grad, expert_up, preferred_element_type=jnp.float32
    ).astype(jnp.bfloat16)
    returned_grad = lax.all_to_all(
        input_grad, ("narrow", "wide"), split_axis=0, concat_axis=0, tiled=True
    )
    routed_grad = jnp.take(
        returned_grad.reshape(experts_total * slots, width),
        target,
        axis=0,
        mode="fill",
        fill_value=0,
    ).astype(jnp.float32)
    logit_grad = gate_pullback(gate_grad)[0].astype(jnp.bfloat16)
    gradient_router = inner_rows(normed_second, logit_grad)
    normed_grad = routed_grad + times_transposed(logit_grad, router)
    residual_part, gradient_second_gain = second_pullback(normed_grad)
    residual_grad = upstream + residual_part
    out_grad = residual_grad.astype(jnp.bfloat16)
    gradient_output = inner_rows(attended, out_grad)
    attended_grad = times_transposed(out_grad, w_output).astype(jnp.bfloat16)
    query_grad, key_parts, value_parts, near, far = attend_back(
        queries, keys, values, attended_grad, attended, logs, band, edges
    )
    gradient_query = inner_rows(normed_first, query_grad)
    gradient_key = inner_rows(normed_first, key_parts)
    gradient_value = inner_rows(normed_first, value_parts)
    normed_first_grad = (
        times_transposed(query_grad, w_query)
        + times_transposed(key_parts, w_key)
        + times_transposed(value_parts, w_value)
    )
    hidden_part, gradient_first_gain = first_pullback(normed_first_grad)
    gradient_hidden = (residual_grad + hidden_part).astype(jnp.bfloat16)
    gradient_table = table_gradient(near, far, bucket_count)
    summed = lax.psum(
        (
            gradient_first_gain,
            gradient_query,
            gradient_key,
            gradient_value,
            gradient_output,
            gradient_table,
            gradient_second_gain,
            gradient_router,
        ),
        ("narrow", "wide"),
    )
    return (
        block_out,
        gradient_hidden,
        summed[0],
        summed[1],
        summed[2],
        summed[3],
        summed[4],
        summed[5],
        summed[6],
        summed[7],
        gradient_expert_up,
        gradient_expert_down,
    )


def solution(mesh):
    placed = (
        P(("narrow", "wide"), None),
        P(),
        P(),
        P(),
        P(),
        P(),
        P(),
        P(),
        P(),
        P(("narrow", "wide"), None, None),
        P(("narrow", "wide"), None, None),
        P(("narrow", "wide"), None),
        P(("narrow", "wide")),
        P(("narrow", "wide"), None),
    )
    return jax.shard_map(
        on_device,
        mesh=mesh,
        in_specs=placed,
        out_specs=(
            P(("narrow", "wide"), None),
            P(("narrow", "wide"), None),
            P(),
            P(),
            P(),
            P(),
            P(),
            P(),
            P(),
            P(),
            P(("narrow", "wide"), None, None),
            P(("narrow", "wide"), None, None),
        ),
        check_vma=False,
    )
```

```python
import functools

import jax
import jax.numpy as jnp
from jax import lax
from jax.experimental import pallas as pl
from jax.experimental.pallas import tpu as pltpu
from jax.sharding import PartitionSpec as P

TILE = 128
STRIP = 256
VMEM_CAP = 60 * 1024 * 1024
eps_norm = 1e-06
bucket_edges = (12, 16, 23, 32, 46, 64, 91)


def bucket_of(offset):
    distance = jnp.abs(offset)
    far_bucket = jnp.full(distance.shape, 8, jnp.int32)
    for edge in bucket_edges:
        far_bucket = far_bucket + (distance >= edge).astype(jnp.int32)
    near_bucket = jnp.where(distance < 8, distance, far_bucket)
    return near_bucket + 16 * (offset > 0).astype(jnp.int32)


def band_buckets():
    rows = lax.broadcasted_iota(jnp.int32, (3 * TILE, TILE), 0)
    lanes = lax.broadcasted_iota(jnp.int32, (3 * TILE, TILE), 1)
    return bucket_of(rows - TILE - lanes)


def times_transposed(left, right):
    return lax.dot_general(
        left, right, (((1,), (1,)), ((), ())), preferred_element_type=jnp.float32
    )


def inner_rows(left, right):
    return lax.dot_general(
        left, right, (((0,), (0,)), ((), ())), preferred_element_type=jnp.float32
    )


def times(left, right):
    return jnp.dot(left, right, preferred_element_type=jnp.float32)


def fill_wide(edge_ref, band_ref, wide):
    length = (wide.shape[1] + TILE) // 2
    pair = pl.program_id(0)
    for side in range(2):
        head = 2 * pair + side
        wide[side, : length - 2 * TILE] = jnp.full(
            (length - 2 * TILE, TILE), edge_ref[head, 0], jnp.float32
        )
        wide[side, length - 2 * TILE : length + TILE] = band_ref[side]
        wide[side, length + TILE :] = jnp.full(
            (length - 2 * TILE, TILE), edge_ref[head, 1], jnp.float32
        )


def strip_bias(wide, side, key_start, keys, query_start):
    length = (wide.shape[1] + TILE) // 2
    parts = []
    for start in range(query_start, query_start + STRIP, TILE):
        first = length - TILE - start + key_start
        parts.append(wide[side, first : first + keys, :])
    return jnp.concatenate(parts, axis=1)


def half_of(rows, side):
    half = rows.shape[1] // 2
    lanes = lax.broadcasted_iota(jnp.int32, rows.shape, 1)
    own = lanes < half if side == 0 else lanes >= half
    return jnp.where(own, rows, jnp.zeros_like(rows))


def attend_kernel(edge_ref, q_ref, k_ref, v_ref, band_ref, out_ref, log_ref, wide):
    length = q_ref.shape[0]
    half = q_ref.shape[1] // 2
    scale = half ** (-0.5)
    fill_wide(edge_ref, band_ref, wide)
    keys = k_ref[...]
    values_t = jnp.transpose(v_ref[...])
    for start in range(0, length, STRIP):
        mixed = []
        for side in range(2):
            query = half_of(q_ref[start : start + STRIP, :] * scale, side)
            scores = times_transposed(keys, query) + strip_bias(wide, side, 0, length, start)
            top = jnp.max(scores, axis=0, keepdims=True)
            powers = jnp.exp(scores - top)
            total = jnp.sum(powers, axis=0, keepdims=True)
            raw = times(values_t[side * half : (side + 1) * half], powers.astype(jnp.bfloat16))
            mixed.append(raw / total)
            log_ref[0, side : side + 1, start : start + STRIP] = top + jnp.log(total)
        both = jnp.concatenate(mixed, axis=0)
        out_ref[start : start + STRIP, :] = jnp.transpose(both).astype(jnp.bfloat16)


def attend(queries, keys, values, band, edges):
    length, width = queries.shape
    heads = edges.shape[0]
    pairs = heads // 2
    columns = width // pairs
    part = pl.BlockSpec((length, columns), lambda pair: (0, pair))
    return pl.pallas_call(
        attend_kernel,
        grid=(pairs,),
        in_specs=[
            pl.BlockSpec(memory_space=pltpu.SMEM),
            part,
            part,
            part,
            pl.BlockSpec((2, 3 * TILE, TILE), lambda pair: (pair, 0, 0)),
        ],
        out_specs=[part, pl.BlockSpec((1, 2, length), lambda pair: (pair, 0, 0))],
        out_shape=[
            jax.ShapeDtypeStruct((length, width), jnp.bfloat16),
            jax.ShapeDtypeStruct((pairs, 2, length), jnp.float32),
        ],
        scratch_shapes=[pltpu.VMEM((2, 2 * length - TILE, TILE), jnp.float32)],
        compiler_params=pltpu.CompilerParams(vmem_limit_bytes=VMEM_CAP),
        cost_estimate=pl.CostEstimate(
            flops=4 * heads * length * length * (width // heads),
            bytes_accessed=8 * length * width,
            transcendentals=heads * length * length,
        ),
        name="attend",
    )(edges, queries, keys, values, band)


def attend_back_kernel(
    edge_ref, q_ref, k_ref, v_ref, grad_ref, out_ref, log_ref, band_ref,
    grads_ref, near_ref, far_ref,
    wide, key_total, value_total,
):
    length = q_ref.shape[0]
    half = q_ref.shape[1] // 2
    scale = half ** (-0.5)
    fill_wide(edge_ref, band_ref, wide)
    keys_t = jnp.transpose(k_ref[...])
    products = jnp.transpose(grad_ref[...].astype(jnp.float32) * out_ref[...].astype(jnp.float32))
    centers = [
        jnp.sum(products[side * half : (side + 1) * half], axis=0, keepdims=True)
        for side in range(2)
    ]
    near_ref[...] = jnp.zeros_like(near_ref)
    far_ref[...] = jnp.zeros_like(far_ref)
    for start in range(0, length, STRIP):
        strip = slice(start, start + STRIP)
        query_parts = []
        for side in range(2):
            query = half_of(q_ref[strip, :] * scale, side)
            grad = half_of(grad_ref[strip, :], side)
            log_total = log_ref[0, side : side + 1, strip]
            center = centers[side][:, strip]
            query_total = None
            for first in range(0, length, STRIP):
                block = slice(first, first + STRIP)
                scores = times_transposed(k_ref[block, :], query) + strip_bias(
                    wide, side, first, STRIP, start
                )
                weights = jnp.exp(scores - log_total)
                weight_grad = times_transposed(v_ref[block, :], grad)
                score_grad = weights * (weight_grad - center)
                score_low = score_grad.astype(jnp.bfloat16)
                value_term = times(weights.astype(jnp.bfloat16), grad)
                key_term = times(score_low, query)
                if start == 0 and side == 0:
                    value_total[block, :] = value_term
                    key_total[block, :] = key_term
                else:
                    value_total[block, :] += value_term
                    key_total[block, :] += key_term
                query_term = times(keys_t[side * half : (side + 1) * half, block], score_low)
                query_total = query_term if query_total is None else query_total + query_term
                for row in range(0, STRIP, TILE):
                    for lane in range(0, STRIP, TILE):
                        piece = score_grad[row : row + TILE, lane : lane + TILE]
                        apart = (first + row - start - lane) // TILE
                        if abs(apart) <= 1:
                            spot = (apart + 1) * TILE
                            near_ref[side, spot : spot + TILE, :] += piece
                        else:
                            far_ref[side, 0 if apart < 0 else 1] += jnp.sum(
                                piece.reshape(TILE // 8, 8, TILE), axis=0
                            )
            query_parts.append(query_total * scale)
        both = jnp.concatenate(query_parts, axis=0)
        grads_ref[0, strip, :] = jnp.transpose(both).astype(jnp.bfloat16)
    grads_ref[1] = key_total[...].astype(jnp.bfloat16)
    grads_ref[2] = value_total[...].astype(jnp.bfloat16)


def attend_back(queries, keys, values, grads, attended, logs, band, edges):
    length, width = queries.shape
    heads = edges.shape[0]
    pairs = heads // 2
    columns = width // pairs
    part = pl.BlockSpec((length, columns), lambda pair: (0, pair))
    band_spec = pl.BlockSpec((2, 3 * TILE, TILE), lambda pair: (pair, 0, 0))
    return pl.pallas_call(
        attend_back_kernel,
        grid=(pairs,),
        in_specs=[
            pl.BlockSpec(memory_space=pltpu.SMEM),
            part, part, part, part, part,
            pl.BlockSpec((1, 2, length), lambda pair: (pair, 0, 0)),
            band_spec,
        ],
        out_specs=[
            pl.BlockSpec((3, length, columns), lambda pair: (0, 0, pair)), band_spec,
            pl.BlockSpec((2, 2, 8, TILE), lambda pair: (pair, 0, 0, 0)),
        ],
        out_shape=[
            jax.ShapeDtypeStruct((3, length, width), jnp.bfloat16),
            jax.ShapeDtypeStruct((heads, 3 * TILE, TILE), jnp.float32),
            jax.ShapeDtypeStruct((heads, 2, 8, TILE), jnp.float32),
        ],
        scratch_shapes=[
            pltpu.VMEM((2, 2 * length - TILE, TILE), jnp.float32),
            pltpu.VMEM((length, columns), jnp.float32),
            pltpu.VMEM((length, columns), jnp.float32),
        ],
        compiler_params=pltpu.CompilerParams(vmem_limit_bytes=VMEM_CAP),
        cost_estimate=pl.CostEstimate(
            flops=10 * heads * length * length * (width // heads),
            bytes_accessed=16 * length * width,
            transcendentals=heads * length * length,
        ),
        name="attend_back",
    )(edges, queries, keys, values, grads, attended, logs, band)


def bias_band(rel_table):
    buckets, heads = rel_table.shape
    labels = band_buckets().reshape(1, -1)
    onehot = (labels == jnp.arange(buckets, dtype=jnp.int32)[:, None]).astype(jnp.bfloat16)
    band = lax.dot_general(
        rel_table, onehot, (((0,), (0,)), ((), ())), preferred_element_type=jnp.float32
    )
    half = buckets // 2
    edges = jnp.stack([rel_table[half - 1], rel_table[buckets - 1]], axis=1).astype(jnp.float32)
    return band.reshape(heads, 3 * TILE, TILE), edges


def table_gradient(near, far, buckets):
    heads = near.shape[0]
    labels = band_buckets().reshape(-1, 1)
    onehot = (labels == jnp.arange(buckets, dtype=jnp.int32)[None, :]).astype(jnp.float32)
    sums = lax.dot_general(
        near.reshape(heads, -1), onehot, (((1,), (0,)), ((), ())),
        precision=lax.Precision.HIGHEST, preferred_element_type=jnp.float32,
    )
    half = buckets // 2
    sides = jnp.sum(far, axis=(2, 3))
    sums = sums.at[:, half - 1].add(sides[:, 0]).at[:, buckets - 1].add(sides[:, 1])
    return jnp.transpose(sums)


normal_tail = (
    0.14372023791716726,
    0.14167152280803838,
    0.14027055919455333,
    0.02504245305870889,
    0.1831401332067321,
    -0.1813703123183242,
    0.04752538660588183,
)
tail_pole = 0.36
normal_height = 0.3989422804014327


def gelu_and_slope(values):
    density = jnp.exp(values * values * -0.5)
    inverse = 1.0 / (1.0 + tail_pole * jnp.abs(values))
    series = jnp.full_like(values, normal_tail[-1])
    for coefficient in normal_tail[-2::-1]:
        series = series * inverse + coefficient
    tail = series * inverse * density
    below = jnp.where(values > 0, 1.0 - tail, tail)
    return values * below, below + values * (density * normal_height)


def send_kernel(
    capacity_ref, route_ref, rows_ref, sent_ref, place_ref, spots_ref, scratch, *, experts, slots, chunks
):
    tokens = route_ref.shape[1]
    block = sent_ref.shape[0]
    step = pl.program_id(0)

    @pl.when(step == 0)
    def _():
        route = route_ref[...]
        names = lax.broadcasted_iota(jnp.int32, (experts, tokens), 0)
        chosen = (names == route).astype(jnp.float32)
        early = lax.broadcasted_iota(jnp.int32, (tokens, tokens), 0)
        late = lax.broadcasted_iota(jnp.int32, (tokens, tokens), 1)
        before = (early < late).astype(jnp.float32).astype(jnp.bfloat16)
        earlier = times(chosen.astype(jnp.bfloat16), before)
        slot = jnp.sum(earlier * chosen, axis=0, keepdims=True).astype(jnp.int32)
        kept = slot < capacity_ref[0]
        share = slots // chunks
        chunk = jnp.zeros_like(slot)
        for later in range(1, chunks):
            chunk = chunk + (slot >= later * share).astype(jnp.int32)
        place = chunk * (experts * share) + route * share + (slot - chunk * share)
        place = jnp.where(kept, place, -1)
        ordered = jnp.where(kept, route * slots + slot, -1)
        scratch[...] = ordered
        place_ref[...] = place
        half = spots_ref.shape[1] // 2
        both = jnp.concatenate(
            [jnp.broadcast_to(place, (half, tokens)), jnp.broadcast_to(ordered, (half, tokens))], axis=0
        )
        spots_ref[...] = jnp.transpose(both)

    places = step * block + lax.broadcasted_iota(jnp.int32, (block, tokens), 0)
    onehot = (places == scratch[...]).astype(jnp.float32).astype(jnp.bfloat16)
    sent_ref[...] = times(onehot, rows_ref[...]).astype(jnp.bfloat16)


def send_first(capacity, route_row, rows, experts, slots, chunks):
    tokens, width = rows.shape
    total = experts * slots
    block = 256
    return pl.pallas_call(
        functools.partial(send_kernel, experts=experts, slots=slots, chunks=chunks),
        grid=(total // block,),
        in_specs=[
            pl.BlockSpec(memory_space=pltpu.SMEM),
            pl.BlockSpec((1, tokens), lambda step: (0, 0)),
            pl.BlockSpec((tokens, width), lambda step: (0, 0)),
        ],
        out_specs=[
            pl.BlockSpec((block, width), lambda step: (step, 0)),
            pl.BlockSpec((1, tokens), lambda step: (0, 0)),
            pl.BlockSpec((tokens, TILE), lambda step: (0, 0)),
        ],
        out_shape=[
            jax.ShapeDtypeStruct((total, width), jnp.bfloat16),
            jax.ShapeDtypeStruct((1, tokens), jnp.int32),
            jax.ShapeDtypeStruct((tokens, TILE), jnp.int32),
        ],
        scratch_shapes=[pltpu.VMEM((1, tokens), jnp.int32)],
        compiler_params=pltpu.CompilerParams(vmem_limit_bytes=VMEM_CAP),
        name="route_and_send",
    )(capacity, route_row, rows)


def send_again_kernel(place_ref, rows_ref, sent_ref):
    block = sent_ref.shape[0]
    tokens = rows_ref.shape[0]
    places = pl.program_id(0) * block + lax.broadcasted_iota(jnp.int32, (block, tokens), 0)
    onehot = (places == place_ref[...]).astype(jnp.float32).astype(jnp.bfloat16)
    sent_ref[...] = times(onehot, rows_ref[...]).astype(jnp.bfloat16)


def send_again(place, rows, total):
    tokens, width = rows.shape
    block = 256
    return pl.pallas_call(
        send_again_kernel,
        grid=(total // block,),
        in_specs=[
            pl.BlockSpec((1, tokens), lambda step: (0, 0)),
            pl.BlockSpec((tokens, width), lambda step: (0, 0)),
        ],
        out_specs=pl.BlockSpec((block, width), lambda step: (step, 0)),
        out_shape=jax.ShapeDtypeStruct((total, width), jnp.bfloat16),
        compiler_params=pltpu.CompilerParams(vmem_limit_bytes=VMEM_CAP),
        name="send_rows",
    )(place, rows)


def expert_kernel(
    own_ref, rows_ref, ups_ref, up_ref, down_ref, router_ref, *rest, experts, piece
):
    (
        input_grad_ref, produced_ref, activated_ref, pre_grad_ref, slot_grad_ref, logit_ref, kept_ref,
    ) = rest[-7:]
    rows = rows_ref[...]
    ups = ups_ref[...]
    router = router_ref[...]
    hidden = up_ref.shape[1]
    logits = times(rows, router)
    lanes = lax.broadcasted_iota(jnp.int32, logits.shape, 1)
    logits = jnp.where(lanes < experts, logits, -jnp.inf)
    powers = jnp.exp(logits - jnp.max(logits, axis=1, keepdims=True))
    chances = powers / jnp.sum(powers, axis=1, keepdims=True)
    mine = (lanes == own_ref[0]).astype(jnp.float32)
    gate = jnp.sum(chances * mine, axis=1, keepdims=True)
    gate_grad = jnp.zeros_like(gate)
    input_grad = jnp.zeros(rows.shape, jnp.float32)
    produced = jnp.zeros(rows.shape, jnp.float32)
    for first in range(0, hidden, piece):
        span = slice(first, first + piece)
        up = up_ref[:, span]
        down = down_ref[span, :]
        activated, slope = gelu_and_slope(times(rows, up))
        activated = activated.astype(jnp.bfloat16)
        back = times_transposed(ups, down)
        gate_grad = gate_grad + jnp.sum(
            activated.astype(jnp.float32) * back, axis=1, keepdims=True
        )
        pre_grad = (back * gate * slope).astype(jnp.bfloat16)
        activated_ref[0, :, span] = activated
        pre_grad_ref[0, :, span] = pre_grad
        input_grad = input_grad + times_transposed(pre_grad, up)
        produced = produced + times(activated, down)
    logit_grad = (gate_grad * gate * (mine - chances)).astype(jnp.bfloat16)
    input_grad_ref[...] = (input_grad + times_transposed(logit_grad, router)).astype(jnp.bfloat16)
    produced_ref[...] = (produced * gate).astype(jnp.bfloat16)
    slot_grad_ref[0] = (ups.astype(jnp.float32) * gate).astype(jnp.bfloat16)
    logit_ref[0] = logit_grad
    kept_ref[0] = rows


def expert_pass(own, rows, ups, up, down, router, experts, chunk, chunks, before):
    count, width = rows.shape
    hidden = up.shape[1]
    block = 256
    lanes = router.shape[1]
    row_spec = pl.BlockSpec((block, width), lambda step: (step, 0))
    whole = lambda shape: pl.BlockSpec(shape, lambda step: (0, 0))
    kept = lambda columns: pl.BlockSpec((1, block, columns), lambda step: (chunk, step, 0))
    stacked = lambda columns: jax.ShapeDtypeStruct((chunks, count, columns), jnp.bfloat16)
    widths = (hidden, hidden, width, lanes, width)
    return pl.pallas_call(
        functools.partial(expert_kernel, experts=experts, piece=512),
        grid=(count // block,),
        in_specs=[
            pl.BlockSpec(memory_space=pltpu.SMEM),
            row_spec, row_spec,
            whole(up.shape), whole(down.shape), whole(router.shape),
        ] + [pl.BlockSpec(memory_space=pl.ANY)] * len(before),
        out_specs=[row_spec, row_spec] + [kept(columns) for columns in widths],
        out_shape=[
            jax.ShapeDtypeStruct((count, width), jnp.bfloat16),
            jax.ShapeDtypeStruct((count, width), jnp.bfloat16),
        ] + [stacked(columns) for columns in widths],
        input_output_aliases={6 + index: 2 + index for index in range(len(before))},
        compiler_params=pltpu.CompilerParams(vmem_limit_bytes=VMEM_CAP),
        cost_estimate=pl.CostEstimate(
            flops=8 * count * width * hidden,
            bytes_accessed=4 * width * hidden + 4 * count * hidden + 12 * count * width,
            transcendentals=2 * count * hidden,
        ),
        name="experts",
    )(own, rows, ups, up, down, router, *before)


def fetch_kernel(
    spots_ref, first_ref, second_ref, residual_ref, gain_ref, upstream_ref, output_ref,
    residual_grad_ref, out_grad_ref, attended_grad_ref, gain_grad_ref,
):
    target = spots_ref[:, :1]
    total = None
    for index, part in enumerate((first_ref, second_ref)):
        count = part.shape[0]
        places = index * count + lax.broadcasted_iota(jnp.int32, (target.shape[0], count), 1)
        onehot = (places == target).astype(jnp.float32).astype(jnp.bfloat16)
        term = times(onehot, part[...])
        total = term if total is None else total + term
    residual = residual_ref[...]
    inverse = lax.rsqrt(jnp.mean(residual * residual, axis=1, keepdims=True) + eps_norm)
    scaled = residual * inverse

    @pl.when(pl.program_id(0) == 0)
    def _():
        gain_grad_ref[...] = jnp.zeros_like(gain_grad_ref)

    gain_grad_ref[...] += jnp.sum((total * scaled).reshape(-1, 8, total.shape[1]), axis=0)
    weighted = total * gain_ref[...]
    spread = jnp.mean(weighted * scaled, axis=1, keepdims=True)
    residual_grad = upstream_ref[...].astype(jnp.float32) + inverse * (weighted - scaled * spread)
    residual_grad_ref[...] = residual_grad
    low = residual_grad.astype(jnp.bfloat16)
    out_grad_ref[...] = low
    attended_grad_ref[...] = times_transposed(low, output_ref[...]).astype(jnp.bfloat16)


def fetch_grads(spots, first, second, residual, gain_row, upstream, w_output):
    tokens, width = residual.shape
    block = 256
    row_spec = pl.BlockSpec((block, width), lambda step: (step, 0))
    whole = lambda shape: pl.BlockSpec(shape, lambda step: (0, 0))
    return pl.pallas_call(
        fetch_kernel,
        grid=(tokens // block,),
        in_specs=[
            pl.BlockSpec((block, TILE), lambda step: (step, 0)),
            whole(first.shape), whole(second.shape),
            row_spec, whole(gain_row.shape), row_spec, whole(w_output.shape),
        ],
        out_specs=[row_spec, row_spec, row_spec, whole((8, width))],
        out_shape=[
            jax.ShapeDtypeStruct((tokens, width), jnp.float32),
            jax.ShapeDtypeStruct((tokens, width), jnp.bfloat16),
            jax.ShapeDtypeStruct((tokens, width), jnp.bfloat16),
            jax.ShapeDtypeStruct((8, width), jnp.float32),
        ],
        compiler_params=pltpu.CompilerParams(vmem_limit_bytes=VMEM_CAP),
        name="fetch_grads",
    )(spots, first, second, residual, gain_row, upstream, w_output)


def combine_kernel(spots_ref, parts_ref, residual_ref, out_ref):
    column = spots_ref.shape[1] // 2
    target = spots_ref[:, column : column + 1]
    count = parts_ref.shape[0]
    places = lax.broadcasted_iota(jnp.int32, (target.shape[0], count), 1)
    onehot = (places == target).astype(jnp.float32).astype(jnp.bfloat16)
    out_ref[...] = (residual_ref[...] + times(onehot, parts_ref[...])).astype(jnp.bfloat16)


def combine(spots, parts, residual):
    tokens, width = residual.shape
    block = 256
    row_spec = pl.BlockSpec((block, width), lambda step: (step, 0))
    return pl.pallas_call(
        combine_kernel,
        grid=(tokens // block,),
        in_specs=[
            pl.BlockSpec((block, TILE), lambda step: (step, 0)),
            pl.BlockSpec(parts.shape, lambda step: (0, 0)),
            row_spec,
        ],
        out_specs=row_spec,
        out_shape=jax.ShapeDtypeStruct((tokens, width), jnp.bfloat16),
        compiler_params=pltpu.CompilerParams(vmem_limit_bytes=VMEM_CAP),
        name="combine",
    )(spots, parts, residual)


def swap_groups(axis, size, shift, count):
    return [
        [(index, index ^ (step << shift)) for index in range(size)] for step in range(1, count)
    ]


def sum_stages(axis_sizes):
    stages = []
    for axis, size in axis_sizes:
        shift = 0
        while (1 << shift) < size:
            count = min(4, size >> shift)
            place = (lax.axis_index(axis) >> shift) & (count - 1)
            stages.append((axis, place, swap_groups(axis, size, shift, count)))
            shift += count.bit_length() - 1
    return stages


def weight_kernel(half_ref, normed_ref, grads_ref, attended_ref, out_grad_ref, out_ref):
    step = pl.program_id(0)

    @pl.when(step == 0)
    def _():
        out_ref[...] = times(attended_ref[...], out_grad_ref[...]).astype(out_ref.dtype)

    @pl.when(step > 0)
    def _():
        out_ref[...] = times(normed_ref[...], grads_ref[0]).astype(out_ref.dtype)


def weight_terms(half, normed_t, grads, attended_t, out_grad):
    width, tokens = normed_t.shape
    matrices = grads.shape[0]
    part = width // 2
    return pl.pallas_call(
        weight_kernel,
        grid_spec=pltpu.PrefetchScalarGridSpec(
            num_scalar_prefetch=1,
            grid=(matrices + 1,),
            in_specs=[
                pl.BlockSpec((part, tokens), lambda step, half: (half[0], 0)),
                pl.BlockSpec(
                    (1, tokens, width), lambda step, half: (jnp.maximum(step - 1, 0), 0, 0)
                ),
                pl.BlockSpec((part, tokens), lambda step, half: (half[0], 0)),
                pl.BlockSpec((tokens, width), lambda step, half: (0, 0)),
            ],
            out_specs=pl.BlockSpec((part, width), lambda step, half: (step, 0)),
        ),
        out_shape=jax.ShapeDtypeStruct(((matrices + 1) * part, width), jnp.bfloat16),
        compiler_params=pltpu.CompilerParams(vmem_limit_bytes=VMEM_CAP),
        cost_estimate=pl.CostEstimate(
            flops=(matrices + 1) * tokens * width * width,
            bytes_accessed=8 * tokens * width,
            transcendentals=0,
        ),
        name="weight_terms",
    )(half, normed_t, grads, attended_t, out_grad)


def pieces_kernel(place_ref, *refs):
    out_ref = refs[-1]
    rows = refs[0].shape[0]
    for step, ref in enumerate(refs[:-1]):
        first = pl.multiple_of((place_ref[0] ^ step) * rows, 16)
        out_ref[pl.ds(first, rows), :] = ref[...]


def join_pieces(place, pieces):
    rows, width = pieces[0].shape
    return pl.pallas_call(
        pieces_kernel,
        in_specs=[pl.BlockSpec(memory_space=pltpu.SMEM)]
        + [pl.BlockSpec(memory_space=pltpu.VMEM)] * len(pieces),
        out_specs=pl.BlockSpec(memory_space=pltpu.VMEM),
        out_shape=jax.ShapeDtypeStruct((len(pieces) * rows, width), pieces[0].dtype),
        compiler_params=pltpu.CompilerParams(vmem_limit_bytes=VMEM_CAP),
        name="join_pieces",
    )(place.reshape(1).astype(jnp.int32), *pieces)


def finish_kernel(
    half_ref, own_ref, other_ref, query_ref, key_ref, value_ref,
    output_out, query_out, key_out, value_out, gain_out, small_out,
):
    width = query_ref.shape[1]
    part = width // 2
    small = small_out.shape[0]
    weights = (None, query_ref, key_ref, value_ref)
    outs = (output_out, query_out, key_out, value_out)
    for half, ref in ((half_ref[0], own_ref), (1 - half_ref[0], other_ref)):
        rows = pl.ds(pl.multiple_of(half * part, 16), part)
        gain = None
        for index, (weight, out) in enumerate(zip(weights, outs)):
            total = ref[index * part : (index + 1) * part, :].astype(jnp.float32)
            out[rows, :] = total
            if weight is None:
                continue
            term = jnp.sum(total * weight[rows, :].astype(jnp.float32), axis=1, keepdims=True)
            gain = term if gain is None else gain + term
        gain_out[rows, :] = jnp.broadcast_to(gain, (part, gain_out.shape[1]))
    first = len(outs) * part
    small_out[...] = own_ref[first : first + small, :].astype(jnp.float32) + other_ref[
        first : first + small, :
    ].astype(jnp.float32)


def finish(half, own, other, weights, small):
    width = weights[0].shape[1]
    square = jax.ShapeDtypeStruct((width, width), jnp.float32)
    vmem = pl.BlockSpec(memory_space=pltpu.VMEM)
    return pl.pallas_call(
        finish_kernel,
        in_specs=[pl.BlockSpec(memory_space=pltpu.SMEM)] + [vmem] * 5,
        out_specs=[vmem] * 6,
        out_shape=[
            square, square, square, square,
            jax.ShapeDtypeStruct((width, TILE), jnp.float32),
            jax.ShapeDtypeStruct((small, width), jnp.float32),
        ],
        compiler_params=pltpu.CompilerParams(vmem_limit_bytes=VMEM_CAP),
        name="finish",
    )(half, own, other, *weights)


def hidden_kernel(
    grads_ref, query_ref, key_ref, value_ref, hidden_ref, gain_ref, residual_grad_ref, out_ref
):
    total = None
    for index, weight in enumerate((query_ref, key_ref, value_ref)):
        term = times_transposed(grads_ref[index], weight[...])
        total = term if total is None else total + term
    hidden = hidden_ref[...].astype(jnp.float32)
    inverse = lax.rsqrt(jnp.mean(hidden * hidden, axis=1, keepdims=True) + eps_norm)
    scaled = hidden * inverse
    weighted = total * gain_ref[...]
    spread = jnp.mean(weighted * scaled, axis=1, keepdims=True)
    out_ref[...] = (residual_grad_ref[...] + inverse * (weighted - scaled * spread)).astype(
        jnp.bfloat16
    )


def hidden_gradient(grads, weights, hidden, gain_row, residual_grad):
    tokens, width = hidden.shape
    block = 256
    row_spec = pl.BlockSpec((block, width), lambda step: (step, 0))
    whole = lambda shape: pl.BlockSpec(shape, lambda step: (0, 0))
    return pl.pallas_call(
        hidden_kernel,
        grid=(tokens // block,),
        in_specs=[pl.BlockSpec((3, block, width), lambda step: (0, step, 0))]
        + [whole(weight.shape) for weight in weights]
        + [row_spec, whole(gain_row.shape), row_spec],
        out_specs=row_spec,
        out_shape=jax.ShapeDtypeStruct((tokens, width), jnp.bfloat16),
        compiler_params=pltpu.CompilerParams(vmem_limit_bytes=VMEM_CAP),
        cost_estimate=pl.CostEstimate(
            flops=6 * tokens * width * width, bytes_accessed=20 * tokens * width, transcendentals=0
        ),
        name="hidden_gradient",
    )(grads, *weights, hidden, gain_row, residual_grad)


def scatter_stage(terms, stage):
    axis, place, swaps = stage
    pieces = terms.reshape(len(swaps) + 1, -1, terms.shape[1])
    total = lax.dynamic_index_in_dim(pieces, place, 0, keepdims=False)
    got = []
    for step, pairs in enumerate(swaps, 1):
        piece = lax.dynamic_index_in_dim(pieces, place ^ step, 0, keepdims=False)
        got.append(lax.ppermute(piece.astype(jnp.bfloat16), axis, pairs))
    for part in got:
        total = total + part.astype(jnp.float32)
    return total


def gather_stage(low, stage):
    axis, place, swaps = stage
    return join_pieces(place, [low] + [lax.ppermute(low, axis, pairs) for pairs in swaps])


def on_device(
    hidden_in,
    first_gain,
    w_query,
    w_key,
    w_value,
    w_output,
    rel_table,
    second_gain,
    router,
    expert_up,
    expert_down,
    routes,
    capacity_factor,
    cotangent,
):
    axes = ("narrow", "wide")
    chunks = 2
    tokens, width = hidden_in.shape
    bucket_count = rel_table.shape[0]
    experts = router.shape[1]
    slots = 2 * tokens // experts
    capacity = capacity_factor * tokens // experts
    devices = lax.axis_size(axes)
    own = lax.axis_index(axes).astype(jnp.int32).reshape(1)
    padded = -(-experts // TILE) * TILE
    router_wide = jnp.pad(router, ((0, 0), (0, padded - experts)))

    def exchange(rows):
        blocks = rows.reshape(experts, -1, width)
        return lax.all_to_all(blocks, axes, split_axis=0, concat_axis=0, tiled=True).reshape(
            -1, width
        )

    def chunk_order(rows):
        return jnp.swapaxes(rows.reshape(experts, chunks, -1, width), 0, 1).reshape(chunks, -1, width)

    def expert_order(rows):
        return jnp.swapaxes(rows.reshape(chunks, experts, -1, width), 0, 1).reshape(-1, width)

    together = lax.optimization_barrier
    sent_ups, place, spots = send_first(
        capacity, routes.reshape(1, tokens), cotangent, experts, slots, chunks
    )
    sent_ups, hidden_in = together((sent_ups, hidden_in))
    ups = exchange(sent_ups)

    band, edges = bias_band(rel_table)
    hidden = hidden_in.astype(jnp.float32)
    gain_one = first_gain.astype(jnp.float32)
    gain_two = second_gain.astype(jnp.float32)
    inverse_one = lax.rsqrt(jnp.mean(hidden * hidden, axis=-1, keepdims=True) + eps_norm)
    normed_first = (hidden * inverse_one * gain_one).astype(jnp.bfloat16)
    queries = times(normed_first, w_query).astype(jnp.bfloat16)
    keys = times(normed_first, w_key).astype(jnp.bfloat16)
    values = times(normed_first, w_value).astype(jnp.bfloat16)
    attended, logs = attend(queries, keys, values, band, edges)
    residual = hidden + times(attended, w_output)
    inverse_two = lax.rsqrt(jnp.mean(residual * residual, axis=-1, keepdims=True) + eps_norm)
    normed_second = (residual * inverse_two * gain_two).astype(jnp.bfloat16)
    sent_rows = send_again(place, normed_second, experts * slots)
    sent_rows, ups = together((sent_rows, ups))
    half = experts * slots // chunks
    rows = []
    for c in range(chunks):
        sent = sent_rows[c * half : (c + 1) * half]
        if rows:
            sent, rows[-1] = together((sent, rows[-1]))
        rows.append(exchange(sent))
    ups = chunk_order(ups)

    saved = ()
    input_grads, produced = [], []
    for c in range(chunks):
        input_grad, output, *saved = expert_pass(
            own, rows[c], ups[c], expert_up[0], expert_down[0], router_wide, experts, c, chunks, saved
        )
        if c + 1 < chunks:
            input_grad, rows[-1] = together((input_grad, rows[-1]))
        if input_grads:
            input_grad, input_grads[-1] = together((input_grad, input_grads[-1]))
        input_grads.append(exchange(input_grad))
        produced.append(output)
    activated, pre_grad, slot_grad, logit_grad, kept_rows = [
        array.reshape(-1, array.shape[-1]) for array in saved
    ]
    gradient_expert_down = inner_rows(activated, slot_grad)[None]
    gradient_expert_up = inner_rows(kept_rows, pre_grad)[None]
    router_terms = inner_rows(logit_grad, kept_rows)[:experts]

    normed_t, attended_t = jnp.transpose(normed_first), jnp.transpose(attended)
    input_grads[-1], gradient_expert_down, gradient_expert_up, router_terms, normed_t, attended_t = together(
        (
            input_grads[-1], gradient_expert_down, gradient_expert_up, router_terms, normed_t,
            attended_t,
        )
    )
    residual_grad, out_grad, attended_grad, gain_terms = fetch_grads(
        spots, *input_grads, residual, gain_two[None], cotangent, w_output
    )
    produced = expert_order(jnp.concatenate(produced, axis=0))
    produced, attended_grad = together((produced, attended_grad))
    produced = exchange(produced)
    grads, near, far = attend_back(
        queries, keys, values, attended_grad, attended, logs, band, edges
    )
    weights = (w_query, w_key, w_value)
    core = lax.axis_index("narrow").astype(jnp.int32).reshape(1)
    swap = [(0, 1), (1, 0)]
    away = weight_terms(1 - core, normed_t, grads, attended_t, out_grad)
    got = lax.ppermute(away, "narrow", swap)
    kept = weight_terms(core, normed_t, grads, attended_t, out_grad)
    share = 16 * lax.axis_size("wide")
    used = 8 + experts + bucket_count
    table_terms = table_gradient(near, far, bucket_count)
    small = jnp.concatenate(
        [
            gain_terms,
            router_terms,
            jnp.pad(table_terms, ((0, 0), (0, width - table_terms.shape[1]))),
            jnp.zeros((-(kept.shape[0] + used) % share, width), jnp.float32),
        ],
        axis=0,
    )
    grads, kept = together((grads, kept))
    gradient_hidden = hidden_gradient(grads, weights, hidden_in, gain_one[None], residual_grad)
    terms = jnp.concatenate([kept.astype(jnp.float32) + got.astype(jnp.float32), small], axis=0)
    stages = sum_stages([("wide", lax.axis_size("wide"))])
    for stage in stages:
        terms = scatter_stage(terms, stage)
        if stage is stages[0]:
            terms, gradient_hidden = together((terms, gradient_hidden))
    low = terms.astype(jnp.bfloat16)
    for stage in reversed(stages):
        if stage is stages[0]:
            low, produced = together((low, produced))
            block_out = combine(spots, produced, residual)
        low = gather_stage(low, stage)
    low, block_out = together((low, block_out))
    other = lax.ppermute(low, "narrow", swap)
    gradient_output, gradient_query, gradient_key, gradient_value, first_terms, small = finish(
        core, low, other, weights, used
    )
    gradient_second_gain = jnp.sum(small[:8], axis=0)
    gradient_router = jnp.transpose(small[8 : 8 + experts])
    gradient_table = small[8 + experts :, : rel_table.shape[1]]
    return (
        block_out,
        gradient_hidden,
        first_terms[:, 0] / gain_one,
        gradient_query,
        gradient_key,
        gradient_value,
        gradient_output,
        gradient_table,
        gradient_second_gain,
        gradient_router,
        gradient_expert_up,
        gradient_expert_down,
    )


def solution(mesh):
    split = ("narrow", "wide")
    rows, experts = P(split, None), P(split, None, None)
    return jax.shard_map(
        on_device,
        mesh=mesh,
        in_specs=(rows,) + (P(),) * 8 + (experts, experts, rows, P(split), rows),
        out_specs=(rows, rows) + (P(),) * 8 + (experts, experts),
        check_vma=False,
    )
```

```python
import functools

import jax
import jax.numpy as jnp
from jax import lax
from jax.experimental import pallas as pl
from jax.experimental.pallas import tpu as pltpu
from jax.sharding import PartitionSpec as P

TILE = 128
STRIP = 256
VMEM_CAP = 60 * 1024 * 1024
eps_norm = 1e-06
bucket_edges = (12, 16, 23, 32, 46, 64, 91)


def bucket_of(offset):
    distance = jnp.abs(offset)
    far_bucket = jnp.full(distance.shape, 8, jnp.int32)
    for edge in bucket_edges:
        far_bucket = far_bucket + (distance >= edge).astype(jnp.int32)
    near_bucket = jnp.where(distance < 8, distance, far_bucket)
    return near_bucket + 16 * (offset > 0).astype(jnp.int32)


def band_buckets():
    rows = lax.broadcasted_iota(jnp.int32, (3 * TILE, TILE), 0)
    lanes = lax.broadcasted_iota(jnp.int32, (3 * TILE, TILE), 1)
    return bucket_of(rows - TILE - lanes)


def times_transposed(left, right):
    return lax.dot_general(
        left, right, (((1,), (1,)), ((), ())), preferred_element_type=jnp.float32
    )


def inner_rows(left, right):
    return lax.dot_general(
        left, right, (((0,), (0,)), ((), ())), preferred_element_type=jnp.float32
    )


def times(left, right):
    return jnp.dot(left, right, preferred_element_type=jnp.float32)


def fill_wide(edge_ref, band_ref, wide):
    length = (wide.shape[1] + TILE) // 2
    pair = pl.program_id(0)
    for side in range(2):
        head = 2 * pair + side
        wide[side, : length - 2 * TILE] = jnp.full(
            (length - 2 * TILE, TILE), edge_ref[head, 0], jnp.float32
        )
        wide[side, length - 2 * TILE : length + TILE] = band_ref[side]
        wide[side, length + TILE :] = jnp.full(
            (length - 2 * TILE, TILE), edge_ref[head, 1], jnp.float32
        )


def strip_bias(wide, side, key_start, keys, query_start):
    length = (wide.shape[1] + TILE) // 2
    parts = []
    for start in range(query_start, query_start + STRIP, TILE):
        first = length - TILE - start + key_start
        parts.append(wide[side, first : first + keys, :])
    return jnp.concatenate(parts, axis=1)


def half_of(rows, side):
    half = rows.shape[1] // 2
    lanes = lax.broadcasted_iota(jnp.int32, rows.shape, 1)
    own = lanes < half if side == 0 else lanes >= half
    return jnp.where(own, rows, jnp.zeros_like(rows))


def attend_kernel(
    edge_ref, q_ref, k_ref, v_ref, band_ref, out_ref, turned_ref, log_ref, wide
):
    length = q_ref.shape[0]
    half = q_ref.shape[1] // 2
    scale = half ** (-0.5)
    fill_wide(edge_ref, band_ref, wide)
    keys = k_ref[...]
    values_t = jnp.transpose(v_ref[...])
    for start in range(0, length, STRIP):
        mixed = []
        for side in range(2):
            query = half_of(q_ref[start : start + STRIP, :] * scale, side)
            scores = times_transposed(keys, query) + strip_bias(wide, side, 0, length, start)
            top = jnp.max(scores, axis=0, keepdims=True)
            powers = jnp.exp(scores - top)
            total = jnp.sum(powers, axis=0, keepdims=True)
            raw = times(values_t[side * half : (side + 1) * half], powers.astype(jnp.bfloat16))
            mixed.append(raw / total)
            log_ref[0, side : side + 1, start : start + STRIP] = top + jnp.log(total)
        both = jnp.concatenate(mixed, axis=0)
        out_ref[start : start + STRIP, :] = jnp.transpose(both).astype(jnp.bfloat16)
        turned_ref[:, start : start + STRIP] = both.astype(jnp.bfloat16)


def attend(queries, keys, values, band, edges):
    length, width = queries.shape
    heads = edges.shape[0]
    pairs = heads // 2
    columns = width // pairs
    part = pl.BlockSpec((length, columns), lambda pair: (0, pair))
    return pl.pallas_call(
        attend_kernel,
        grid=(pairs,),
        in_specs=[
            pl.BlockSpec(memory_space=pltpu.SMEM),
            part,
            part,
            part,
            pl.BlockSpec((2, 3 * TILE, TILE), lambda pair: (pair, 0, 0)),
        ],
        out_specs=[
            part,
            pl.BlockSpec((columns, length), lambda pair: (pair, 0)),
            pl.BlockSpec((1, 2, length), lambda pair: (pair, 0, 0)),
        ],
        out_shape=[
            jax.ShapeDtypeStruct((length, width), jnp.bfloat16),
            jax.ShapeDtypeStruct((width, length), jnp.bfloat16),
            jax.ShapeDtypeStruct((pairs, 2, length), jnp.float32),
        ],
        scratch_shapes=[pltpu.VMEM((2, 2 * length - TILE, TILE), jnp.float32)],
        compiler_params=pltpu.CompilerParams(vmem_limit_bytes=VMEM_CAP),
        cost_estimate=pl.CostEstimate(
            flops=4 * heads * length * length * (width // heads),
            bytes_accessed=8 * length * width,
            transcendentals=heads * length * length,
        ),
        name="attend",
    )(edges, queries, keys, values, band)


def weights_kernel(
    edge_ref, q_ref, k_ref, log_ref, band_ref, normed_ref, weights_ref, turned_ref, wide
):
    length = q_ref.shape[0]
    scale = (q_ref.shape[1] // 2) ** (-0.5)
    fill_wide(edge_ref, band_ref, wide)
    keys = k_ref[...]
    turned_ref[...] = jnp.transpose(normed_ref[...])
    for start in range(0, length, STRIP):
        strip = slice(start, start + STRIP)
        for side in range(2):
            query = half_of(q_ref[strip, :] * scale, side)
            bias = strip_bias(wide, side, 0, length, start)
            scores = times_transposed(keys, query) + bias
            weights_ref[side, :, strip] = jnp.exp(
                scores - log_ref[0, side : side + 1, strip]
            ).astype(jnp.bfloat16)


def attend_weights(queries, keys, logs, band, edges, normed):
    length, width = queries.shape
    heads = edges.shape[0]
    pairs = heads // 2
    columns = width // pairs
    part = pl.BlockSpec((length, columns), lambda pair: (0, pair))
    return pl.pallas_call(
        weights_kernel,
        grid=(pairs,),
        in_specs=[
            pl.BlockSpec(memory_space=pltpu.SMEM),
            part,
            part,
            pl.BlockSpec((1, 2, length), lambda pair: (pair, 0, 0)),
            pl.BlockSpec((2, 3 * TILE, TILE), lambda pair: (pair, 0, 0)),
            part,
        ],
        out_specs=[
            pl.BlockSpec((2, length, length), lambda pair: (pair, 0, 0)),
            pl.BlockSpec((columns, length), lambda pair: (pair, 0)),
        ],
        out_shape=[
            jax.ShapeDtypeStruct((heads, length, length), jnp.bfloat16),
            jax.ShapeDtypeStruct((width, length), jnp.bfloat16),
        ],
        scratch_shapes=[pltpu.VMEM((2, 2 * length - TILE, TILE), jnp.float32)],
        compiler_params=pltpu.CompilerParams(vmem_limit_bytes=VMEM_CAP),
        cost_estimate=pl.CostEstimate(
            flops=2 * heads * length * length * (width // heads),
            bytes_accessed=4 * length * width + 2 * heads * length * length,
            transcendentals=heads * length * length,
        ),
        name="attend_weights",
    )(edges, queries, keys, logs, band, normed)


def diagonal_sums(near_ref, side, beyond):
    span = 4 * TILE
    zeros = jnp.zeros((8, span - TILE), jnp.float32)
    total = jnp.zeros((8, span), jnp.float32)
    for row in range(0, 3 * TILE, 8):
        wide = jnp.concatenate([near_ref[side, row : row + 8, :], zeros], axis=1)
        total = total + pltpu.roll(wide, 3 * TILE - 1 - row, 1)
    rows = lax.broadcasted_iota(jnp.int32, total.shape, 0)
    for bit in (1, 2, 4):
        total = jnp.where((rows & bit) != 0, pltpu.roll(total, span - bit, 1), total)
    sums = jnp.sum(total, axis=0, keepdims=True)
    lanes = lax.broadcasted_iota(jnp.int32, sums.shape, 1)
    sums = sums + jnp.where(lanes == span - 2, beyond[0], 0.0)
    return sums + jnp.where(lanes == 0, beyond[1], 0.0)


def attend_back_kernel(
    core_ref, q_ref, k_ref, v_ref, grad_ref, out_ref, weights_ref, normed_ref,
    grads_ref, away_ref, kept_ref, sums_ref,
    near_ref, key_total, value_total, square,
):
    length = q_ref.shape[0]
    half = q_ref.shape[1] // 2
    blocks = length // TILE
    scale = half ** (-0.5)
    keys_t = jnp.transpose(k_ref[...])
    products = jnp.transpose(grad_ref[...].astype(jnp.float32) * out_ref[...].astype(jnp.float32))
    names = lax.broadcasted_iota(jnp.int32, (2 * blocks, length), 0)
    owners = lax.broadcasted_iota(jnp.int32, (2 * blocks, length), 1) // TILE
    picks = (names == owners).astype(jnp.float32).astype(jnp.bfloat16)
    near_ref[...] = jnp.zeros_like(near_ref)
    query_parts = []
    for side in range(2):
        rows = slice(side * half, (side + 1) * half)
        query = half_of(q_ref[...] * scale, side)
        grad = half_of(grad_ref[...], side)
        center = jnp.sum(products[rows], axis=0, keepdims=True)
        left = jnp.concatenate([keys_t[rows], picks], axis=0)
        total = None
        for first in range(0, length, STRIP):
            block = slice(first, first + STRIP)
            weights = weights_ref[side, block, :]
            weight_grad = times_transposed(v_ref[block, :], grad)
            score_grad = weights.astype(jnp.float32) * (weight_grad - center)
            score_low = score_grad.astype(jnp.bfloat16)
            value_term = times(weights, grad)
            key_term = times(score_low, query)
            if side == 0:
                value_total[block, :] = value_term
                key_total[block, :] = key_term
            else:
                value_total[block, :] += value_term
                key_total[block, :] += key_term
            term = times(left[:, block], score_low)
            total = term if total is None else total + term
            for row in range(0, STRIP, TILE):
                for lane in range(0, length, TILE):
                    apart = (first + row - lane) // TILE
                    if abs(apart) <= 1:
                        spot = (apart + 1) * TILE
                        near_ref[side, spot : spot + TILE, :] += score_grad[
                            row : row + TILE, lane : lane + TILE
                        ]
        query_parts.append(total[:half] * scale)
        sums = total[half:]
        beyond = [
            jnp.sum(jnp.where(keep, sums, 0.0), keepdims=True)
            for keep in (names <= owners - 2, names >= owners + 2)
        ]
        sums_ref[0, side : side + 1, :] = diagonal_sums(near_ref, side, beyond)
    both = jnp.concatenate(query_parts, axis=0)
    grads_ref[0] = jnp.transpose(both).astype(jnp.bfloat16)
    grads_ref[1] = key_total[...].astype(jnp.bfloat16)
    grads_ref[2] = value_total[...].astype(jnp.bfloat16)
    part = normed_ref.shape[0] // 2
    columns = q_ref.shape[1]
    stacked = jnp.concatenate([grads_ref[index] for index in range(3)], axis=1)
    square[...] = times(normed_ref[...], stacked)
    away = pl.ds(pl.multiple_of((1 - core_ref[0]) * part, 16), part)
    kept = pl.ds(pl.multiple_of(core_ref[0] * part, 16), part)
    for index in range(3):
        span = slice(index * columns, (index + 1) * columns)
        away_ref[index] = square[away, span].astype(jnp.bfloat16)
        kept_ref[index] = square[kept, span].astype(jnp.bfloat16)


def attend_back(core, queries, keys, values, grads, attended, weights, normed_t):
    length, width = queries.shape
    heads = weights.shape[0]
    pairs = heads // 2
    columns = width // pairs
    part = pl.BlockSpec((length, columns), lambda pair: (0, pair))
    square = pl.BlockSpec((3, width // 2, columns), lambda pair: (0, 0, pair))
    return pl.pallas_call(
        attend_back_kernel,
        grid=(pairs,),
        in_specs=[
            pl.BlockSpec(memory_space=pltpu.SMEM),
            part, part, part, part, part,
            pl.BlockSpec((2, length, length), lambda pair: (pair, 0, 0)),
            pl.BlockSpec((width, length), lambda pair: (0, 0)),
        ],
        out_specs=[
            pl.BlockSpec((3, length, columns), lambda pair: (0, 0, pair)),
            square, square,
            pl.BlockSpec((1, 2, 4 * TILE), lambda pair: (pair, 0, 0)),
        ],
        out_shape=[
            jax.ShapeDtypeStruct((3, length, width), jnp.bfloat16),
            jax.ShapeDtypeStruct((3, width // 2, width), jnp.bfloat16),
            jax.ShapeDtypeStruct((3, width // 2, width), jnp.bfloat16),
            jax.ShapeDtypeStruct((pairs, 2, 4 * TILE), jnp.float32),
        ],
        scratch_shapes=[
            pltpu.VMEM((2, 3 * TILE, TILE), jnp.float32),
            pltpu.VMEM((length, columns), jnp.float32),
            pltpu.VMEM((length, columns), jnp.float32),
            pltpu.VMEM((width, 3 * columns), jnp.float32),
        ],
        compiler_params=pltpu.CompilerParams(vmem_limit_bytes=VMEM_CAP),
        cost_estimate=pl.CostEstimate(
            flops=10 * heads * length * length * (width // heads),
            bytes_accessed=16 * length * width + 2 * heads * length * length,
            transcendentals=0,
        ),
        name="attend_back",
    )(core, queries, keys, values, grads, attended, weights, normed_t)


def bias_band(rel_table):
    buckets, heads = rel_table.shape
    labels = band_buckets().reshape(1, -1)
    onehot = (labels == jnp.arange(buckets, dtype=jnp.int32)[:, None]).astype(jnp.bfloat16)
    band = lax.dot_general(
        rel_table, onehot, (((0,), (0,)), ((), ())), preferred_element_type=jnp.float32
    )
    half = buckets // 2
    edges = jnp.stack([rel_table[half - 1], rel_table[buckets - 1]], axis=1).astype(jnp.float32)
    return band.reshape(heads, 3 * TILE, TILE), edges


def table_gradient(sums, buckets):
    span = sums.shape[2]
    labels = bucket_of(2 * TILE - 1 - jnp.arange(span, dtype=jnp.int32))
    onehot = (labels[None, :] == jnp.arange(buckets, dtype=jnp.int32)[:, None]).astype(jnp.float32)
    return lax.dot_general(
        onehot, sums.reshape(-1, span), (((1,), (1,)), ((), ())),
        precision=lax.Precision.HIGHEST, preferred_element_type=jnp.float32,
    )


normal_tail = (
    0.14372023791716726,
    0.14167152280803838,
    0.14027055919455333,
    0.02504245305870889,
    0.1831401332067321,
    -0.1813703123183242,
    0.04752538660588183,
)
tail_pole = 0.36
normal_height = 0.3989422804014327


def gelu_and_slope(values):
    density = jnp.exp(values * values * -0.5)
    inverse = 1.0 / (1.0 + tail_pole * jnp.abs(values))
    series = jnp.full_like(values, normal_tail[-1])
    for coefficient in normal_tail[-2::-1]:
        series = series * inverse + coefficient
    tail = series * inverse * density
    below = jnp.where(values > 0, 1.0 - tail, tail)
    return values * below, below + values * (density * normal_height)


def send_kernel(
    capacity_ref, route_ref, rows_ref, sent_ref, place_ref, spots_ref, scratch, *, experts, slots, chunks
):
    tokens = route_ref.shape[1]
    block = sent_ref.shape[0]
    step = pl.program_id(0)

    @pl.when(step == 0)
    def _():
        route = route_ref[...]
        names = lax.broadcasted_iota(jnp.int32, (experts, tokens), 0)
        chosen = (names == route).astype(jnp.float32)
        early = lax.broadcasted_iota(jnp.int32, (tokens, tokens), 0)
        late = lax.broadcasted_iota(jnp.int32, (tokens, tokens), 1)
        before = (early < late).astype(jnp.float32).astype(jnp.bfloat16)
        earlier = times(chosen.astype(jnp.bfloat16), before)
        slot = jnp.sum(earlier * chosen, axis=0, keepdims=True).astype(jnp.int32)
        kept = slot < capacity_ref[0]
        share = slots // chunks
        chunk = jnp.zeros_like(slot)
        for later in range(1, chunks):
            chunk = chunk + (slot >= later * share).astype(jnp.int32)
        place = chunk * (experts * share) + route * share + (slot - chunk * share)
        place = jnp.where(kept, place, -1)
        ordered = jnp.where(kept, route * slots + slot, -1)
        scratch[...] = ordered
        place_ref[...] = place
        half = spots_ref.shape[1] // 2
        both = jnp.concatenate(
            [jnp.broadcast_to(place, (half, tokens)), jnp.broadcast_to(ordered, (half, tokens))], axis=0
        )
        spots_ref[...] = jnp.transpose(both)

    places = step * block + lax.broadcasted_iota(jnp.int32, (block, tokens), 0)
    onehot = (places == scratch[...]).astype(jnp.float32).astype(jnp.bfloat16)
    sent_ref[...] = times(onehot, rows_ref[...]).astype(jnp.bfloat16)


def send_first(capacity, route_row, rows, experts, slots, chunks):
    tokens, width = rows.shape
    total = experts * slots
    block = 256
    return pl.pallas_call(
        functools.partial(send_kernel, experts=experts, slots=slots, chunks=chunks),
        grid=(total // block,),
        in_specs=[
            pl.BlockSpec(memory_space=pltpu.SMEM),
            pl.BlockSpec((1, tokens), lambda step: (0, 0)),
            pl.BlockSpec((tokens, width), lambda step: (0, 0)),
        ],
        out_specs=[
            pl.BlockSpec((block, width), lambda step: (step, 0)),
            pl.BlockSpec((1, tokens), lambda step: (0, 0)),
            pl.BlockSpec((tokens, TILE), lambda step: (0, 0)),
        ],
        out_shape=[
            jax.ShapeDtypeStruct((total, width), jnp.bfloat16),
            jax.ShapeDtypeStruct((1, tokens), jnp.int32),
            jax.ShapeDtypeStruct((tokens, TILE), jnp.int32),
        ],
        scratch_shapes=[pltpu.VMEM((1, tokens), jnp.int32)],
        compiler_params=pltpu.CompilerParams(vmem_limit_bytes=VMEM_CAP),
        name="route_and_send",
    )(capacity, route_row, rows)


def send_again_kernel(place_ref, rows_ref, sent_ref, *, first):
    block = sent_ref.shape[0]
    tokens = rows_ref.shape[0]
    start = first + pl.program_id(0) * block
    places = start + lax.broadcasted_iota(jnp.int32, (block, tokens), 0)
    onehot = (places == place_ref[...]).astype(jnp.float32).astype(jnp.bfloat16)
    sent_ref[...] = times(onehot, rows_ref[...]).astype(jnp.bfloat16)


def send_again(place, rows, first, count):
    tokens, width = rows.shape
    block = 512
    return pl.pallas_call(
        functools.partial(send_again_kernel, first=first),
        grid=(count // block,),
        in_specs=[
            pl.BlockSpec((1, tokens), lambda step: (0, 0)),
            pl.BlockSpec((tokens, width), lambda step: (0, 0)),
        ],
        out_specs=pl.BlockSpec((block, width), lambda step: (step, 0)),
        out_shape=jax.ShapeDtypeStruct((count, width), jnp.bfloat16),
        compiler_params=pltpu.CompilerParams(vmem_limit_bytes=VMEM_CAP),
        cost_estimate=pl.CostEstimate(
            flops=2 * count * tokens * width,
            bytes_accessed=2 * (count + tokens) * width,
            transcendentals=0,
        ),
        name="send_rows",
    )(place, rows)


def expert_kernel(
    own_ref, rows_ref, ups_ref, up_ref, down_ref, router_ref, *rest, experts, piece
):
    (
        input_grad_ref, router_grad_ref, produced_ref, activated_ref, pre_grad_ref, slot_grad_ref,
        kept_ref,
    ) = rest[-7:]
    rows = rows_ref[...]
    ups = ups_ref[...].astype(jnp.float32).reshape(rows.shape)
    low_ups = ups.astype(jnp.bfloat16)
    router = router_ref[...]
    hidden = up_ref.shape[1]
    logits = times(rows, router)
    lanes = lax.broadcasted_iota(jnp.int32, logits.shape, 1)
    logits = jnp.where(lanes < experts, logits, -jnp.inf)
    powers = jnp.exp(logits - jnp.max(logits, axis=1, keepdims=True))
    chances = powers / jnp.sum(powers, axis=1, keepdims=True)
    mine = (lanes == own_ref[0]).astype(jnp.float32)
    gate = jnp.sum(chances * mine, axis=1, keepdims=True)
    gate_grad = jnp.zeros_like(gate)
    input_grad = jnp.zeros(rows.shape, jnp.float32)
    produced = jnp.zeros(rows.shape, jnp.float32)
    for first in range(0, hidden, piece):
        span = slice(first, first + piece)
        up = up_ref[:, span]
        down = down_ref[span, :]
        activated, slope = gelu_and_slope(times(rows, up))
        activated = activated.astype(jnp.bfloat16)
        back = times_transposed(low_ups, down)
        gate_grad = gate_grad + jnp.sum(
            activated.astype(jnp.float32) * back, axis=1, keepdims=True
        )
        pre_grad = (back * gate * slope).astype(jnp.bfloat16)
        activated_ref[0, :, span] = activated
        pre_grad_ref[0, :, span] = pre_grad
        input_grad = input_grad + times_transposed(pre_grad, up)
        produced = produced + times(activated, down)
    logit_grad = gate_grad * gate * (mine - chances)
    low_logit = logit_grad.astype(jnp.bfloat16)
    input_grad_ref[...] = (input_grad + times_transposed(low_logit, router)).astype(jnp.bfloat16)
    produced_ref[...] = (produced * gate).reshape(produced_ref.shape).astype(jnp.bfloat16)
    slot_grad_ref[0] = (ups * gate).astype(jnp.bfloat16)
    kept_ref[0] = rows

    @pl.when(pl.program_id(0) == 0)
    def _():
        router_grad_ref[...] = jnp.zeros_like(router_grad_ref)

    router_grad_ref[...] += times(jnp.transpose(logit_grad).astype(jnp.bfloat16), rows)


def expert_pass(own, rows, ups, up, down, router, experts, chunk, before):
    count, width = rows.shape
    groups, chunks, half = ups.shape[:3]
    hidden = up.shape[1]
    block = 256
    lanes = router.shape[1]
    row_spec = pl.BlockSpec((block, width), lambda step: (step, 0))
    whole = lambda shape: pl.BlockSpec(shape, lambda step: (0, 0))
    kept = lambda columns: pl.BlockSpec((1, block, columns), lambda step: (chunk, step, 0))
    stacked = lambda columns: jax.ShapeDtypeStruct((chunks, count, columns), jnp.bfloat16)
    slot_spec = pl.BlockSpec((block // half, 1, half, width), lambda step: (step, chunk, 0, 0))
    widths = (hidden, hidden, width, width)
    return pl.pallas_call(
        functools.partial(expert_kernel, experts=experts, piece=512),
        grid=(count // block,),
        in_specs=[
            pl.BlockSpec(memory_space=pltpu.SMEM),
            row_spec, slot_spec,
            whole(up.shape), whole(down.shape), whole(router.shape),
        ] + [pl.BlockSpec(memory_space=pl.ANY)] * len(before),
        out_specs=[row_spec, whole((lanes, width)), slot_spec]
        + [kept(columns) for columns in widths],
        out_shape=[
            jax.ShapeDtypeStruct((count, width), jnp.bfloat16),
            jax.ShapeDtypeStruct((lanes, width), jnp.float32),
            jax.ShapeDtypeStruct((groups, chunks, half, width), jnp.bfloat16),
        ] + [stacked(columns) for columns in widths],
        input_output_aliases={6 + index: 2 + index for index in range(len(before))},
        compiler_params=pltpu.CompilerParams(vmem_limit_bytes=VMEM_CAP),
        cost_estimate=pl.CostEstimate(
            flops=8 * count * width * hidden,
            bytes_accessed=4 * width * hidden + 4 * count * hidden + 12 * count * width,
            transcendentals=2 * count * hidden,
        ),
        name="experts",
    )(own, rows, ups, up, down, router, *before)


def spread_rows(spots_ref, part_ref, first):
    target = spots_ref[:, :1]
    count = part_ref.shape[0]
    places = first + lax.broadcasted_iota(jnp.int32, (target.shape[0], count), 1)
    onehot = (places == target).astype(jnp.float32).astype(jnp.bfloat16)
    return times(onehot, part_ref[...])


def fetch_first_kernel(spots_ref, part_ref, out_ref):
    out_ref[...] = spread_rows(spots_ref, part_ref, 0).astype(jnp.bfloat16)


def fetch_first(spots, part):
    tokens = spots.shape[0]
    count, width = part.shape
    block = 256
    return pl.pallas_call(
        fetch_first_kernel,
        grid=(tokens // block,),
        in_specs=[
            pl.BlockSpec((block, TILE), lambda step: (step, 0)),
            pl.BlockSpec((count, width), lambda step: (0, 0)),
        ],
        out_specs=pl.BlockSpec((block, width), lambda step: (step, 0)),
        out_shape=jax.ShapeDtypeStruct((tokens, width), jnp.bfloat16),
        compiler_params=pltpu.CompilerParams(vmem_limit_bytes=VMEM_CAP),
        cost_estimate=pl.CostEstimate(
            flops=2 * count * tokens * width,
            bytes_accessed=4 * tokens * width,
            transcendentals=0,
        ),
        name="fetch_first",
    )(spots, part)


def fetch_kernel(
    spots_ref, early_ref, second_ref, residual_ref, gain_ref, upstream_ref, output_ref,
    out_grad_ref, attended_grad_ref, gain_grad_ref,
):
    total = early_ref[...].astype(jnp.float32) + spread_rows(spots_ref, second_ref, second_ref.shape[0])
    residual = residual_ref[...]
    inverse = lax.rsqrt(jnp.mean(residual * residual, axis=1, keepdims=True) + eps_norm)
    scaled = residual * inverse

    @pl.when(pl.program_id(0) == 0)
    def _():
        gain_grad_ref[...] = jnp.zeros_like(gain_grad_ref)

    gain_grad_ref[...] += jnp.sum((total * scaled).reshape(-1, 8, total.shape[1]), axis=0)
    weighted = total * gain_ref[...]
    spread = jnp.mean(weighted * scaled, axis=1, keepdims=True)
    residual_grad = upstream_ref[...].astype(jnp.float32) + inverse * (weighted - scaled * spread)
    low = residual_grad.astype(jnp.bfloat16)
    out_grad_ref[...] = low
    attended_grad_ref[...] = times_transposed(low, output_ref[...]).astype(jnp.bfloat16)


def fetch_grads(spots, early, second, residual, gain_row, upstream, w_output):
    tokens, width = residual.shape
    block = 256
    row_spec = pl.BlockSpec((block, width), lambda step: (step, 0))
    whole = lambda shape: pl.BlockSpec(shape, lambda step: (0, 0))
    return pl.pallas_call(
        fetch_kernel,
        grid=(tokens // block,),
        in_specs=[
            pl.BlockSpec((block, TILE), lambda step: (step, 0)),
            row_spec, whole(second.shape),
            row_spec, whole(gain_row.shape), row_spec, whole(w_output.shape),
        ],
        out_specs=[row_spec, row_spec, whole((8, width))],
        out_shape=[
            jax.ShapeDtypeStruct((tokens, width), jnp.bfloat16),
            jax.ShapeDtypeStruct((tokens, width), jnp.bfloat16),
            jax.ShapeDtypeStruct((8, width), jnp.float32),
        ],
        compiler_params=pltpu.CompilerParams(vmem_limit_bytes=VMEM_CAP),
        name="fetch_grads",
    )(spots, early, second, residual, gain_row, upstream, w_output)


def combine_kernel(spots_ref, parts_ref, residual_ref, out_ref):
    column = spots_ref.shape[1] // 2
    target = spots_ref[:, column : column + 1]
    count = parts_ref.shape[0]
    places = lax.broadcasted_iota(jnp.int32, (target.shape[0], count), 1)
    onehot = (places == target).astype(jnp.float32).astype(jnp.bfloat16)
    out_ref[...] = (residual_ref[...] + times(onehot, parts_ref[...])).astype(jnp.bfloat16)


def combine(spots, parts, residual):
    tokens, width = residual.shape
    block = 256
    row_spec = pl.BlockSpec((block, width), lambda step: (step, 0))
    return pl.pallas_call(
        combine_kernel,
        grid=(tokens // block,),
        in_specs=[
            pl.BlockSpec((block, TILE), lambda step: (step, 0)),
            pl.BlockSpec(parts.shape, lambda step: (0, 0)),
            row_spec,
        ],
        out_specs=row_spec,
        out_shape=jax.ShapeDtypeStruct((tokens, width), jnp.bfloat16),
        compiler_params=pltpu.CompilerParams(vmem_limit_bytes=VMEM_CAP),
        name="combine",
    )(spots, parts, residual)


def swap_groups(axis, size, shift, count):
    return [
        [(index, index ^ (step << shift)) for index in range(size)] for step in range(1, count)
    ]


def sum_stages(axis_sizes):
    stages = []
    for axis, size in axis_sizes:
        shift = 0
        while (1 << shift) < size:
            count = min(4, size >> shift)
            place = (lax.axis_index(axis) >> shift) & (count - 1)
            stages.append((axis, place, swap_groups(axis, size, shift, count)))
            shift += count.bit_length() - 1
    return stages


def weight_kernel(core_ref, left_ref, right_ref, away_ref, kept_ref, square):
    square[...] = times(left_ref[...], right_ref[...])
    part = away_ref.shape[0]
    away = pl.ds(pl.multiple_of((1 - core_ref[0]) * part, 16), part)
    kept = pl.ds(pl.multiple_of(core_ref[0] * part, 16), part)
    away_ref[...] = square[away, :].astype(jnp.bfloat16)
    kept_ref[...] = square[kept, :].astype(jnp.bfloat16)


def weight_terms(core, left_t, right):
    width = left_t.shape[0]
    vmem = pl.BlockSpec(memory_space=pltpu.VMEM)
    half = jax.ShapeDtypeStruct((width // 2, right.shape[1]), jnp.bfloat16)
    return pl.pallas_call(
        weight_kernel,
        in_specs=[pl.BlockSpec(memory_space=pltpu.SMEM), vmem, vmem],
        out_specs=[vmem, vmem],
        out_shape=[half, half],
        scratch_shapes=[pltpu.VMEM((width, right.shape[1]), jnp.float32)],
        compiler_params=pltpu.CompilerParams(vmem_limit_bytes=VMEM_CAP),
        cost_estimate=pl.CostEstimate(
            flops=2 * width * left_t.shape[1] * right.shape[1],
            bytes_accessed=2 * (width + right.shape[1]) * left_t.shape[1],
            transcendentals=0,
        ),
        name="weight_terms",
    )(core, left_t, right)


def cut_pieces(place, source, own_ref, sent_refs):
    rows = own_ref.shape[0]
    for step, ref in enumerate((own_ref, *sent_refs)):
        first = pl.multiple_of((place ^ step) * rows, 16)
        ref[...] = source[pl.ds(first, rows), :].astype(ref.dtype)


def padded_rows(rows, count):
    return -(-rows // (16 * count)) * 16 * count


def piece_shapes(rows, width, count):
    own = jax.ShapeDtypeStruct((rows // count, width), jnp.float32)
    sent = jax.ShapeDtypeStruct((rows // count, width), jnp.bfloat16)
    return [own] + [sent] * (count - 1)


def first_pieces_kernel(place_ref, kept_ref, got_ref, kept_out, got_out, small_ref, *outs):
    matrices, part = kept_ref.shape[:2]
    share = part // len(outs)
    extra = small_ref.shape[0] // len(outs)
    for step, ref in enumerate(outs):
        place = place_ref[0] ^ step
        rows = pl.ds(pl.multiple_of(place * share, 16), share)
        for index in range(matrices):
            ref[index * share : (index + 1) * share, :] = (
                kept_ref[index, rows, :].astype(jnp.float32)
                + got_ref[index, rows, :].astype(jnp.float32)
            ).astype(ref.dtype)
        first = matrices * share
        ref[first : first + share, :] = (
            kept_out[rows, :].astype(jnp.float32) + got_out[rows, :].astype(jnp.float32)
        ).astype(ref.dtype)
        rows = pl.ds(pl.multiple_of(place * extra, 16), extra)
        ref[first + share :, :] = small_ref[rows, :].astype(ref.dtype)


def first_pieces(place, kept, got, kept_out, got_out, small, count):
    matrices, part, width = kept.shape
    rows = (matrices + 1) * part + small.shape[0]
    vmem = pl.BlockSpec(memory_space=pltpu.VMEM)
    shapes = piece_shapes(rows, width, count)
    return pl.pallas_call(
        first_pieces_kernel,
        in_specs=[pl.BlockSpec(memory_space=pltpu.SMEM)] + [vmem] * 5,
        out_specs=[vmem] * len(shapes),
        out_shape=shapes,
        compiler_params=pltpu.CompilerParams(vmem_limit_bytes=VMEM_CAP),
        name="first_pieces",
    )(place.reshape(1).astype(jnp.int32), kept, got, kept_out, got_out, small)


def next_pieces_kernel(place_ref, *rest, received):
    total = rest[0][...]
    for ref in rest[1 : received + 1]:
        total = total + ref[...].astype(jnp.float32)
    outs = rest[received + 1 : -1]
    rows = total.shape[0]
    rest[-1][:rows, :] = total
    if rest[-1].shape[0] > rows:
        extra = rest[-1].shape[0] - rows
        rest[-1][rows:, :] = jnp.zeros((extra, total.shape[1]), jnp.float32)
    cut_pieces(place_ref[0], rest[-1], outs[0], outs[1:])


def next_pieces(place, own, got, count):
    rows, width = own.shape
    vmem = pl.BlockSpec(memory_space=pltpu.VMEM)
    padded = padded_rows(rows, count)
    shapes = piece_shapes(padded, width, count)
    if count == 1:
        shapes = [jax.ShapeDtypeStruct((rows, width), jnp.bfloat16)]
    return pl.pallas_call(
        functools.partial(next_pieces_kernel, received=len(got)),
        in_specs=[pl.BlockSpec(memory_space=pltpu.SMEM)] + [vmem] * (1 + len(got)),
        out_specs=[vmem] * len(shapes),
        out_shape=shapes,
        scratch_shapes=[pltpu.VMEM((padded, width), jnp.float32)],
        compiler_params=pltpu.CompilerParams(vmem_limit_bytes=VMEM_CAP),
        name="next_pieces",
    )(place.reshape(1).astype(jnp.int32), own, *got)


def pieces_kernel(place_ref, *refs):
    pieces, out_ref, joined = refs[:-2], refs[-2], refs[-1]
    rows = pieces[0].shape[0]
    for step, ref in enumerate(pieces):
        first = pl.multiple_of((place_ref[0] ^ step) * rows, 16)
        joined[pl.ds(first, rows), :] = ref[...]
    out_ref[...] = joined[: out_ref.shape[0], :]


def join_pieces(place, pieces, kept):
    rows, width = pieces[0].shape
    return pl.pallas_call(
        pieces_kernel,
        in_specs=[pl.BlockSpec(memory_space=pltpu.SMEM)]
        + [pl.BlockSpec(memory_space=pltpu.VMEM)] * len(pieces),
        out_specs=pl.BlockSpec(memory_space=pltpu.VMEM),
        out_shape=jax.ShapeDtypeStruct((kept, width), pieces[0].dtype),
        scratch_shapes=[pltpu.VMEM((len(pieces) * rows, width), pieces[0].dtype)],
        compiler_params=pltpu.CompilerParams(vmem_limit_bytes=VMEM_CAP),
        name="join_pieces",
    )(place.reshape(1).astype(jnp.int32), *pieces)


def finish_kernel(
    core_ref, own_ref, other_ref, query_ref, key_ref, value_ref, gain_ref,
    query_out, key_out, value_out, output_out, gain_out, second_out, router_out, table_out, *, count
):
    width = query_ref.shape[1]
    part = width // 2
    share = part // count
    piece = own_ref.shape[0] // count
    weights = (query_ref, key_ref, value_ref, None)
    outs = (query_out, key_out, value_out, output_out)
    gains = []
    for half, ref in ((core_ref[0], own_ref), (1 - core_ref[0], other_ref)):
        terms = []
        for place in range(count):
            rows = pl.ds(pl.multiple_of(half * part + place * share, 16), share)
            gain = None
            for index, (weight, out) in enumerate(zip(weights, outs)):
                first = place * piece + index * share
                total = ref[first : first + share, :].astype(jnp.float32)
                out[rows, :] = total
                if weight is None:
                    continue
                term = jnp.sum(
                    total * weight[rows, :].astype(jnp.float32), axis=1, keepdims=True
                )
                gain = term if gain is None else gain + term
            terms.append(gain)
        gain = jnp.concatenate(terms, axis=0)
        gains.append(jnp.transpose(jnp.broadcast_to(gain, (part, TILE)))[:1])
    lower = core_ref[0] == 0
    ordered = [jnp.where(lower, gains[side], gains[1 - side]) for side in range(2)]
    gain_out[...] = jnp.concatenate(ordered, axis=1) / gain_ref[...]
    small = []
    for place in range(count):
        rows = slice(place * piece + 4 * share, (place + 1) * piece)
        small.append(own_ref[rows, :].astype(jnp.float32) + other_ref[rows, :].astype(jnp.float32))
    small = jnp.concatenate(small, axis=0)
    experts = router_out.shape[0]
    second_out[...] = jnp.sum(small[:8], axis=0, keepdims=True)
    router_out[...] = small[8 : 8 + experts]
    table_out[...] = small[8 + experts : 9 + experts]


def finish(core, own, other, weights, gain_row, experts, count):
    width = weights[0].shape[1]
    square = jax.ShapeDtypeStruct((width, width), jnp.float32)
    row = jax.ShapeDtypeStruct((1, width), jnp.float32)
    vmem = pl.BlockSpec(memory_space=pltpu.VMEM)
    return pl.pallas_call(
        functools.partial(finish_kernel, count=count),
        in_specs=[pl.BlockSpec(memory_space=pltpu.SMEM)] + [vmem] * 6,
        out_specs=[vmem] * 8,
        out_shape=[
            square, square, square, square, row, row,
            jax.ShapeDtypeStruct((experts, width), jnp.float32),
            row,
        ],
        compiler_params=pltpu.CompilerParams(vmem_limit_bytes=VMEM_CAP),
        name="finish",
    )(core, own, other, *weights, gain_row)


def hidden_kernel(
    grads_ref, query_ref, key_ref, value_ref, hidden_ref, gain_ref, residual_grad_ref, out_ref
):
    total = None
    for index, weight in enumerate((query_ref, key_ref, value_ref)):
        term = times_transposed(grads_ref[index], weight[...])
        total = term if total is None else total + term
    hidden = hidden_ref[...].astype(jnp.float32)
    inverse = lax.rsqrt(jnp.mean(hidden * hidden, axis=1, keepdims=True) + eps_norm)
    scaled = hidden * inverse
    weighted = total * gain_ref[...]
    spread = jnp.mean(weighted * scaled, axis=1, keepdims=True)
    out_ref[...] = (
        residual_grad_ref[...].astype(jnp.float32) + inverse * (weighted - scaled * spread)
    ).astype(jnp.bfloat16)


def hidden_gradient(grads, weights, hidden, gain_row, residual_grad):
    tokens, width = hidden.shape
    block = 256
    row_spec = pl.BlockSpec((block, width), lambda step: (step, 0))
    whole = lambda shape: pl.BlockSpec(shape, lambda step: (0, 0))
    return pl.pallas_call(
        hidden_kernel,
        grid=(tokens // block,),
        in_specs=[pl.BlockSpec((3, block, width), lambda step: (0, step, 0))]
        + [whole(weight.shape) for weight in weights]
        + [row_spec, whole(gain_row.shape), row_spec],
        out_specs=row_spec,
        out_shape=jax.ShapeDtypeStruct((tokens, width), jnp.bfloat16),
        compiler_params=pltpu.CompilerParams(vmem_limit_bytes=VMEM_CAP),
        cost_estimate=pl.CostEstimate(
            flops=6 * tokens * width * width, bytes_accessed=20 * tokens * width, transcendentals=0
        ),
        name="hidden_gradient",
    )(grads, *weights, hidden, gain_row, residual_grad)


def exchange_pieces(stage, pieces):
    axis, _, swaps = stage
    return [lax.ppermute(piece, axis, pairs) for piece, pairs in zip(pieces, swaps)]


def gather_stage(low, stage, kept):
    return join_pieces(stage[1], [low] + exchange_pieces(stage, [low] * len(stage[2])), kept)


def on_device(
    hidden_in,
    first_gain,
    w_query,
    w_key,
    w_value,
    w_output,
    rel_table,
    second_gain,
    router,
    expert_up,
    expert_down,
    routes,
    capacity_factor,
    cotangent,
):
    axes = ("narrow", "wide")
    chunks = 2
    tokens, width = hidden_in.shape
    bucket_count = rel_table.shape[0]
    experts = router.shape[1]
    slots = 2 * tokens // experts
    capacity = capacity_factor * tokens // experts
    devices = lax.axis_size(axes)
    own = lax.axis_index(axes).astype(jnp.int32).reshape(1)
    padded = -(-experts // TILE) * TILE
    router_wide = jnp.pad(router, ((0, 0), (0, padded - experts)))

    def exchange(rows):
        blocks = rows.reshape(experts, -1, width)
        return lax.all_to_all(blocks, axes, split_axis=0, concat_axis=0, tiled=True).reshape(
            -1, width
        )

    together = lax.optimization_barrier
    sent_ups, place, spots = send_first(
        capacity, routes.reshape(1, tokens), cotangent, experts, slots, chunks
    )
    sent_ups, hidden_in = together((sent_ups, hidden_in))
    ups = exchange(sent_ups)

    band, edges = bias_band(rel_table)
    hidden = hidden_in.astype(jnp.float32)
    gain_one = first_gain.astype(jnp.float32)
    gain_two = second_gain.astype(jnp.float32)
    inverse_one = lax.rsqrt(jnp.mean(hidden * hidden, axis=-1, keepdims=True) + eps_norm)
    normed_first = (hidden * inverse_one * gain_one).astype(jnp.bfloat16)
    queries = times(normed_first, w_query).astype(jnp.bfloat16)
    keys = times(normed_first, w_key).astype(jnp.bfloat16)
    values = times(normed_first, w_value).astype(jnp.bfloat16)
    attended, attended_t, logs = attend(queries, keys, values, band, edges)
    residual = hidden + times(attended, w_output)
    inverse_two = lax.rsqrt(jnp.mean(residual * residual, axis=-1, keepdims=True) + eps_norm)
    normed_second = (residual * inverse_two * gain_two).astype(jnp.bfloat16)
    half = experts * slots // chunks
    sent = send_again(place, normed_second, 0, half)
    sent, ups = together((sent, ups))
    rows = [exchange(sent)]
    queries_again, _ = together((queries, ups))
    weights, normed_t = attend_weights(queries_again, keys, logs, band, edges, normed_first)
    sent = send_again(place, normed_second, half, half)
    sent, rows[0], weights, normed_t = together((sent, rows[0], weights, normed_t))
    rows.append(exchange(sent))
    ups = ups.reshape(experts, chunks, slots // chunks, width)

    saved = ()
    input_grads, router_terms = [], []
    for c in range(chunks):
        input_grad, router_term, *saved = expert_pass(
            own, rows[c], ups, expert_up[0], expert_down[0], router_wide, experts, c, saved
        )
        if c + 1 < chunks:
            input_grad, rows[-1] = together((input_grad, rows[-1]))
        if input_grads:
            input_grad, input_grads[-1] = together((input_grad, input_grads[-1]))
        input_grads.append(exchange(input_grad))
        router_terms.append(router_term[:experts])
    saved, input_grads[0] = together((saved, input_grads[0]))
    produced = saved[0].reshape(-1, width)
    activated, pre_grad, slot_grad, kept_rows = [
        array.reshape(-1, array.shape[-1]) for array in saved[1:]
    ]
    gradient_expert_down = inner_rows(activated, slot_grad)[None]
    gradient_expert_up = inner_rows(kept_rows, pre_grad)[None]
    fetched = fetch_first(spots, input_grads[0])
    input_grads[-1], fetched, gradient_expert_down, gradient_expert_up, produced = together(
        (input_grads[-1], fetched, gradient_expert_down, gradient_expert_up, produced)
    )
    produced = exchange(produced)
    out_grad, attended_grad, gain_terms = fetch_grads(
        spots, fetched, input_grads[-1], residual, gain_two[None], cotangent, w_output
    )
    core = lax.axis_index("narrow").astype(jnp.int32).reshape(1)
    swap = [(0, 1), (1, 0)]
    grads, away, kept, sums = attend_back(
        core, queries, keys, values, attended_grad, attended, weights, normed_t
    )
    got = lax.ppermute(away, "narrow", swap)
    out_grad, kept = together((out_grad, kept))
    away_out, kept_out = weight_terms(core, attended_t, out_grad)
    got_out = lax.ppermute(away_out, "narrow", swap)
    table_terms = table_gradient(sums, bucket_count)
    stages = sum_stages([("wide", lax.axis_size("wide"))])
    counts = [len(stage[2]) + 1 for stage in stages]
    used = 8 + experts + 8
    table_row = jnp.pad(
        table_terms.reshape(1, -1), ((0, 7), (0, width - table_terms.size))
    )
    small = jnp.concatenate(
        [
            gain_terms,
            router_terms[0] + router_terms[1],
            table_row,
            jnp.zeros((-used % (16 * counts[0]), width), jnp.float32),
        ],
        axis=0,
    )
    own, *sent = first_pieces(stages[0][1], kept, got, kept_out, got_out, small, counts[0])
    projections = (w_query, w_key, w_value)
    grads, kept = together((grads, kept))
    gradient_hidden = hidden_gradient(
        grads, projections, hidden_in, gain_one[None], out_grad
    )
    rows_at = []
    for level, stage in enumerate(stages):
        rows_at.append(own.shape[0])
        got = exchange_pieces(stage, sent)
        last = level + 1 == len(stages)
        place_next = jnp.zeros((), jnp.int32) if last else stages[level + 1][1]
        own, *sent = next_pieces(place_next, own, got, 1 if last else counts[level + 1])
        if level == 0:
            own, gradient_hidden = together((own, gradient_hidden))
    low = own
    for level in reversed(range(len(stages))):
        if level == 0:
            low, produced = together((low, produced))
            block_out = combine(spots, produced, residual)
        kept_rows = rows_at[level - 1] if level else counts[0] * rows_at[0]
        low = gather_stage(low, stages[level], kept_rows)
    low, block_out = together((low, block_out))
    other = lax.ppermute(low, "narrow", swap)
    (
        gradient_query, gradient_key, gradient_value, gradient_output, gradient_first_gain,
        gradient_second_gain, gradient_router, gradient_table,
    ) = finish(core, low, other, projections, gain_one[None], experts, counts[0])
    return (
        block_out,
        gradient_hidden,
        gradient_first_gain.reshape(width),
        gradient_query,
        gradient_key,
        gradient_value,
        gradient_output,
        gradient_table[0, : rel_table.size].reshape(rel_table.shape),
        gradient_second_gain.reshape(width),
        jnp.transpose(gradient_router),
        gradient_expert_up,
        gradient_expert_down,
    )


def solution(mesh):
    split = ("narrow", "wide")
    rows, experts = P(split, None), P(split, None, None)
    return jax.shard_map(
        on_device,
        mesh=mesh,
        in_specs=(rows,) + (P(),) * 8 + (experts, experts, rows, P(split), rows),
        out_specs=(rows, rows) + (P(),) * 8 + (experts, experts),
        check_vma=False,
    )
```

```python
import functools

import jax
import jax.numpy as jnp
from jax import lax
from jax.experimental import pallas as pl
from jax.experimental.pallas import tpu as pltpu
from jax.sharding import PartitionSpec as P

TILE = 128
STRIP = 256
VMEM_CAP = 60 * 1024 * 1024
eps_norm = 1e-06
bucket_edges = (12, 16, 23, 32, 46, 64, 91)


def bucket_of(offset):
    distance = jnp.abs(offset)
    far_bucket = jnp.full(distance.shape, 8, jnp.int32)
    for edge in bucket_edges:
        far_bucket = far_bucket + (distance >= edge).astype(jnp.int32)
    near_bucket = jnp.where(distance < 8, distance, far_bucket)
    return near_bucket + 16 * (offset > 0).astype(jnp.int32)


def band_buckets():
    rows = lax.broadcasted_iota(jnp.int32, (3 * TILE, TILE), 0)
    lanes = lax.broadcasted_iota(jnp.int32, (3 * TILE, TILE), 1)
    return bucket_of(rows - TILE - lanes)


def times_transposed(left, right):
    return lax.dot_general(
        left, right, (((1,), (1,)), ((), ())), preferred_element_type=jnp.float32
    )


def inner_rows(left, right):
    return lax.dot_general(
        left, right, (((0,), (0,)), ((), ())), preferred_element_type=jnp.float32
    )


def times(left, right):
    return jnp.dot(left, right, preferred_element_type=jnp.float32)


def fill_wide(edge_ref, band_ref, wide):
    length = (wide.shape[1] + TILE) // 2
    pair = pl.program_id(0)
    for side in range(2):
        head = 2 * pair + side
        wide[side, : length - 2 * TILE] = jnp.full(
            (length - 2 * TILE, TILE), edge_ref[head, 0], jnp.float32
        )
        wide[side, length - 2 * TILE : length + TILE] = band_ref[side]
        wide[side, length + TILE :] = jnp.full(
            (length - 2 * TILE, TILE), edge_ref[head, 1], jnp.float32
        )


def strip_bias(wide, side, key_start, keys, query_start):
    length = (wide.shape[1] + TILE) // 2
    parts = []
    for start in range(query_start, query_start + STRIP, TILE):
        first = length - TILE - start + key_start
        parts.append(wide[side, first : first + keys, :])
    return jnp.concatenate(parts, axis=1)


def half_of(rows, side):
    half = rows.shape[1] // 2
    lanes = lax.broadcasted_iota(jnp.int32, rows.shape, 1)
    own = lanes < half if side == 0 else lanes >= half
    return jnp.where(own, rows, jnp.zeros_like(rows))


def attend_kernel(
    edge_ref, q_ref, k_ref, v_ref, band_ref, out_ref, turned_ref, log_ref, wide
):
    length = q_ref.shape[0]
    half = q_ref.shape[1] // 2
    scale = half ** (-0.5)
    fill_wide(edge_ref, band_ref, wide)
    keys = k_ref[...]
    values_t = jnp.transpose(v_ref[...])
    for start in range(0, length, STRIP):
        mixed = []
        for side in range(2):
            query = half_of(q_ref[start : start + STRIP, :] * scale, side)
            scores = times_transposed(keys, query) + strip_bias(wide, side, 0, length, start)
            top = jnp.max(scores, axis=0, keepdims=True)
            powers = jnp.exp(scores - top)
            total = jnp.sum(powers, axis=0, keepdims=True)
            raw = times(values_t[side * half : (side + 1) * half], powers.astype(jnp.bfloat16))
            mixed.append(raw / total)
            log_ref[0, side : side + 1, start : start + STRIP] = top + jnp.log(total)
        both = jnp.concatenate(mixed, axis=0)
        out_ref[start : start + STRIP, :] = jnp.transpose(both).astype(jnp.bfloat16)
        turned_ref[:, start : start + STRIP] = both.astype(jnp.bfloat16)


def attend(queries, keys, values, band, edges):
    length, width = queries.shape
    heads = edges.shape[0]
    pairs = heads // 2
    columns = width // pairs
    part = pl.BlockSpec((length, columns), lambda pair: (0, pair))
    return pl.pallas_call(
        attend_kernel,
        grid=(pairs,),
        in_specs=[
            pl.BlockSpec(memory_space=pltpu.SMEM),
            part,
            part,
            part,
            pl.BlockSpec((2, 3 * TILE, TILE), lambda pair: (pair, 0, 0)),
        ],
        out_specs=[
            part,
            pl.BlockSpec((columns, length), lambda pair: (pair, 0)),
            pl.BlockSpec((1, 2, length), lambda pair: (pair, 0, 0)),
        ],
        out_shape=[
            jax.ShapeDtypeStruct((length, width), jnp.bfloat16),
            jax.ShapeDtypeStruct((width, length), jnp.bfloat16),
            jax.ShapeDtypeStruct((pairs, 2, length), jnp.float32),
        ],
        scratch_shapes=[pltpu.VMEM((2, 2 * length - TILE, TILE), jnp.float32)],
        compiler_params=pltpu.CompilerParams(vmem_limit_bytes=VMEM_CAP),
        cost_estimate=pl.CostEstimate(
            flops=4 * heads * length * length * (width // heads),
            bytes_accessed=8 * length * width,
            transcendentals=heads * length * length,
        ),
        name="attend",
    )(edges, queries, keys, values, band)


def weights_kernel(
    edge_ref, q_ref, k_ref, log_ref, band_ref, normed_ref, weights_ref, turned_ref, wide
):
    length = q_ref.shape[0]
    scale = (q_ref.shape[1] // 2) ** (-0.5)
    fill_wide(edge_ref, band_ref, wide)
    keys = k_ref[...]
    turned_ref[...] = jnp.transpose(normed_ref[...])
    for start in range(0, length, STRIP):
        strip = slice(start, start + STRIP)
        for side in range(2):
            query = half_of(q_ref[strip, :] * scale, side)
            bias = strip_bias(wide, side, 0, length, start)
            scores = times_transposed(keys, query) + bias
            weights_ref[side, :, strip] = jnp.exp(
                scores - log_ref[0, side : side + 1, strip]
            ).astype(jnp.bfloat16)


def attend_weights(queries, keys, logs, band, edges, normed):
    length, width = queries.shape
    heads = edges.shape[0]
    pairs = heads // 2
    columns = width // pairs
    part = pl.BlockSpec((length, columns), lambda pair: (0, pair))
    return pl.pallas_call(
        weights_kernel,
        grid=(pairs,),
        in_specs=[
            pl.BlockSpec(memory_space=pltpu.SMEM),
            part,
            part,
            pl.BlockSpec((1, 2, length), lambda pair: (pair, 0, 0)),
            pl.BlockSpec((2, 3 * TILE, TILE), lambda pair: (pair, 0, 0)),
            part,
        ],
        out_specs=[
            pl.BlockSpec((2, length, length), lambda pair: (pair, 0, 0)),
            pl.BlockSpec((columns, length), lambda pair: (pair, 0)),
        ],
        out_shape=[
            jax.ShapeDtypeStruct((heads, length, length), jnp.bfloat16),
            jax.ShapeDtypeStruct((width, length), jnp.bfloat16),
        ],
        scratch_shapes=[pltpu.VMEM((2, 2 * length - TILE, TILE), jnp.float32)],
        compiler_params=pltpu.CompilerParams(vmem_limit_bytes=VMEM_CAP),
        cost_estimate=pl.CostEstimate(
            flops=2 * heads * length * length * (width // heads),
            bytes_accessed=4 * length * width + 2 * heads * length * length,
            transcendentals=heads * length * length,
        ),
        name="attend_weights",
    )(edges, queries, keys, logs, band, normed)


def diagonal_sums(near_ref, side, beyond):
    span = 4 * TILE
    zeros = jnp.zeros((8, span - TILE), jnp.float32)
    total = jnp.zeros((8, span), jnp.float32)
    for row in range(0, 3 * TILE, 8):
        wide = jnp.concatenate([near_ref[side, row : row + 8, :], zeros], axis=1)
        total = total + pltpu.roll(wide, 3 * TILE - 1 - row, 1)
    rows = lax.broadcasted_iota(jnp.int32, total.shape, 0)
    for bit in (1, 2, 4):
        total = jnp.where((rows & bit) != 0, pltpu.roll(total, span - bit, 1), total)
    sums = jnp.sum(total, axis=0, keepdims=True)
    lanes = lax.broadcasted_iota(jnp.int32, sums.shape, 1)
    sums = sums + jnp.where(lanes == span - 2, beyond[0], 0.0)
    return sums + jnp.where(lanes == 0, beyond[1], 0.0)


def attend_back_kernel(
    core_ref, q_ref, k_ref, v_ref, grad_ref, out_ref, weights_ref, normed_ref,
    grads_ref, away_ref, kept_ref, sums_ref,
    near_ref, key_total, value_total, square,
):
    length = q_ref.shape[0]
    half = q_ref.shape[1] // 2
    blocks = length // TILE
    scale = half ** (-0.5)
    keys_t = jnp.transpose(k_ref[...])
    products = jnp.transpose(grad_ref[...].astype(jnp.float32) * out_ref[...].astype(jnp.float32))
    names = lax.broadcasted_iota(jnp.int32, (2 * blocks, length), 0)
    owners = lax.broadcasted_iota(jnp.int32, (2 * blocks, length), 1) // TILE
    picks = (names == owners).astype(jnp.float32).astype(jnp.bfloat16)
    near_ref[...] = jnp.zeros_like(near_ref)
    query_parts = []
    for side in range(2):
        rows = slice(side * half, (side + 1) * half)
        query = half_of(q_ref[...] * scale, side)
        grad = half_of(grad_ref[...], side)
        center = jnp.sum(products[rows], axis=0, keepdims=True)
        left = jnp.concatenate([keys_t[rows], picks], axis=0)
        total = None
        for first in range(0, length, STRIP):
            block = slice(first, first + STRIP)
            weights = weights_ref[side, block, :]
            weight_grad = times_transposed(v_ref[block, :], grad)
            score_grad = weights.astype(jnp.float32) * (weight_grad - center)
            score_low = score_grad.astype(jnp.bfloat16)
            value_term = times(weights, grad)
            key_term = times(score_low, query)
            if side == 0:
                value_total[block, :] = value_term
                key_total[block, :] = key_term
            else:
                value_total[block, :] += value_term
                key_total[block, :] += key_term
            term = times(left[:, block], score_low)
            total = term if total is None else total + term
            for row in range(0, STRIP, TILE):
                for lane in range(0, length, TILE):
                    apart = (first + row - lane) // TILE
                    if abs(apart) <= 1:
                        spot = (apart + 1) * TILE
                        near_ref[side, spot : spot + TILE, :] += score_grad[
                            row : row + TILE, lane : lane + TILE
                        ]
        query_parts.append(total[:half] * scale)
        sums = total[half:]
        beyond = [
            jnp.sum(jnp.where(keep, sums, 0.0), keepdims=True)
            for keep in (names <= owners - 2, names >= owners + 2)
        ]
        sums_ref[0, side : side + 1, :] = diagonal_sums(near_ref, side, beyond)
    both = jnp.concatenate(query_parts, axis=0)
    grads_ref[0] = jnp.transpose(both).astype(jnp.bfloat16)
    grads_ref[1] = key_total[...].astype(jnp.bfloat16)
    grads_ref[2] = value_total[...].astype(jnp.bfloat16)
    part = normed_ref.shape[0] // 2
    columns = q_ref.shape[1]
    stacked = jnp.concatenate([grads_ref[index] for index in range(3)], axis=1)
    square[...] = times(normed_ref[...], stacked)
    away = pl.ds(pl.multiple_of((1 - core_ref[0]) * part, 16), part)
    kept = pl.ds(pl.multiple_of(core_ref[0] * part, 16), part)
    for index in range(3):
        span = slice(index * columns, (index + 1) * columns)
        away_ref[index] = square[away, span].astype(jnp.bfloat16)
        kept_ref[index] = square[kept, span].astype(jnp.bfloat16)


def attend_back(core, queries, keys, values, grads, attended, weights, normed_t):
    length, width = queries.shape
    heads = weights.shape[0]
    pairs = heads // 2
    columns = width // pairs
    part = pl.BlockSpec((length, columns), lambda pair: (0, pair))
    square = pl.BlockSpec((3, width // 2, columns), lambda pair: (0, 0, pair))
    return pl.pallas_call(
        attend_back_kernel,
        grid=(pairs,),
        in_specs=[
            pl.BlockSpec(memory_space=pltpu.SMEM),
            part, part, part, part, part,
            pl.BlockSpec((2, length, length), lambda pair: (pair, 0, 0)),
            pl.BlockSpec((width, length), lambda pair: (0, 0)),
        ],
        out_specs=[
            pl.BlockSpec((3, length, columns), lambda pair: (0, 0, pair)),
            square, square,
            pl.BlockSpec((1, 2, 4 * TILE), lambda pair: (pair, 0, 0)),
        ],
        out_shape=[
            jax.ShapeDtypeStruct((3, length, width), jnp.bfloat16),
            jax.ShapeDtypeStruct((3, width // 2, width), jnp.bfloat16),
            jax.ShapeDtypeStruct((3, width // 2, width), jnp.bfloat16),
            jax.ShapeDtypeStruct((pairs, 2, 4 * TILE), jnp.float32),
        ],
        scratch_shapes=[
            pltpu.VMEM((2, 3 * TILE, TILE), jnp.float32),
            pltpu.VMEM((length, columns), jnp.float32),
            pltpu.VMEM((length, columns), jnp.float32),
            pltpu.VMEM((width, 3 * columns), jnp.float32),
        ],
        compiler_params=pltpu.CompilerParams(vmem_limit_bytes=VMEM_CAP),
        cost_estimate=pl.CostEstimate(
            flops=10 * heads * length * length * (width // heads),
            bytes_accessed=16 * length * width + 2 * heads * length * length,
            transcendentals=0,
        ),
        name="attend_back",
    )(core, queries, keys, values, grads, attended, weights, normed_t)


def bias_band(rel_table):
    buckets, heads = rel_table.shape
    labels = band_buckets().reshape(1, -1)
    onehot = (labels == jnp.arange(buckets, dtype=jnp.int32)[:, None]).astype(jnp.bfloat16)
    band = lax.dot_general(
        rel_table, onehot, (((0,), (0,)), ((), ())), preferred_element_type=jnp.float32
    )
    half = buckets // 2
    edges = jnp.stack([rel_table[half - 1], rel_table[buckets - 1]], axis=1).astype(jnp.float32)
    return band.reshape(heads, 3 * TILE, TILE), edges


normal_tail = (
    0.14372023791716726,
    0.14167152280803838,
    0.14027055919455333,
    0.02504245305870889,
    0.1831401332067321,
    -0.1813703123183242,
    0.04752538660588183,
)
tail_pole = 0.36
normal_height = 0.3989422804014327


def gelu_and_slope(values):
    density = jnp.exp(values * values * -0.5)
    inverse = 1.0 / (1.0 + tail_pole * jnp.abs(values))
    series = jnp.full_like(values, normal_tail[-1])
    for coefficient in normal_tail[-2::-1]:
        series = series * inverse + coefficient
    tail = series * inverse * density
    below = jnp.where(values > 0, 1.0 - tail, tail)
    return values * below, below + values * (density * normal_height)


def send_kernel(
    capacity_ref, route_ref, rows_ref, sent_ref, place_ref, spots_ref, scratch, *, experts, slots, chunks
):
    tokens = route_ref.shape[1]
    block = sent_ref.shape[0]
    step = pl.program_id(0)

    @pl.when(step == 0)
    def _():
        route = route_ref[...]
        names = lax.broadcasted_iota(jnp.int32, (experts, tokens), 0)
        chosen = (names == route).astype(jnp.float32)
        early = lax.broadcasted_iota(jnp.int32, (tokens, tokens), 0)
        late = lax.broadcasted_iota(jnp.int32, (tokens, tokens), 1)
        before = (early < late).astype(jnp.float32).astype(jnp.bfloat16)
        earlier = times(chosen.astype(jnp.bfloat16), before)
        slot = jnp.sum(earlier * chosen, axis=0, keepdims=True).astype(jnp.int32)
        kept = slot < capacity_ref[0]
        share = slots // chunks
        chunk = jnp.zeros_like(slot)
        for later in range(1, chunks):
            chunk = chunk + (slot >= later * share).astype(jnp.int32)
        place = chunk * (experts * share) + route * share + (slot - chunk * share)
        place = jnp.where(kept, place, -1)
        ordered = jnp.where(kept, route * slots + slot, -1)
        scratch[...] = ordered
        place_ref[...] = place
        half = spots_ref.shape[1] // 2
        both = jnp.concatenate(
            [jnp.broadcast_to(place, (half, tokens)), jnp.broadcast_to(ordered, (half, tokens))], axis=0
        )
        spots_ref[...] = jnp.transpose(both)

    places = step * block + lax.broadcasted_iota(jnp.int32, (block, tokens), 0)
    onehot = (places == scratch[...]).astype(jnp.float32).astype(jnp.bfloat16)
    sent_ref[...] = times(onehot, rows_ref[...]).astype(jnp.bfloat16)


def send_first(capacity, route_row, rows, experts, slots, chunks):
    tokens, width = rows.shape
    total = experts * slots
    block = 256
    return pl.pallas_call(
        functools.partial(send_kernel, experts=experts, slots=slots, chunks=chunks),
        grid=(total // block,),
        in_specs=[
            pl.BlockSpec(memory_space=pltpu.SMEM),
            pl.BlockSpec((1, tokens), lambda step: (0, 0)),
            pl.BlockSpec((tokens, width), lambda step: (0, 0)),
        ],
        out_specs=[
            pl.BlockSpec((block, width), lambda step: (step, 0)),
            pl.BlockSpec((1, tokens), lambda step: (0, 0)),
            pl.BlockSpec((tokens, TILE), lambda step: (0, 0)),
        ],
        out_shape=[
            jax.ShapeDtypeStruct((total, width), jnp.bfloat16),
            jax.ShapeDtypeStruct((1, tokens), jnp.int32),
            jax.ShapeDtypeStruct((tokens, TILE), jnp.int32),
        ],
        scratch_shapes=[pltpu.VMEM((1, tokens), jnp.int32)],
        compiler_params=pltpu.CompilerParams(vmem_limit_bytes=VMEM_CAP),
        name="route_and_send",
    )(capacity, route_row, rows)


def send_again_kernel(place_ref, rows_ref, sent_ref, *, first):
    block = sent_ref.shape[0]
    tokens = rows_ref.shape[0]
    start = first + pl.program_id(0) * block
    places = start + lax.broadcasted_iota(jnp.int32, (block, tokens), 0)
    onehot = (places == place_ref[...]).astype(jnp.float32).astype(jnp.bfloat16)
    sent_ref[...] = times(onehot, rows_ref[...]).astype(jnp.bfloat16)


def send_again(place, rows, first, count):
    tokens, width = rows.shape
    block = 512
    return pl.pallas_call(
        functools.partial(send_again_kernel, first=first),
        grid=(count // block,),
        in_specs=[
            pl.BlockSpec((1, tokens), lambda step: (0, 0)),
            pl.BlockSpec((tokens, width), lambda step: (0, 0)),
        ],
        out_specs=pl.BlockSpec((block, width), lambda step: (step, 0)),
        out_shape=jax.ShapeDtypeStruct((count, width), jnp.bfloat16),
        compiler_params=pltpu.CompilerParams(vmem_limit_bytes=VMEM_CAP),
        cost_estimate=pl.CostEstimate(
            flops=2 * count * tokens * width,
            bytes_accessed=2 * (count + tokens) * width,
            transcendentals=0,
        ),
        name="send_rows",
    )(place, rows)


def expert_kernel(
    own_ref, rows_ref, ups_ref, up_ref, down_ref, router_ref, *rest, experts, piece
):
    (
        input_grad_ref, router_grad_ref, produced_ref, activated_ref, pre_grad_ref, slot_grad_ref,
        kept_ref,
    ) = rest[-7:]
    rows = rows_ref[...]
    ups = ups_ref[...].astype(jnp.float32).reshape(rows.shape)
    low_ups = ups.astype(jnp.bfloat16)
    router = router_ref[...]
    hidden = up_ref.shape[1]
    logits = times(rows, router)
    lanes = lax.broadcasted_iota(jnp.int32, logits.shape, 1)
    logits = jnp.where(lanes < experts, logits, -jnp.inf)
    powers = jnp.exp(logits - jnp.max(logits, axis=1, keepdims=True))
    chances = powers / jnp.sum(powers, axis=1, keepdims=True)
    mine = (lanes == own_ref[0]).astype(jnp.float32)
    gate = jnp.sum(chances * mine, axis=1, keepdims=True)
    gate_grad = jnp.zeros_like(gate)
    input_grad = jnp.zeros(rows.shape, jnp.float32)
    produced = jnp.zeros(rows.shape, jnp.float32)
    for first in range(0, hidden, piece):
        span = slice(first, first + piece)
        up = up_ref[:, span]
        down = down_ref[span, :]
        activated, slope = gelu_and_slope(times(rows, up))
        activated = activated.astype(jnp.bfloat16)
        back = times_transposed(low_ups, down)
        gate_grad = gate_grad + jnp.sum(
            activated.astype(jnp.float32) * back, axis=1, keepdims=True
        )
        pre_grad = (back * gate * slope).astype(jnp.bfloat16)
        activated_ref[0, :, span] = activated
        pre_grad_ref[0, :, span] = pre_grad
        input_grad = input_grad + times_transposed(pre_grad, up)
        produced = produced + times(activated, down)
    logit_grad = gate_grad * gate * (mine - chances)
    low_logit = logit_grad.astype(jnp.bfloat16)
    input_grad_ref[...] = (input_grad + times_transposed(low_logit, router)).astype(jnp.bfloat16)
    produced_ref[...] = (produced * gate).reshape(produced_ref.shape).astype(jnp.bfloat16)
    slot_grad_ref[0] = (ups * gate).astype(jnp.bfloat16)
    kept_ref[0] = rows

    @pl.when(pl.program_id(0) == 0)
    def _():
        router_grad_ref[...] = jnp.zeros_like(router_grad_ref)

    router_grad_ref[...] += times(jnp.transpose(logit_grad).astype(jnp.bfloat16), rows)


def expert_pass(own, rows, ups, up, down, router, experts, chunk, before):
    count, width = rows.shape
    groups, chunks, half = ups.shape[:3]
    hidden = up.shape[1]
    block = 256
    lanes = router.shape[1]
    row_spec = pl.BlockSpec((block, width), lambda step: (step, 0))
    whole = lambda shape: pl.BlockSpec(shape, lambda step: (0, 0))
    kept = lambda columns: pl.BlockSpec((1, block, columns), lambda step: (chunk, step, 0))
    stacked = lambda columns: jax.ShapeDtypeStruct((chunks, count, columns), jnp.bfloat16)
    slot_spec = pl.BlockSpec((block // half, 1, half, width), lambda step: (step, chunk, 0, 0))
    widths = (hidden, hidden, width, width)
    return pl.pallas_call(
        functools.partial(expert_kernel, experts=experts, piece=512),
        grid=(count // block,),
        in_specs=[
            pl.BlockSpec(memory_space=pltpu.SMEM),
            row_spec, slot_spec,
            whole(up.shape), whole(down.shape), whole(router.shape),
        ] + [pl.BlockSpec(memory_space=pl.ANY)] * len(before),
        out_specs=[row_spec, whole((lanes, width)), slot_spec]
        + [kept(columns) for columns in widths],
        out_shape=[
            jax.ShapeDtypeStruct((count, width), jnp.bfloat16),
            jax.ShapeDtypeStruct((lanes, width), jnp.float32),
            jax.ShapeDtypeStruct((groups, chunks, half, width), jnp.bfloat16),
        ] + [stacked(columns) for columns in widths],
        input_output_aliases={6 + index: 2 + index for index in range(len(before))},
        compiler_params=pltpu.CompilerParams(vmem_limit_bytes=VMEM_CAP),
        cost_estimate=pl.CostEstimate(
            flops=8 * count * width * hidden,
            bytes_accessed=4 * width * hidden + 4 * count * hidden + 12 * count * width,
            transcendentals=2 * count * hidden,
        ),
        name="experts",
    )(own, rows, ups, up, down, router, *before)


def spread_rows(spots_ref, part_ref, first):
    target = spots_ref[:, :1]
    count = part_ref.shape[0]
    places = first + lax.broadcasted_iota(jnp.int32, (target.shape[0], count), 1)
    onehot = (places == target).astype(jnp.float32).astype(jnp.bfloat16)
    return times(onehot, part_ref[...])


def fetch_first_kernel(spots_ref, part_ref, out_ref):
    out_ref[...] = spread_rows(spots_ref, part_ref, 0).astype(jnp.bfloat16)


def fetch_first(spots, part):
    tokens = spots.shape[0]
    count, width = part.shape
    block = 256
    return pl.pallas_call(
        fetch_first_kernel,
        grid=(tokens // block,),
        in_specs=[
            pl.BlockSpec((block, TILE), lambda step: (step, 0)),
            pl.BlockSpec((count, width), lambda step: (0, 0)),
        ],
        out_specs=pl.BlockSpec((block, width), lambda step: (step, 0)),
        out_shape=jax.ShapeDtypeStruct((tokens, width), jnp.bfloat16),
        compiler_params=pltpu.CompilerParams(vmem_limit_bytes=VMEM_CAP),
        cost_estimate=pl.CostEstimate(
            flops=2 * count * tokens * width,
            bytes_accessed=4 * tokens * width,
            transcendentals=0,
        ),
        name="fetch_first",
    )(spots, part)


def fetch_kernel(
    spots_ref, early_ref, second_ref, residual_ref, gain_ref, upstream_ref, output_ref,
    out_grad_ref, attended_grad_ref, gain_grad_ref,
):
    total = early_ref[...].astype(jnp.float32) + spread_rows(spots_ref, second_ref, second_ref.shape[0])
    residual = residual_ref[...]
    inverse = lax.rsqrt(jnp.mean(residual * residual, axis=1, keepdims=True) + eps_norm)
    scaled = residual * inverse

    @pl.when(pl.program_id(0) == 0)
    def _():
        gain_grad_ref[...] = jnp.zeros_like(gain_grad_ref)

    gain_grad_ref[...] += jnp.sum((total * scaled).reshape(-1, 8, total.shape[1]), axis=0)
    weighted = total * gain_ref[...]
    spread = jnp.mean(weighted * scaled, axis=1, keepdims=True)
    residual_grad = upstream_ref[...].astype(jnp.float32) + inverse * (weighted - scaled * spread)
    low = residual_grad.astype(jnp.bfloat16)
    out_grad_ref[...] = low
    attended_grad_ref[...] = times_transposed(low, output_ref[...]).astype(jnp.bfloat16)


def fetch_grads(spots, early, second, residual, gain_row, upstream, w_output):
    tokens, width = residual.shape
    block = 256
    row_spec = pl.BlockSpec((block, width), lambda step: (step, 0))
    whole = lambda shape: pl.BlockSpec(shape, lambda step: (0, 0))
    return pl.pallas_call(
        fetch_kernel,
        grid=(tokens // block,),
        in_specs=[
            pl.BlockSpec((block, TILE), lambda step: (step, 0)),
            row_spec, whole(second.shape),
            row_spec, whole(gain_row.shape), row_spec, whole(w_output.shape),
        ],
        out_specs=[row_spec, row_spec, whole((8, width))],
        out_shape=[
            jax.ShapeDtypeStruct((tokens, width), jnp.bfloat16),
            jax.ShapeDtypeStruct((tokens, width), jnp.bfloat16),
            jax.ShapeDtypeStruct((8, width), jnp.float32),
        ],
        compiler_params=pltpu.CompilerParams(vmem_limit_bytes=VMEM_CAP),
        name="fetch_grads",
    )(spots, early, second, residual, gain_row, upstream, w_output)


def combine_kernel(spots_ref, parts_ref, residual_ref, out_ref):
    column = spots_ref.shape[1] // 2
    target = spots_ref[:, column : column + 1]
    count = parts_ref.shape[0]
    places = lax.broadcasted_iota(jnp.int32, (target.shape[0], count), 1)
    onehot = (places == target).astype(jnp.float32).astype(jnp.bfloat16)
    out_ref[...] = (residual_ref[...] + times(onehot, parts_ref[...])).astype(jnp.bfloat16)


def combine(spots, parts, residual):
    tokens, width = residual.shape
    block = 256
    row_spec = pl.BlockSpec((block, width), lambda step: (step, 0))
    return pl.pallas_call(
        combine_kernel,
        grid=(tokens // block,),
        in_specs=[
            pl.BlockSpec((block, TILE), lambda step: (step, 0)),
            pl.BlockSpec(parts.shape, lambda step: (0, 0)),
            row_spec,
        ],
        out_specs=row_spec,
        out_shape=jax.ShapeDtypeStruct((tokens, width), jnp.bfloat16),
        compiler_params=pltpu.CompilerParams(vmem_limit_bytes=VMEM_CAP),
        name="combine",
    )(spots, parts, residual)


def swap_groups(axis, size, shift, count):
    return [
        [(index, index ^ (step << shift)) for index in range(size)] for step in range(1, count)
    ]


def sum_stages(axis_sizes):
    stages = []
    for axis, size in axis_sizes:
        shift = 0
        while (1 << shift) < size:
            count = min(4, size >> shift)
            place = (lax.axis_index(axis) >> shift) & (count - 1)
            stages.append((axis, place, swap_groups(axis, size, shift, count)))
            shift += count.bit_length() - 1
    return stages


def weight_kernel(core_ref, left_ref, right_ref, away_ref, kept_ref, square):
    square[...] = times(left_ref[...], right_ref[...])
    part = away_ref.shape[0]
    away = pl.ds(pl.multiple_of((1 - core_ref[0]) * part, 16), part)
    kept = pl.ds(pl.multiple_of(core_ref[0] * part, 16), part)
    away_ref[...] = square[away, :].astype(jnp.bfloat16)
    kept_ref[...] = square[kept, :].astype(jnp.bfloat16)


def weight_terms(core, left_t, right):
    width = left_t.shape[0]
    vmem = pl.BlockSpec(memory_space=pltpu.VMEM)
    half = jax.ShapeDtypeStruct((width // 2, right.shape[1]), jnp.bfloat16)
    return pl.pallas_call(
        weight_kernel,
        in_specs=[pl.BlockSpec(memory_space=pltpu.SMEM), vmem, vmem],
        out_specs=[vmem, vmem],
        out_shape=[half, half],
        scratch_shapes=[pltpu.VMEM((width, right.shape[1]), jnp.float32)],
        compiler_params=pltpu.CompilerParams(vmem_limit_bytes=VMEM_CAP),
        cost_estimate=pl.CostEstimate(
            flops=2 * width * left_t.shape[1] * right.shape[1],
            bytes_accessed=2 * (width + right.shape[1]) * left_t.shape[1],
            transcendentals=0,
        ),
        name="weight_terms",
    )(core, left_t, right)


def cut_pieces(place, source, own_ref, sent_refs):
    rows = own_ref.shape[0]
    for step, ref in enumerate((own_ref, *sent_refs)):
        first = pl.multiple_of((place ^ step) * rows, 16)
        ref[...] = source[pl.ds(first, rows), :].astype(ref.dtype)


def padded_rows(rows, count):
    return -(-rows // (16 * count)) * 16 * count


def piece_shapes(rows, width, count):
    own = jax.ShapeDtypeStruct((rows // count, width), jnp.float32)
    sent = jax.ShapeDtypeStruct((rows // count, width), jnp.bfloat16)
    return [own] + [sent] * (count - 1)


def first_pieces_kernel(
    place_ref, kept_ref, got_ref, kept_out, got_out, gain_ref, router_one, router_two, sums_ref,
    *rest, experts,
):
    outs, small, sums = rest[:-2], rest[-2], rest[-1]
    small[...] = jnp.zeros_like(small)
    sums[...] = jnp.zeros_like(sums)
    for pair in range(sums_ref.shape[0]):
        sums[2 * pair : 2 * pair + 2, :] = sums_ref[pair]
    small[:8, :] = gain_ref[...]
    small[8 : 8 + experts, :] = router_one[:experts] + router_two[:experts]
    lanes = lax.broadcasted_iota(jnp.int32, (TILE, sums.shape[1]), 1)
    names = lax.broadcasted_iota(jnp.int32, (TILE, sums.shape[1]), 0)
    onehot = (bucket_of(2 * TILE - 1 - lanes) == names).astype(jnp.float32)
    small[8 + experts : 8 + experts + sums.shape[0], :TILE] = lax.dot_general(
        sums[...], onehot, (((1,), (1,)), ((), ())),
        precision=lax.Precision.HIGHEST, preferred_element_type=jnp.float32,
    )
    matrices, part = kept_ref.shape[:2]
    share = part // len(outs)
    extra = small.shape[0] // len(outs)
    for step, ref in enumerate(outs):
        place = place_ref[0] ^ step
        rows = pl.ds(pl.multiple_of(place * share, 16), share)
        for index in range(matrices):
            ref[index * share : (index + 1) * share, :] = (
                kept_ref[index, rows, :].astype(jnp.float32)
                + got_ref[index, rows, :].astype(jnp.float32)
            ).astype(ref.dtype)
        first = matrices * share
        ref[first : first + share, :] = (
            kept_out[rows, :].astype(jnp.float32) + got_out[rows, :].astype(jnp.float32)
        ).astype(ref.dtype)
        rows = pl.ds(pl.multiple_of(place * extra, 16), extra)
        ref[first + share :, :] = small[rows, :].astype(ref.dtype)


def first_pieces(place, kept, got, kept_out, got_out, gain_terms, router_terms, sums, experts, count):
    matrices, part, width = kept.shape
    sum_rows = -(-2 * sums.shape[0] // 8) * 8
    extra = padded_rows(8 + experts + sum_rows, count)
    rows = (matrices + 1) * part + extra
    vmem = pl.BlockSpec(memory_space=pltpu.VMEM)
    shapes = piece_shapes(rows, width, count)
    return pl.pallas_call(
        functools.partial(first_pieces_kernel, experts=experts),
        in_specs=[pl.BlockSpec(memory_space=pltpu.SMEM)] + [vmem] * 8,
        out_specs=[vmem] * len(shapes),
        out_shape=shapes,
        scratch_shapes=[
            pltpu.VMEM((extra, width), jnp.float32),
            pltpu.VMEM((sum_rows, sums.shape[2]), jnp.float32),
        ],
        compiler_params=pltpu.CompilerParams(vmem_limit_bytes=VMEM_CAP),
        name="first_pieces",
    )(
        place.reshape(1).astype(jnp.int32), kept, got, kept_out, got_out, gain_terms,
        *router_terms, sums,
    )


def next_pieces_kernel(place_ref, *rest, received):
    total = rest[0][...]
    for ref in rest[1 : received + 1]:
        total = total + ref[...].astype(jnp.float32)
    outs = rest[received + 1 : -1]
    rows = total.shape[0]
    rest[-1][:rows, :] = total
    if rest[-1].shape[0] > rows:
        extra = rest[-1].shape[0] - rows
        rest[-1][rows:, :] = jnp.zeros((extra, total.shape[1]), jnp.float32)
    cut_pieces(place_ref[0], rest[-1], outs[0], outs[1:])


def next_pieces(place, own, got, count):
    rows, width = own.shape
    vmem = pl.BlockSpec(memory_space=pltpu.VMEM)
    padded = padded_rows(rows, count)
    shapes = piece_shapes(padded, width, count)
    if count == 1:
        shapes = [jax.ShapeDtypeStruct((rows, width), jnp.bfloat16)]
    return pl.pallas_call(
        functools.partial(next_pieces_kernel, received=len(got)),
        in_specs=[pl.BlockSpec(memory_space=pltpu.SMEM)] + [vmem] * (1 + len(got)),
        out_specs=[vmem] * len(shapes),
        out_shape=shapes,
        scratch_shapes=[pltpu.VMEM((padded, width), jnp.float32)],
        compiler_params=pltpu.CompilerParams(vmem_limit_bytes=20 * 1024 * 1024),
        name="next_pieces",
    )(place.reshape(1).astype(jnp.int32), own, *got)


def pieces_kernel(place_ref, *refs):
    pieces, out_ref, joined = refs[:-2], refs[-2], refs[-1]
    rows = pieces[0].shape[0]
    for step, ref in enumerate(pieces):
        first = pl.multiple_of((place_ref[0] ^ step) * rows, 16)
        joined[pl.ds(first, rows), :] = ref[...]
    out_ref[...] = joined[: out_ref.shape[0], :]


def join_pieces(place, pieces, kept):
    rows, width = pieces[0].shape
    return pl.pallas_call(
        pieces_kernel,
        in_specs=[pl.BlockSpec(memory_space=pltpu.SMEM)]
        + [pl.BlockSpec(memory_space=pltpu.VMEM)] * len(pieces),
        out_specs=pl.BlockSpec(memory_space=pltpu.VMEM),
        out_shape=jax.ShapeDtypeStruct((kept, width), pieces[0].dtype),
        scratch_shapes=[pltpu.VMEM((len(pieces) * rows, width), pieces[0].dtype)],
        compiler_params=pltpu.CompilerParams(vmem_limit_bytes=20 * 1024 * 1024),
        name="join_pieces",
    )(place.reshape(1).astype(jnp.int32), *pieces)


def finish_kernel(
    place_ref, *rest, count, table
):
    pieces, rest = rest[: 2 * count], rest[2 * count :]
    weight_refs, gain_ref, rest = rest[:3], rest[3], rest[4:]
    square_outs, (gain_out, second_out, router_out, table_out), rest = rest[:4], rest[4:8], rest[8:]
    weights, squares, columns, small, load_sems, store_sems = rest
    core, place = place_ref[0], place_ref[1]
    width = weights.shape[2]
    part = width // 2
    share = part // count
    loads = [
        pltpu.make_async_copy(ref, weights.at[index], load_sems.at[index])
        for index, ref in enumerate(weight_refs)
    ]
    for load in loads:
        load.start()
    spots = []
    for step in range(count):
        for other in range(2):
            half = 1 - core if other else core
            first = half * part + (place ^ step) * share
            spots.append((pieces[2 * step + other], pl.ds(pl.multiple_of(first, 16), share)))
    stores = []
    for index in (3, 0, 1, 2):
        if index < 3:
            loads[index].wait()
        for ref, rows in spots:
            total = ref[index * share : (index + 1) * share, :].astype(jnp.float32)
            squares[index, rows, :] = total
            if index == 3:
                continue
            term = jnp.sum(
                total * weights[index, rows, :].astype(jnp.float32), axis=1, keepdims=True
            )
            if index == 0:
                columns[rows, :] = jnp.broadcast_to(term, (share, TILE))
            else:
                columns[rows, :] += jnp.broadcast_to(term, (share, TILE))
        store = pltpu.make_async_copy(squares.at[index], square_outs[index], store_sems.at[index])
        store.start()
        stores.append(store)
    gain = jnp.transpose(columns[...])[:1] / gain_ref[...]
    gain_out[...] = gain.reshape(width)
    extra = small.shape[0] // count
    for step in range(count):
        rows = pl.ds(pl.multiple_of((place ^ step) * extra, 16), extra)
        small[rows, :] = pieces[2 * step][4 * share :, :].astype(jnp.float32) + pieces[2 * step + 1][
            4 * share :, :
        ].astype(jnp.float32)
    experts = router_out.shape[0]
    buckets, heads = table
    second_out[...] = jnp.sum(small[:8, :], axis=0, keepdims=True).reshape(width)
    router_out[...] = small[8 : 8 + experts, :]
    table_out[...] = small[8 + experts : 8 + experts + heads, :buckets]
    for store in stores:
        store.wait()


def finish(core, place, pieces, weights, gain_row, experts, table):
    width = weights[0].shape[1]
    count = len(pieces) // 2
    square = jax.ShapeDtypeStruct((width, width), jnp.float32)
    row = jax.ShapeDtypeStruct((width,), jnp.float32)
    vmem = pl.BlockSpec(memory_space=pltpu.VMEM)
    extra = pieces[0].shape[0] - 4 * (width // 2 // count)
    places = jnp.concatenate([core, place.reshape(1).astype(jnp.int32)])
    return pl.pallas_call(
        functools.partial(finish_kernel, count=count, table=table),
        in_specs=[pl.BlockSpec(memory_space=pltpu.SMEM)]
        + [vmem] * len(pieces)
        + [pl.BlockSpec(memory_space=pl.ANY)] * 3
        + [vmem],
        out_specs=[pl.BlockSpec(memory_space=pl.ANY)] * 4 + [vmem] * 4,
        out_shape=[
            square, square, square, square, row, row,
            jax.ShapeDtypeStruct((experts, width), jnp.float32),
            jax.ShapeDtypeStruct(table[::-1], jnp.float32),
        ],
        scratch_shapes=[
            pltpu.VMEM((3, width, width), jnp.bfloat16),
            pltpu.VMEM((4, width, width), jnp.float32),
            pltpu.VMEM((width, TILE), jnp.float32),
            pltpu.VMEM((count * extra, width), jnp.float32),
            pltpu.SemaphoreType.DMA((3,)),
            pltpu.SemaphoreType.DMA((4,)),
        ],
        compiler_params=pltpu.CompilerParams(vmem_limit_bytes=VMEM_CAP),
        name="finish",
    )(places, *pieces, *weights, gain_row)


def hidden_kernel(
    grads_ref, query_ref, key_ref, value_ref, hidden_ref, gain_ref, residual_grad_ref, out_ref
):
    total = None
    for index, weight in enumerate((query_ref, key_ref, value_ref)):
        term = times_transposed(grads_ref[index], weight[...])
        total = term if total is None else total + term
    hidden = hidden_ref[...].astype(jnp.float32)
    inverse = lax.rsqrt(jnp.mean(hidden * hidden, axis=1, keepdims=True) + eps_norm)
    scaled = hidden * inverse
    weighted = total * gain_ref[...]
    spread = jnp.mean(weighted * scaled, axis=1, keepdims=True)
    out_ref[...] = (
        residual_grad_ref[...].astype(jnp.float32) + inverse * (weighted - scaled * spread)
    ).astype(jnp.bfloat16)


def hidden_gradient(grads, weights, hidden, gain_row, residual_grad):
    tokens, width = hidden.shape
    block = 256
    row_spec = pl.BlockSpec((block, width), lambda step: (step, 0))
    whole = lambda shape: pl.BlockSpec(shape, lambda step: (0, 0))
    return pl.pallas_call(
        hidden_kernel,
        grid=(tokens // block,),
        in_specs=[pl.BlockSpec((3, block, width), lambda step: (0, step, 0))]
        + [whole(weight.shape) for weight in weights]
        + [row_spec, whole(gain_row.shape), row_spec],
        out_specs=row_spec,
        out_shape=jax.ShapeDtypeStruct((tokens, width), jnp.bfloat16),
        compiler_params=pltpu.CompilerParams(vmem_limit_bytes=VMEM_CAP),
        cost_estimate=pl.CostEstimate(
            flops=6 * tokens * width * width, bytes_accessed=20 * tokens * width, transcendentals=0
        ),
        name="hidden_gradient",
    )(grads, *weights, hidden, gain_row, residual_grad)


def exchange_pieces(stage, pieces):
    axis, _, swaps = stage
    return [lax.ppermute(piece, axis, pairs) for piece, pairs in zip(pieces, swaps)]


def gather_stage(low, stage, kept):
    return join_pieces(stage[1], [low] + exchange_pieces(stage, [low] * len(stage[2])), kept)


def on_device(
    hidden_in,
    first_gain,
    w_query,
    w_key,
    w_value,
    w_output,
    rel_table,
    second_gain,
    router,
    expert_up,
    expert_down,
    routes,
    capacity_factor,
    cotangent,
):
    axes = ("narrow", "wide")
    chunks = 2
    tokens, width = hidden_in.shape
    bucket_count = rel_table.shape[0]
    experts = router.shape[1]
    slots = 2 * tokens // experts
    capacity = capacity_factor * tokens // experts
    devices = lax.axis_size(axes)
    own = lax.axis_index(axes).astype(jnp.int32).reshape(1)
    padded = -(-experts // TILE) * TILE
    router_wide = jnp.pad(router, ((0, 0), (0, padded - experts)))

    def exchange(rows):
        blocks = rows.reshape(experts, -1, width)
        return lax.all_to_all(blocks, axes, split_axis=0, concat_axis=0, tiled=True).reshape(
            -1, width
        )

    together = lax.optimization_barrier
    sent_ups, place, spots = send_first(
        capacity, routes.reshape(1, tokens), cotangent, experts, slots, chunks
    )
    sent_ups, hidden_in = together((sent_ups, hidden_in))
    ups = exchange(sent_ups)

    band, edges = bias_band(rel_table)
    hidden = hidden_in.astype(jnp.float32)
    gain_one = first_gain.astype(jnp.float32)
    gain_two = second_gain.astype(jnp.float32)
    inverse_one = lax.rsqrt(jnp.mean(hidden * hidden, axis=-1, keepdims=True) + eps_norm)
    normed_first = (hidden * inverse_one * gain_one).astype(jnp.bfloat16)
    queries = times(normed_first, w_query).astype(jnp.bfloat16)
    keys = times(normed_first, w_key).astype(jnp.bfloat16)
    values = times(normed_first, w_value).astype(jnp.bfloat16)
    attended, attended_t, logs = attend(queries, keys, values, band, edges)
    residual = hidden + times(attended, w_output)
    inverse_two = lax.rsqrt(jnp.mean(residual * residual, axis=-1, keepdims=True) + eps_norm)
    normed_second = (residual * inverse_two * gain_two).astype(jnp.bfloat16)
    half = experts * slots // chunks
    sent = send_again(place, normed_second, 0, half)
    sent, ups = together((sent, ups))
    rows = [exchange(sent)]
    queries_again, _ = together((queries, ups))
    weights, normed_t = attend_weights(queries_again, keys, logs, band, edges, normed_first)
    sent = send_again(place, normed_second, half, half)
    sent, rows[0], weights, normed_t = together((sent, rows[0], weights, normed_t))
    rows.append(exchange(sent))
    ups = ups.reshape(experts, chunks, slots // chunks, width)

    saved = ()
    input_grads, router_terms = [], []
    for c in range(chunks):
        input_grad, router_term, *saved = expert_pass(
            own, rows[c], ups, expert_up[0], expert_down[0], router_wide, experts, c, saved
        )
        if c + 1 < chunks:
            input_grad, rows[-1] = together((input_grad, rows[-1]))
        if input_grads:
            input_grad, input_grads[-1] = together((input_grad, input_grads[-1]))
        input_grads.append(exchange(input_grad))
        router_terms.append(router_term)
    saved, input_grads[0] = together((saved, input_grads[0]))
    produced = saved[0].reshape(-1, width)
    activated, pre_grad, slot_grad, kept_rows = [
        array.reshape(-1, array.shape[-1]) for array in saved[1:]
    ]
    gradient_expert_down = inner_rows(activated, slot_grad)[None]
    gradient_expert_up = inner_rows(kept_rows, pre_grad)[None]
    fetched = fetch_first(spots, input_grads[0])
    input_grads[-1], fetched, gradient_expert_down, gradient_expert_up, produced = together(
        (input_grads[-1], fetched, gradient_expert_down, gradient_expert_up, produced)
    )
    produced = exchange(produced)
    out_grad, attended_grad, gain_terms = fetch_grads(
        spots, fetched, input_grads[-1], residual, gain_two[None], cotangent, w_output
    )
    core = lax.axis_index("narrow").astype(jnp.int32).reshape(1)
    swap = [(0, 1), (1, 0)]
    grads, away, kept, sums = attend_back(
        core, queries, keys, values, attended_grad, attended, weights, normed_t
    )
    got = lax.ppermute(away, "narrow", swap)
    out_grad, kept = together((out_grad, kept))
    away_out, kept_out = weight_terms(core, attended_t, out_grad)
    got_out = lax.ppermute(away_out, "narrow", swap)
    stages = sum_stages([("wide", lax.axis_size("wide"))])
    counts = [len(stage[2]) + 1 for stage in stages]
    own, *sent = first_pieces(
        stages[0][1], kept, got, kept_out, got_out, gain_terms, router_terms, sums, experts, counts[0]
    )
    projections = (w_query, w_key, w_value)
    grads, kept = together((grads, kept))
    gradient_hidden = hidden_gradient(
        grads, projections, hidden_in, gain_one[None], out_grad
    )
    rows_at = []
    for level, stage in enumerate(stages):
        rows_at.append(own.shape[0])
        got = exchange_pieces(stage, sent)
        last = level + 1 == len(stages)
        place_next = jnp.zeros((), jnp.int32) if last else stages[level + 1][1]
        own, *sent = next_pieces(place_next, own, got, 1 if last else counts[level + 1])
        if level == 0:
            own, gradient_hidden = together((own, gradient_hidden))
    low = own
    for level in reversed(range(1, len(stages))):
        low = gather_stage(low, stages[level], rows_at[level - 1])
    low, produced = together((low, produced))
    block_out = combine(spots, produced, residual)
    pieces = [low] + exchange_pieces(stages[0], [low] * (counts[0] - 1))
    pieces[1], block_out = together((pieces[1], block_out))
    others = [lax.ppermute(piece, "narrow", swap) for piece in pieces]
    (
        gradient_query, gradient_key, gradient_value, gradient_output, gradient_first_gain,
        gradient_second_gain, gradient_router, gradient_table,
    ) = finish(
        core, stages[0][1], [piece for both in zip(pieces, others) for piece in both], projections,
        gain_one[None], experts, rel_table.shape,
    )
    return (
        block_out,
        gradient_hidden,
        gradient_first_gain,
        gradient_query,
        gradient_key,
        gradient_value,
        gradient_output,
        jnp.transpose(gradient_table),
        gradient_second_gain,
        jnp.transpose(gradient_router),
        gradient_expert_up,
        gradient_expert_down,
    )


def solution(mesh):
    split = ("narrow", "wide")
    rows, experts = P(split, None), P(split, None, None)
    return jax.shard_map(
        on_device,
        mesh=mesh,
        in_specs=(rows,) + (P(),) * 8 + (experts, experts, rows, P(split), rows),
        out_specs=(rows, rows) + (P(),) * 8 + (experts, experts),
        check_vma=False,
    )
```

```python
import functools

import jax
import jax.numpy as jnp
from jax import lax
from jax.experimental import pallas as pl
from jax.experimental.pallas import tpu as pltpu
from jax.sharding import PartitionSpec as P

TILE = 128
STRIP = 256
BACK_STRIP = 512
VMEM_CAP = 60 * 1024 * 1024
eps_norm = 1e-06
bucket_edges = (12, 16, 23, 32, 46, 64, 91)


def bucket_of(offset):
    distance = jnp.abs(offset)
    far_bucket = jnp.full(distance.shape, 8, jnp.int32)
    for edge in bucket_edges:
        far_bucket = far_bucket + (distance >= edge).astype(jnp.int32)
    near_bucket = jnp.where(distance < 8, distance, far_bucket)
    return near_bucket + 16 * (offset > 0).astype(jnp.int32)


def band_buckets():
    rows = lax.broadcasted_iota(jnp.int32, (3 * TILE, TILE), 0)
    lanes = lax.broadcasted_iota(jnp.int32, (3 * TILE, TILE), 1)
    return bucket_of(rows - TILE - lanes)


def times_transposed(left, right):
    return lax.dot_general(
        left, right, (((1,), (1,)), ((), ())), preferred_element_type=jnp.float32
    )


def inner_rows(left, right):
    return lax.dot_general(
        left, right, (((0,), (0,)), ((), ())), preferred_element_type=jnp.float32
    )


def times(left, right):
    return jnp.dot(left, right, preferred_element_type=jnp.float32)


def fill_wide(edge_ref, band_ref, wide):
    length = (wide.shape[1] + TILE) // 2
    pair = pl.program_id(0)
    for side in range(2):
        head = 2 * pair + side
        wide[side, : length - 2 * TILE] = jnp.full(
            (length - 2 * TILE, TILE), edge_ref[head, 0], jnp.float32
        )
        wide[side, length - 2 * TILE : length + TILE] = band_ref[side]
        wide[side, length + TILE :] = jnp.full(
            (length - 2 * TILE, TILE), edge_ref[head, 1], jnp.float32
        )


def strip_bias(wide, side, key_start, keys, query_start):
    length = (wide.shape[1] + TILE) // 2
    parts = []
    for start in range(query_start, query_start + STRIP, TILE):
        first = length - TILE - start + key_start
        parts.append(wide[side, first : first + keys, :])
    return jnp.concatenate(parts, axis=1)


def half_of(rows, side):
    half = rows.shape[1] // 2
    lanes = lax.broadcasted_iota(jnp.int32, rows.shape, 1)
    own = lanes < half if side == 0 else lanes >= half
    return jnp.where(own, rows, jnp.zeros_like(rows))


def attend_kernel(
    edge_ref, q_ref, k_ref, v_ref, band_ref, out_ref, turned_ref, log_ref, wide
):
    length = q_ref.shape[0]
    half = q_ref.shape[1] // 2
    scale = half ** (-0.5)
    fill_wide(edge_ref, band_ref, wide)
    keys = k_ref[...]
    values_t = jnp.transpose(v_ref[...])
    for start in range(0, length, STRIP):
        mixed = []
        for side in range(2):
            query = half_of(q_ref[start : start + STRIP, :] * scale, side)
            scores = times_transposed(keys, query) + strip_bias(wide, side, 0, length, start)
            top = jnp.max(scores, axis=0, keepdims=True)
            powers = jnp.exp(scores - top)
            total = jnp.sum(powers, axis=0, keepdims=True)
            raw = times(values_t[side * half : (side + 1) * half], powers.astype(jnp.bfloat16))
            mixed.append(raw / total)
            log_ref[0, side : side + 1, start : start + STRIP] = top + jnp.log(total)
        both = jnp.concatenate(mixed, axis=0)
        out_ref[start : start + STRIP, :] = jnp.transpose(both).astype(jnp.bfloat16)
        turned_ref[:, start : start + STRIP] = both.astype(jnp.bfloat16)


def attend(queries, keys, values, band, edges):
    length, width = queries.shape
    heads = edges.shape[0]
    pairs = heads // 2
    columns = width // pairs
    part = pl.BlockSpec((length, columns), lambda pair: (0, pair))
    return pl.pallas_call(
        attend_kernel,
        grid=(pairs,),
        in_specs=[
            pl.BlockSpec(memory_space=pltpu.SMEM),
            part,
            part,
            part,
            pl.BlockSpec((2, 3 * TILE, TILE), lambda pair: (pair, 0, 0)),
        ],
        out_specs=[
            part,
            pl.BlockSpec((columns, length), lambda pair: (pair, 0)),
            pl.BlockSpec((1, 2, length), lambda pair: (pair, 0, 0)),
        ],
        out_shape=[
            jax.ShapeDtypeStruct((length, width), jnp.bfloat16),
            jax.ShapeDtypeStruct((width, length), jnp.bfloat16),
            jax.ShapeDtypeStruct((pairs, 2, length), jnp.float32),
        ],
        scratch_shapes=[pltpu.VMEM((2, 2 * length - TILE, TILE), jnp.float32)],
        compiler_params=pltpu.CompilerParams(vmem_limit_bytes=VMEM_CAP),
        cost_estimate=pl.CostEstimate(
            flops=4 * heads * length * length * (width // heads),
            bytes_accessed=8 * length * width,
            transcendentals=heads * length * length,
        ),
        name="attend",
    )(edges, queries, keys, values, band)


def weights_kernel(
    edge_ref, q_ref, k_ref, log_ref, band_ref, normed_ref, weights_ref, turned_ref, wide
):
    length = q_ref.shape[0]
    scale = (q_ref.shape[1] // 2) ** (-0.5)
    head = 2 * pl.program_id(0)
    for side in range(2):
        turned = [
            jnp.transpose(band_ref[side, part : part + TILE, :]) for part in range(0, 3 * TILE, TILE)
        ]
        wide[side, :, : length - 2 * TILE] = jnp.full(
            (TILE, length - 2 * TILE), edge_ref[head + side, 0], jnp.float32
        )
        wide[side, :, length - 2 * TILE : length + TILE] = jnp.concatenate(turned, axis=1)
        wide[side, :, length + TILE :] = jnp.full(
            (TILE, length - 2 * TILE), edge_ref[head + side, 1], jnp.float32
        )
    keys = k_ref[...]
    turned_ref[...] = jnp.transpose(normed_ref[...])
    for start in range(0, length, STRIP):
        strip = slice(start, start + STRIP)
        for side in range(2):
            query = half_of(q_ref[strip, :] * scale, side)
            bias = jnp.concatenate(
                [
                    wide[side, :, length - TILE - first : 2 * length - TILE - first]
                    for first in range(start, start + STRIP, TILE)
                ],
                axis=0,
            )
            logs = jnp.transpose(
                jnp.broadcast_to(log_ref[0, side : side + 1, strip], (TILE, STRIP))
            )[:, :1]
            scores = times_transposed(query, keys) + bias
            weights_ref[side, strip, :] = jnp.exp(scores - logs).astype(jnp.bfloat16)


def attend_weights(queries, keys, logs, band, edges, normed):
    length, width = queries.shape
    heads = edges.shape[0]
    pairs = heads // 2
    columns = width // pairs
    part = pl.BlockSpec((length, columns), lambda pair: (0, pair))
    return pl.pallas_call(
        weights_kernel,
        grid=(pairs,),
        in_specs=[
            pl.BlockSpec(memory_space=pltpu.SMEM),
            part,
            part,
            pl.BlockSpec((1, 2, length), lambda pair: (pair, 0, 0)),
            pl.BlockSpec((2, 3 * TILE, TILE), lambda pair: (pair, 0, 0)),
            part,
        ],
        out_specs=[
            pl.BlockSpec((2, length, length), lambda pair: (pair, 0, 0)),
            pl.BlockSpec((columns, length), lambda pair: (pair, 0)),
        ],
        out_shape=[
            jax.ShapeDtypeStruct((heads, length, length), jnp.bfloat16),
            jax.ShapeDtypeStruct((width, length), jnp.bfloat16),
        ],
        scratch_shapes=[pltpu.VMEM((2, TILE, 2 * length - TILE), jnp.float32)],
        compiler_params=pltpu.CompilerParams(vmem_limit_bytes=VMEM_CAP),
        cost_estimate=pl.CostEstimate(
            flops=2 * heads * length * length * (width // heads),
            bytes_accessed=4 * length * width + 2 * heads * length * length,
            transcendentals=heads * length * length,
        ),
        name="attend_weights",
    )(edges, queries, keys, logs, band, normed)


def diagonal_sums(near_ref, side, beyond):
    span = 4 * TILE
    zeros = jnp.zeros((8, span - TILE), jnp.float32)
    total = jnp.zeros((8, span), jnp.float32)
    for block in range(3):
        for row in range(0, TILE, 8):
            first = block * TILE + row
            wide = jnp.concatenate([near_ref[side, first : first + 8, :], zeros], axis=1)
            total = total + pltpu.roll(wide, (block + 1) * TILE - 1 - row, 1)
    rows = lax.broadcasted_iota(jnp.int32, total.shape, 0)
    for bit in (1, 2, 4):
        total = jnp.where((rows & bit) != 0, pltpu.roll(total, span - bit, 1), total)
    sums = jnp.sum(total, axis=0, keepdims=True)
    lanes = lax.broadcasted_iota(jnp.int32, sums.shape, 1)
    sums = sums + jnp.where(lanes == 0, beyond[0], 0.0)
    return sums + jnp.where(lanes == span - 2, beyond[1], 0.0)


def attend_back_kernel(
    core_ref, q_ref, k_ref, v_ref, grad_ref, out_ref, weights_ref, normed_ref,
    grads_ref, away_ref, kept_ref, sums_ref,
    near_ref, query_total, square,
):
    length = q_ref.shape[0]
    columns = q_ref.shape[1]
    half = columns // 2
    blocks = length // TILE
    scale = half ** (-0.5)
    names = lax.broadcasted_iota(jnp.int32, (2 * blocks, length), 0)
    owners = lax.broadcasted_iota(jnp.int32, (2 * blocks, length), 1) // TILE
    picks = (names == owners).astype(jnp.float32).astype(jnp.bfloat16)
    queries_t = jnp.transpose(q_ref[...] * scale)
    grads_t = jnp.transpose(grad_ref[...])
    near_ref[...] = jnp.zeros_like(near_ref)
    key_parts, value_parts = [], []
    for side in range(2):
        rows = slice(side * half, (side + 1) * half)
        grad = half_of(grad_ref[...], side)
        keys = half_of(k_ref[...], side)
        center = jnp.sum(
            grad.astype(jnp.float32) * out_ref[...].astype(jnp.float32), axis=1, keepdims=True
        )
        left = jnp.concatenate([queries_t[rows], picks], axis=0)
        key_total, value_total = None, None
        for start in range(0, length, BACK_STRIP):
            strip = slice(start, start + BACK_STRIP)
            weights = weights_ref[side, strip, :]
            weight_grad = times_transposed(grad[strip], v_ref[...])
            score_grad = weights.astype(jnp.float32) * (weight_grad - center[strip])
            score_low = score_grad.astype(jnp.bfloat16)
            value_term = times(grads_t[rows, strip], weights)
            value_total = value_term if value_total is None else value_total + value_term
            key_term = times(left[:, strip], score_low)
            key_total = key_term if key_total is None else key_total + key_term
            query_term = times(score_low, keys)
            if side == 0:
                query_total[strip, :] = query_term
            else:
                query_total[strip, :] += query_term
            for row in range(0, BACK_STRIP, TILE):
                for lane in range(0, length, TILE):
                    apart = (lane - start - row) // TILE
                    if abs(apart) <= 1:
                        spot = (apart + 1) * TILE
                        near_ref[side, spot : spot + TILE, :] += score_grad[
                            row : row + TILE, lane : lane + TILE
                        ]
        key_parts.append(key_total[:half])
        value_parts.append(value_total)
        sums = key_total[half:]
        beyond = [
            jnp.sum(jnp.where(keep, sums, 0.0), keepdims=True)
            for keep in (names >= owners + 2, (names <= owners - 2) & (names < blocks))
        ]
        sums_ref[0, side : side + 1, :] = diagonal_sums(near_ref, side, beyond)
    grads_ref[0] = (query_total[...] * scale).astype(jnp.bfloat16)
    grads_ref[1] = jnp.transpose(jnp.concatenate(key_parts, axis=0)).astype(jnp.bfloat16)
    grads_ref[2] = jnp.transpose(jnp.concatenate(value_parts, axis=0)).astype(jnp.bfloat16)
    part = normed_ref.shape[0] // 2
    stacked = jnp.concatenate([grads_ref[index] for index in range(3)], axis=1)
    square[...] = times(normed_ref[...], stacked)
    away = pl.ds(pl.multiple_of((1 - core_ref[0]) * part, 16), part)
    kept = pl.ds(pl.multiple_of(core_ref[0] * part, 16), part)
    for index in range(3):
        span = slice(index * columns, (index + 1) * columns)
        away_ref[index] = square[away, span].astype(jnp.bfloat16)
        kept_ref[index] = square[kept, span].astype(jnp.bfloat16)


def attend_back(core, queries, keys, values, grads, attended, weights, normed_t):
    length, width = queries.shape
    heads = weights.shape[0]
    pairs = heads // 2
    columns = width // pairs
    part = pl.BlockSpec((length, columns), lambda pair: (0, pair))
    square = pl.BlockSpec((3, width // 2, columns), lambda pair: (0, 0, pair))
    return pl.pallas_call(
        attend_back_kernel,
        grid=(pairs,),
        in_specs=[
            pl.BlockSpec(memory_space=pltpu.SMEM),
            part, part, part, part, part,
            pl.BlockSpec((2, length, length), lambda pair: (pair, 0, 0)),
            pl.BlockSpec((width, length), lambda pair: (0, 0)),
        ],
        out_specs=[
            pl.BlockSpec((3, length, columns), lambda pair: (0, 0, pair)),
            square, square,
            pl.BlockSpec((1, 2, 4 * TILE), lambda pair: (pair, 0, 0)),
        ],
        out_shape=[
            jax.ShapeDtypeStruct((3, length, width), jnp.bfloat16),
            jax.ShapeDtypeStruct((3, width // 2, width), jnp.bfloat16),
            jax.ShapeDtypeStruct((3, width // 2, width), jnp.bfloat16),
            jax.ShapeDtypeStruct((pairs, 2, 4 * TILE), jnp.float32),
        ],
        scratch_shapes=[
            pltpu.VMEM((2, 3 * TILE, TILE), jnp.float32),
            pltpu.VMEM((length, columns), jnp.float32),
            pltpu.VMEM((width, 3 * columns), jnp.float32),
        ],
        compiler_params=pltpu.CompilerParams(vmem_limit_bytes=VMEM_CAP),
        cost_estimate=pl.CostEstimate(
            flops=10 * heads * length * length * (width // heads),
            bytes_accessed=16 * length * width + 2 * heads * length * length,
            transcendentals=0,
        ),
        name="attend_back",
    )(core, queries, keys, values, grads, attended, weights, normed_t)


def bias_band(rel_table):
    buckets, heads = rel_table.shape
    labels = band_buckets().reshape(1, -1)
    onehot = (labels == jnp.arange(buckets, dtype=jnp.int32)[:, None]).astype(jnp.bfloat16)
    band = lax.dot_general(
        rel_table, onehot, (((0,), (0,)), ((), ())), preferred_element_type=jnp.float32
    )
    half = buckets // 2
    edges = jnp.stack([rel_table[half - 1], rel_table[buckets - 1]], axis=1).astype(jnp.float32)
    return band.reshape(heads, 3 * TILE, TILE), edges


normal_tail = (
    0.14372023791716726,
    0.14167152280803838,
    0.14027055919455333,
    0.02504245305870889,
    0.1831401332067321,
    -0.1813703123183242,
    0.04752538660588183,
)
tail_pole = 0.36
normal_height = 0.3989422804014327


def gelu_and_slope(values):
    density = jnp.exp(values * values * -0.5)
    inverse = 1.0 / (1.0 + tail_pole * jnp.abs(values))
    series = jnp.full_like(values, normal_tail[-1])
    for coefficient in normal_tail[-2::-1]:
        series = series * inverse + coefficient
    tail = series * inverse * density
    below = jnp.where(values > 0, 1.0 - tail, tail)
    return values * below, below + values * (density * normal_height)


def send_kernel(
    capacity_ref, route_ref, rows_ref, sent_ref, place_ref, spots_ref, scratch, *, experts, slots, chunks
):
    tokens = route_ref.shape[1]
    block = sent_ref.shape[0]
    step = pl.program_id(0)

    @pl.when(step == 0)
    def _():
        route = route_ref[...]
        names = lax.broadcasted_iota(jnp.int32, (experts, tokens), 0)
        chosen = (names == route).astype(jnp.float32)
        early = lax.broadcasted_iota(jnp.int32, (tokens, tokens), 0)
        late = lax.broadcasted_iota(jnp.int32, (tokens, tokens), 1)
        before = (early < late).astype(jnp.float32).astype(jnp.bfloat16)
        earlier = times(chosen.astype(jnp.bfloat16), before)
        slot = jnp.sum(earlier * chosen, axis=0, keepdims=True).astype(jnp.int32)
        kept = slot < capacity_ref[0]
        share = slots // chunks
        chunk = jnp.zeros_like(slot)
        for later in range(1, chunks):
            chunk = chunk + (slot >= later * share).astype(jnp.int32)
        place = chunk * (experts * share) + route * share + (slot - chunk * share)
        place = jnp.where(kept, place, -1)
        ordered = jnp.where(kept, route * slots + slot, -1)
        scratch[...] = ordered
        place_ref[...] = place
        half = spots_ref.shape[1] // 2
        both = jnp.concatenate(
            [jnp.broadcast_to(place, (half, tokens)), jnp.broadcast_to(ordered, (half, tokens))], axis=0
        )
        spots_ref[...] = jnp.transpose(both)

    places = step * block + lax.broadcasted_iota(jnp.int32, (block, tokens), 0)
    onehot = (places == scratch[...]).astype(jnp.float32).astype(jnp.bfloat16)
    sent_ref[...] = times(onehot, rows_ref[...]).astype(jnp.bfloat16)


def send_first(capacity, route_row, rows, experts, slots, chunks):
    tokens, width = rows.shape
    total = experts * slots
    block = 512
    return pl.pallas_call(
        functools.partial(send_kernel, experts=experts, slots=slots, chunks=chunks),
        grid=(total // block,),
        in_specs=[
            pl.BlockSpec(memory_space=pltpu.SMEM),
            pl.BlockSpec((1, tokens), lambda step: (0, 0)),
            pl.BlockSpec((tokens, width), lambda step: (0, 0)),
        ],
        out_specs=[
            pl.BlockSpec((block, width), lambda step: (step, 0)),
            pl.BlockSpec((1, tokens), lambda step: (0, 0)),
            pl.BlockSpec((tokens, TILE), lambda step: (0, 0)),
        ],
        out_shape=[
            jax.ShapeDtypeStruct((total, width), jnp.bfloat16),
            jax.ShapeDtypeStruct((1, tokens), jnp.int32),
            jax.ShapeDtypeStruct((tokens, TILE), jnp.int32),
        ],
        scratch_shapes=[pltpu.VMEM((1, tokens), jnp.int32)],
        compiler_params=pltpu.CompilerParams(vmem_limit_bytes=VMEM_CAP),
        name="route_and_send",
    )(capacity, route_row, rows)


def send_again_kernel(place_ref, rows_ref, sent_ref, *, first):
    block = sent_ref.shape[0]
    tokens = rows_ref.shape[0]
    start = first + pl.program_id(0) * block
    places = start + lax.broadcasted_iota(jnp.int32, (block, tokens), 0)
    onehot = (places == place_ref[...]).astype(jnp.float32).astype(jnp.bfloat16)
    sent_ref[...] = times(onehot, rows_ref[...]).astype(jnp.bfloat16)


def send_again(place, rows, first, count):
    tokens, width = rows.shape
    block = 512
    return pl.pallas_call(
        functools.partial(send_again_kernel, first=first),
        grid=(count // block,),
        in_specs=[
            pl.BlockSpec((1, tokens), lambda step: (0, 0)),
            pl.BlockSpec((tokens, width), lambda step: (0, 0)),
        ],
        out_specs=pl.BlockSpec((block, width), lambda step: (step, 0)),
        out_shape=jax.ShapeDtypeStruct((count, width), jnp.bfloat16),
        compiler_params=pltpu.CompilerParams(vmem_limit_bytes=VMEM_CAP),
        cost_estimate=pl.CostEstimate(
            flops=2 * count * tokens * width,
            bytes_accessed=2 * (count + tokens) * width,
            transcendentals=0,
        ),
        name="send_rows",
    )(place, rows)


def expert_kernel(
    own_ref, rows_ref, ups_ref, up_ref, down_ref, router_ref, *rest, experts, piece
):
    (
        input_grad_ref, router_grad_ref, produced_ref, activated_ref, pre_grad_ref, slot_grad_ref,
        kept_ref,
    ) = rest[-7:]
    rows = rows_ref[...]
    ups = ups_ref[...].astype(jnp.float32).reshape(rows.shape)
    low_ups = ups.astype(jnp.bfloat16)
    router = router_ref[...]
    hidden = up_ref.shape[1]
    logits = times(rows, router)
    lanes = lax.broadcasted_iota(jnp.int32, logits.shape, 1)
    logits = jnp.where(lanes < experts, logits, -jnp.inf)
    powers = jnp.exp(logits - jnp.max(logits, axis=1, keepdims=True))
    chances = powers / jnp.sum(powers, axis=1, keepdims=True)
    mine = (lanes == own_ref[0]).astype(jnp.float32)
    gate = jnp.sum(chances * mine, axis=1, keepdims=True)
    gate_grad = jnp.zeros_like(gate)
    input_grad = jnp.zeros(rows.shape, jnp.float32)
    produced = jnp.zeros(rows.shape, jnp.float32)
    for first in range(0, hidden, piece):
        span = slice(first, first + piece)
        up = up_ref[:, span]
        down = down_ref[span, :]
        activated, slope = gelu_and_slope(times(rows, up))
        activated = activated.astype(jnp.bfloat16)
        back = times_transposed(low_ups, down)
        gate_grad = gate_grad + jnp.sum(
            activated.astype(jnp.float32) * back, axis=1, keepdims=True
        )
        pre_grad = (back * gate * slope).astype(jnp.bfloat16)
        activated_ref[0, :, span] = activated
        pre_grad_ref[0, :, span] = pre_grad
        input_grad = input_grad + times_transposed(pre_grad, up)
        produced = produced + times(activated, down)
    logit_grad = gate_grad * gate * (mine - chances)
    low_logit = logit_grad.astype(jnp.bfloat16)
    input_grad_ref[...] = (input_grad + times_transposed(low_logit, router)).astype(jnp.bfloat16)
    produced_ref[...] = (produced * gate).reshape(produced_ref.shape).astype(jnp.bfloat16)
    slot_grad_ref[0] = (ups * gate).astype(jnp.bfloat16)
    kept_ref[0] = rows

    @pl.when(pl.program_id(0) == 0)
    def _():
        router_grad_ref[...] = jnp.zeros_like(router_grad_ref)

    router_grad_ref[...] += times(jnp.transpose(logit_grad).astype(jnp.bfloat16), rows)


def expert_pass(own, rows, ups, up, down, router, experts, chunk, before):
    count, width = rows.shape
    groups, chunks, half = ups.shape[:3]
    hidden = up.shape[1]
    block = 256
    lanes = router.shape[1]
    row_spec = pl.BlockSpec((block, width), lambda step: (step, 0))
    whole = lambda shape: pl.BlockSpec(shape, lambda step: (0, 0))
    kept = lambda columns: pl.BlockSpec((1, block, columns), lambda step: (chunk, step, 0))
    stacked = lambda columns: jax.ShapeDtypeStruct((chunks, count, columns), jnp.bfloat16)
    slot_spec = pl.BlockSpec((block // half, 1, half, width), lambda step: (step, chunk, 0, 0))
    widths = (hidden, hidden, width, width)
    return pl.pallas_call(
        functools.partial(expert_kernel, experts=experts, piece=1024),
        grid=(count // block,),
        in_specs=[
            pl.BlockSpec(memory_space=pltpu.SMEM),
            row_spec, slot_spec,
            whole(up.shape), whole(down.shape), whole(router.shape),
        ] + [pl.BlockSpec(memory_space=pl.ANY)] * len(before),
        out_specs=[row_spec, whole((lanes, width)), slot_spec]
        + [kept(columns) for columns in widths],
        out_shape=[
            jax.ShapeDtypeStruct((count, width), jnp.bfloat16),
            jax.ShapeDtypeStruct((lanes, width), jnp.float32),
            jax.ShapeDtypeStruct((groups, chunks, half, width), jnp.bfloat16),
        ] + [stacked(columns) for columns in widths],
        input_output_aliases={6 + index: 2 + index for index in range(len(before))},
        compiler_params=pltpu.CompilerParams(vmem_limit_bytes=VMEM_CAP),
        cost_estimate=pl.CostEstimate(
            flops=8 * count * width * hidden,
            bytes_accessed=4 * width * hidden + 4 * count * hidden + 12 * count * width,
            transcendentals=2 * count * hidden,
        ),
        name="experts",
    )(own, rows, ups, up, down, router, *before)


def spread_rows(spots_ref, part_ref, first):
    target = spots_ref[:, :1]
    count = part_ref.shape[0]
    places = first + lax.broadcasted_iota(jnp.int32, (target.shape[0], count), 1)
    onehot = (places == target).astype(jnp.float32).astype(jnp.bfloat16)
    return times(onehot, part_ref[...])


def fetch_first_kernel(spots_ref, part_ref, out_ref):
    out_ref[...] = spread_rows(spots_ref, part_ref, 0).astype(jnp.bfloat16)


def fetch_first(spots, part):
    tokens = spots.shape[0]
    count, width = part.shape
    block = 256
    return pl.pallas_call(
        fetch_first_kernel,
        grid=(tokens // block,),
        in_specs=[
            pl.BlockSpec((block, TILE), lambda step: (step, 0)),
            pl.BlockSpec((count, width), lambda step: (0, 0)),
        ],
        out_specs=pl.BlockSpec((block, width), lambda step: (step, 0)),
        out_shape=jax.ShapeDtypeStruct((tokens, width), jnp.bfloat16),
        compiler_params=pltpu.CompilerParams(vmem_limit_bytes=VMEM_CAP),
        cost_estimate=pl.CostEstimate(
            flops=2 * count * tokens * width,
            bytes_accessed=4 * tokens * width,
            transcendentals=0,
        ),
        name="fetch_first",
    )(spots, part)


def fetch_kernel(
    spots_ref, early_ref, second_ref, residual_ref, gain_ref, upstream_ref, output_ref,
    out_grad_ref, attended_grad_ref, gain_grad_ref,
):
    total = early_ref[...].astype(jnp.float32) + spread_rows(spots_ref, second_ref, second_ref.shape[0])
    residual = residual_ref[...]
    inverse = lax.rsqrt(jnp.mean(residual * residual, axis=1, keepdims=True) + eps_norm)
    scaled = residual * inverse

    @pl.when(pl.program_id(0) == 0)
    def _():
        gain_grad_ref[...] = jnp.zeros_like(gain_grad_ref)

    gain_grad_ref[...] += jnp.sum((total * scaled).reshape(-1, 8, total.shape[1]), axis=0)
    weighted = total * gain_ref[...]
    spread = jnp.mean(weighted * scaled, axis=1, keepdims=True)
    residual_grad = upstream_ref[...].astype(jnp.float32) + inverse * (weighted - scaled * spread)
    low = residual_grad.astype(jnp.bfloat16)
    out_grad_ref[...] = low
    attended_grad_ref[...] = times_transposed(low, output_ref[...]).astype(jnp.bfloat16)


def fetch_grads(spots, early, second, residual, gain_row, upstream, w_output):
    tokens, width = residual.shape
    block = 256
    row_spec = pl.BlockSpec((block, width), lambda step: (step, 0))
    whole = lambda shape: pl.BlockSpec(shape, lambda step: (0, 0))
    return pl.pallas_call(
        fetch_kernel,
        grid=(tokens // block,),
        in_specs=[
            pl.BlockSpec((block, TILE), lambda step: (step, 0)),
            row_spec, whole(second.shape),
            row_spec, whole(gain_row.shape), row_spec, whole(w_output.shape),
        ],
        out_specs=[row_spec, row_spec, whole((8, width))],
        out_shape=[
            jax.ShapeDtypeStruct((tokens, width), jnp.bfloat16),
            jax.ShapeDtypeStruct((tokens, width), jnp.bfloat16),
            jax.ShapeDtypeStruct((8, width), jnp.float32),
        ],
        compiler_params=pltpu.CompilerParams(vmem_limit_bytes=63 * 1024 * 1024),
        name="fetch_grads",
    )(spots, early, second, residual, gain_row, upstream, w_output)


def combine_kernel(spots_ref, parts_ref, residual_ref, out_ref):
    column = spots_ref.shape[1] // 2
    target = spots_ref[:, column : column + 1]
    count = parts_ref.shape[0]
    places = lax.broadcasted_iota(jnp.int32, (target.shape[0], count), 1)
    onehot = (places == target).astype(jnp.float32).astype(jnp.bfloat16)
    out_ref[...] = (residual_ref[...] + times(onehot, parts_ref[...])).astype(jnp.bfloat16)


def combine(spots, parts, residual):
    tokens, width = residual.shape
    block = 256
    row_spec = pl.BlockSpec((block, width), lambda step: (step, 0))
    return pl.pallas_call(
        combine_kernel,
        grid=(tokens // block,),
        in_specs=[
            pl.BlockSpec((block, TILE), lambda step: (step, 0)),
            pl.BlockSpec(parts.shape, lambda step: (0, 0)),
            row_spec,
        ],
        out_specs=row_spec,
        out_shape=jax.ShapeDtypeStruct((tokens, width), jnp.bfloat16),
        compiler_params=pltpu.CompilerParams(vmem_limit_bytes=VMEM_CAP),
        name="combine",
    )(spots, parts, residual)


def swap_groups(axis, size, shift, count):
    return [
        [(index, index ^ (step << shift)) for index in range(size)] for step in range(1, count)
    ]


def sum_stages(axis_sizes):
    stages = []
    for axis, size in axis_sizes:
        shift = 0
        while (1 << shift) < size:
            count = min(4, size >> shift)
            place = (lax.axis_index(axis) >> shift) & (count - 1)
            stages.append((axis, place, swap_groups(axis, size, shift, count)))
            shift += count.bit_length() - 1
    return stages


def weight_kernel(core_ref, left_ref, right_ref, away_ref, kept_ref, square):
    square[...] = times(left_ref[...], right_ref[...])
    part = away_ref.shape[0]
    away = pl.ds(pl.multiple_of((1 - core_ref[0]) * part, 16), part)
    kept = pl.ds(pl.multiple_of(core_ref[0] * part, 16), part)
    away_ref[...] = square[away, :].astype(jnp.bfloat16)
    kept_ref[...] = square[kept, :].astype(jnp.bfloat16)


def weight_terms(core, left_t, right):
    width = left_t.shape[0]
    vmem = pl.BlockSpec(memory_space=pltpu.VMEM)
    half = jax.ShapeDtypeStruct((width // 2, right.shape[1]), jnp.bfloat16)
    return pl.pallas_call(
        weight_kernel,
        in_specs=[pl.BlockSpec(memory_space=pltpu.SMEM), vmem, vmem],
        out_specs=[vmem, vmem],
        out_shape=[half, half],
        scratch_shapes=[pltpu.VMEM((width, right.shape[1]), jnp.float32)],
        compiler_params=pltpu.CompilerParams(vmem_limit_bytes=VMEM_CAP),
        cost_estimate=pl.CostEstimate(
            flops=2 * width * left_t.shape[1] * right.shape[1],
            bytes_accessed=2 * (width + right.shape[1]) * left_t.shape[1],
            transcendentals=0,
        ),
        name="weight_terms",
    )(core, left_t, right)


def cut_pieces(place, source, own_ref, sent_refs):
    rows = own_ref.shape[0]
    for step, ref in enumerate((own_ref, *sent_refs)):
        first = pl.multiple_of((place ^ step) * rows, 16)
        ref[...] = source[pl.ds(first, rows), :].astype(ref.dtype)


def padded_rows(rows, count):
    return -(-rows // (16 * count)) * 16 * count


def piece_shapes(rows, width, count):
    own = jax.ShapeDtypeStruct((rows // count, width), jnp.float32)
    sent = jax.ShapeDtypeStruct((rows // count, width), jnp.bfloat16)
    return [own] + [sent] * (count - 1)


def first_pieces_kernel(
    place_ref, kept_ref, got_ref, kept_out, got_out, gain_ref, router_one, router_two, sums_ref,
    *rest, experts,
):
    outs, small, sums = rest[:-2], rest[-2], rest[-1]
    small[...] = jnp.zeros_like(small)
    sums[...] = jnp.zeros_like(sums)
    for pair in range(sums_ref.shape[0]):
        sums[2 * pair : 2 * pair + 2, :] = sums_ref[pair]
    small[:8, :] = gain_ref[...]
    small[8 : 8 + experts, :] = router_one[:experts] + router_two[:experts]
    lanes = lax.broadcasted_iota(jnp.int32, (TILE, sums.shape[1]), 1)
    names = lax.broadcasted_iota(jnp.int32, (TILE, sums.shape[1]), 0)
    onehot = (bucket_of(lanes - (2 * TILE - 1)) == names).astype(jnp.float32)
    small[8 + experts : 8 + experts + sums.shape[0], :TILE] = lax.dot_general(
        sums[...], onehot, (((1,), (1,)), ((), ())),
        precision=lax.Precision.HIGHEST, preferred_element_type=jnp.float32,
    )
    matrices, part = kept_ref.shape[:2]
    share = part // len(outs)
    extra = small.shape[0] // len(outs)
    for step, ref in enumerate(outs):
        place = place_ref[0] ^ step
        rows = pl.ds(pl.multiple_of(place * share, 16), share)
        for index in range(matrices):
            ref[index * share : (index + 1) * share, :] = (
                kept_ref[index, rows, :].astype(jnp.float32)
                + got_ref[index, rows, :].astype(jnp.float32)
            ).astype(ref.dtype)
        first = matrices * share
        ref[first : first + share, :] = (
            kept_out[rows, :].astype(jnp.float32) + got_out[rows, :].astype(jnp.float32)
        ).astype(ref.dtype)
        rows = pl.ds(pl.multiple_of(place * extra, 16), extra)
        ref[first + share :, :] = small[rows, :].astype(ref.dtype)


def first_pieces(place, kept, got, kept_out, got_out, gain_terms, router_terms, sums, experts, count):
    matrices, part, width = kept.shape
    sum_rows = -(-2 * sums.shape[0] // 8) * 8
    extra = padded_rows(8 + experts + sum_rows, count)
    rows = (matrices + 1) * part + extra
    vmem = pl.BlockSpec(memory_space=pltpu.VMEM)
    shapes = piece_shapes(rows, width, count)
    return pl.pallas_call(
        functools.partial(first_pieces_kernel, experts=experts),
        in_specs=[pl.BlockSpec(memory_space=pltpu.SMEM)] + [vmem] * 8,
        out_specs=[vmem] * len(shapes),
        out_shape=shapes,
        scratch_shapes=[
            pltpu.VMEM((extra, width), jnp.float32),
            pltpu.VMEM((sum_rows, sums.shape[2]), jnp.float32),
        ],
        compiler_params=pltpu.CompilerParams(vmem_limit_bytes=63 * 1024 * 1024),
        name="first_pieces",
    )(
        place.reshape(1).astype(jnp.int32), kept, got, kept_out, got_out, gain_terms,
        *router_terms, sums,
    )


def next_pieces_kernel(place_ref, *rest, received):
    total = rest[0][...]
    for ref in rest[1 : received + 1]:
        total = total + ref[...].astype(jnp.float32)
    outs = rest[received + 1 : -1]
    rows = total.shape[0]
    rest[-1][:rows, :] = total
    if rest[-1].shape[0] > rows:
        extra = rest[-1].shape[0] - rows
        rest[-1][rows:, :] = jnp.zeros((extra, total.shape[1]), jnp.float32)
    cut_pieces(place_ref[0], rest[-1], outs[0], outs[1:])


def next_pieces(place, own, got, count):
    rows, width = own.shape
    vmem = pl.BlockSpec(memory_space=pltpu.VMEM)
    padded = padded_rows(rows, count)
    shapes = piece_shapes(padded, width, count)
    if count == 1:
        shapes = [jax.ShapeDtypeStruct((rows, width), jnp.bfloat16)]
    return pl.pallas_call(
        functools.partial(next_pieces_kernel, received=len(got)),
        in_specs=[pl.BlockSpec(memory_space=pltpu.SMEM)] + [vmem] * (1 + len(got)),
        out_specs=[vmem] * len(shapes),
        out_shape=shapes,
        scratch_shapes=[pltpu.VMEM((padded, width), jnp.float32)],
        compiler_params=pltpu.CompilerParams(vmem_limit_bytes=20 * 1024 * 1024),
        name="next_pieces",
    )(place.reshape(1).astype(jnp.int32), own, *got)


def pieces_kernel(place_ref, *refs):
    pieces, out_ref, joined = refs[:-2], refs[-2], refs[-1]
    rows = pieces[0].shape[0]
    for step, ref in enumerate(pieces):
        first = pl.multiple_of((place_ref[0] ^ step) * rows, 16)
        joined[pl.ds(first, rows), :] = ref[...]
    out_ref[...] = joined[: out_ref.shape[0], :]


def join_pieces(place, pieces, kept):
    rows, width = pieces[0].shape
    return pl.pallas_call(
        pieces_kernel,
        in_specs=[pl.BlockSpec(memory_space=pltpu.SMEM)]
        + [pl.BlockSpec(memory_space=pltpu.VMEM)] * len(pieces),
        out_specs=pl.BlockSpec(memory_space=pltpu.VMEM),
        out_shape=jax.ShapeDtypeStruct((kept, width), pieces[0].dtype),
        scratch_shapes=[pltpu.VMEM((len(pieces) * rows, width), pieces[0].dtype)],
        compiler_params=pltpu.CompilerParams(vmem_limit_bytes=20 * 1024 * 1024),
        name="join_pieces",
    )(place.reshape(1).astype(jnp.int32), *pieces)


def finish_kernel(
    place_ref, *rest, count, table
):
    pieces, rest = rest[: 2 * count], rest[2 * count :]
    weight_refs, gain_ref, rest = rest[:3], rest[3], rest[4:]
    square_outs, (gain_out, second_out, router_out, table_out), rest = rest[:4], rest[4:8], rest[8:]
    weights, squares, columns, small, load_sems, store_sems = rest
    core, place = place_ref[0], place_ref[1]
    width = weights.shape[2]
    part = width // 2
    share = part // count
    loads = [
        pltpu.make_async_copy(ref, weights.at[index], load_sems.at[index])
        for index, ref in enumerate(weight_refs)
    ]
    for load in loads:
        load.start()
    spots = []
    for step in range(count):
        for other in range(2):
            half = 1 - core if other else core
            first = half * part + (place ^ step) * share
            spots.append((pieces[2 * step + other], pl.ds(pl.multiple_of(first, 16), share)))
    stores = []
    for index in (3, 0, 1, 2):
        if index < 3:
            loads[index].wait()
        for ref, rows in spots:
            total = ref[index * share : (index + 1) * share, :].astype(jnp.float32)
            squares[index, rows, :] = total
            if index == 3:
                continue
            term = jnp.sum(
                total * weights[index, rows, :].astype(jnp.float32), axis=1, keepdims=True
            )
            if index == 0:
                columns[rows, :] = jnp.broadcast_to(term, (share, TILE))
            else:
                columns[rows, :] += jnp.broadcast_to(term, (share, TILE))
        store = pltpu.make_async_copy(squares.at[index], square_outs[index], store_sems.at[index])
        store.start()
        stores.append(store)
    gain = jnp.transpose(columns[...])[:1] / gain_ref[...]
    gain_out[...] = gain.reshape(width)
    extra = small.shape[0] // count
    for step in range(count):
        rows = pl.ds(pl.multiple_of((place ^ step) * extra, 16), extra)
        small[rows, :] = pieces[2 * step][4 * share :, :].astype(jnp.float32) + pieces[2 * step + 1][
            4 * share :, :
        ].astype(jnp.float32)
    experts = router_out.shape[0]
    buckets, heads = table
    second_out[...] = jnp.sum(small[:8, :], axis=0, keepdims=True).reshape(width)
    router_out[...] = small[8 : 8 + experts, :]
    table_out[...] = small[8 + experts : 8 + experts + heads, :buckets]
    for store in stores:
        store.wait()


def finish(places, pieces, weights, gain_row, experts, table):
    width = weights[0].shape[1]
    count = len(pieces) // 2
    square = jax.ShapeDtypeStruct((width, width), jnp.float32)
    row = jax.ShapeDtypeStruct((width,), jnp.float32)
    vmem = pl.BlockSpec(memory_space=pltpu.VMEM)
    extra = pieces[0].shape[0] - 4 * (width // 2 // count)
    return pl.pallas_call(
        functools.partial(finish_kernel, count=count, table=table),
        in_specs=[pl.BlockSpec(memory_space=pltpu.SMEM)]
        + [vmem] * len(pieces)
        + [pl.BlockSpec(memory_space=pl.ANY)] * 3
        + [vmem],
        out_specs=[pl.BlockSpec(memory_space=pl.ANY)] * 4 + [vmem] * 4,
        out_shape=[
            square, square, square, square, row, row,
            jax.ShapeDtypeStruct((experts, width), jnp.float32),
            jax.ShapeDtypeStruct(table[::-1], jnp.float32),
        ],
        scratch_shapes=[
            pltpu.VMEM((3, width, width), jnp.bfloat16),
            pltpu.VMEM((4, width, width), jnp.float32),
            pltpu.VMEM((width, TILE), jnp.float32),
            pltpu.VMEM((count * extra, width), jnp.float32),
            pltpu.SemaphoreType.DMA((3,)),
            pltpu.SemaphoreType.DMA((4,)),
        ],
        compiler_params=pltpu.CompilerParams(vmem_limit_bytes=VMEM_CAP),
        name="finish",
    )(places, *pieces, *weights, gain_row)


def hidden_kernel(
    grads_ref, query_ref, key_ref, value_ref, hidden_ref, gain_ref, residual_grad_ref, out_ref
):
    total = None
    for index, weight in enumerate((query_ref, key_ref, value_ref)):
        term = times_transposed(grads_ref[index], weight[...])
        total = term if total is None else total + term
    hidden = hidden_ref[...].astype(jnp.float32)
    inverse = lax.rsqrt(jnp.mean(hidden * hidden, axis=1, keepdims=True) + eps_norm)
    scaled = hidden * inverse
    weighted = total * gain_ref[...]
    spread = jnp.mean(weighted * scaled, axis=1, keepdims=True)
    out_ref[...] = (
        residual_grad_ref[...].astype(jnp.float32) + inverse * (weighted - scaled * spread)
    ).astype(jnp.bfloat16)


def hidden_gradient(grads, weights, hidden, gain_row, residual_grad):
    tokens, width = hidden.shape
    block = 256
    row_spec = pl.BlockSpec((block, width), lambda step: (step, 0))
    whole = lambda shape: pl.BlockSpec(shape, lambda step: (0, 0))
    return pl.pallas_call(
        hidden_kernel,
        grid=(tokens // block,),
        in_specs=[pl.BlockSpec((3, block, width), lambda step: (0, step, 0))]
        + [whole(weight.shape) for weight in weights]
        + [row_spec, whole(gain_row.shape), row_spec],
        out_specs=row_spec,
        out_shape=jax.ShapeDtypeStruct((tokens, width), jnp.bfloat16),
        compiler_params=pltpu.CompilerParams(vmem_limit_bytes=VMEM_CAP),
        cost_estimate=pl.CostEstimate(
            flops=6 * tokens * width * width, bytes_accessed=20 * tokens * width, transcendentals=0
        ),
        name="hidden_gradient",
    )(grads, *weights, hidden, gain_row, residual_grad)


def exchange_pieces(stage, pieces):
    axis, _, swaps = stage
    return [lax.ppermute(piece, axis, pairs) for piece, pairs in zip(pieces, swaps)]


def gather_stage(low, stage, kept):
    return join_pieces(stage[1], [low] + exchange_pieces(stage, [low] * len(stage[2])), kept)


def on_device(
    hidden_in,
    first_gain,
    w_query,
    w_key,
    w_value,
    w_output,
    rel_table,
    second_gain,
    router,
    expert_up,
    expert_down,
    routes,
    capacity_factor,
    cotangent,
):
    axes = ("narrow", "wide")
    chunks = 2
    tokens, width = hidden_in.shape
    bucket_count = rel_table.shape[0]
    experts = router.shape[1]
    slots = 2 * tokens // experts
    capacity = capacity_factor * tokens // experts
    devices = lax.axis_size(axes)
    own = lax.axis_index(axes).astype(jnp.int32).reshape(1)
    padded = -(-experts // TILE) * TILE
    router_wide = jnp.pad(router, ((0, 0), (0, padded - experts)))

    def exchange(rows):
        blocks = rows.reshape(experts, -1, width)
        return lax.all_to_all(blocks, axes, split_axis=0, concat_axis=0, tiled=True).reshape(
            -1, width
        )

    together = lax.optimization_barrier
    sent_ups, place, spots = send_first(
        capacity, routes.reshape(1, tokens), cotangent, experts, slots, chunks
    )
    sent_ups, hidden_in = together((sent_ups, hidden_in))
    ups = exchange(sent_ups)

    band, edges = bias_band(rel_table)
    hidden = hidden_in.astype(jnp.float32)
    gain_one = first_gain.astype(jnp.float32)
    gain_two = second_gain.astype(jnp.float32)
    inverse_one = lax.rsqrt(jnp.mean(hidden * hidden, axis=-1, keepdims=True) + eps_norm)
    normed_first = (hidden * inverse_one * gain_one).astype(jnp.bfloat16)
    queries = times(normed_first, w_query).astype(jnp.bfloat16)
    keys = times(normed_first, w_key).astype(jnp.bfloat16)
    values = times(normed_first, w_value).astype(jnp.bfloat16)
    attended, attended_t, logs = attend(queries, keys, values, band, edges)
    residual = hidden + times(attended, w_output)
    inverse_two = lax.rsqrt(jnp.mean(residual * residual, axis=-1, keepdims=True) + eps_norm)
    normed_second = (residual * inverse_two * gain_two).astype(jnp.bfloat16)
    half = experts * slots // chunks
    sent = send_again(place, normed_second, 0, half)
    sent, ups = together((sent, ups))
    rows = [exchange(sent)]
    queries_again, _ = together((queries, ups))
    weights, normed_t = attend_weights(queries_again, keys, logs, band, edges, normed_first)
    sent = send_again(place, normed_second, half, half)
    sent, rows[0], weights, normed_t = together((sent, rows[0], weights, normed_t))
    rows.append(exchange(sent))
    ups = ups.reshape(experts, chunks, slots // chunks, width)

    saved = ()
    input_grads, router_terms = [], []
    for c in range(chunks):
        input_grad, router_term, *saved = expert_pass(
            own, rows[c], ups, expert_up[0], expert_down[0], router_wide, experts, c, saved
        )
        if c + 1 < chunks:
            input_grad, rows[-1] = together((input_grad, rows[-1]))
        if input_grads:
            input_grad, input_grads[-1] = together((input_grad, input_grads[-1]))
        input_grads.append(exchange(input_grad))
        router_terms.append(router_term)
    saved, input_grads[0] = together((saved, input_grads[0]))
    produced = saved[0].reshape(-1, width)
    activated, pre_grad, slot_grad, kept_rows = [
        array.reshape(-1, array.shape[-1]) for array in saved[1:]
    ]
    gradient_expert_down = inner_rows(activated, slot_grad)[None]
    gradient_expert_up = inner_rows(kept_rows, pre_grad)[None]
    fetched = fetch_first(spots, input_grads[0])
    gain_row = gain_two[None]
    input_grads[-1], fetched, gradient_expert_down, gradient_expert_up, produced, gain_row = together(
        (input_grads[-1], fetched, gradient_expert_down, gradient_expert_up, produced, gain_row)
    )
    produced = exchange(produced)
    out_grad, attended_grad, gain_terms = fetch_grads(
        spots, fetched, input_grads[-1], residual, gain_row, cotangent, w_output
    )
    core = lax.axis_index("narrow").astype(jnp.int32).reshape(1)
    swap = [(0, 1), (1, 0)]
    grads, away, kept, sums = attend_back(
        core, queries, keys, values, attended_grad, attended, weights, normed_t
    )
    got = lax.ppermute(away, "narrow", swap)
    out_grad, kept = together((out_grad, kept))
    away_out, kept_out = weight_terms(core, attended_t, out_grad)
    got_out = lax.ppermute(away_out, "narrow", swap)
    stages = sum_stages([("wide", lax.axis_size("wide"))])
    counts = [len(stage[2]) + 1 for stage in stages]
    own, *sent = first_pieces(
        stages[0][1], kept, got, kept_out, got_out, gain_terms, router_terms, sums, experts, counts[0]
    )
    projections = (w_query, w_key, w_value)
    grads, kept = together((grads, kept))
    gradient_hidden = hidden_gradient(
        grads, projections, hidden_in, gain_one[None], out_grad
    )
    rows_at = []
    for level, stage in enumerate(stages):
        rows_at.append(own.shape[0])
        got = exchange_pieces(stage, sent)
        last = level + 1 == len(stages)
        place_next = jnp.zeros((), jnp.int32) if last else stages[level + 1][1]
        own, *sent = next_pieces(place_next, own, got, 1 if last else counts[level + 1])
        if level == 0:
            own, gradient_hidden = together((own, gradient_hidden))
    low = own
    for level in reversed(range(1, len(stages))):
        low = gather_stage(low, stages[level], rows_at[level - 1])
    low, produced = together((low, produced))
    block_out = combine(spots, produced, residual)
    pieces = [low] + exchange_pieces(stages[0], [low] * (counts[0] - 1))
    places = jnp.concatenate([core, stages[0][1].reshape(1).astype(jnp.int32)])
    pieces[1], block_out, places = together((pieces[1], block_out, places))
    others = [lax.ppermute(piece, "narrow", swap) for piece in pieces]
    (
        gradient_query, gradient_key, gradient_value, gradient_output, gradient_first_gain,
        gradient_second_gain, gradient_router, gradient_table,
    ) = finish(
        places, [piece for both in zip(pieces, others) for piece in both], projections,
        gain_one[None], experts, rel_table.shape,
    )
    return (
        block_out,
        gradient_hidden,
        gradient_first_gain,
        gradient_query,
        gradient_key,
        gradient_value,
        gradient_output,
        jnp.transpose(gradient_table),
        gradient_second_gain,
        jnp.transpose(gradient_router),
        gradient_expert_up,
        gradient_expert_down,
    )


def solution(mesh):
    split = ("narrow", "wide")
    rows, experts = P(split, None), P(split, None, None)
    return jax.shard_map(
        on_device,
        mesh=mesh,
        in_specs=(rows,) + (P(),) * 8 + (experts, experts, rows, P(split), rows),
        out_specs=(rows, rows) + (P(),) * 8 + (experts, experts),
        check_vma=False,
    )
```

```python
import functools

import jax
import jax.numpy as jnp
from jax import lax
from jax.experimental import pallas as pl
from jax.experimental.pallas import tpu as pltpu
from jax.sharding import PartitionSpec as P

TILE = 128
STRIP = 256
BACK_STRIP = 512
VMEM_CAP = 60 * 1024 * 1024
eps_norm = 1e-06
bucket_edges = (12, 16, 23, 32, 46, 64, 91)


def bucket_of(offset):
    distance = jnp.abs(offset)
    far_bucket = jnp.full(distance.shape, 8, jnp.int32)
    for edge in bucket_edges:
        far_bucket = far_bucket + (distance >= edge).astype(jnp.int32)
    near_bucket = jnp.where(distance < 8, distance, far_bucket)
    return near_bucket + 16 * (offset > 0).astype(jnp.int32)


def band_buckets():
    rows = lax.broadcasted_iota(jnp.int32, (3 * TILE, TILE), 0)
    lanes = lax.broadcasted_iota(jnp.int32, (3 * TILE, TILE), 1)
    return bucket_of(rows - TILE - lanes)


def times_transposed(left, right):
    return lax.dot_general(
        left, right, (((1,), (1,)), ((), ())), preferred_element_type=jnp.float32
    )


def inner_rows(left, right):
    return lax.dot_general(
        left, right, (((0,), (0,)), ((), ())), preferred_element_type=jnp.float32
    )


def times(left, right):
    return jnp.dot(left, right, preferred_element_type=jnp.float32)


def fill_wide(edge_ref, band_ref, wide):
    length = (wide.shape[1] + TILE) // 2
    pair = pl.program_id(0)
    for side in range(2):
        head = 2 * pair + side
        wide[side, : length - 2 * TILE] = jnp.full(
            (length - 2 * TILE, TILE), edge_ref[head, 0], jnp.float32
        )
        wide[side, length - 2 * TILE : length + TILE] = band_ref[side]
        wide[side, length + TILE :] = jnp.full(
            (length - 2 * TILE, TILE), edge_ref[head, 1], jnp.float32
        )


def strip_bias(wide, side, key_start, keys, query_start):
    length = (wide.shape[1] + TILE) // 2
    parts = []
    for start in range(query_start, query_start + STRIP, TILE):
        first = length - TILE - start + key_start
        parts.append(wide[side, first : first + keys, :])
    return jnp.concatenate(parts, axis=1)


def half_of(rows, side):
    half = rows.shape[1] // 2
    lanes = lax.broadcasted_iota(jnp.int32, rows.shape, 1)
    own = lanes < half if side == 0 else lanes >= half
    return jnp.where(own, rows, jnp.zeros_like(rows))


def attend_kernel(
    edge_ref, q_ref, k_ref, v_ref, band_ref, out_ref, turned_ref, log_ref, wide
):
    length = q_ref.shape[0]
    half = q_ref.shape[1] // 2
    scale = half ** (-0.5)
    fill_wide(edge_ref, band_ref, wide)
    keys = k_ref[...]
    values_t = jnp.transpose(v_ref[...])
    for start in range(0, length, STRIP):
        mixed = []
        for side in range(2):
            query = half_of(q_ref[start : start + STRIP, :] * scale, side)
            scores = times_transposed(keys, query) + strip_bias(wide, side, 0, length, start)
            top = jnp.max(scores, axis=0, keepdims=True)
            powers = jnp.exp(scores - top)
            total = jnp.sum(powers, axis=0, keepdims=True)
            raw = times(values_t[side * half : (side + 1) * half], powers.astype(jnp.bfloat16))
            mixed.append(raw / total)
            log_ref[0, side : side + 1, start : start + STRIP] = top + jnp.log(total)
        both = jnp.concatenate(mixed, axis=0)
        out_ref[start : start + STRIP, :] = jnp.transpose(both).astype(jnp.bfloat16)
        turned_ref[:, start : start + STRIP] = both.astype(jnp.bfloat16)


def attend(queries, keys, values, band, edges):
    length, width = queries.shape
    heads = edges.shape[0]
    pairs = heads // 2
    columns = width // pairs
    part = pl.BlockSpec((length, columns), lambda pair: (0, pair))
    return pl.pallas_call(
        attend_kernel,
        grid=(pairs,),
        in_specs=[
            pl.BlockSpec(memory_space=pltpu.SMEM),
            part,
            part,
            part,
            pl.BlockSpec((2, 3 * TILE, TILE), lambda pair: (pair, 0, 0)),
        ],
        out_specs=[
            part,
            pl.BlockSpec((columns, length), lambda pair: (pair, 0)),
            pl.BlockSpec((1, 2, length), lambda pair: (pair, 0, 0)),
        ],
        out_shape=[
            jax.ShapeDtypeStruct((length, width), jnp.bfloat16),
            jax.ShapeDtypeStruct((width, length), jnp.bfloat16),
            jax.ShapeDtypeStruct((pairs, 2, length), jnp.float32),
        ],
        scratch_shapes=[pltpu.VMEM((2, 2 * length - TILE, TILE), jnp.float32)],
        compiler_params=pltpu.CompilerParams(vmem_limit_bytes=VMEM_CAP),
        cost_estimate=pl.CostEstimate(
            flops=4 * heads * length * length * (width // heads),
            bytes_accessed=8 * length * width,
            transcendentals=heads * length * length,
        ),
        name="attend",
    )(edges, queries, keys, values, band)


def weights_kernel(
    edge_ref, q_ref, k_ref, log_ref, band_ref, normed_ref, weights_ref, turned_ref, wide
):
    length = q_ref.shape[0]
    scale = (q_ref.shape[1] // 2) ** (-0.5)
    head = 2 * pl.program_id(0)
    for side in range(2):
        turned = [
            jnp.transpose(band_ref[side, part : part + TILE, :]) for part in range(0, 3 * TILE, TILE)
        ]
        wide[side, :, : length - 2 * TILE] = jnp.full(
            (TILE, length - 2 * TILE), edge_ref[head + side, 0], jnp.float32
        )
        wide[side, :, length - 2 * TILE : length + TILE] = jnp.concatenate(turned, axis=1)
        wide[side, :, length + TILE :] = jnp.full(
            (TILE, length - 2 * TILE), edge_ref[head + side, 1], jnp.float32
        )
    keys = k_ref[...]
    turned_ref[...] = jnp.transpose(normed_ref[...])
    for start in range(0, length, STRIP):
        strip = slice(start, start + STRIP)
        for side in range(2):
            query = half_of(q_ref[strip, :] * scale, side)
            bias = jnp.concatenate(
                [
                    wide[side, :, length - TILE - first : 2 * length - TILE - first]
                    for first in range(start, start + STRIP, TILE)
                ],
                axis=0,
            )
            logs = jnp.transpose(
                jnp.broadcast_to(log_ref[0, side : side + 1, strip], (TILE, STRIP))
            )[:, :1]
            scores = times_transposed(query, keys) + bias
            weights_ref[side, strip, :] = jnp.exp(scores - logs).astype(jnp.bfloat16)


def attend_weights(queries, keys, logs, band, edges, normed):
    length, width = queries.shape
    heads = edges.shape[0]
    pairs = heads // 2
    columns = width // pairs
    part = pl.BlockSpec((length, columns), lambda pair: (0, pair))
    return pl.pallas_call(
        weights_kernel,
        grid=(pairs,),
        in_specs=[
            pl.BlockSpec(memory_space=pltpu.SMEM),
            part,
            part,
            pl.BlockSpec((1, 2, length), lambda pair: (pair, 0, 0)),
            pl.BlockSpec((2, 3 * TILE, TILE), lambda pair: (pair, 0, 0)),
            part,
        ],
        out_specs=[
            pl.BlockSpec((2, length, length), lambda pair: (pair, 0, 0)),
            pl.BlockSpec((columns, length), lambda pair: (pair, 0)),
        ],
        out_shape=[
            jax.ShapeDtypeStruct((heads, length, length), jnp.bfloat16),
            jax.ShapeDtypeStruct((width, length), jnp.bfloat16),
        ],
        scratch_shapes=[pltpu.VMEM((2, TILE, 2 * length - TILE), jnp.float32)],
        compiler_params=pltpu.CompilerParams(vmem_limit_bytes=VMEM_CAP),
        cost_estimate=pl.CostEstimate(
            flops=2 * heads * length * length * (width // heads),
            bytes_accessed=4 * length * width + 2 * heads * length * length,
            transcendentals=heads * length * length,
        ),
        name="attend_weights",
    )(edges, queries, keys, logs, band, normed)


def diagonal_sums(near_ref, side, beyond):
    span = 4 * TILE
    zeros = jnp.zeros((8, span - TILE), jnp.float32)
    total = jnp.zeros((8, span), jnp.float32)
    for block in range(3):
        for row in range(0, TILE, 8):
            first = block * TILE + row
            wide = jnp.concatenate([near_ref[side, first : first + 8, :], zeros], axis=1)
            total = total + pltpu.roll(wide, (block + 1) * TILE - 1 - row, 1)
    rows = lax.broadcasted_iota(jnp.int32, total.shape, 0)
    for bit in (1, 2, 4):
        total = jnp.where((rows & bit) != 0, pltpu.roll(total, span - bit, 1), total)
    sums = jnp.sum(total, axis=0, keepdims=True)
    lanes = lax.broadcasted_iota(jnp.int32, sums.shape, 1)
    sums = sums + jnp.where(lanes == 0, beyond[0], 0.0)
    return sums + jnp.where(lanes == span - 2, beyond[1], 0.0)


def attend_back_kernel(
    core_ref, q_ref, k_ref, v_ref, grad_ref, out_ref, weights_ref, normed_ref,
    grads_ref, away_ref, kept_ref, sums_ref,
    near_ref, query_total, square,
):
    length = q_ref.shape[0]
    columns = q_ref.shape[1]
    half = columns // 2
    blocks = length // TILE
    scale = half ** (-0.5)
    names = lax.broadcasted_iota(jnp.int32, (2 * blocks, length), 0)
    owners = lax.broadcasted_iota(jnp.int32, (2 * blocks, length), 1) // TILE
    picks = (names == owners).astype(jnp.float32).astype(jnp.bfloat16)
    queries_t = jnp.transpose(q_ref[...] * scale)
    grads_t = jnp.transpose(grad_ref[...])
    near_ref[...] = jnp.zeros_like(near_ref)
    key_parts, value_parts = [], []
    for side in range(2):
        rows = slice(side * half, (side + 1) * half)
        grad = half_of(grad_ref[...], side)
        keys = half_of(k_ref[...], side)
        center = jnp.sum(
            grad.astype(jnp.float32) * out_ref[...].astype(jnp.float32), axis=1, keepdims=True
        )
        left = jnp.concatenate([queries_t[rows], picks], axis=0)
        key_total, value_total = None, None
        for start in range(0, length, BACK_STRIP):
            strip = slice(start, start + BACK_STRIP)
            weights = weights_ref[side, strip, :]
            weight_grad = times_transposed(grad[strip], v_ref[...])
            score_grad = weights.astype(jnp.float32) * (weight_grad - center[strip])
            score_low = score_grad.astype(jnp.bfloat16)
            value_term = times(grads_t[rows, strip], weights)
            value_total = value_term if value_total is None else value_total + value_term
            key_term = times(left[:, strip], score_low)
            key_total = key_term if key_total is None else key_total + key_term
            query_term = times(score_low, keys)
            if side == 0:
                query_total[strip, :] = query_term
            else:
                query_total[strip, :] += query_term
            for row in range(0, BACK_STRIP, TILE):
                for lane in range(0, length, TILE):
                    apart = (lane - start - row) // TILE
                    if abs(apart) <= 1:
                        spot = (apart + 1) * TILE
                        near_ref[side, spot : spot + TILE, :] += score_grad[
                            row : row + TILE, lane : lane + TILE
                        ]
        key_parts.append(key_total[:half])
        value_parts.append(value_total)
        sums = key_total[half:]
        beyond = [
            jnp.sum(jnp.where(keep, sums, 0.0), keepdims=True)
            for keep in (names >= owners + 2, (names <= owners - 2) & (names < blocks))
        ]
        sums_ref[0, side : side + 1, :] = diagonal_sums(near_ref, side, beyond)
    grads_ref[0] = (query_total[...] * scale).astype(jnp.bfloat16)
    grads_ref[1] = jnp.transpose(jnp.concatenate(key_parts, axis=0)).astype(jnp.bfloat16)
    grads_ref[2] = jnp.transpose(jnp.concatenate(value_parts, axis=0)).astype(jnp.bfloat16)
    part = normed_ref.shape[0] // 2
    stacked = jnp.concatenate([grads_ref[index] for index in range(3)], axis=1)
    square[...] = times(normed_ref[...], stacked)
    away = pl.ds(pl.multiple_of((1 - core_ref[0]) * part, 16), part)
    kept = pl.ds(pl.multiple_of(core_ref[0] * part, 16), part)
    for index in range(3):
        span = slice(index * columns, (index + 1) * columns)
        away_ref[index] = square[away, span].astype(jnp.bfloat16)
        kept_ref[index] = square[kept, span].astype(jnp.bfloat16)


def attend_back(core, queries, keys, values, grads, attended, weights, normed_t):
    length, width = queries.shape
    heads = weights.shape[0]
    pairs = heads // 2
    columns = width // pairs
    part = pl.BlockSpec((length, columns), lambda pair: (0, pair))
    square = pl.BlockSpec((3, width // 2, columns), lambda pair: (0, 0, pair))
    return pl.pallas_call(
        attend_back_kernel,
        grid=(pairs,),
        in_specs=[
            pl.BlockSpec(memory_space=pltpu.SMEM),
            part, part, part, part, part,
            pl.BlockSpec((2, length, length), lambda pair: (pair, 0, 0)),
            pl.BlockSpec((width, length), lambda pair: (0, 0)),
        ],
        out_specs=[
            pl.BlockSpec((3, length, columns), lambda pair: (0, 0, pair)),
            square, square,
            pl.BlockSpec((1, 2, 4 * TILE), lambda pair: (pair, 0, 0)),
        ],
        out_shape=[
            jax.ShapeDtypeStruct((3, length, width), jnp.bfloat16),
            jax.ShapeDtypeStruct((3, width // 2, width), jnp.bfloat16),
            jax.ShapeDtypeStruct((3, width // 2, width), jnp.bfloat16),
            jax.ShapeDtypeStruct((pairs, 2, 4 * TILE), jnp.float32),
        ],
        scratch_shapes=[
            pltpu.VMEM((2, 3 * TILE, TILE), jnp.float32),
            pltpu.VMEM((length, columns), jnp.float32),
            pltpu.VMEM((width, 3 * columns), jnp.float32),
        ],
        compiler_params=pltpu.CompilerParams(vmem_limit_bytes=VMEM_CAP),
        cost_estimate=pl.CostEstimate(
            flops=10 * heads * length * length * (width // heads),
            bytes_accessed=16 * length * width + 2 * heads * length * length,
            transcendentals=0,
        ),
        name="attend_back",
    )(core, queries, keys, values, grads, attended, weights, normed_t)


def bias_band(rel_table):
    buckets, heads = rel_table.shape
    labels = band_buckets().reshape(1, -1)
    onehot = (labels == jnp.arange(buckets, dtype=jnp.int32)[:, None]).astype(jnp.bfloat16)
    band = lax.dot_general(
        rel_table, onehot, (((0,), (0,)), ((), ())), preferred_element_type=jnp.float32
    )
    half = buckets // 2
    edges = jnp.stack([rel_table[half - 1], rel_table[buckets - 1]], axis=1).astype(jnp.float32)
    return band.reshape(heads, 3 * TILE, TILE), edges


normal_tail = (
    0.14372023791716726,
    0.14167152280803838,
    0.14027055919455333,
    0.02504245305870889,
    0.1831401332067321,
    -0.1813703123183242,
    0.04752538660588183,
)
tail_pole = 0.36
normal_height = 0.3989422804014327


def gelu_and_slope(values):
    density = jnp.exp(values * values * -0.5)
    inverse = 1.0 / (1.0 + tail_pole * jnp.abs(values))
    series = jnp.full_like(values, normal_tail[-1])
    for coefficient in normal_tail[-2::-1]:
        series = series * inverse + coefficient
    tail = series * inverse * density
    below = jnp.where(values > 0, 1.0 - tail, tail)
    return values * below, below + values * (density * normal_height)


def send_kernel(
    capacity_ref, route_ref, rows_ref, sent_ref, place_ref, spots_ref, scratch, *, experts, slots, chunks
):
    tokens = route_ref.shape[1]
    block = sent_ref.shape[0]
    step = pl.program_id(0)

    @pl.when(step == 0)
    def _():
        route = route_ref[...]
        names = lax.broadcasted_iota(jnp.int32, (experts, tokens), 0)
        chosen = (names == route).astype(jnp.float32)
        early = lax.broadcasted_iota(jnp.int32, (tokens, tokens), 0)
        late = lax.broadcasted_iota(jnp.int32, (tokens, tokens), 1)
        before = (early < late).astype(jnp.float32).astype(jnp.bfloat16)
        earlier = times(chosen.astype(jnp.bfloat16), before)
        slot = jnp.sum(earlier * chosen, axis=0, keepdims=True).astype(jnp.int32)
        kept = slot < capacity_ref[0]
        share = slots // chunks
        chunk = jnp.zeros_like(slot)
        for later in range(1, chunks):
            chunk = chunk + (slot >= later * share).astype(jnp.int32)
        place = chunk * (experts * share) + route * share + (slot - chunk * share)
        place = jnp.where(kept, place, -1)
        ordered = jnp.where(kept, route * slots + slot, -1)
        scratch[...] = ordered
        place_ref[...] = place
        half = spots_ref.shape[1] // 2
        both = jnp.concatenate(
            [jnp.broadcast_to(place, (half, tokens)), jnp.broadcast_to(ordered, (half, tokens))], axis=0
        )
        spots_ref[...] = jnp.transpose(both)

    places = step * block + lax.broadcasted_iota(jnp.int32, (block, tokens), 0)
    onehot = (places == scratch[...]).astype(jnp.float32).astype(jnp.bfloat16)
    sent_ref[...] = times(onehot, rows_ref[...]).astype(jnp.bfloat16)


def send_first(capacity, route_row, rows, experts, slots, chunks):
    tokens, width = rows.shape
    total = experts * slots
    block = 512
    return pl.pallas_call(
        functools.partial(send_kernel, experts=experts, slots=slots, chunks=chunks),
        grid=(total // block,),
        in_specs=[
            pl.BlockSpec(memory_space=pltpu.SMEM),
            pl.BlockSpec((1, tokens), lambda step: (0, 0)),
            pl.BlockSpec((tokens, width), lambda step: (0, 0)),
        ],
        out_specs=[
            pl.BlockSpec((block, width), lambda step: (step, 0)),
            pl.BlockSpec((1, tokens), lambda step: (0, 0)),
            pl.BlockSpec((tokens, TILE), lambda step: (0, 0)),
        ],
        out_shape=[
            jax.ShapeDtypeStruct((total, width), jnp.bfloat16),
            jax.ShapeDtypeStruct((1, tokens), jnp.int32),
            jax.ShapeDtypeStruct((tokens, TILE), jnp.int32),
        ],
        scratch_shapes=[pltpu.VMEM((1, tokens), jnp.int32)],
        compiler_params=pltpu.CompilerParams(vmem_limit_bytes=VMEM_CAP),
        name="route_and_send",
    )(capacity, route_row, rows)


def send_again_kernel(place_ref, rows_ref, sent_ref, *, first):
    block = sent_ref.shape[0]
    tokens = rows_ref.shape[0]
    start = first + pl.program_id(0) * block
    places = start + lax.broadcasted_iota(jnp.int32, (block, tokens), 0)
    onehot = (places == place_ref[...]).astype(jnp.float32).astype(jnp.bfloat16)
    sent_ref[...] = times(onehot, rows_ref[...]).astype(jnp.bfloat16)


def send_again(place, rows, first, count):
    tokens, width = rows.shape
    block = 512
    return pl.pallas_call(
        functools.partial(send_again_kernel, first=first),
        grid=(count // block,),
        in_specs=[
            pl.BlockSpec((1, tokens), lambda step: (0, 0)),
            pl.BlockSpec((tokens, width), lambda step: (0, 0)),
        ],
        out_specs=pl.BlockSpec((block, width), lambda step: (step, 0)),
        out_shape=jax.ShapeDtypeStruct((count, width), jnp.bfloat16),
        compiler_params=pltpu.CompilerParams(vmem_limit_bytes=VMEM_CAP),
        cost_estimate=pl.CostEstimate(
            flops=2 * count * tokens * width,
            bytes_accessed=2 * (count + tokens) * width,
            transcendentals=0,
        ),
        name="send_rows",
    )(place, rows)


def expert_kernel(
    own_ref, rows_ref, ups_ref, up_ref, down_ref, router_ref, *rest, experts, piece
):
    (
        input_grad_ref, router_grad_ref, produced_ref, activated_ref, pre_grad_ref, slot_grad_ref,
        kept_ref,
    ) = rest[-7:]
    rows = rows_ref[...]
    ups = ups_ref[...].astype(jnp.float32).reshape(rows.shape)
    low_ups = ups.astype(jnp.bfloat16)
    router = router_ref[...]
    hidden = up_ref.shape[1]
    logits = times(rows, router)
    lanes = lax.broadcasted_iota(jnp.int32, logits.shape, 1)
    logits = jnp.where(lanes < experts, logits, -jnp.inf)
    powers = jnp.exp(logits - jnp.max(logits, axis=1, keepdims=True))
    chances = powers / jnp.sum(powers, axis=1, keepdims=True)
    mine = (lanes == own_ref[0]).astype(jnp.float32)
    gate = jnp.sum(chances * mine, axis=1, keepdims=True)
    gate_grad = jnp.zeros_like(gate)
    input_grad = jnp.zeros(rows.shape, jnp.float32)
    produced = jnp.zeros(rows.shape, jnp.float32)
    for first in range(0, hidden, piece):
        span = slice(first, first + piece)
        up = up_ref[:, span]
        down = down_ref[span, :]
        activated, slope = gelu_and_slope(times(rows, up))
        activated = activated.astype(jnp.bfloat16)
        back = times_transposed(low_ups, down)
        gate_grad = gate_grad + jnp.sum(
            activated.astype(jnp.float32) * back, axis=1, keepdims=True
        )
        pre_grad = (back * gate * slope).astype(jnp.bfloat16)
        activated_ref[0, :, span] = activated
        pre_grad_ref[0, :, span] = pre_grad
        input_grad = input_grad + times_transposed(pre_grad, up)
        produced = produced + times(activated, down)
    logit_grad = gate_grad * gate * (mine - chances)
    low_logit = logit_grad.astype(jnp.bfloat16)
    input_grad_ref[...] = (input_grad + times_transposed(low_logit, router)).astype(jnp.bfloat16)
    produced_ref[...] = (produced * gate).reshape(produced_ref.shape).astype(jnp.bfloat16)
    slot_grad_ref[0] = (ups * gate).astype(jnp.bfloat16)
    kept_ref[0] = rows

    @pl.when(pl.program_id(0) == 0)
    def _():
        router_grad_ref[...] = jnp.zeros_like(router_grad_ref)

    router_grad_ref[...] += times(jnp.transpose(logit_grad).astype(jnp.bfloat16), rows)


def expert_pass(own, rows, ups, up, down, router, experts, chunk, before):
    count, width = rows.shape
    groups, chunks, half = ups.shape[:3]
    hidden = up.shape[1]
    block = 256
    lanes = router.shape[1]
    row_spec = pl.BlockSpec((block, width), lambda step: (step, 0))
    whole = lambda shape: pl.BlockSpec(shape, lambda step: (0, 0))
    kept = lambda columns: pl.BlockSpec((1, block, columns), lambda step: (chunk, step, 0))
    stacked = lambda columns: jax.ShapeDtypeStruct((chunks, count, columns), jnp.bfloat16)
    slot_spec = pl.BlockSpec((block // half, 1, half, width), lambda step: (step, chunk, 0, 0))
    widths = (hidden, hidden, width, width)
    return pl.pallas_call(
        functools.partial(expert_kernel, experts=experts, piece=1024),
        grid=(count // block,),
        in_specs=[
            pl.BlockSpec(memory_space=pltpu.SMEM),
            row_spec, slot_spec,
            whole(up.shape), whole(down.shape), whole(router.shape),
        ] + [pl.BlockSpec(memory_space=pl.ANY)] * len(before),
        out_specs=[row_spec, whole((lanes, width)), slot_spec]
        + [kept(columns) for columns in widths],
        out_shape=[
            jax.ShapeDtypeStruct((count, width), jnp.bfloat16),
            jax.ShapeDtypeStruct((lanes, width), jnp.float32),
            jax.ShapeDtypeStruct((groups, chunks, half, width), jnp.bfloat16),
        ] + [stacked(columns) for columns in widths],
        input_output_aliases={6 + index: 2 + index for index in range(len(before))},
        compiler_params=pltpu.CompilerParams(vmem_limit_bytes=VMEM_CAP),
        cost_estimate=pl.CostEstimate(
            flops=8 * count * width * hidden,
            bytes_accessed=4 * width * hidden + 4 * count * hidden + 12 * count * width,
            transcendentals=2 * count * hidden,
        ),
        name="experts",
    )(own, rows, ups, up, down, router, *before)


def spread_rows(spots_ref, part_ref, first):
    target = spots_ref[:, :1]
    count = part_ref.shape[0]
    places = first + lax.broadcasted_iota(jnp.int32, (target.shape[0], count), 1)
    onehot = (places == target).astype(jnp.float32).astype(jnp.bfloat16)
    return times(onehot, part_ref[...])


def fetch_first_kernel(spots_ref, part_ref, out_ref):
    out_ref[...] = spread_rows(spots_ref, part_ref, 0).astype(jnp.bfloat16)


def fetch_first(spots, part):
    tokens = spots.shape[0]
    count, width = part.shape
    block = 256
    return pl.pallas_call(
        fetch_first_kernel,
        grid=(tokens // block,),
        in_specs=[
            pl.BlockSpec((block, TILE), lambda step: (step, 0)),
            pl.BlockSpec((count, width), lambda step: (0, 0)),
        ],
        out_specs=pl.BlockSpec((block, width), lambda step: (step, 0)),
        out_shape=jax.ShapeDtypeStruct((tokens, width), jnp.bfloat16),
        compiler_params=pltpu.CompilerParams(vmem_limit_bytes=VMEM_CAP),
        cost_estimate=pl.CostEstimate(
            flops=2 * count * tokens * width,
            bytes_accessed=4 * tokens * width,
            transcendentals=0,
        ),
        name="fetch_first",
    )(spots, part)


def fetch_kernel(
    spots_ref, early_ref, second_ref, residual_ref, gain_ref, upstream_ref, output_ref,
    out_grad_ref, attended_grad_ref, gain_grad_ref,
):
    total = early_ref[...].astype(jnp.float32) + spread_rows(spots_ref, second_ref, second_ref.shape[0])
    residual = residual_ref[...]
    inverse = lax.rsqrt(jnp.mean(residual * residual, axis=1, keepdims=True) + eps_norm)
    scaled = residual * inverse

    @pl.when(pl.program_id(0) == 0)
    def _():
        gain_grad_ref[...] = jnp.zeros_like(gain_grad_ref)

    gain_grad_ref[...] += jnp.sum((total * scaled).reshape(-1, 8, total.shape[1]), axis=0)
    weighted = total * gain_ref[...]
    spread = jnp.mean(weighted * scaled, axis=1, keepdims=True)
    residual_grad = upstream_ref[...].astype(jnp.float32) + inverse * (weighted - scaled * spread)
    low = residual_grad.astype(jnp.bfloat16)
    out_grad_ref[...] = low
    attended_grad_ref[...] = times_transposed(low, output_ref[...]).astype(jnp.bfloat16)


def fetch_grads(spots, early, second, residual, gain_row, upstream, w_output):
    tokens, width = residual.shape
    block = 256
    row_spec = pl.BlockSpec((block, width), lambda step: (step, 0))
    whole = lambda shape: pl.BlockSpec(shape, lambda step: (0, 0))
    return pl.pallas_call(
        fetch_kernel,
        grid=(tokens // block,),
        in_specs=[
            pl.BlockSpec((block, TILE), lambda step: (step, 0)),
            row_spec, whole(second.shape),
            row_spec, whole(gain_row.shape), row_spec, whole(w_output.shape),
        ],
        out_specs=[row_spec, row_spec, whole((8, width))],
        out_shape=[
            jax.ShapeDtypeStruct((tokens, width), jnp.bfloat16),
            jax.ShapeDtypeStruct((tokens, width), jnp.bfloat16),
            jax.ShapeDtypeStruct((8, width), jnp.float32),
        ],
        compiler_params=pltpu.CompilerParams(vmem_limit_bytes=63 * 1024 * 1024),
        name="fetch_grads",
    )(spots, early, second, residual, gain_row, upstream, w_output)


def combine_kernel(spots_ref, parts_ref, residual_ref, out_ref):
    column = spots_ref.shape[1] // 2
    target = spots_ref[:, column : column + 1]
    count = parts_ref.shape[0]
    places = lax.broadcasted_iota(jnp.int32, (target.shape[0], count), 1)
    onehot = (places == target).astype(jnp.float32).astype(jnp.bfloat16)
    out_ref[...] = (residual_ref[...] + times(onehot, parts_ref[...])).astype(jnp.bfloat16)


def combine(spots, parts, residual):
    tokens, width = residual.shape
    block = 256
    row_spec = pl.BlockSpec((block, width), lambda step: (step, 0))
    return pl.pallas_call(
        combine_kernel,
        grid=(tokens // block,),
        in_specs=[
            pl.BlockSpec((block, TILE), lambda step: (step, 0)),
            pl.BlockSpec(parts.shape, lambda step: (0, 0)),
            row_spec,
        ],
        out_specs=row_spec,
        out_shape=jax.ShapeDtypeStruct((tokens, width), jnp.bfloat16),
        compiler_params=pltpu.CompilerParams(vmem_limit_bytes=VMEM_CAP),
        name="combine",
    )(spots, parts, residual)


def swap_groups(axis, size, shift, count):
    return [
        [(index, index ^ (step << shift)) for index in range(size)] for step in range(1, count)
    ]


def sum_stages(axis_sizes):
    stages = []
    for axis, size in axis_sizes:
        shift = 0
        while (1 << shift) < size:
            count = min(4, size >> shift)
            place = (lax.axis_index(axis) >> shift) & (count - 1)
            stages.append((axis, place, swap_groups(axis, size, shift, count)))
            shift += count.bit_length() - 1
    return stages


def weight_kernel(core_ref, left_ref, right_ref, away_ref, kept_ref, square):
    square[...] = times(left_ref[...], right_ref[...])
    part = away_ref.shape[0]
    away = pl.ds(pl.multiple_of((1 - core_ref[0]) * part, 16), part)
    kept = pl.ds(pl.multiple_of(core_ref[0] * part, 16), part)
    away_ref[...] = square[away, :].astype(jnp.bfloat16)
    kept_ref[...] = square[kept, :].astype(jnp.bfloat16)


def weight_terms(core, left_t, right):
    width = left_t.shape[0]
    vmem = pl.BlockSpec(memory_space=pltpu.VMEM)
    half = jax.ShapeDtypeStruct((width // 2, right.shape[1]), jnp.bfloat16)
    return pl.pallas_call(
        weight_kernel,
        in_specs=[pl.BlockSpec(memory_space=pltpu.SMEM), vmem, vmem],
        out_specs=[vmem, vmem],
        out_shape=[half, half],
        scratch_shapes=[pltpu.VMEM((width, right.shape[1]), jnp.float32)],
        compiler_params=pltpu.CompilerParams(vmem_limit_bytes=24 * 1024 * 1024),
        cost_estimate=pl.CostEstimate(
            flops=2 * width * left_t.shape[1] * right.shape[1],
            bytes_accessed=2 * (width + right.shape[1]) * left_t.shape[1],
            transcendentals=0,
        ),
        name="weight_terms",
    )(core, left_t, right)


def cut_pieces(place, source, own_ref, sent_refs):
    rows = own_ref.shape[0]
    for step, ref in enumerate((own_ref, *sent_refs)):
        first = pl.multiple_of((place ^ step) * rows, 16)
        ref[...] = source[pl.ds(first, rows), :].astype(ref.dtype)


def padded_rows(rows, count):
    return -(-rows // (16 * count)) * 16 * count


def piece_shapes(rows, width, count):
    own = jax.ShapeDtypeStruct((rows // count, width), jnp.float32)
    sent = jax.ShapeDtypeStruct((rows // count, width), jnp.bfloat16)
    return [own] + [sent] * (count - 1)


def first_pieces_kernel(
    place_ref, kept_ref, got_ref, kept_out, got_out, gain_ref, router_one, router_two, sums_ref,
    *rest, experts,
):
    outs, small, sums = rest[:-2], rest[-2], rest[-1]
    small[...] = jnp.zeros_like(small)
    sums[...] = jnp.zeros_like(sums)
    for pair in range(sums_ref.shape[0]):
        sums[2 * pair : 2 * pair + 2, :] = sums_ref[pair]
    small[:8, :] = gain_ref[...]
    small[8 : 8 + experts, :] = router_one[:experts] + router_two[:experts]
    lanes = lax.broadcasted_iota(jnp.int32, (TILE, sums.shape[1]), 1)
    names = lax.broadcasted_iota(jnp.int32, (TILE, sums.shape[1]), 0)
    onehot = (bucket_of(lanes - (2 * TILE - 1)) == names).astype(jnp.float32)
    small[8 + experts : 8 + experts + sums.shape[0], :TILE] = lax.dot_general(
        sums[...], onehot, (((1,), (1,)), ((), ())),
        precision=lax.Precision.HIGHEST, preferred_element_type=jnp.float32,
    )
    matrices, part = kept_ref.shape[:2]
    share = part // len(outs)
    extra = small.shape[0] // len(outs)
    for step, ref in enumerate(outs):
        place = place_ref[0] ^ step
        rows = pl.ds(pl.multiple_of(place * share, 16), share)
        for index in range(matrices):
            ref[index * share : (index + 1) * share, :] = (
                kept_ref[index, rows, :].astype(jnp.float32)
                + got_ref[index, rows, :].astype(jnp.float32)
            ).astype(ref.dtype)
        first = matrices * share
        ref[first : first + share, :] = (
            kept_out[rows, :].astype(jnp.float32) + got_out[rows, :].astype(jnp.float32)
        ).astype(ref.dtype)
        rows = pl.ds(pl.multiple_of(place * extra, 16), extra)
        ref[first + share :, :] = small[rows, :].astype(ref.dtype)


def first_pieces(place, kept, got, kept_out, got_out, gain_terms, router_terms, sums, experts, count):
    matrices, part, width = kept.shape
    sum_rows = -(-2 * sums.shape[0] // 8) * 8
    extra = padded_rows(8 + experts + sum_rows, count)
    rows = (matrices + 1) * part + extra
    vmem = pl.BlockSpec(memory_space=pltpu.VMEM)
    shapes = piece_shapes(rows, width, count)
    return pl.pallas_call(
        functools.partial(first_pieces_kernel, experts=experts),
        in_specs=[pl.BlockSpec(memory_space=pltpu.SMEM)] + [vmem] * 8,
        out_specs=[vmem] * len(shapes),
        out_shape=shapes,
        scratch_shapes=[
            pltpu.VMEM((extra, width), jnp.float32),
            pltpu.VMEM((sum_rows, sums.shape[2]), jnp.float32),
        ],
        compiler_params=pltpu.CompilerParams(vmem_limit_bytes=63 * 1024 * 1024),
        name="first_pieces",
    )(
        place.reshape(1).astype(jnp.int32), kept, got, kept_out, got_out, gain_terms,
        *router_terms, sums,
    )


def next_pieces_kernel(place_ref, *rest, received):
    total = rest[0][...]
    for ref in rest[1 : received + 1]:
        total = total + ref[...].astype(jnp.float32)
    outs = rest[received + 1 : -1]
    rows = total.shape[0]
    rest[-1][:rows, :] = total
    if rest[-1].shape[0] > rows:
        extra = rest[-1].shape[0] - rows
        rest[-1][rows:, :] = jnp.zeros((extra, total.shape[1]), jnp.float32)
    cut_pieces(place_ref[0], rest[-1], outs[0], outs[1:])


def next_pieces(place, own, got, count):
    rows, width = own.shape
    vmem = pl.BlockSpec(memory_space=pltpu.VMEM)
    padded = padded_rows(rows, count)
    shapes = piece_shapes(padded, width, count)
    if count == 1:
        shapes = [jax.ShapeDtypeStruct((rows, width), jnp.bfloat16)]
    return pl.pallas_call(
        functools.partial(next_pieces_kernel, received=len(got)),
        in_specs=[pl.BlockSpec(memory_space=pltpu.SMEM)] + [vmem] * (1 + len(got)),
        out_specs=[vmem] * len(shapes),
        out_shape=shapes,
        scratch_shapes=[pltpu.VMEM((padded, width), jnp.float32)],
        compiler_params=pltpu.CompilerParams(vmem_limit_bytes=20 * 1024 * 1024),
        name="next_pieces",
    )(place.reshape(1).astype(jnp.int32), own, *got)


def pieces_kernel(place_ref, *refs):
    pieces, out_ref, joined = refs[:-2], refs[-2], refs[-1]
    rows = pieces[0].shape[0]
    for step, ref in enumerate(pieces):
        first = pl.multiple_of((place_ref[0] ^ step) * rows, 16)
        joined[pl.ds(first, rows), :] = ref[...]
    out_ref[...] = joined[: out_ref.shape[0], :]


def join_pieces(place, pieces, kept):
    rows, width = pieces[0].shape
    return pl.pallas_call(
        pieces_kernel,
        in_specs=[pl.BlockSpec(memory_space=pltpu.SMEM)]
        + [pl.BlockSpec(memory_space=pltpu.VMEM)] * len(pieces),
        out_specs=pl.BlockSpec(memory_space=pltpu.VMEM),
        out_shape=jax.ShapeDtypeStruct((kept, width), pieces[0].dtype),
        scratch_shapes=[pltpu.VMEM((len(pieces) * rows, width), pieces[0].dtype)],
        compiler_params=pltpu.CompilerParams(vmem_limit_bytes=20 * 1024 * 1024),
        name="join_pieces",
    )(place.reshape(1).astype(jnp.int32), *pieces)


def finish_kernel(
    place_ref, *rest, count, table
):
    pieces, rest = rest[: 2 * count], rest[2 * count :]
    weight_refs, gain_ref, rest = rest[:3], rest[3], rest[4:]
    square_outs, (gain_out, second_out, router_out, table_out), rest = rest[:4], rest[4:8], rest[8:]
    weights, squares, columns, small, load_sems, store_sems = rest
    core, place = place_ref[0], place_ref[1]
    width = weights.shape[2]
    part = width // 2
    share = part // count
    loads = [
        pltpu.make_async_copy(ref, weights.at[index], load_sems.at[index])
        for index, ref in enumerate(weight_refs)
    ]
    for load in loads:
        load.start()
    spots = []
    for step in range(count):
        for other in range(2):
            half = 1 - core if other else core
            first = half * part + (place ^ step) * share
            spots.append((pieces[2 * step + other], pl.ds(pl.multiple_of(first, 16), share)))
    stores = []
    for index in (3, 0, 1, 2):
        if index < 3:
            loads[index].wait()
        for ref, rows in spots:
            total = ref[index * share : (index + 1) * share, :].astype(jnp.float32)
            squares[index, rows, :] = total
            if index == 3:
                continue
            term = jnp.sum(
                total * weights[index, rows, :].astype(jnp.float32), axis=1, keepdims=True
            )
            if index == 0:
                columns[rows, :] = jnp.broadcast_to(term, (share, TILE))
            else:
                columns[rows, :] += jnp.broadcast_to(term, (share, TILE))
        store = pltpu.make_async_copy(squares.at[index], square_outs[index], store_sems.at[index])
        store.start()
        stores.append(store)
    gain = jnp.transpose(columns[...])[:1] / gain_ref[...]
    gain_out[...] = gain.reshape(width)
    extra = small.shape[0] // count
    for step in range(count):
        rows = pl.ds(pl.multiple_of((place ^ step) * extra, 16), extra)
        small[rows, :] = pieces[2 * step][4 * share :, :].astype(jnp.float32) + pieces[2 * step + 1][
            4 * share :, :
        ].astype(jnp.float32)
    experts = router_out.shape[0]
    buckets, heads = table
    second_out[...] = jnp.sum(small[:8, :], axis=0, keepdims=True).reshape(width)
    router_out[...] = small[8 : 8 + experts, :]
    table_out[...] = small[8 + experts : 8 + experts + heads, :buckets]
    for store in stores:
        store.wait()


def finish(places, pieces, weights, gain_row, experts, table):
    width = weights[0].shape[1]
    count = len(pieces) // 2
    square = jax.ShapeDtypeStruct((width, width), jnp.float32)
    row = jax.ShapeDtypeStruct((width,), jnp.float32)
    vmem = pl.BlockSpec(memory_space=pltpu.VMEM)
    extra = pieces[0].shape[0] - 4 * (width // 2 // count)
    return pl.pallas_call(
        functools.partial(finish_kernel, count=count, table=table),
        in_specs=[pl.BlockSpec(memory_space=pltpu.SMEM)]
        + [vmem] * len(pieces)
        + [pl.BlockSpec(memory_space=pl.ANY)] * 3
        + [vmem],
        out_specs=[pl.BlockSpec(memory_space=pl.ANY)] * 4 + [vmem] * 4,
        out_shape=[
            square, square, square, square, row, row,
            jax.ShapeDtypeStruct((experts, width), jnp.float32),
            jax.ShapeDtypeStruct(table[::-1], jnp.float32),
        ],
        scratch_shapes=[
            pltpu.VMEM((3, width, width), jnp.bfloat16),
            pltpu.VMEM((4, width, width), jnp.float32),
            pltpu.VMEM((width, TILE), jnp.float32),
            pltpu.VMEM((count * extra, width), jnp.float32),
            pltpu.SemaphoreType.DMA((3,)),
            pltpu.SemaphoreType.DMA((4,)),
        ],
        compiler_params=pltpu.CompilerParams(vmem_limit_bytes=VMEM_CAP),
        name="finish",
    )(places, *pieces, *weights, gain_row)


def hidden_kernel(
    grads_ref, query_ref, key_ref, value_ref, hidden_ref, gain_ref, residual_grad_ref, out_ref
):
    total = None
    for index, weight in enumerate((query_ref, key_ref, value_ref)):
        term = times_transposed(grads_ref[index], weight[...])
        total = term if total is None else total + term
    hidden = hidden_ref[...].astype(jnp.float32)
    inverse = lax.rsqrt(jnp.mean(hidden * hidden, axis=1, keepdims=True) + eps_norm)
    scaled = hidden * inverse
    weighted = total * gain_ref[...]
    spread = jnp.mean(weighted * scaled, axis=1, keepdims=True)
    out_ref[...] = (
        residual_grad_ref[...].astype(jnp.float32) + inverse * (weighted - scaled * spread)
    ).astype(jnp.bfloat16)


def hidden_gradient(grads, weights, hidden, gain_row, residual_grad):
    tokens, width = hidden.shape
    block = 256
    row_spec = pl.BlockSpec((block, width), lambda step: (step, 0))
    whole = lambda shape: pl.BlockSpec(shape, lambda step: (0, 0))
    return pl.pallas_call(
        hidden_kernel,
        grid=(tokens // block,),
        in_specs=[pl.BlockSpec((3, block, width), lambda step: (0, step, 0))]
        + [whole(weight.shape) for weight in weights]
        + [row_spec, whole(gain_row.shape), row_spec],
        out_specs=row_spec,
        out_shape=jax.ShapeDtypeStruct((tokens, width), jnp.bfloat16),
        compiler_params=pltpu.CompilerParams(vmem_limit_bytes=VMEM_CAP),
        cost_estimate=pl.CostEstimate(
            flops=6 * tokens * width * width, bytes_accessed=20 * tokens * width, transcendentals=0
        ),
        name="hidden_gradient",
    )(grads, *weights, hidden, gain_row, residual_grad)


def exchange_pieces(stage, pieces):
    axis, _, swaps = stage
    return [lax.ppermute(piece, axis, pairs) for piece, pairs in zip(pieces, swaps)]


def gather_stage(low, stage, kept):
    return join_pieces(stage[1], [low] + exchange_pieces(stage, [low] * len(stage[2])), kept)


def on_device(
    hidden_in,
    first_gain,
    w_query,
    w_key,
    w_value,
    w_output,
    rel_table,
    second_gain,
    router,
    expert_up,
    expert_down,
    routes,
    capacity_factor,
    cotangent,
):
    axes = ("narrow", "wide")
    chunks = 2
    tokens, width = hidden_in.shape
    bucket_count = rel_table.shape[0]
    experts = router.shape[1]
    slots = 2 * tokens // experts
    capacity = capacity_factor * tokens // experts
    devices = lax.axis_size(axes)
    own = lax.axis_index(axes).astype(jnp.int32).reshape(1)
    padded = -(-experts // TILE) * TILE
    router_wide = jnp.pad(router, ((0, 0), (0, padded - experts)))

    def exchange(rows):
        blocks = rows.reshape(experts, -1, width)
        return lax.all_to_all(blocks, axes, split_axis=0, concat_axis=0, tiled=True).reshape(
            -1, width
        )

    together = lax.optimization_barrier
    sent_ups, place, spots = send_first(
        capacity, routes.reshape(1, tokens), cotangent, experts, slots, chunks
    )
    sent_ups, hidden_in = together((sent_ups, hidden_in))
    ups = exchange(sent_ups)

    band, edges = bias_band(rel_table)
    hidden = hidden_in.astype(jnp.float32)
    gain_one = first_gain.astype(jnp.float32)
    gain_two = second_gain.astype(jnp.float32)
    inverse_one = lax.rsqrt(jnp.mean(hidden * hidden, axis=-1, keepdims=True) + eps_norm)
    normed_first = (hidden * inverse_one * gain_one).astype(jnp.bfloat16)
    queries = times(normed_first, w_query).astype(jnp.bfloat16)
    keys = times(normed_first, w_key).astype(jnp.bfloat16)
    values = times(normed_first, w_value).astype(jnp.bfloat16)
    attended, attended_t, logs = attend(queries, keys, values, band, edges)
    residual = hidden + times(attended, w_output)
    inverse_two = lax.rsqrt(jnp.mean(residual * residual, axis=-1, keepdims=True) + eps_norm)
    normed_second = (residual * inverse_two * gain_two).astype(jnp.bfloat16)
    half = experts * slots // chunks
    sent = send_again(place, normed_second, 0, half)
    sent, ups = together((sent, ups))
    rows = [exchange(sent)]
    queries_again, _ = together((queries, ups))
    weights, normed_t = attend_weights(queries_again, keys, logs, band, edges, normed_first)
    sent = send_again(place, normed_second, half, half)
    sent, rows[0], weights, normed_t = together((sent, rows[0], weights, normed_t))
    rows.append(exchange(sent))
    ups = ups.reshape(experts, chunks, slots // chunks, width)

    saved = ()
    input_grads, router_terms = [], []
    for c in range(chunks):
        input_grad, router_term, *saved = expert_pass(
            own, rows[c], ups, expert_up[0], expert_down[0], router_wide, experts, c, saved
        )
        if c + 1 < chunks:
            input_grad, rows[-1] = together((input_grad, rows[-1]))
        if input_grads:
            input_grad, input_grads[-1] = together((input_grad, input_grads[-1]))
        input_grads.append(exchange(input_grad))
        router_terms.append(router_term)
    saved, input_grads[0] = together((saved, input_grads[0]))
    produced = saved[0].reshape(-1, width)
    activated, pre_grad, slot_grad, kept_rows = [
        array.reshape(-1, array.shape[-1]) for array in saved[1:]
    ]
    gradient_expert_down = inner_rows(activated, slot_grad)[None]
    gradient_expert_up = inner_rows(kept_rows, pre_grad)[None]
    fetched = fetch_first(spots, input_grads[0])
    gain_row = gain_two[None]
    input_grads[-1], fetched, gradient_expert_down, gradient_expert_up, produced, gain_row = together(
        (input_grads[-1], fetched, gradient_expert_down, gradient_expert_up, produced, gain_row)
    )
    produced = exchange(produced)
    out_grad, attended_grad, gain_terms = fetch_grads(
        spots, fetched, input_grads[-1], residual, gain_row, cotangent, w_output
    )
    core = lax.axis_index("narrow").astype(jnp.int32).reshape(1)
    swap = [(0, 1), (1, 0)]
    grads, away, kept, sums = attend_back(
        core, queries, keys, values, attended_grad, attended, weights, normed_t
    )
    got = lax.ppermute(away, "narrow", swap)
    out_grad, kept = together((out_grad, kept))
    away_out, kept_out = weight_terms(core, attended_t, out_grad)
    got_out = lax.ppermute(away_out, "narrow", swap)
    stages = sum_stages([("wide", lax.axis_size("wide"))])
    counts = [len(stage[2]) + 1 for stage in stages]
    own, *sent = first_pieces(
        stages[0][1], kept, got, kept_out, got_out, gain_terms, router_terms, sums, experts, counts[0]
    )
    projections = (w_query, w_key, w_value)
    grads, kept = together((grads, kept))
    gradient_hidden = hidden_gradient(
        grads, projections, hidden_in, gain_one[None], out_grad
    )
    rows_at = []
    for level, stage in enumerate(stages):
        rows_at.append(own.shape[0])
        got = exchange_pieces(stage, sent)
        last = level + 1 == len(stages)
        place_next = jnp.zeros((), jnp.int32) if last else stages[level + 1][1]
        own, *sent = next_pieces(place_next, own, got, 1 if last else counts[level + 1])
        if level == 0:
            own, gradient_hidden = together((own, gradient_hidden))
    low = own
    for level in reversed(range(1, len(stages))):
        low = gather_stage(low, stages[level], rows_at[level - 1])
    low, produced = together((low, produced))
    block_out = combine(spots, produced, residual)
    pieces = [low] + exchange_pieces(stages[0], [low] * (counts[0] - 1))
    places = jnp.concatenate([core, stages[0][1].reshape(1).astype(jnp.int32)])
    pieces[1], block_out, places = together((pieces[1], block_out, places))
    others = [lax.ppermute(piece, "narrow", swap) for piece in pieces]
    (
        gradient_query, gradient_key, gradient_value, gradient_output, gradient_first_gain,
        gradient_second_gain, gradient_router, gradient_table,
    ) = finish(
        places, [piece for both in zip(pieces, others) for piece in both], projections,
        gain_one[None], experts, rel_table.shape,
    )
    return (
        block_out,
        gradient_hidden,
        gradient_first_gain,
        gradient_query,
        gradient_key,
        gradient_value,
        gradient_output,
        jnp.transpose(gradient_table),
        gradient_second_gain,
        jnp.transpose(gradient_router),
        gradient_expert_up,
        gradient_expert_down,
    )


def solution(mesh):
    split = ("narrow", "wide")
    rows, experts = P(split, None), P(split, None, None)
    return jax.shard_map(
        on_device,
        mesh=mesh,
        in_specs=(rows,) + (P(),) * 8 + (experts, experts, rows, P(split), rows),
        out_specs=(rows, rows) + (P(),) * 8 + (experts, experts),
        check_vma=False,
    )
```

```python
import functools

import jax
import jax.numpy as jnp
from jax import lax
from jax.experimental import pallas as pl
from jax.experimental.pallas import tpu as pltpu
from jax.sharding import PartitionSpec as P

TILE = 128
STRIP = 256
BACK_STRIP = 512
VMEM_CAP = 60 * 1024 * 1024
eps_norm = 1e-06
bucket_edges = (12, 16, 23, 32, 46, 64, 91)


def bucket_of(offset):
    distance = jnp.abs(offset)
    far_bucket = jnp.full(distance.shape, 8, jnp.int32)
    for edge in bucket_edges:
        far_bucket = far_bucket + (distance >= edge).astype(jnp.int32)
    near_bucket = jnp.where(distance < 8, distance, far_bucket)
    return near_bucket + 16 * (offset > 0).astype(jnp.int32)


def band_buckets():
    rows = lax.broadcasted_iota(jnp.int32, (3 * TILE, TILE), 0)
    lanes = lax.broadcasted_iota(jnp.int32, (3 * TILE, TILE), 1)
    return bucket_of(rows - TILE - lanes)


def times_transposed(left, right):
    return lax.dot_general(
        left, right, (((1,), (1,)), ((), ())), preferred_element_type=jnp.float32
    )


def inner_rows(left, right):
    return lax.dot_general(
        left, right, (((0,), (0,)), ((), ())), preferred_element_type=jnp.float32
    )


def times(left, right):
    return jnp.dot(left, right, preferred_element_type=jnp.float32)


def fill_wide(edge_ref, band_ref, wide):
    length = (wide.shape[1] + TILE) // 2
    pair = pl.program_id(0)
    for side in range(2):
        head = 2 * pair + side
        wide[side, : length - 2 * TILE] = jnp.full(
            (length - 2 * TILE, TILE), edge_ref[head, 0], jnp.float32
        )
        wide[side, length - 2 * TILE : length + TILE] = band_ref[side]
        wide[side, length + TILE :] = jnp.full(
            (length - 2 * TILE, TILE), edge_ref[head, 1], jnp.float32
        )


def strip_bias(wide, side, key_start, keys, query_start):
    length = (wide.shape[1] + TILE) // 2
    parts = []
    for start in range(query_start, query_start + STRIP, TILE):
        first = length - TILE - start + key_start
        parts.append(wide[side, first : first + keys, :])
    return jnp.concatenate(parts, axis=1)


def half_of(rows, side):
    half = rows.shape[1] // 2
    lanes = lax.broadcasted_iota(jnp.int32, rows.shape, 1)
    own = lanes < half if side == 0 else lanes >= half
    return jnp.where(own, rows, jnp.zeros_like(rows))


def attend_kernel(
    edge_ref, q_ref, k_ref, v_ref, band_ref, out_ref, turned_ref, log_ref, wide
):
    length = q_ref.shape[0]
    half = q_ref.shape[1] // 2
    scale = half ** (-0.5)
    fill_wide(edge_ref, band_ref, wide)
    keys = k_ref[...]
    values_t = jnp.transpose(v_ref[...])
    for start in range(0, length, STRIP):
        mixed = []
        for side in range(2):
            query = half_of(q_ref[start : start + STRIP, :] * scale, side)
            scores = times_transposed(keys, query) + strip_bias(wide, side, 0, length, start)
            top = jnp.max(scores, axis=0, keepdims=True)
            powers = jnp.exp(scores - top)
            total = jnp.sum(powers, axis=0, keepdims=True)
            raw = times(values_t[side * half : (side + 1) * half], powers.astype(jnp.bfloat16))
            mixed.append(raw / total)
            log_ref[0, side : side + 1, start : start + STRIP] = top + jnp.log(total)
        both = jnp.concatenate(mixed, axis=0)
        out_ref[start : start + STRIP, :] = jnp.transpose(both).astype(jnp.bfloat16)
        turned_ref[:, start : start + STRIP] = both.astype(jnp.bfloat16)


def attend(queries, keys, values, band, edges):
    length, width = queries.shape
    heads = edges.shape[0]
    pairs = heads // 2
    columns = width // pairs
    part = pl.BlockSpec((length, columns), lambda pair: (0, pair))
    return pl.pallas_call(
        attend_kernel,
        grid=(pairs,),
        in_specs=[
            pl.BlockSpec(memory_space=pltpu.SMEM),
            part,
            part,
            part,
            pl.BlockSpec((2, 3 * TILE, TILE), lambda pair: (pair, 0, 0)),
        ],
        out_specs=[
            part,
            pl.BlockSpec((columns, length), lambda pair: (pair, 0)),
            pl.BlockSpec((1, 2, length), lambda pair: (pair, 0, 0)),
        ],
        out_shape=[
            jax.ShapeDtypeStruct((length, width), jnp.bfloat16),
            jax.ShapeDtypeStruct((width, length), jnp.bfloat16),
            jax.ShapeDtypeStruct((pairs, 2, length), jnp.float32),
        ],
        scratch_shapes=[pltpu.VMEM((2, 2 * length - TILE, TILE), jnp.float32)],
        compiler_params=pltpu.CompilerParams(vmem_limit_bytes=VMEM_CAP),
        cost_estimate=pl.CostEstimate(
            flops=4 * heads * length * length * (width // heads),
            bytes_accessed=8 * length * width,
            transcendentals=heads * length * length,
        ),
        name="attend",
    )(edges, queries, keys, values, band)


def weights_kernel(
    edge_ref, q_ref, k_ref, log_ref, band_ref, normed_ref, weights_ref, turned_ref, wide
):
    length = q_ref.shape[0]
    scale = (q_ref.shape[1] // 2) ** (-0.5)
    head = 2 * pl.program_id(0)
    for side in range(2):
        turned = [
            jnp.transpose(band_ref[side, part : part + TILE, :]) for part in range(0, 3 * TILE, TILE)
        ]
        wide[side, :, : length - 2 * TILE] = jnp.full(
            (TILE, length - 2 * TILE), edge_ref[head + side, 0], jnp.float32
        )
        wide[side, :, length - 2 * TILE : length + TILE] = jnp.concatenate(turned, axis=1)
        wide[side, :, length + TILE :] = jnp.full(
            (TILE, length - 2 * TILE), edge_ref[head + side, 1], jnp.float32
        )
    keys = k_ref[...]
    turned_ref[...] = jnp.transpose(normed_ref[...])
    for start in range(0, length, STRIP):
        strip = slice(start, start + STRIP)
        for side in range(2):
            query = half_of(q_ref[strip, :] * scale, side)
            bias = jnp.concatenate(
                [
                    wide[side, :, length - TILE - first : 2 * length - TILE - first]
                    for first in range(start, start + STRIP, TILE)
                ],
                axis=0,
            )
            logs = jnp.transpose(
                jnp.broadcast_to(log_ref[0, side : side + 1, strip], (TILE, STRIP))
            )[:, :1]
            scores = times_transposed(query, keys) + bias
            weights_ref[side, strip, :] = jnp.exp(scores - logs).astype(jnp.bfloat16)


def attend_weights(queries, keys, logs, band, edges, normed):
    length, width = queries.shape
    heads = edges.shape[0]
    pairs = heads // 2
    columns = width // pairs
    part = pl.BlockSpec((length, columns), lambda pair: (0, pair))
    return pl.pallas_call(
        weights_kernel,
        grid=(pairs,),
        in_specs=[
            pl.BlockSpec(memory_space=pltpu.SMEM),
            part,
            part,
            pl.BlockSpec((1, 2, length), lambda pair: (pair, 0, 0)),
            pl.BlockSpec((2, 3 * TILE, TILE), lambda pair: (pair, 0, 0)),
            part,
        ],
        out_specs=[
            pl.BlockSpec((2, length, length), lambda pair: (pair, 0, 0)),
            pl.BlockSpec((columns, length), lambda pair: (pair, 0)),
        ],
        out_shape=[
            jax.ShapeDtypeStruct((heads, length, length), jnp.bfloat16),
            jax.ShapeDtypeStruct((width, length), jnp.bfloat16),
        ],
        scratch_shapes=[pltpu.VMEM((2, TILE, 2 * length - TILE), jnp.float32)],
        compiler_params=pltpu.CompilerParams(vmem_limit_bytes=VMEM_CAP),
        cost_estimate=pl.CostEstimate(
            flops=2 * heads * length * length * (width // heads),
            bytes_accessed=4 * length * width + 2 * heads * length * length,
            transcendentals=heads * length * length,
        ),
        name="attend_weights",
    )(edges, queries, keys, logs, band, normed)


def diagonal_sums(near_ref, side, beyond):
    span = 4 * TILE
    zeros = jnp.zeros((8, span - TILE), jnp.float32)
    total = jnp.zeros((8, span), jnp.float32)
    for block in range(3):
        for row in range(0, TILE, 8):
            first = block * TILE + row
            wide = jnp.concatenate([near_ref[side, first : first + 8, :], zeros], axis=1)
            total = total + pltpu.roll(wide, (block + 1) * TILE - 1 - row, 1)
    rows = lax.broadcasted_iota(jnp.int32, total.shape, 0)
    for bit in (1, 2, 4):
        total = jnp.where((rows & bit) != 0, pltpu.roll(total, span - bit, 1), total)
    sums = jnp.sum(total, axis=0, keepdims=True)
    lanes = lax.broadcasted_iota(jnp.int32, sums.shape, 1)
    sums = sums + jnp.where(lanes == 0, beyond[0], 0.0)
    return sums + jnp.where(lanes == span - 2, beyond[1], 0.0)


def attend_back_kernel(
    core_ref, q_ref, k_ref, v_ref, grad_ref, out_ref, weights_ref, normed_ref,
    grads_ref, away_ref, kept_ref, sums_ref,
    near_ref, query_total, square,
):
    length = q_ref.shape[0]
    columns = q_ref.shape[1]
    half = columns // 2
    blocks = length // TILE
    scale = half ** (-0.5)
    names = lax.broadcasted_iota(jnp.int32, (2 * blocks, length), 0)
    owners = lax.broadcasted_iota(jnp.int32, (2 * blocks, length), 1) // TILE
    picks = (names == owners).astype(jnp.float32).astype(jnp.bfloat16)
    queries_t = jnp.transpose(q_ref[...] * scale)
    grads_t = jnp.transpose(grad_ref[...])
    near_ref[...] = jnp.zeros_like(near_ref)
    key_parts, value_parts = [], []
    for side in range(2):
        rows = slice(side * half, (side + 1) * half)
        grad = half_of(grad_ref[...], side)
        keys = half_of(k_ref[...], side)
        center = jnp.sum(
            grad.astype(jnp.float32) * out_ref[...].astype(jnp.float32), axis=1, keepdims=True
        )
        left = jnp.concatenate([queries_t[rows], picks], axis=0)
        key_total, value_total = None, None
        for start in range(0, length, BACK_STRIP):
            strip = slice(start, start + BACK_STRIP)
            weights = weights_ref[side, strip, :]
            weight_grad = times_transposed(grad[strip], v_ref[...])
            score_grad = weights.astype(jnp.float32) * (weight_grad - center[strip])
            score_low = score_grad.astype(jnp.bfloat16)
            value_term = times(grads_t[rows, strip], weights)
            value_total = value_term if value_total is None else value_total + value_term
            key_term = times(left[:, strip], score_low)
            key_total = key_term if key_total is None else key_total + key_term
            query_term = times(score_low, keys)
            if side == 0:
                query_total[strip, :] = query_term
            else:
                query_total[strip, :] += query_term
            for row in range(0, BACK_STRIP, TILE):
                for lane in range(0, length, TILE):
                    apart = (lane - start - row) // TILE
                    if abs(apart) <= 1:
                        spot = (apart + 1) * TILE
                        near_ref[side, spot : spot + TILE, :] += score_grad[
                            row : row + TILE, lane : lane + TILE
                        ]
        key_parts.append(key_total[:half])
        value_parts.append(value_total)
        sums = key_total[half:]
        beyond = [
            jnp.sum(jnp.where(keep, sums, 0.0), keepdims=True)
            for keep in (names >= owners + 2, (names <= owners - 2) & (names < blocks))
        ]
        sums_ref[0, side : side + 1, :] = diagonal_sums(near_ref, side, beyond)
    grads_ref[0] = (query_total[...] * scale).astype(jnp.bfloat16)
    grads_ref[1] = jnp.transpose(jnp.concatenate(key_parts, axis=0)).astype(jnp.bfloat16)
    grads_ref[2] = jnp.transpose(jnp.concatenate(value_parts, axis=0)).astype(jnp.bfloat16)
    part = normed_ref.shape[0] // 2
    stacked = jnp.concatenate([grads_ref[index] for index in range(3)], axis=1)
    square[...] = times(normed_ref[...], stacked)
    away = pl.ds(pl.multiple_of((1 - core_ref[0]) * part, 16), part)
    kept = pl.ds(pl.multiple_of(core_ref[0] * part, 16), part)
    for index in range(3):
        span = slice(index * columns, (index + 1) * columns)
        away_ref[index] = square[away, span].astype(jnp.bfloat16)
        kept_ref[index] = square[kept, span].astype(jnp.bfloat16)


def attend_back(core, queries, keys, values, grads, attended, weights, normed_t):
    length, width = queries.shape
    heads = weights.shape[0]
    pairs = heads // 2
    columns = width // pairs
    part = pl.BlockSpec((length, columns), lambda pair: (0, pair))
    square = pl.BlockSpec((3, width // 2, columns), lambda pair: (0, 0, pair))
    return pl.pallas_call(
        attend_back_kernel,
        grid=(pairs,),
        in_specs=[
            pl.BlockSpec(memory_space=pltpu.SMEM),
            part, part, part, part, part,
            pl.BlockSpec((2, length, length), lambda pair: (pair, 0, 0)),
            pl.BlockSpec((width, length), lambda pair: (0, 0)),
        ],
        out_specs=[
            pl.BlockSpec((3, length, columns), lambda pair: (0, 0, pair)),
            square, square,
            pl.BlockSpec((1, 2, 4 * TILE), lambda pair: (pair, 0, 0)),
        ],
        out_shape=[
            jax.ShapeDtypeStruct((3, length, width), jnp.bfloat16),
            jax.ShapeDtypeStruct((3, width // 2, width), jnp.bfloat16),
            jax.ShapeDtypeStruct((3, width // 2, width), jnp.bfloat16),
            jax.ShapeDtypeStruct((pairs, 2, 4 * TILE), jnp.float32),
        ],
        scratch_shapes=[
            pltpu.VMEM((2, 3 * TILE, TILE), jnp.float32),
            pltpu.VMEM((length, columns), jnp.float32),
            pltpu.VMEM((width, 3 * columns), jnp.float32),
        ],
        compiler_params=pltpu.CompilerParams(vmem_limit_bytes=VMEM_CAP),
        cost_estimate=pl.CostEstimate(
            flops=10 * heads * length * length * (width // heads),
            bytes_accessed=16 * length * width + 2 * heads * length * length,
            transcendentals=0,
        ),
        name="attend_back",
    )(core, queries, keys, values, grads, attended, weights, normed_t)


def bias_band(rel_table):
    buckets, heads = rel_table.shape
    labels = band_buckets().reshape(1, -1)
    onehot = (labels == jnp.arange(buckets, dtype=jnp.int32)[:, None]).astype(jnp.bfloat16)
    band = lax.dot_general(
        rel_table, onehot, (((0,), (0,)), ((), ())), preferred_element_type=jnp.float32
    )
    half = buckets // 2
    edges = jnp.stack([rel_table[half - 1], rel_table[buckets - 1]], axis=1).astype(jnp.float32)
    return band.reshape(heads, 3 * TILE, TILE), edges


normal_tail = (
    0.14372023791716726,
    0.14167152280803838,
    0.14027055919455333,
    0.02504245305870889,
    0.1831401332067321,
    -0.1813703123183242,
    0.04752538660588183,
)
tail_pole = 0.36
normal_height = 0.3989422804014327


def gelu_and_slope(values):
    density = jnp.exp(values * values * -0.5)
    inverse = 1.0 / (1.0 + tail_pole * jnp.abs(values))
    series = jnp.full_like(values, normal_tail[-1])
    for coefficient in normal_tail[-2::-1]:
        series = series * inverse + coefficient
    tail = series * inverse * density
    below = jnp.where(values > 0, 1.0 - tail, tail)
    return values * below, below + values * (density * normal_height)


def send_kernel(
    capacity_ref, route_ref, rows_ref, sent_ref, place_ref, spots_ref, scratch, *, experts, slots, chunks
):
    tokens = route_ref.shape[1]
    block = sent_ref.shape[0]
    step = pl.program_id(0)

    @pl.when(step == 0)
    def _():
        route = route_ref[...]
        names = lax.broadcasted_iota(jnp.int32, (experts, tokens), 0)
        chosen = (names == route).astype(jnp.float32)
        early = lax.broadcasted_iota(jnp.int32, (tokens, tokens), 0)
        late = lax.broadcasted_iota(jnp.int32, (tokens, tokens), 1)
        before = (early < late).astype(jnp.float32).astype(jnp.bfloat16)
        earlier = times(chosen.astype(jnp.bfloat16), before)
        slot = jnp.sum(earlier * chosen, axis=0, keepdims=True).astype(jnp.int32)
        kept = slot < capacity_ref[0]
        share = slots // chunks
        chunk = jnp.zeros_like(slot)
        for later in range(1, chunks):
            chunk = chunk + (slot >= later * share).astype(jnp.int32)
        place = chunk * (experts * share) + route * share + (slot - chunk * share)
        place = jnp.where(kept, place, -1)
        ordered = jnp.where(kept, route * slots + slot, -1)
        scratch[...] = ordered
        place_ref[...] = place
        half = spots_ref.shape[1] // 2
        both = jnp.concatenate(
            [jnp.broadcast_to(place, (half, tokens)), jnp.broadcast_to(ordered, (half, tokens))], axis=0
        )
        spots_ref[...] = jnp.transpose(both)

    places = step * block + lax.broadcasted_iota(jnp.int32, (block, tokens), 0)
    onehot = (places == scratch[...]).astype(jnp.float32).astype(jnp.bfloat16)
    sent_ref[...] = times(onehot, rows_ref[...]).astype(jnp.bfloat16)


def send_first(capacity, route_row, rows, experts, slots, chunks):
    tokens, width = rows.shape
    total = experts * slots
    block = 512
    return pl.pallas_call(
        functools.partial(send_kernel, experts=experts, slots=slots, chunks=chunks),
        grid=(total // block,),
        in_specs=[
            pl.BlockSpec(memory_space=pltpu.SMEM),
            pl.BlockSpec((1, tokens), lambda step: (0, 0)),
            pl.BlockSpec((tokens, width), lambda step: (0, 0)),
        ],
        out_specs=[
            pl.BlockSpec((block, width), lambda step: (step, 0)),
            pl.BlockSpec((1, tokens), lambda step: (0, 0)),
            pl.BlockSpec((tokens, TILE), lambda step: (0, 0)),
        ],
        out_shape=[
            jax.ShapeDtypeStruct((total, width), jnp.bfloat16),
            jax.ShapeDtypeStruct((1, tokens), jnp.int32),
            jax.ShapeDtypeStruct((tokens, TILE), jnp.int32),
        ],
        scratch_shapes=[pltpu.VMEM((1, tokens), jnp.int32)],
        compiler_params=pltpu.CompilerParams(vmem_limit_bytes=VMEM_CAP),
        name="route_and_send",
    )(capacity, route_row, rows)


def send_again_kernel(place_ref, rows_ref, sent_ref, *, first):
    block = sent_ref.shape[0]
    tokens = rows_ref.shape[0]
    start = first + pl.program_id(0) * block
    places = start + lax.broadcasted_iota(jnp.int32, (block, tokens), 0)
    onehot = (places == place_ref[...]).astype(jnp.float32).astype(jnp.bfloat16)
    sent_ref[...] = times(onehot, rows_ref[...]).astype(jnp.bfloat16)


def send_again(place, rows, first, count):
    tokens, width = rows.shape
    block = 512
    return pl.pallas_call(
        functools.partial(send_again_kernel, first=first),
        grid=(count // block,),
        in_specs=[
            pl.BlockSpec((1, tokens), lambda step: (0, 0)),
            pl.BlockSpec((tokens, width), lambda step: (0, 0)),
        ],
        out_specs=pl.BlockSpec((block, width), lambda step: (step, 0)),
        out_shape=jax.ShapeDtypeStruct((count, width), jnp.bfloat16),
        compiler_params=pltpu.CompilerParams(vmem_limit_bytes=VMEM_CAP),
        cost_estimate=pl.CostEstimate(
            flops=2 * count * tokens * width,
            bytes_accessed=2 * (count + tokens) * width,
            transcendentals=0,
        ),
        name="send_rows",
    )(place, rows)


def expert_kernel(
    own_ref, rows_ref, ups_ref, up_ref, down_ref, router_ref, *rest, experts, piece
):
    (
        input_grad_ref, router_grad_ref, produced_ref, activated_ref, pre_grad_ref, slot_grad_ref,
        kept_ref,
    ) = rest[-7:]
    rows = rows_ref[...]
    ups = ups_ref[...].astype(jnp.float32).reshape(rows.shape)
    low_ups = ups.astype(jnp.bfloat16)
    router = router_ref[...]
    hidden = up_ref.shape[1]
    logits = times(rows, router)
    lanes = lax.broadcasted_iota(jnp.int32, logits.shape, 1)
    logits = jnp.where(lanes < experts, logits, -jnp.inf)
    powers = jnp.exp(logits - jnp.max(logits, axis=1, keepdims=True))
    chances = powers / jnp.sum(powers, axis=1, keepdims=True)
    mine = (lanes == own_ref[0]).astype(jnp.float32)
    gate = jnp.sum(chances * mine, axis=1, keepdims=True)
    gate_grad = jnp.zeros_like(gate)
    input_grad = jnp.zeros(rows.shape, jnp.float32)
    produced = jnp.zeros(rows.shape, jnp.float32)
    for first in range(0, hidden, piece):
        span = slice(first, first + piece)
        up = up_ref[:, span]
        down = down_ref[span, :]
        activated, slope = gelu_and_slope(times(rows, up))
        activated = activated.astype(jnp.bfloat16)
        back = times_transposed(low_ups, down)
        gate_grad = gate_grad + jnp.sum(
            activated.astype(jnp.float32) * back, axis=1, keepdims=True
        )
        pre_grad = (back * gate * slope).astype(jnp.bfloat16)
        activated_ref[0, :, span] = activated
        pre_grad_ref[0, :, span] = pre_grad
        input_grad = input_grad + times_transposed(pre_grad, up)
        produced = produced + times(activated, down)
    logit_grad = gate_grad * gate * (mine - chances)
    low_logit = logit_grad.astype(jnp.bfloat16)
    input_grad_ref[...] = (input_grad + times_transposed(low_logit, router)).astype(jnp.bfloat16)
    produced_ref[...] = (produced * gate).reshape(produced_ref.shape).astype(jnp.bfloat16)
    slot_grad_ref[0] = (ups * gate).astype(jnp.bfloat16)
    kept_ref[0] = rows

    @pl.when(pl.program_id(0) == 0)
    def _():
        router_grad_ref[...] = jnp.zeros_like(router_grad_ref)

    router_grad_ref[...] += times(jnp.transpose(logit_grad).astype(jnp.bfloat16), rows)


def expert_pass(own, rows, ups, up, down, router, experts, chunk, before):
    count, width = rows.shape
    groups, chunks, half = ups.shape[:3]
    hidden = up.shape[1]
    block = 256
    lanes = router.shape[1]
    row_spec = pl.BlockSpec((block, width), lambda step: (step, 0))
    whole = lambda shape: pl.BlockSpec(shape, lambda step: (0, 0))
    kept = lambda columns: pl.BlockSpec((1, block, columns), lambda step: (chunk, step, 0))
    stacked = lambda columns: jax.ShapeDtypeStruct((chunks, count, columns), jnp.bfloat16)
    slot_spec = pl.BlockSpec((block // half, 1, half, width), lambda step: (step, chunk, 0, 0))
    widths = (hidden, hidden, width, width)
    return pl.pallas_call(
        functools.partial(expert_kernel, experts=experts, piece=1024),
        grid=(count // block,),
        in_specs=[
            pl.BlockSpec(memory_space=pltpu.SMEM),
            row_spec, slot_spec,
            whole(up.shape), whole(down.shape), whole(router.shape),
        ] + [pl.BlockSpec(memory_space=pl.ANY)] * len(before),
        out_specs=[row_spec, whole((lanes, width)), slot_spec]
        + [kept(columns) for columns in widths],
        out_shape=[
            jax.ShapeDtypeStruct((count, width), jnp.bfloat16),
            jax.ShapeDtypeStruct((lanes, width), jnp.float32),
            jax.ShapeDtypeStruct((groups, chunks, half, width), jnp.bfloat16),
        ] + [stacked(columns) for columns in widths],
        input_output_aliases={6 + index: 2 + index for index in range(len(before))},
        compiler_params=pltpu.CompilerParams(vmem_limit_bytes=VMEM_CAP),
        cost_estimate=pl.CostEstimate(
            flops=8 * count * width * hidden,
            bytes_accessed=4 * width * hidden + 4 * count * hidden + 12 * count * width,
            transcendentals=2 * count * hidden,
        ),
        name="experts",
    )(own, rows, ups, up, down, router, *before)


def spread_rows(spots_ref, part_ref, first):
    target = spots_ref[:, :1]
    count = part_ref.shape[0]
    places = first + lax.broadcasted_iota(jnp.int32, (target.shape[0], count), 1)
    onehot = (places == target).astype(jnp.float32).astype(jnp.bfloat16)
    return times(onehot, part_ref[...])


def fetch_first_kernel(spots_ref, part_ref, out_ref):
    out_ref[...] = spread_rows(spots_ref, part_ref, 0).astype(jnp.bfloat16)


def fetch_first(spots, part):
    tokens = spots.shape[0]
    count, width = part.shape
    block = 256
    return pl.pallas_call(
        fetch_first_kernel,
        grid=(tokens // block,),
        in_specs=[
            pl.BlockSpec((block, TILE), lambda step: (step, 0)),
            pl.BlockSpec((count, width), lambda step: (0, 0)),
        ],
        out_specs=pl.BlockSpec((block, width), lambda step: (step, 0)),
        out_shape=jax.ShapeDtypeStruct((tokens, width), jnp.bfloat16),
        compiler_params=pltpu.CompilerParams(vmem_limit_bytes=VMEM_CAP),
        cost_estimate=pl.CostEstimate(
            flops=2 * count * tokens * width,
            bytes_accessed=4 * tokens * width,
            transcendentals=0,
        ),
        name="fetch_first",
    )(spots, part)


def fetch_kernel(
    spots_ref, early_ref, second_ref, residual_ref, gain_ref, upstream_ref, output_ref,
    out_grad_ref, attended_grad_ref, gain_grad_ref,
):
    total = early_ref[...].astype(jnp.float32) + spread_rows(spots_ref, second_ref, second_ref.shape[0])
    residual = residual_ref[...]
    inverse = lax.rsqrt(jnp.mean(residual * residual, axis=1, keepdims=True) + eps_norm)
    scaled = residual * inverse

    @pl.when(pl.program_id(0) == 0)
    def _():
        gain_grad_ref[...] = jnp.zeros_like(gain_grad_ref)

    gain_grad_ref[...] += jnp.sum((total * scaled).reshape(-1, 8, total.shape[1]), axis=0)
    weighted = total * gain_ref[...]
    spread = jnp.mean(weighted * scaled, axis=1, keepdims=True)
    residual_grad = upstream_ref[...].astype(jnp.float32) + inverse * (weighted - scaled * spread)
    low = residual_grad.astype(jnp.bfloat16)
    out_grad_ref[...] = low
    attended_grad_ref[...] = times_transposed(low, output_ref[...]).astype(jnp.bfloat16)


def fetch_grads(spots, early, second, residual, gain_row, upstream, w_output):
    tokens, width = residual.shape
    block = 256
    row_spec = pl.BlockSpec((block, width), lambda step: (step, 0))
    whole = lambda shape: pl.BlockSpec(shape, lambda step: (0, 0))
    return pl.pallas_call(
        fetch_kernel,
        grid=(tokens // block,),
        in_specs=[
            pl.BlockSpec((block, TILE), lambda step: (step, 0)),
            row_spec, whole(second.shape),
            row_spec, whole(gain_row.shape), row_spec, whole(w_output.shape),
        ],
        out_specs=[row_spec, row_spec, whole((8, width))],
        out_shape=[
            jax.ShapeDtypeStruct((tokens, width), jnp.bfloat16),
            jax.ShapeDtypeStruct((tokens, width), jnp.bfloat16),
            jax.ShapeDtypeStruct((8, width), jnp.float32),
        ],
        compiler_params=pltpu.CompilerParams(vmem_limit_bytes=63 * 1024 * 1024),
        name="fetch_grads",
    )(spots, early, second, residual, gain_row, upstream, w_output)


def combine_kernel(spots_ref, parts_ref, residual_ref, out_ref):
    column = spots_ref.shape[1] // 2
    target = spots_ref[:, column : column + 1]
    count = parts_ref.shape[0]
    places = lax.broadcasted_iota(jnp.int32, (target.shape[0], count), 1)
    onehot = (places == target).astype(jnp.float32).astype(jnp.bfloat16)
    out_ref[...] = (residual_ref[...] + times(onehot, parts_ref[...])).astype(jnp.bfloat16)


def combine(spots, parts, residual):
    tokens, width = residual.shape
    block = 256
    row_spec = pl.BlockSpec((block, width), lambda step: (step, 0))
    return pl.pallas_call(
        combine_kernel,
        grid=(tokens // block,),
        in_specs=[
            pl.BlockSpec((block, TILE), lambda step: (step, 0)),
            pl.BlockSpec(parts.shape, lambda step: (0, 0)),
            row_spec,
        ],
        out_specs=row_spec,
        out_shape=jax.ShapeDtypeStruct((tokens, width), jnp.bfloat16),
        compiler_params=pltpu.CompilerParams(vmem_limit_bytes=VMEM_CAP),
        name="combine",
    )(spots, parts, residual)


def swap_groups(axis, size, shift, count):
    return [
        [(index, index ^ (step << shift)) for index in range(size)] for step in range(1, count)
    ]


def sum_stages(axis_sizes):
    stages = []
    for axis, size in axis_sizes:
        shift = 0
        while (1 << shift) < size:
            count = min(4, size >> shift)
            place = (lax.axis_index(axis) >> shift) & (count - 1)
            stages.append((axis, place, swap_groups(axis, size, shift, count)))
            shift += count.bit_length() - 1
    return stages


def weight_kernel(core_ref, left_ref, right_ref, away_ref, kept_ref, square):
    square[...] = times(left_ref[...], right_ref[...])
    part = away_ref.shape[0]
    away = pl.ds(pl.multiple_of((1 - core_ref[0]) * part, 16), part)
    kept = pl.ds(pl.multiple_of(core_ref[0] * part, 16), part)
    away_ref[...] = square[away, :].astype(jnp.bfloat16)
    kept_ref[...] = square[kept, :].astype(jnp.bfloat16)


def weight_terms(core, left_t, right):
    width = left_t.shape[0]
    vmem = pl.BlockSpec(memory_space=pltpu.VMEM)
    half = jax.ShapeDtypeStruct((width // 2, right.shape[1]), jnp.bfloat16)
    return pl.pallas_call(
        weight_kernel,
        in_specs=[pl.BlockSpec(memory_space=pltpu.SMEM), vmem, vmem],
        out_specs=[vmem, vmem],
        out_shape=[half, half],
        scratch_shapes=[pltpu.VMEM((width, right.shape[1]), jnp.float32)],
        compiler_params=pltpu.CompilerParams(vmem_limit_bytes=24 * 1024 * 1024),
        cost_estimate=pl.CostEstimate(
            flops=2 * width * left_t.shape[1] * right.shape[1],
            bytes_accessed=2 * (width + right.shape[1]) * left_t.shape[1],
            transcendentals=0,
        ),
        name="weight_terms",
    )(core, left_t, right)


def cut_pieces(place, source, own_ref, sent_refs):
    rows = own_ref.shape[0]
    for step, ref in enumerate((own_ref, *sent_refs)):
        first = pl.multiple_of((place ^ step) * rows, 16)
        ref[...] = source[pl.ds(first, rows), :].astype(ref.dtype)


def padded_rows(rows, count):
    return -(-rows // (16 * count)) * 16 * count


def piece_shapes(rows, width, count):
    own = jax.ShapeDtypeStruct((rows // count, width), jnp.float32)
    sent = jax.ShapeDtypeStruct((rows // count, width), jnp.bfloat16)
    return [own] + [sent] * (count - 1)


def first_pieces_kernel(
    place_ref, kept_ref, got_ref, kept_out, got_out, gain_ref, router_one, router_two, sums_ref,
    *rest, experts, counts,
):
    outs, outs_two, (small, sums) = rest[: counts[0]], rest[counts[0] : sum(counts)], rest[sum(counts) :]
    small[...] = jnp.zeros_like(small)
    sums[...] = jnp.zeros_like(sums)
    for pair in range(sums_ref.shape[0]):
        sums[2 * pair : 2 * pair + 2, :] = sums_ref[pair]
    small[:8, :] = gain_ref[...]
    small[8 : 8 + experts, :] = router_one[:experts] + router_two[:experts]
    lanes = lax.broadcasted_iota(jnp.int32, (TILE, sums.shape[1]), 1)
    names = lax.broadcasted_iota(jnp.int32, (TILE, sums.shape[1]), 0)
    onehot = (bucket_of(lanes - (2 * TILE - 1)) == names).astype(jnp.float32)
    small[8 + experts : 8 + experts + sums.shape[0], :TILE] = lax.dot_general(
        sums[...], onehot, (((1,), (1,)), ((), ())),
        precision=lax.Precision.HIGHEST, preferred_element_type=jnp.float32,
    )
    matrices, part = kept_ref.shape[:2]
    share = part // len(outs)
    extra = small.shape[0] // len(outs)
    for step, ref in enumerate(outs):
        place = place_ref[0] ^ step
        rows = pl.ds(pl.multiple_of(place * share, 16), share)
        for index in range(matrices):
            ref[index * share : (index + 1) * share, :] = (
                kept_ref[index, rows, :].astype(jnp.float32)
                + got_ref[index, rows, :].astype(jnp.float32)
            ).astype(ref.dtype)
        rows = pl.ds(pl.multiple_of(place * extra, 16), extra)
        ref[matrices * share :, :] = small[rows, :].astype(ref.dtype)
    share = part // len(outs_two)
    for step, ref in enumerate(outs_two):
        rows = pl.ds(pl.multiple_of((place_ref[1] ^ step) * share, 16), share)
        ref[...] = (
            kept_out[rows, :].astype(jnp.float32) + got_out[rows, :].astype(jnp.float32)
        ).astype(ref.dtype)


def first_pieces(
    places, kept, got, kept_out, got_out, gain_terms, router_terms, sums, experts, counts
):
    matrices, part, width = kept.shape
    sum_rows = -(-2 * sums.shape[0] // 8) * 8
    extra = padded_rows(8 + experts + sum_rows, counts[0])
    vmem = pl.BlockSpec(memory_space=pltpu.VMEM)
    shapes = piece_shapes(matrices * part + extra, width, counts[0])
    shapes += piece_shapes(part, width, counts[1])
    outs = pl.pallas_call(
        functools.partial(first_pieces_kernel, experts=experts, counts=counts),
        in_specs=[pl.BlockSpec(memory_space=pltpu.SMEM)] + [vmem] * 8,
        out_specs=[vmem] * len(shapes),
        out_shape=shapes,
        scratch_shapes=[
            pltpu.VMEM((extra, width), jnp.float32),
            pltpu.VMEM((sum_rows, sums.shape[2]), jnp.float32),
        ],
        compiler_params=pltpu.CompilerParams(vmem_limit_bytes=63 * 1024 * 1024),
        name="first_pieces",
    )(places, kept, got, kept_out, got_out, gain_terms, *router_terms, sums)
    return outs[: counts[0]], outs[counts[0] :]


def next_pieces_kernel(place_ref, *rest, received, counts):
    operands, rest = rest[: sum(received) + len(received)], rest[sum(received) + len(received) :]
    outs, sources = rest[: sum(counts)], rest[sum(counts) :]
    for chain, (count, made) in enumerate(zip(received, counts)):
        parts, operands = operands[: count + 1], operands[count + 1 :]
        cuts, outs = outs[:made], outs[made:]
        total = parts[0][...]
        for ref in parts[1:]:
            total = total + ref[...].astype(jnp.float32)
        rows = total.shape[0]
        source = sources[chain]
        source[:rows, :] = total
        if source.shape[0] > rows:
            source[rows:, :] = jnp.zeros((source.shape[0] - rows, total.shape[1]), jnp.float32)
        cut_pieces(place_ref[chain], source, cuts[0], cuts[1:])


def next_pieces(places, chains, counts):
    width = chains[0][0].shape[1]
    vmem = pl.BlockSpec(memory_space=pltpu.VMEM)
    shapes, scratch = [], []
    for (own, _), count in zip(chains, counts):
        rows = own.shape[0]
        padded = padded_rows(rows, count)
        scratch.append(pltpu.VMEM((padded, width), jnp.float32))
        if count == 1:
            shapes.append(jax.ShapeDtypeStruct((rows, width), jnp.bfloat16))
        else:
            shapes += piece_shapes(padded, width, count)
    operands = [array for own, got in chains for array in (own, *got)]
    outs = pl.pallas_call(
        functools.partial(
            next_pieces_kernel, received=tuple(len(got) for _, got in chains), counts=tuple(counts)
        ),
        in_specs=[pl.BlockSpec(memory_space=pltpu.SMEM)] + [vmem] * len(operands),
        out_specs=[vmem] * len(shapes),
        out_shape=shapes,
        scratch_shapes=scratch,
        compiler_params=pltpu.CompilerParams(vmem_limit_bytes=20 * 1024 * 1024),
        name="next_pieces",
    )(places, *operands)
    return outs[: counts[0]], outs[counts[0] :]


def join_kernel(place_ref, *rest, counts):
    pieces, rest = rest[: sum(counts)], rest[sum(counts) :]
    outs, joined = rest[: len(counts)], rest[len(counts) :]
    for chain, count in enumerate(counts):
        parts, pieces = pieces[:count], pieces[count:]
        rows = parts[0].shape[0]
        for step, ref in enumerate(parts):
            first = pl.multiple_of((place_ref[chain] ^ step) * rows, 16)
            joined[chain][pl.ds(first, rows), :] = ref[...]
        outs[chain][...] = joined[chain][: outs[chain].shape[0], :]


def join_pieces(places, chains, kept):
    width = chains[0][0].shape[1]
    vmem = pl.BlockSpec(memory_space=pltpu.VMEM)
    operands = [piece for pieces in chains for piece in pieces]
    return pl.pallas_call(
        functools.partial(join_kernel, counts=tuple(len(pieces) for pieces in chains)),
        in_specs=[pl.BlockSpec(memory_space=pltpu.SMEM)] + [vmem] * len(operands),
        out_specs=[vmem] * len(chains),
        out_shape=[jax.ShapeDtypeStruct((rows, width), jnp.bfloat16) for rows in kept],
        scratch_shapes=[
            pltpu.VMEM((len(pieces) * pieces[0].shape[0], width), jnp.bfloat16) for pieces in chains
        ],
        compiler_params=pltpu.CompilerParams(vmem_limit_bytes=20 * 1024 * 1024),
        name="join_pieces",
    )(places, *operands)


def finish_kernel(place_ref, *rest, counts, table):
    ones, twos = rest[: 2 * counts[0]], rest[2 * counts[0] : 2 * sum(counts)]
    rest = rest[2 * sum(counts) :]
    weight_refs, gain_ref, rest = rest[:3], rest[3], rest[4:]
    square_outs, (gain_out, second_out, router_out, table_out), rest = rest[:4], rest[4:8], rest[8:]
    weights, squares, columns, small, load_sems, store_sems = rest
    core = place_ref[0]
    width = weights.shape[2]
    part = width // 2
    share = part // counts[0]
    loads = [
        pltpu.make_async_copy(ref, weights.at[index], load_sems.at[index])
        for index, ref in enumerate(weight_refs)
    ]
    for load in loads:
        load.start()

    def spots(place, count, rows):
        found = []
        for step in range(count):
            for other in range(2):
                half = 1 - core if other else core
                first = half * part + (place ^ step) * rows
                found.append(pl.ds(pl.multiple_of(first, 16), rows))
        return found

    stores = []
    for index in (3, 0, 1, 2):
        if index == 3:
            rows_two = part // counts[1]
            for ref, rows in zip(twos, spots(place_ref[2], counts[1], rows_two)):
                squares[index, rows, :] = ref[:rows_two, :].astype(jnp.float32)
        else:
            loads[index].wait()
            for ref, rows in zip(ones, spots(place_ref[1], counts[0], share)):
                total = ref[index * share : (index + 1) * share, :].astype(jnp.float32)
                squares[index, rows, :] = total
                term = jnp.sum(
                    total * weights[index, rows, :].astype(jnp.float32), axis=1, keepdims=True
                )
                if index == 0:
                    columns[rows, :] = jnp.broadcast_to(term, (share, TILE))
                else:
                    columns[rows, :] += jnp.broadcast_to(term, (share, TILE))
        store = pltpu.make_async_copy(squares.at[index], square_outs[index], store_sems.at[index])
        store.start()
        stores.append(store)
    gain = jnp.transpose(columns[...])[:1] / gain_ref[...]
    gain_out[...] = gain.reshape(width)
    extra = small.shape[0] // counts[0]
    for step in range(counts[0]):
        rows = pl.ds(pl.multiple_of((place_ref[1] ^ step) * extra, 16), extra)
        small[rows, :] = ones[2 * step][3 * share :, :].astype(jnp.float32) + ones[2 * step + 1][
            3 * share :, :
        ].astype(jnp.float32)
    experts = router_out.shape[0]
    buckets, heads = table
    second_out[...] = jnp.sum(small[:8, :], axis=0, keepdims=True).reshape(width)
    router_out[...] = small[8 : 8 + experts, :]
    table_out[...] = small[8 + experts : 8 + experts + heads, :buckets]
    for store in stores:
        store.wait()


def finish(places, chains, weights, gain_row, experts, table):
    width = weights[0].shape[1]
    counts = tuple(len(pieces) // 2 for pieces in chains)
    square = jax.ShapeDtypeStruct((width, width), jnp.float32)
    row = jax.ShapeDtypeStruct((width,), jnp.float32)
    vmem = pl.BlockSpec(memory_space=pltpu.VMEM)
    extra = chains[0][0].shape[0] - 3 * (width // 2 // counts[0])
    pieces = [piece for chain in chains for piece in chain]
    return pl.pallas_call(
        functools.partial(finish_kernel, counts=counts, table=table),
        in_specs=[pl.BlockSpec(memory_space=pltpu.SMEM)]
        + [vmem] * len(pieces)
        + [pl.BlockSpec(memory_space=pl.ANY)] * 3
        + [vmem],
        out_specs=[pl.BlockSpec(memory_space=pl.ANY)] * 4 + [vmem] * 4,
        out_shape=[
            square, square, square, square, row, row,
            jax.ShapeDtypeStruct((experts, width), jnp.float32),
            jax.ShapeDtypeStruct(table[::-1], jnp.float32),
        ],
        scratch_shapes=[
            pltpu.VMEM((3, width, width), jnp.bfloat16),
            pltpu.VMEM((4, width, width), jnp.float32),
            pltpu.VMEM((width, TILE), jnp.float32),
            pltpu.VMEM((counts[0] * extra, width), jnp.float32),
            pltpu.SemaphoreType.DMA((3,)),
            pltpu.SemaphoreType.DMA((4,)),
        ],
        compiler_params=pltpu.CompilerParams(vmem_limit_bytes=VMEM_CAP),
        name="finish",
    )(places, *pieces, *weights, gain_row)


def hidden_kernel(
    grads_ref, query_ref, key_ref, value_ref, hidden_ref, gain_ref, residual_grad_ref, out_ref
):
    total = None
    for index, weight in enumerate((query_ref, key_ref, value_ref)):
        term = times_transposed(grads_ref[index], weight[...])
        total = term if total is None else total + term
    hidden = hidden_ref[...].astype(jnp.float32)
    inverse = lax.rsqrt(jnp.mean(hidden * hidden, axis=1, keepdims=True) + eps_norm)
    scaled = hidden * inverse
    weighted = total * gain_ref[...]
    spread = jnp.mean(weighted * scaled, axis=1, keepdims=True)
    out_ref[...] = (
        residual_grad_ref[...].astype(jnp.float32) + inverse * (weighted - scaled * spread)
    ).astype(jnp.bfloat16)


def hidden_gradient(grads, weights, hidden, gain_row, residual_grad):
    tokens, width = hidden.shape
    block = 256
    row_spec = pl.BlockSpec((block, width), lambda step: (step, 0))
    whole = lambda shape: pl.BlockSpec(shape, lambda step: (0, 0))
    return pl.pallas_call(
        hidden_kernel,
        grid=(tokens // block,),
        in_specs=[pl.BlockSpec((3, block, width), lambda step: (0, step, 0))]
        + [whole(weight.shape) for weight in weights]
        + [row_spec, whole(gain_row.shape), row_spec],
        out_specs=row_spec,
        out_shape=jax.ShapeDtypeStruct((tokens, width), jnp.bfloat16),
        compiler_params=pltpu.CompilerParams(vmem_limit_bytes=VMEM_CAP),
        cost_estimate=pl.CostEstimate(
            flops=6 * tokens * width * width, bytes_accessed=20 * tokens * width, transcendentals=0
        ),
        name="hidden_gradient",
    )(grads, *weights, hidden, gain_row, residual_grad)


def exchange_pieces(stage, pieces):
    axis, _, swaps = stage
    return [lax.ppermute(piece, axis, pairs) for piece, pairs in zip(pieces, swaps)]


def on_device(
    hidden_in,
    first_gain,
    w_query,
    w_key,
    w_value,
    w_output,
    rel_table,
    second_gain,
    router,
    expert_up,
    expert_down,
    routes,
    capacity_factor,
    cotangent,
):
    axes = ("narrow", "wide")
    chunks = 2
    tokens, width = hidden_in.shape
    bucket_count = rel_table.shape[0]
    experts = router.shape[1]
    slots = 2 * tokens // experts
    capacity = capacity_factor * tokens // experts
    devices = lax.axis_size(axes)
    own = lax.axis_index(axes).astype(jnp.int32).reshape(1)
    padded = -(-experts // TILE) * TILE
    router_wide = jnp.pad(router, ((0, 0), (0, padded - experts)))

    def exchange(rows):
        blocks = rows.reshape(experts, -1, width)
        return lax.all_to_all(blocks, axes, split_axis=0, concat_axis=0, tiled=True).reshape(
            -1, width
        )

    together = lax.optimization_barrier
    sent_ups, place, spots = send_first(
        capacity, routes.reshape(1, tokens), cotangent, experts, slots, chunks
    )
    sent_ups, hidden_in = together((sent_ups, hidden_in))
    ups = exchange(sent_ups)

    band, edges = bias_band(rel_table)
    hidden = hidden_in.astype(jnp.float32)
    gain_one = first_gain.astype(jnp.float32)
    gain_two = second_gain.astype(jnp.float32)
    inverse_one = lax.rsqrt(jnp.mean(hidden * hidden, axis=-1, keepdims=True) + eps_norm)
    normed_first = (hidden * inverse_one * gain_one).astype(jnp.bfloat16)
    queries = times(normed_first, w_query).astype(jnp.bfloat16)
    keys = times(normed_first, w_key).astype(jnp.bfloat16)
    values = times(normed_first, w_value).astype(jnp.bfloat16)
    attended, attended_t, logs = attend(queries, keys, values, band, edges)
    residual = hidden + times(attended, w_output)
    inverse_two = lax.rsqrt(jnp.mean(residual * residual, axis=-1, keepdims=True) + eps_norm)
    normed_second = (residual * inverse_two * gain_two).astype(jnp.bfloat16)
    half = experts * slots // chunks
    sent = send_again(place, normed_second, 0, half)
    sent, ups = together((sent, ups))
    rows = [exchange(sent)]
    queries_again, _ = together((queries, ups))
    weights, normed_t = attend_weights(queries_again, keys, logs, band, edges, normed_first)
    sent = send_again(place, normed_second, half, half)
    sent, rows[0], weights, normed_t = together((sent, rows[0], weights, normed_t))
    rows.append(exchange(sent))
    ups = ups.reshape(experts, chunks, slots // chunks, width)

    saved = ()
    input_grads, router_terms = [], []
    for c in range(chunks):
        input_grad, router_term, *saved = expert_pass(
            own, rows[c], ups, expert_up[0], expert_down[0], router_wide, experts, c, saved
        )
        if c + 1 < chunks:
            input_grad, rows[-1] = together((input_grad, rows[-1]))
        if input_grads:
            input_grad, input_grads[-1] = together((input_grad, input_grads[-1]))
        input_grads.append(exchange(input_grad))
        router_terms.append(router_term)
    saved, input_grads[0] = together((saved, input_grads[0]))
    produced = saved[0].reshape(-1, width)
    activated, pre_grad, slot_grad, kept_rows = [
        array.reshape(-1, array.shape[-1]) for array in saved[1:]
    ]
    gradient_expert_down = inner_rows(activated, slot_grad)[None]
    gradient_expert_up = inner_rows(kept_rows, pre_grad)[None]
    fetched = fetch_first(spots, input_grads[0])
    gain_row = gain_two[None]
    input_grads[-1], fetched, gradient_expert_down, gradient_expert_up, produced, gain_row = together(
        (input_grads[-1], fetched, gradient_expert_down, gradient_expert_up, produced, gain_row)
    )
    produced = exchange(produced)
    out_grad, attended_grad, gain_terms = fetch_grads(
        spots, fetched, input_grads[-1], residual, gain_row, cotangent, w_output
    )
    core = lax.axis_index("narrow").astype(jnp.int32).reshape(1)
    swap = [(0, 1), (1, 0)]
    grads, away, kept, sums = attend_back(
        core, queries, keys, values, attended_grad, attended, weights, normed_t
    )
    got = lax.ppermute(away, "narrow", swap)
    out_grad, kept = together((out_grad, kept))
    away_out, kept_out = weight_terms(core, attended_t, out_grad)
    got_out = lax.ppermute(away_out, "narrow", swap)
    stages = sum_stages([("wide", lax.axis_size("wide"))])
    levels = len(stages)
    orders = (stages, stages[1:] + stages[:1])
    counts = [[len(stage[2]) + 1 for stage in order] for order in orders]

    def places_at(level):
        return jnp.stack([order[level][1] for order in orders]).astype(jnp.int32)

    chains = first_pieces(
        places_at(0), kept, got, kept_out, got_out, gain_terms, router_terms, sums, experts,
        (counts[0][0], counts[1][0]),
    )
    projections = (w_query, w_key, w_value)
    grads, kept = together((grads, kept))
    gradient_hidden = hidden_gradient(
        grads, projections, hidden_in, gain_one[None], out_grad
    )
    rows_at = []
    for level in range(levels):
        rows_at.append([chain[0].shape[0] for chain in chains])
        received = [
            (chain[0], exchange_pieces(order[level], chain[1:]))
            for chain, order in zip(chains, orders)
        ]
        last = level + 1 == levels
        places = jnp.zeros((2,), jnp.int32) if last else places_at(level + 1)
        cuts = [1 if last else count[level + 1] for count in counts]
        own = received[0][0]
        if level == 0:
            own, gradient_hidden = together((own, gradient_hidden))
        if level == 0:
            block_out = combine(spots, produced, residual)
            own, block_out = together((own, block_out))
        received[0] = (own, received[0][1])
        chains = next_pieces(places, received, cuts)
    lows = [chain[0] for chain in chains]
    for level in reversed(range(1, levels)):
        parts = [
            [low] + exchange_pieces(order[level], [low] * len(order[level][2]))
            for low, order in zip(lows, orders)
        ]
        lows = list(join_pieces(places_at(level), parts, rows_at[level - 1]))
    parts = [
        [low] + exchange_pieces(order[0], [low] * len(order[0][2]))
        for low, order in zip(lows, orders)
    ]
    places = jnp.concatenate([core, places_at(0)])
    parts[0][1], places = together((parts[0][1], places))
    others = [[], [lax.ppermute(piece, "narrow", swap) for piece in parts[1]]]
    parts[0][-1] = together((parts[0][-1], *others[1]))[0]
    others[0] = [lax.ppermute(piece, "narrow", swap) for piece in parts[0]]
    parts = [
        [piece for both in zip(own, other) for piece in both] for own, other in zip(parts, others)
    ]
    (
        gradient_query, gradient_key, gradient_value, gradient_output, gradient_first_gain,
        gradient_second_gain, gradient_router, gradient_table,
    ) = finish(places, parts, projections, gain_one[None], experts, rel_table.shape)
    return (
        block_out,
        gradient_hidden,
        gradient_first_gain,
        gradient_query,
        gradient_key,
        gradient_value,
        gradient_output,
        jnp.transpose(gradient_table),
        gradient_second_gain,
        jnp.transpose(gradient_router),
        gradient_expert_up,
        gradient_expert_down,
    )


def solution(mesh):
    split = ("narrow", "wide")
    rows, experts = P(split, None), P(split, None, None)
    return jax.shard_map(
        on_device,
        mesh=mesh,
        in_specs=(rows,) + (P(),) * 8 + (experts, experts, rows, P(split), rows),
        out_specs=(rows, rows) + (P(),) * 8 + (experts, experts),
        check_vma=False,
    )
```

```python
import functools

import jax
import jax.numpy as jnp
from jax import lax
from jax.experimental import pallas as pl
from jax.experimental.pallas import tpu as pltpu
from jax.sharding import PartitionSpec as P

TILE = 128
STRIP = 256
BACK_STRIP = 512
VMEM_CAP = 60 * 1024 * 1024
eps_norm = 1e-06
bucket_edges = (12, 16, 23, 32, 46, 64, 91)


def bucket_of(offset):
    distance = jnp.abs(offset)
    far_bucket = jnp.full(distance.shape, 8, jnp.int32)
    for edge in bucket_edges:
        far_bucket = far_bucket + (distance >= edge).astype(jnp.int32)
    near_bucket = jnp.where(distance < 8, distance, far_bucket)
    return near_bucket + 16 * (offset > 0).astype(jnp.int32)


def band_buckets():
    rows = lax.broadcasted_iota(jnp.int32, (3 * TILE, TILE), 0)
    lanes = lax.broadcasted_iota(jnp.int32, (3 * TILE, TILE), 1)
    return bucket_of(rows - TILE - lanes)


def times_transposed(left, right):
    return lax.dot_general(
        left, right, (((1,), (1,)), ((), ())), preferred_element_type=jnp.float32
    )


def inner_rows(left, right):
    return lax.dot_general(
        left, right, (((0,), (0,)), ((), ())), preferred_element_type=jnp.float32
    )


def times(left, right):
    return jnp.dot(left, right, preferred_element_type=jnp.float32)


def fill_wide(edge_ref, band_ref, wide):
    length = (wide.shape[1] + TILE) // 2
    pair = pl.program_id(0)
    for side in range(2):
        head = 2 * pair + side
        wide[side, : length - 2 * TILE] = jnp.full(
            (length - 2 * TILE, TILE), edge_ref[head, 0], jnp.float32
        )
        wide[side, length - 2 * TILE : length + TILE] = band_ref[side]
        wide[side, length + TILE :] = jnp.full(
            (length - 2 * TILE, TILE), edge_ref[head, 1], jnp.float32
        )


def strip_bias(wide, side, key_start, keys, query_start):
    length = (wide.shape[1] + TILE) // 2
    parts = []
    for start in range(query_start, query_start + STRIP, TILE):
        first = length - TILE - start + key_start
        parts.append(wide[side, first : first + keys, :])
    return jnp.concatenate(parts, axis=1)


def half_of(rows, side):
    half = rows.shape[1] // 2
    lanes = lax.broadcasted_iota(jnp.int32, rows.shape, 1)
    own = lanes < half if side == 0 else lanes >= half
    return jnp.where(own, rows, jnp.zeros_like(rows))


def attend_kernel(
    edge_ref, q_ref, k_ref, v_ref, band_ref, out_ref, turned_ref, log_ref, wide
):
    length = q_ref.shape[0]
    half = q_ref.shape[1] // 2
    scale = half ** (-0.5)
    fill_wide(edge_ref, band_ref, wide)
    keys = k_ref[...]
    values_t = jnp.transpose(v_ref[...])
    for start in range(0, length, STRIP):
        mixed = []
        for side in range(2):
            query = half_of(q_ref[start : start + STRIP, :] * scale, side)
            scores = times_transposed(keys, query) + strip_bias(wide, side, 0, length, start)
            top = jnp.max(scores, axis=0, keepdims=True)
            powers = jnp.exp(scores - top)
            total = jnp.sum(powers, axis=0, keepdims=True)
            raw = times(values_t[side * half : (side + 1) * half], powers.astype(jnp.bfloat16))
            mixed.append(raw / total)
            log_ref[0, side : side + 1, start : start + STRIP] = top + jnp.log(total)
        both = jnp.concatenate(mixed, axis=0)
        out_ref[start : start + STRIP, :] = jnp.transpose(both).astype(jnp.bfloat16)
        turned_ref[:, start : start + STRIP] = both.astype(jnp.bfloat16)


def attend(queries, keys, values, band, edges):
    length, width = queries.shape
    heads = edges.shape[0]
    pairs = heads // 2
    columns = width // pairs
    part = pl.BlockSpec((length, columns), lambda pair: (0, pair))
    return pl.pallas_call(
        attend_kernel,
        grid=(pairs,),
        in_specs=[
            pl.BlockSpec(memory_space=pltpu.SMEM),
            part,
            part,
            part,
            pl.BlockSpec((2, 3 * TILE, TILE), lambda pair: (pair, 0, 0)),
        ],
        out_specs=[
            part,
            pl.BlockSpec((columns, length), lambda pair: (pair, 0)),
            pl.BlockSpec((1, 2, length), lambda pair: (pair, 0, 0)),
        ],
        out_shape=[
            jax.ShapeDtypeStruct((length, width), jnp.bfloat16),
            jax.ShapeDtypeStruct((width, length), jnp.bfloat16),
            jax.ShapeDtypeStruct((pairs, 2, length), jnp.float32),
        ],
        scratch_shapes=[pltpu.VMEM((2, 2 * length - TILE, TILE), jnp.float32)],
        compiler_params=pltpu.CompilerParams(vmem_limit_bytes=VMEM_CAP),
        cost_estimate=pl.CostEstimate(
            flops=4 * heads * length * length * (width // heads),
            bytes_accessed=8 * length * width,
            transcendentals=heads * length * length,
        ),
        name="attend",
    )(edges, queries, keys, values, band)


def weights_kernel(
    edge_ref, q_ref, k_ref, log_ref, band_ref, normed_ref, weights_ref, turned_ref, wide
):
    length = q_ref.shape[0]
    scale = (q_ref.shape[1] // 2) ** (-0.5)
    head = 2 * pl.program_id(0)
    for side in range(2):
        turned = [
            jnp.transpose(band_ref[side, part : part + TILE, :]) for part in range(0, 3 * TILE, TILE)
        ]
        wide[side, :, : length - 2 * TILE] = jnp.full(
            (TILE, length - 2 * TILE), edge_ref[head + side, 0], jnp.float32
        )
        wide[side, :, length - 2 * TILE : length + TILE] = jnp.concatenate(turned, axis=1)
        wide[side, :, length + TILE :] = jnp.full(
            (TILE, length - 2 * TILE), edge_ref[head + side, 1], jnp.float32
        )
    keys = k_ref[...]
    turned_ref[...] = jnp.transpose(normed_ref[...])
    for start in range(0, length, STRIP):
        strip = slice(start, start + STRIP)
        for side in range(2):
            query = half_of(q_ref[strip, :] * scale, side)
            bias = jnp.concatenate(
                [
                    wide[side, :, length - TILE - first : 2 * length - TILE - first]
                    for first in range(start, start + STRIP, TILE)
                ],
                axis=0,
            )
            logs = jnp.transpose(
                jnp.broadcast_to(log_ref[0, side : side + 1, strip], (TILE, STRIP))
            )[:, :1]
            scores = times_transposed(query, keys) + bias
            weights_ref[side, strip, :] = jnp.exp(scores - logs).astype(jnp.bfloat16)


def attend_weights(queries, keys, logs, band, edges, normed):
    length, width = queries.shape
    heads = edges.shape[0]
    pairs = heads // 2
    columns = width // pairs
    part = pl.BlockSpec((length, columns), lambda pair: (0, pair))
    return pl.pallas_call(
        weights_kernel,
        grid=(pairs,),
        in_specs=[
            pl.BlockSpec(memory_space=pltpu.SMEM),
            part,
            part,
            pl.BlockSpec((1, 2, length), lambda pair: (pair, 0, 0)),
            pl.BlockSpec((2, 3 * TILE, TILE), lambda pair: (pair, 0, 0)),
            part,
        ],
        out_specs=[
            pl.BlockSpec((2, length, length), lambda pair: (pair, 0, 0)),
            pl.BlockSpec((columns, length), lambda pair: (pair, 0)),
        ],
        out_shape=[
            jax.ShapeDtypeStruct((heads, length, length), jnp.bfloat16),
            jax.ShapeDtypeStruct((width, length), jnp.bfloat16),
        ],
        scratch_shapes=[pltpu.VMEM((2, TILE, 2 * length - TILE), jnp.float32)],
        compiler_params=pltpu.CompilerParams(vmem_limit_bytes=VMEM_CAP),
        cost_estimate=pl.CostEstimate(
            flops=2 * heads * length * length * (width // heads),
            bytes_accessed=4 * length * width + 2 * heads * length * length,
            transcendentals=heads * length * length,
        ),
        name="attend_weights",
    )(edges, queries, keys, logs, band, normed)


def diagonal_sums(near_ref, side, beyond):
    span = 4 * TILE
    zeros = jnp.zeros((8, span - TILE), jnp.float32)
    total = jnp.zeros((8, span), jnp.float32)
    for block in range(3):
        for row in range(0, TILE, 8):
            first = block * TILE + row
            wide = jnp.concatenate([near_ref[side, first : first + 8, :], zeros], axis=1)
            total = total + pltpu.roll(wide, (block + 1) * TILE - 1 - row, 1)
    rows = lax.broadcasted_iota(jnp.int32, total.shape, 0)
    for bit in (1, 2, 4):
        total = jnp.where((rows & bit) != 0, pltpu.roll(total, span - bit, 1), total)
    sums = jnp.sum(total, axis=0, keepdims=True)
    lanes = lax.broadcasted_iota(jnp.int32, sums.shape, 1)
    sums = sums + jnp.where(lanes == 0, beyond[0], 0.0)
    return sums + jnp.where(lanes == span - 2, beyond[1], 0.0)


def attend_back_kernel(
    core_ref, q_ref, k_ref, v_ref, grad_ref, out_ref, weights_ref, normed_ref,
    grads_ref, away_ref, kept_ref, sums_ref,
    near_ref, query_total, square,
):
    length = q_ref.shape[0]
    columns = q_ref.shape[1]
    half = columns // 2
    blocks = length // TILE
    scale = half ** (-0.5)
    names = lax.broadcasted_iota(jnp.int32, (2 * blocks, length), 0)
    owners = lax.broadcasted_iota(jnp.int32, (2 * blocks, length), 1) // TILE
    picks = (names == owners).astype(jnp.float32).astype(jnp.bfloat16)
    queries_t = jnp.transpose(q_ref[...] * scale)
    grads_t = jnp.transpose(grad_ref[...])
    near_ref[...] = jnp.zeros_like(near_ref)
    key_parts, value_parts = [], []
    for side in range(2):
        rows = slice(side * half, (side + 1) * half)
        grad = half_of(grad_ref[...], side)
        keys = half_of(k_ref[...], side)
        center = jnp.sum(
            grad.astype(jnp.float32) * out_ref[...].astype(jnp.float32), axis=1, keepdims=True
        )
        left = jnp.concatenate([queries_t[rows], picks], axis=0)
        key_total, value_total = None, None
        for start in range(0, length, BACK_STRIP):
            strip = slice(start, start + BACK_STRIP)
            weights = weights_ref[side, strip, :]
            weight_grad = times_transposed(grad[strip], v_ref[...])
            score_grad = weights.astype(jnp.float32) * (weight_grad - center[strip])
            score_low = score_grad.astype(jnp.bfloat16)
            value_term = times(grads_t[rows, strip], weights)
            value_total = value_term if value_total is None else value_total + value_term
            key_term = times(left[:, strip], score_low)
            key_total = key_term if key_total is None else key_total + key_term
            query_term = times(score_low, keys)
            if side == 0:
                query_total[strip, :] = query_term
            else:
                query_total[strip, :] += query_term
            for row in range(0, BACK_STRIP, TILE):
                for lane in range(0, length, TILE):
                    apart = (lane - start - row) // TILE
                    if abs(apart) <= 1:
                        spot = (apart + 1) * TILE
                        near_ref[side, spot : spot + TILE, :] += score_grad[
                            row : row + TILE, lane : lane + TILE
                        ]
        key_parts.append(key_total[:half])
        value_parts.append(value_total)
        sums = key_total[half:]
        beyond = [
            jnp.sum(jnp.where(keep, sums, 0.0), keepdims=True)
            for keep in (names >= owners + 2, (names <= owners - 2) & (names < blocks))
        ]
        sums_ref[0, side : side + 1, :] = diagonal_sums(near_ref, side, beyond)
    grads_ref[0] = (query_total[...] * scale).astype(jnp.bfloat16)
    grads_ref[1] = jnp.transpose(jnp.concatenate(key_parts, axis=0)).astype(jnp.bfloat16)
    grads_ref[2] = jnp.transpose(jnp.concatenate(value_parts, axis=0)).astype(jnp.bfloat16)
    part = normed_ref.shape[0] // 2
    stacked = jnp.concatenate([grads_ref[index] for index in range(3)], axis=1)
    square[...] = times(normed_ref[...], stacked)
    away = pl.ds(pl.multiple_of((1 - core_ref[0]) * part, 16), part)
    kept = pl.ds(pl.multiple_of(core_ref[0] * part, 16), part)
    for index in range(3):
        span = slice(index * columns, (index + 1) * columns)
        away_ref[index] = square[away, span].astype(jnp.bfloat16)
        kept_ref[index] = square[kept, span].astype(jnp.bfloat16)


def attend_back(core, queries, keys, values, grads, attended, weights, normed_t):
    length, width = queries.shape
    heads = weights.shape[0]
    pairs = heads // 2
    columns = width // pairs
    part = pl.BlockSpec((length, columns), lambda pair: (0, pair))
    square = pl.BlockSpec((3, width // 2, columns), lambda pair: (0, 0, pair))
    return pl.pallas_call(
        attend_back_kernel,
        grid=(pairs,),
        in_specs=[
            pl.BlockSpec(memory_space=pltpu.SMEM),
            part, part, part, part, part,
            pl.BlockSpec((2, length, length), lambda pair: (pair, 0, 0)),
            pl.BlockSpec((width, length), lambda pair: (0, 0)),
        ],
        out_specs=[
            pl.BlockSpec((3, length, columns), lambda pair: (0, 0, pair)),
            square, square,
            pl.BlockSpec((1, 2, 4 * TILE), lambda pair: (pair, 0, 0)),
        ],
        out_shape=[
            jax.ShapeDtypeStruct((3, length, width), jnp.bfloat16),
            jax.ShapeDtypeStruct((3, width // 2, width), jnp.bfloat16),
            jax.ShapeDtypeStruct((3, width // 2, width), jnp.bfloat16),
            jax.ShapeDtypeStruct((pairs, 2, 4 * TILE), jnp.float32),
        ],
        scratch_shapes=[
            pltpu.VMEM((2, 3 * TILE, TILE), jnp.float32),
            pltpu.VMEM((length, columns), jnp.float32),
            pltpu.VMEM((width, 3 * columns), jnp.float32),
        ],
        compiler_params=pltpu.CompilerParams(vmem_limit_bytes=VMEM_CAP),
        cost_estimate=pl.CostEstimate(
            flops=10 * heads * length * length * (width // heads),
            bytes_accessed=16 * length * width + 2 * heads * length * length,
            transcendentals=0,
        ),
        name="attend_back",
    )(core, queries, keys, values, grads, attended, weights, normed_t)


def bias_band(rel_table):
    buckets, heads = rel_table.shape
    labels = band_buckets().reshape(1, -1)
    onehot = (labels == jnp.arange(buckets, dtype=jnp.int32)[:, None]).astype(jnp.bfloat16)
    band = lax.dot_general(
        rel_table, onehot, (((0,), (0,)), ((), ())), preferred_element_type=jnp.float32
    )
    half = buckets // 2
    edges = jnp.stack([rel_table[half - 1], rel_table[buckets - 1]], axis=1).astype(jnp.float32)
    return band.reshape(heads, 3 * TILE, TILE), edges


normal_tail = (
    0.14372023791716726,
    0.14167152280803838,
    0.14027055919455333,
    0.02504245305870889,
    0.1831401332067321,
    -0.1813703123183242,
    0.04752538660588183,
)
tail_pole = 0.36
normal_height = 0.3989422804014327


def gelu_and_slope(values):
    density = jnp.exp(values * values * -0.5)
    inverse = 1.0 / (1.0 + tail_pole * jnp.abs(values))
    series = jnp.full_like(values, normal_tail[-1])
    for coefficient in normal_tail[-2::-1]:
        series = series * inverse + coefficient
    tail = series * inverse * density
    below = jnp.where(values > 0, 1.0 - tail, tail)
    return values * below, below + values * (density * normal_height)


def send_kernel(
    capacity_ref, route_ref, rows_ref, sent_ref, place_ref, spots_ref, scratch, *, experts, slots, chunks
):
    tokens = route_ref.shape[1]
    block = sent_ref.shape[0]
    step = pl.program_id(0)

    @pl.when(step == 0)
    def _():
        route = route_ref[...]
        names = lax.broadcasted_iota(jnp.int32, (experts, tokens), 0)
        chosen = (names == route).astype(jnp.float32)
        early = lax.broadcasted_iota(jnp.int32, (tokens, tokens), 0)
        late = lax.broadcasted_iota(jnp.int32, (tokens, tokens), 1)
        before = (early < late).astype(jnp.float32).astype(jnp.bfloat16)
        earlier = times(chosen.astype(jnp.bfloat16), before)
        slot = jnp.sum(earlier * chosen, axis=0, keepdims=True).astype(jnp.int32)
        kept = slot < capacity_ref[0]
        share = slots // chunks
        chunk = jnp.zeros_like(slot)
        for later in range(1, chunks):
            chunk = chunk + (slot >= later * share).astype(jnp.int32)
        place = chunk * (experts * share) + route * share + (slot - chunk * share)
        place = jnp.where(kept, place, -1)
        ordered = jnp.where(kept, route * slots + slot, -1)
        scratch[...] = ordered
        place_ref[...] = place
        half = spots_ref.shape[1] // 2
        both = jnp.concatenate(
            [jnp.broadcast_to(place, (half, tokens)), jnp.broadcast_to(ordered, (half, tokens))], axis=0
        )
        spots_ref[...] = jnp.transpose(both)

    places = step * block + lax.broadcasted_iota(jnp.int32, (block, tokens), 0)
    onehot = (places == scratch[...]).astype(jnp.float32).astype(jnp.bfloat16)
    sent_ref[...] = times(onehot, rows_ref[...]).astype(jnp.bfloat16)


def send_first(capacity, route_row, rows, experts, slots, chunks):
    tokens, width = rows.shape
    total = experts * slots
    block = 512
    return pl.pallas_call(
        functools.partial(send_kernel, experts=experts, slots=slots, chunks=chunks),
        grid=(total // block,),
        in_specs=[
            pl.BlockSpec(memory_space=pltpu.SMEM),
            pl.BlockSpec((1, tokens), lambda step: (0, 0)),
            pl.BlockSpec((tokens, width), lambda step: (0, 0)),
        ],
        out_specs=[
            pl.BlockSpec((block, width), lambda step: (step, 0)),
            pl.BlockSpec((1, tokens), lambda step: (0, 0)),
            pl.BlockSpec((tokens, TILE), lambda step: (0, 0)),
        ],
        out_shape=[
            jax.ShapeDtypeStruct((total, width), jnp.bfloat16),
            jax.ShapeDtypeStruct((1, tokens), jnp.int32),
            jax.ShapeDtypeStruct((tokens, TILE), jnp.int32),
        ],
        scratch_shapes=[pltpu.VMEM((1, tokens), jnp.int32)],
        compiler_params=pltpu.CompilerParams(vmem_limit_bytes=VMEM_CAP),
        name="route_and_send",
    )(capacity, route_row, rows)


def send_again_kernel(place_ref, rows_ref, sent_ref, *, first):
    block = sent_ref.shape[0]
    tokens = rows_ref.shape[0]
    start = first + pl.program_id(0) * block
    places = start + lax.broadcasted_iota(jnp.int32, (block, tokens), 0)
    onehot = (places == place_ref[...]).astype(jnp.float32).astype(jnp.bfloat16)
    sent_ref[...] = times(onehot, rows_ref[...]).astype(jnp.bfloat16)


def send_again(place, rows, first, count):
    tokens, width = rows.shape
    block = 512
    return pl.pallas_call(
        functools.partial(send_again_kernel, first=first),
        grid=(count // block,),
        in_specs=[
            pl.BlockSpec((1, tokens), lambda step: (0, 0)),
            pl.BlockSpec((tokens, width), lambda step: (0, 0)),
        ],
        out_specs=pl.BlockSpec((block, width), lambda step: (step, 0)),
        out_shape=jax.ShapeDtypeStruct((count, width), jnp.bfloat16),
        compiler_params=pltpu.CompilerParams(vmem_limit_bytes=VMEM_CAP),
        cost_estimate=pl.CostEstimate(
            flops=2 * count * tokens * width,
            bytes_accessed=2 * (count + tokens) * width,
            transcendentals=0,
        ),
        name="send_rows",
    )(place, rows)


def expert_kernel(
    own_ref, rows_ref, ups_ref, up_ref, down_ref, router_ref, *rest, experts, piece
):
    (
        input_grad_ref, router_grad_ref, produced_ref, activated_ref, pre_grad_ref, slot_grad_ref,
        kept_ref,
    ) = rest[-7:]
    rows = rows_ref[...]
    ups = ups_ref[...].astype(jnp.float32).reshape(rows.shape)
    low_ups = ups.astype(jnp.bfloat16)
    router = router_ref[...]
    hidden = up_ref.shape[1]
    logits = times(rows, router)
    lanes = lax.broadcasted_iota(jnp.int32, logits.shape, 1)
    logits = jnp.where(lanes < experts, logits, -jnp.inf)
    powers = jnp.exp(logits - jnp.max(logits, axis=1, keepdims=True))
    chances = powers / jnp.sum(powers, axis=1, keepdims=True)
    mine = (lanes == own_ref[0]).astype(jnp.float32)
    gate = jnp.sum(chances * mine, axis=1, keepdims=True)
    gate_grad = jnp.zeros_like(gate)
    input_grad = jnp.zeros(rows.shape, jnp.float32)
    produced = jnp.zeros(rows.shape, jnp.float32)
    for first in range(0, hidden, piece):
        span = slice(first, first + piece)
        up = up_ref[:, span]
        down = down_ref[span, :]
        activated, slope = gelu_and_slope(times(rows, up))
        activated = activated.astype(jnp.bfloat16)
        back = times_transposed(low_ups, down)
        gate_grad = gate_grad + jnp.sum(
            activated.astype(jnp.float32) * back, axis=1, keepdims=True
        )
        pre_grad = (back * gate * slope).astype(jnp.bfloat16)
        activated_ref[0, :, span] = activated
        pre_grad_ref[0, :, span] = pre_grad
        input_grad = input_grad + times_transposed(pre_grad, up)
        produced = produced + times(activated, down)
    logit_grad = gate_grad * gate * (mine - chances)
    low_logit = logit_grad.astype(jnp.bfloat16)
    input_grad_ref[...] = (input_grad + times_transposed(low_logit, router)).astype(jnp.bfloat16)
    produced_ref[...] = (produced * gate).reshape(produced_ref.shape).astype(jnp.bfloat16)
    slot_grad_ref[0] = (ups * gate).astype(jnp.bfloat16)
    kept_ref[0] = rows

    @pl.when(pl.program_id(0) == 0)
    def _():
        router_grad_ref[...] = jnp.zeros_like(router_grad_ref)

    router_grad_ref[...] += times(jnp.transpose(logit_grad).astype(jnp.bfloat16), rows)


def expert_pass(own, rows, ups, up, down, router, experts, chunk, before):
    count, width = rows.shape
    groups, chunks, half = ups.shape[:3]
    hidden = up.shape[1]
    block = 256
    lanes = router.shape[1]
    row_spec = pl.BlockSpec((block, width), lambda step: (step, 0))
    whole = lambda shape: pl.BlockSpec(shape, lambda step: (0, 0))
    kept = lambda columns: pl.BlockSpec((1, block, columns), lambda step: (chunk, step, 0))
    stacked = lambda columns: jax.ShapeDtypeStruct((chunks, count, columns), jnp.bfloat16)
    slot_spec = pl.BlockSpec((block // half, 1, half, width), lambda step: (step, chunk, 0, 0))
    widths = (hidden, hidden, width, width)
    return pl.pallas_call(
        functools.partial(expert_kernel, experts=experts, piece=1024),
        grid=(count // block,),
        in_specs=[
            pl.BlockSpec(memory_space=pltpu.SMEM),
            row_spec, slot_spec,
            whole(up.shape), whole(down.shape), whole(router.shape),
        ] + [pl.BlockSpec(memory_space=pl.ANY)] * len(before),
        out_specs=[row_spec, whole((lanes, width)), slot_spec]
        + [kept(columns) for columns in widths],
        out_shape=[
            jax.ShapeDtypeStruct((count, width), jnp.bfloat16),
            jax.ShapeDtypeStruct((lanes, width), jnp.float32),
            jax.ShapeDtypeStruct((groups, chunks, half, width), jnp.bfloat16),
        ] + [stacked(columns) for columns in widths],
        input_output_aliases={6 + index: 2 + index for index in range(len(before))},
        compiler_params=pltpu.CompilerParams(vmem_limit_bytes=VMEM_CAP),
        cost_estimate=pl.CostEstimate(
            flops=8 * count * width * hidden,
            bytes_accessed=4 * width * hidden + 4 * count * hidden + 12 * count * width,
            transcendentals=2 * count * hidden,
        ),
        name="experts",
    )(own, rows, ups, up, down, router, *before)


def spread_rows(spots_ref, part_ref, first):
    target = spots_ref[:, :1]
    count = part_ref.shape[0]
    places = first + lax.broadcasted_iota(jnp.int32, (target.shape[0], count), 1)
    onehot = (places == target).astype(jnp.float32).astype(jnp.bfloat16)
    return times(onehot, part_ref[...])


def fetch_first_kernel(spots_ref, part_ref, out_ref):
    out_ref[...] = spread_rows(spots_ref, part_ref, 0).astype(jnp.bfloat16)


def fetch_first(spots, part):
    tokens = spots.shape[0]
    count, width = part.shape
    block = 256
    return pl.pallas_call(
        fetch_first_kernel,
        grid=(tokens // block,),
        in_specs=[
            pl.BlockSpec((block, TILE), lambda step: (step, 0)),
            pl.BlockSpec((count, width), lambda step: (0, 0)),
        ],
        out_specs=pl.BlockSpec((block, width), lambda step: (step, 0)),
        out_shape=jax.ShapeDtypeStruct((tokens, width), jnp.bfloat16),
        compiler_params=pltpu.CompilerParams(vmem_limit_bytes=64 * 1024 * 1024),
        cost_estimate=pl.CostEstimate(
            flops=2 * count * tokens * width,
            bytes_accessed=4 * tokens * width,
            transcendentals=0,
        ),
        name="fetch_first",
    )(spots, part)


def fetch_kernel(
    spots_ref, early_ref, second_ref, residual_ref, gain_ref, upstream_ref, output_ref,
    out_grad_ref, attended_grad_ref, gain_grad_ref,
):
    total = early_ref[...].astype(jnp.float32) + spread_rows(spots_ref, second_ref, second_ref.shape[0])
    residual = residual_ref[...]
    inverse = lax.rsqrt(jnp.mean(residual * residual, axis=1, keepdims=True) + eps_norm)
    scaled = residual * inverse

    @pl.when(pl.program_id(0) == 0)
    def _():
        gain_grad_ref[...] = jnp.zeros_like(gain_grad_ref)

    gain_grad_ref[...] += jnp.sum((total * scaled).reshape(-1, 8, total.shape[1]), axis=0)
    weighted = total * gain_ref[...]
    spread = jnp.mean(weighted * scaled, axis=1, keepdims=True)
    residual_grad = upstream_ref[...].astype(jnp.float32) + inverse * (weighted - scaled * spread)
    low = residual_grad.astype(jnp.bfloat16)
    out_grad_ref[...] = low
    attended_grad_ref[...] = times_transposed(low, output_ref[...]).astype(jnp.bfloat16)


def fetch_grads(spots, early, second, residual, gain_row, upstream, w_output):
    tokens, width = residual.shape
    block = 256
    row_spec = pl.BlockSpec((block, width), lambda step: (step, 0))
    whole = lambda shape: pl.BlockSpec(shape, lambda step: (0, 0))
    return pl.pallas_call(
        fetch_kernel,
        grid=(tokens // block,),
        in_specs=[
            pl.BlockSpec((block, TILE), lambda step: (step, 0)),
            row_spec, whole(second.shape),
            row_spec, whole(gain_row.shape), row_spec, whole(w_output.shape),
        ],
        out_specs=[row_spec, row_spec, whole((8, width))],
        out_shape=[
            jax.ShapeDtypeStruct((tokens, width), jnp.bfloat16),
            jax.ShapeDtypeStruct((tokens, width), jnp.bfloat16),
            jax.ShapeDtypeStruct((8, width), jnp.float32),
        ],
        compiler_params=pltpu.CompilerParams(vmem_limit_bytes=64 * 1024 * 1024),
        name="fetch_grads",
    )(spots, early, second, residual, gain_row, upstream, w_output)


def combine_kernel(spots_ref, parts_ref, residual_ref, out_ref):
    column = spots_ref.shape[1] // 2
    target = spots_ref[:, column : column + 1]
    count = parts_ref.shape[0]
    places = lax.broadcasted_iota(jnp.int32, (target.shape[0], count), 1)
    onehot = (places == target).astype(jnp.float32).astype(jnp.bfloat16)
    out_ref[...] = (residual_ref[...] + times(onehot, parts_ref[...])).astype(jnp.bfloat16)


def combine(spots, parts, residual):
    tokens, width = residual.shape
    block = 256
    row_spec = pl.BlockSpec((block, width), lambda step: (step, 0))
    return pl.pallas_call(
        combine_kernel,
        grid=(tokens // block,),
        in_specs=[
            pl.BlockSpec((block, TILE), lambda step: (step, 0)),
            pl.BlockSpec(parts.shape, lambda step: (0, 0)),
            row_spec,
        ],
        out_specs=row_spec,
        out_shape=jax.ShapeDtypeStruct((tokens, width), jnp.bfloat16),
        compiler_params=pltpu.CompilerParams(vmem_limit_bytes=VMEM_CAP),
        name="combine",
    )(spots, parts, residual)


def swap_groups(axis, size, shift, count):
    return [
        [(index, index ^ (step << shift)) for index in range(size)] for step in range(1, count)
    ]


def sum_stages(axis_sizes):
    stages = []
    for axis, size in axis_sizes:
        shift = 0
        while (1 << shift) < size:
            count = min(4, size >> shift)
            place = (lax.axis_index(axis) >> shift) & (count - 1)
            stages.append((axis, place, swap_groups(axis, size, shift, count)))
            shift += count.bit_length() - 1
    return stages


def weight_kernel(core_ref, left_ref, right_ref, away_ref, kept_ref, square):
    square[...] = times(left_ref[...], right_ref[...])
    part = away_ref.shape[0]
    away = pl.ds(pl.multiple_of((1 - core_ref[0]) * part, 16), part)
    kept = pl.ds(pl.multiple_of(core_ref[0] * part, 16), part)
    away_ref[...] = square[away, :].astype(jnp.bfloat16)
    kept_ref[...] = square[kept, :].astype(jnp.bfloat16)


def weight_terms(core, left_t, right):
    width = left_t.shape[0]
    vmem = pl.BlockSpec(memory_space=pltpu.VMEM)
    half = jax.ShapeDtypeStruct((width // 2, right.shape[1]), jnp.bfloat16)
    return pl.pallas_call(
        weight_kernel,
        in_specs=[pl.BlockSpec(memory_space=pltpu.SMEM), vmem, vmem],
        out_specs=[vmem, vmem],
        out_shape=[half, half],
        scratch_shapes=[pltpu.VMEM((width, right.shape[1]), jnp.float32)],
        compiler_params=pltpu.CompilerParams(vmem_limit_bytes=24 * 1024 * 1024),
        cost_estimate=pl.CostEstimate(
            flops=2 * width * left_t.shape[1] * right.shape[1],
            bytes_accessed=2 * (width + right.shape[1]) * left_t.shape[1],
            transcendentals=0,
        ),
        name="weight_terms",
    )(core, left_t, right)


def cut_pieces(place, source, own_ref, sent_refs):
    rows = own_ref.shape[0]
    for step, ref in enumerate((own_ref, *sent_refs)):
        first = pl.multiple_of((place ^ step) * rows, 16)
        ref[...] = source[pl.ds(first, rows), :].astype(ref.dtype)


def padded_rows(rows, count):
    return -(-rows // (16 * count)) * 16 * count


def piece_shapes(rows, width, count):
    own = jax.ShapeDtypeStruct((rows // count, width), jnp.float32)
    sent = jax.ShapeDtypeStruct((rows // count, width), jnp.bfloat16)
    return [own] + [sent] * (count - 1)


def first_pieces_kernel(
    place_ref, kept_ref, got_ref, kept_out, got_out, gain_ref, router_one, router_two, sums_ref,
    *rest, experts, counts,
):
    outs, outs_two, (small, sums) = rest[: counts[0]], rest[counts[0] : sum(counts)], rest[sum(counts) :]
    small[...] = jnp.zeros_like(small)
    sums[...] = jnp.zeros_like(sums)
    for pair in range(sums_ref.shape[0]):
        sums[2 * pair : 2 * pair + 2, :] = sums_ref[pair]
    small[:8, :] = gain_ref[...]
    small[8 : 8 + experts, :] = router_one[:experts] + router_two[:experts]
    lanes = lax.broadcasted_iota(jnp.int32, (TILE, sums.shape[1]), 1)
    names = lax.broadcasted_iota(jnp.int32, (TILE, sums.shape[1]), 0)
    onehot = (bucket_of(lanes - (2 * TILE - 1)) == names).astype(jnp.float32)
    small[8 + experts : 8 + experts + sums.shape[0], :TILE] = lax.dot_general(
        sums[...], onehot, (((1,), (1,)), ((), ())),
        precision=lax.Precision.HIGHEST, preferred_element_type=jnp.float32,
    )
    matrices, part = kept_ref.shape[:2]
    share = part // len(outs)
    extra = small.shape[0] // len(outs)
    for step, ref in enumerate(outs):
        place = place_ref[0] ^ step
        rows = pl.ds(pl.multiple_of(place * share, 16), share)
        for index in range(matrices):
            ref[index * share : (index + 1) * share, :] = (
                kept_ref[index, rows, :].astype(jnp.float32)
                + got_ref[index, rows, :].astype(jnp.float32)
            ).astype(ref.dtype)
        rows = pl.ds(pl.multiple_of(place * extra, 16), extra)
        ref[matrices * share :, :] = small[rows, :].astype(ref.dtype)
    share = part // len(outs_two)
    for step, ref in enumerate(outs_two):
        rows = pl.ds(pl.multiple_of((place_ref[1] ^ step) * share, 16), share)
        ref[...] = (
            kept_out[rows, :].astype(jnp.float32) + got_out[rows, :].astype(jnp.float32)
        ).astype(ref.dtype)


def first_pieces(
    places, kept, got, kept_out, got_out, gain_terms, router_terms, sums, experts, counts
):
    matrices, part, width = kept.shape
    sum_rows = -(-2 * sums.shape[0] // 8) * 8
    extra = padded_rows(8 + experts + sum_rows, counts[0])
    vmem = pl.BlockSpec(memory_space=pltpu.VMEM)
    shapes = piece_shapes(matrices * part + extra, width, counts[0])
    shapes += piece_shapes(part, width, counts[1])
    outs = pl.pallas_call(
        functools.partial(first_pieces_kernel, experts=experts, counts=counts),
        in_specs=[pl.BlockSpec(memory_space=pltpu.SMEM)] + [vmem] * 8,
        out_specs=[vmem] * len(shapes),
        out_shape=shapes,
        scratch_shapes=[
            pltpu.VMEM((extra, width), jnp.float32),
            pltpu.VMEM((sum_rows, sums.shape[2]), jnp.float32),
        ],
        compiler_params=pltpu.CompilerParams(vmem_limit_bytes=64 * 1024 * 1024),
        name="first_pieces",
    )(places, kept, got, kept_out, got_out, gain_terms, *router_terms, sums)
    return outs[: counts[0]], outs[counts[0] :]


def next_pieces_kernel(place_ref, *rest, received, counts):
    operands, rest = rest[: sum(received) + len(received)], rest[sum(received) + len(received) :]
    outs, sources = rest[: sum(counts)], rest[sum(counts) :]
    for chain, (count, made) in enumerate(zip(received, counts)):
        parts, operands = operands[: count + 1], operands[count + 1 :]
        cuts, outs = outs[:made], outs[made:]
        total = parts[0][...]
        for ref in parts[1:]:
            total = total + ref[...].astype(jnp.float32)
        rows = total.shape[0]
        source = sources[chain]
        source[:rows, :] = total
        if source.shape[0] > rows:
            source[rows:, :] = jnp.zeros((source.shape[0] - rows, total.shape[1]), jnp.float32)
        cut_pieces(place_ref[chain], source, cuts[0], cuts[1:])


def next_pieces(places, chains, counts):
    width = chains[0][0].shape[1]
    vmem = pl.BlockSpec(memory_space=pltpu.VMEM)
    shapes, scratch = [], []
    for (own, _), count in zip(chains, counts):
        rows = own.shape[0]
        padded = padded_rows(rows, count)
        scratch.append(pltpu.VMEM((padded, width), jnp.float32))
        if count == 1:
            shapes.append(jax.ShapeDtypeStruct((rows, width), jnp.bfloat16))
        else:
            shapes += piece_shapes(padded, width, count)
    operands = [array for own, got in chains for array in (own, *got)]
    outs = pl.pallas_call(
        functools.partial(
            next_pieces_kernel, received=tuple(len(got) for _, got in chains), counts=tuple(counts)
        ),
        in_specs=[pl.BlockSpec(memory_space=pltpu.SMEM)] + [vmem] * len(operands),
        out_specs=[vmem] * len(shapes),
        out_shape=shapes,
        scratch_shapes=scratch,
        compiler_params=pltpu.CompilerParams(vmem_limit_bytes=20 * 1024 * 1024),
        name="next_pieces",
    )(places, *operands)
    return outs[: counts[0]], outs[counts[0] :]


def join_kernel(place_ref, *rest, counts):
    pieces, rest = rest[: sum(counts)], rest[sum(counts) :]
    outs, joined = rest[: len(counts)], rest[len(counts) :]
    for chain, count in enumerate(counts):
        parts, pieces = pieces[:count], pieces[count:]
        rows = parts[0].shape[0]
        for step, ref in enumerate(parts):
            first = pl.multiple_of((place_ref[chain] ^ step) * rows, 16)
            joined[chain][pl.ds(first, rows), :] = ref[...]
        outs[chain][...] = joined[chain][: outs[chain].shape[0], :]


def join_pieces(places, chains, kept):
    width = chains[0][0].shape[1]
    vmem = pl.BlockSpec(memory_space=pltpu.VMEM)
    operands = [piece for pieces in chains for piece in pieces]
    return pl.pallas_call(
        functools.partial(join_kernel, counts=tuple(len(pieces) for pieces in chains)),
        in_specs=[pl.BlockSpec(memory_space=pltpu.SMEM)] + [vmem] * len(operands),
        out_specs=[vmem] * len(chains),
        out_shape=[jax.ShapeDtypeStruct((rows, width), jnp.bfloat16) for rows in kept],
        scratch_shapes=[
            pltpu.VMEM((len(pieces) * pieces[0].shape[0], width), jnp.bfloat16) for pieces in chains
        ],
        compiler_params=pltpu.CompilerParams(vmem_limit_bytes=20 * 1024 * 1024),
        name="join_pieces",
    )(places, *operands)


def finish_kernel(place_ref, *rest, counts, table):
    ones, twos = rest[: 2 * counts[0]], rest[2 * counts[0] : 2 * sum(counts)]
    rest = rest[2 * sum(counts) :]
    weight_refs, gain_ref, rest = rest[:3], rest[3], rest[4:]
    square_outs, (gain_out, second_out, router_out, table_out), rest = rest[:4], rest[4:8], rest[8:]
    weights, squares, columns, small, load_sems, store_sems = rest
    core = place_ref[0]
    width = weights.shape[2]
    part = width // 2
    share = part // counts[0]
    loads = [
        pltpu.make_async_copy(ref, weights.at[index], load_sems.at[index])
        for index, ref in enumerate(weight_refs)
    ]
    for load in loads:
        load.start()

    def spots(place, count, rows):
        found = []
        for step in range(count):
            for other in range(2):
                half = 1 - core if other else core
                first = half * part + (place ^ step) * rows
                found.append(pl.ds(pl.multiple_of(first, 16), rows))
        return found

    stores = []
    for index in (3, 0, 1, 2):
        if index == 3:
            rows_two = part // counts[1]
            for ref, rows in zip(twos, spots(place_ref[2], counts[1], rows_two)):
                squares[index, rows, :] = ref[:rows_two, :].astype(jnp.float32)
        else:
            loads[index].wait()
            for ref, rows in zip(ones, spots(place_ref[1], counts[0], share)):
                total = ref[index * share : (index + 1) * share, :].astype(jnp.float32)
                squares[index, rows, :] = total
                term = jnp.sum(
                    total * weights[index, rows, :].astype(jnp.float32), axis=1, keepdims=True
                )
                if index == 0:
                    columns[rows, :] = jnp.broadcast_to(term, (share, TILE))
                else:
                    columns[rows, :] += jnp.broadcast_to(term, (share, TILE))
        store = pltpu.make_async_copy(squares.at[index], square_outs[index], store_sems.at[index])
        store.start()
        stores.append(store)
    gain = jnp.transpose(columns[...])[:1] / gain_ref[...]
    gain_out[...] = gain.reshape(width)
    extra = small.shape[0] // counts[0]
    for step in range(counts[0]):
        rows = pl.ds(pl.multiple_of((place_ref[1] ^ step) * extra, 16), extra)
        small[rows, :] = ones[2 * step][3 * share :, :].astype(jnp.float32) + ones[2 * step + 1][
            3 * share :, :
        ].astype(jnp.float32)
    experts = router_out.shape[0]
    buckets, heads = table
    second_out[...] = jnp.sum(small[:8, :], axis=0, keepdims=True).reshape(width)
    router_out[...] = small[8 : 8 + experts, :]
    table_out[...] = small[8 + experts : 8 + experts + heads, :buckets]
    for store in stores:
        store.wait()


def finish(places, chains, weights, gain_row, experts, table):
    width = weights[0].shape[1]
    counts = tuple(len(pieces) // 2 for pieces in chains)
    square = jax.ShapeDtypeStruct((width, width), jnp.float32)
    row = jax.ShapeDtypeStruct((width,), jnp.float32)
    vmem = pl.BlockSpec(memory_space=pltpu.VMEM)
    extra = chains[0][0].shape[0] - 3 * (width // 2 // counts[0])
    pieces = [piece for chain in chains for piece in chain]
    return pl.pallas_call(
        functools.partial(finish_kernel, counts=counts, table=table),
        in_specs=[pl.BlockSpec(memory_space=pltpu.SMEM)]
        + [vmem] * len(pieces)
        + [pl.BlockSpec(memory_space=pl.ANY)] * 3
        + [vmem],
        out_specs=[pl.BlockSpec(memory_space=pl.ANY)] * 4 + [vmem] * 4,
        out_shape=[
            square, square, square, square, row, row,
            jax.ShapeDtypeStruct((experts, width), jnp.float32),
            jax.ShapeDtypeStruct(table[::-1], jnp.float32),
        ],
        scratch_shapes=[
            pltpu.VMEM((3, width, width), jnp.bfloat16),
            pltpu.VMEM((4, width, width), jnp.float32),
            pltpu.VMEM((width, TILE), jnp.float32),
            pltpu.VMEM((counts[0] * extra, width), jnp.float32),
            pltpu.SemaphoreType.DMA((3,)),
            pltpu.SemaphoreType.DMA((4,)),
        ],
        compiler_params=pltpu.CompilerParams(vmem_limit_bytes=40 * 1024 * 1024),
        name="finish",
    )(places, *pieces, *weights, gain_row)


def hidden_kernel(
    grads_ref, query_ref, key_ref, value_ref, hidden_ref, gain_ref, residual_grad_ref, out_ref
):
    total = None
    for index, weight in enumerate((query_ref, key_ref, value_ref)):
        term = times_transposed(grads_ref[index], weight[...])
        total = term if total is None else total + term
    hidden = hidden_ref[...].astype(jnp.float32)
    inverse = lax.rsqrt(jnp.mean(hidden * hidden, axis=1, keepdims=True) + eps_norm)
    scaled = hidden * inverse
    weighted = total * gain_ref[...]
    spread = jnp.mean(weighted * scaled, axis=1, keepdims=True)
    out_ref[...] = (
        residual_grad_ref[...].astype(jnp.float32) + inverse * (weighted - scaled * spread)
    ).astype(jnp.bfloat16)


def hidden_gradient(grads, weights, hidden, gain_row, residual_grad):
    tokens, width = hidden.shape
    block = 256
    row_spec = pl.BlockSpec((block, width), lambda step: (step, 0))
    whole = lambda shape: pl.BlockSpec(shape, lambda step: (0, 0))
    return pl.pallas_call(
        hidden_kernel,
        grid=(tokens // block,),
        in_specs=[pl.BlockSpec((3, block, width), lambda step: (0, step, 0))]
        + [whole(weight.shape) for weight in weights]
        + [row_spec, whole(gain_row.shape), row_spec],
        out_specs=row_spec,
        out_shape=jax.ShapeDtypeStruct((tokens, width), jnp.bfloat16),
        compiler_params=pltpu.CompilerParams(vmem_limit_bytes=VMEM_CAP),
        cost_estimate=pl.CostEstimate(
            flops=6 * tokens * width * width, bytes_accessed=20 * tokens * width, transcendentals=0
        ),
        name="hidden_gradient",
    )(grads, *weights, hidden, gain_row, residual_grad)


def exchange_pieces(stage, pieces):
    axis, _, swaps = stage
    return [lax.ppermute(piece, axis, pairs) for piece, pairs in zip(pieces, swaps)]


def on_device(
    hidden_in,
    first_gain,
    w_query,
    w_key,
    w_value,
    w_output,
    rel_table,
    second_gain,
    router,
    expert_up,
    expert_down,
    routes,
    capacity_factor,
    cotangent,
):
    axes = ("narrow", "wide")
    chunks = 2
    tokens, width = hidden_in.shape
    bucket_count = rel_table.shape[0]
    experts = router.shape[1]
    slots = 2 * tokens // experts
    capacity = capacity_factor * tokens // experts
    devices = lax.axis_size(axes)
    own = lax.axis_index(axes).astype(jnp.int32).reshape(1)
    padded = -(-experts // TILE) * TILE
    router_wide = jnp.pad(router, ((0, 0), (0, padded - experts)))

    def exchange(rows):
        blocks = rows.reshape(experts, -1, width)
        return lax.all_to_all(blocks, axes, split_axis=0, concat_axis=0, tiled=True).reshape(
            -1, width
        )

    together = lax.optimization_barrier
    sent_ups, place, spots = send_first(
        capacity, routes.reshape(1, tokens), cotangent, experts, slots, chunks
    )
    sent_ups, hidden_in = together((sent_ups, hidden_in))
    ups = exchange(sent_ups)

    band, edges = bias_band(rel_table)
    hidden = hidden_in.astype(jnp.float32)
    gain_one = first_gain.astype(jnp.float32)
    gain_two = second_gain.astype(jnp.float32)
    inverse_one = lax.rsqrt(jnp.mean(hidden * hidden, axis=-1, keepdims=True) + eps_norm)
    normed_first = (hidden * inverse_one * gain_one).astype(jnp.bfloat16)
    queries = times(normed_first, w_query).astype(jnp.bfloat16)
    keys = times(normed_first, w_key).astype(jnp.bfloat16)
    values = times(normed_first, w_value).astype(jnp.bfloat16)
    attended, attended_t, logs = attend(queries, keys, values, band, edges)
    residual = hidden + times(attended, w_output)
    inverse_two = lax.rsqrt(jnp.mean(residual * residual, axis=-1, keepdims=True) + eps_norm)
    normed_second = (residual * inverse_two * gain_two).astype(jnp.bfloat16)
    half = experts * slots // chunks
    sent = send_again(place, normed_second, 0, half)
    sent, ups = together((sent, ups))
    rows = [exchange(sent)]
    queries_again, _ = together((queries, ups))
    weights, normed_t = attend_weights(queries_again, keys, logs, band, edges, normed_first)
    sent = send_again(place, normed_second, half, half)
    sent, rows[0], weights, normed_t = together((sent, rows[0], weights, normed_t))
    rows.append(exchange(sent))
    ups = ups.reshape(experts, chunks, slots // chunks, width)

    saved = ()
    input_grads, router_terms = [], []
    for c in range(chunks):
        input_grad, router_term, *saved = expert_pass(
            own, rows[c], ups, expert_up[0], expert_down[0], router_wide, experts, c, saved
        )
        if c + 1 < chunks:
            input_grad, rows[-1] = together((input_grad, rows[-1]))
        if input_grads:
            input_grad, input_grads[-1] = together((input_grad, input_grads[-1]))
        input_grads.append(exchange(input_grad))
        router_terms.append(router_term)
    saved, input_grads[0] = together((saved, input_grads[0]))
    produced = saved[0].reshape(-1, width)
    activated, pre_grad, slot_grad, kept_rows = [
        array.reshape(-1, array.shape[-1]) for array in saved[1:]
    ]
    gradient_expert_down = inner_rows(activated, slot_grad)[None]
    gradient_expert_up = inner_rows(kept_rows, pre_grad)[None]
    fetched = fetch_first(spots, input_grads[0])
    gain_row = gain_two[None]
    input_grads[-1], fetched, gradient_expert_down, gradient_expert_up, produced, gain_row = together(
        (input_grads[-1], fetched, gradient_expert_down, gradient_expert_up, produced, gain_row)
    )
    produced = exchange(produced)
    out_grad, attended_grad, gain_terms = fetch_grads(
        spots, fetched, input_grads[-1], residual, gain_row, cotangent, w_output
    )
    core = lax.axis_index("narrow").astype(jnp.int32).reshape(1)
    swap = [(0, 1), (1, 0)]
    grads, away, kept, sums = attend_back(
        core, queries, keys, values, attended_grad, attended, weights, normed_t
    )
    got = lax.ppermute(away, "narrow", swap)
    out_grad, kept = together((out_grad, kept))
    away_out, kept_out = weight_terms(core, attended_t, out_grad)
    got_out = lax.ppermute(away_out, "narrow", swap)
    stages = sum_stages([("wide", lax.axis_size("wide"))])
    levels = len(stages)
    orders = (stages, stages[1:] + stages[:1])
    counts = [[len(stage[2]) + 1 for stage in order] for order in orders]

    def places_at(level):
        return jnp.stack([order[level][1] for order in orders]).astype(jnp.int32)

    chains = first_pieces(
        places_at(0), kept, got, kept_out, got_out, gain_terms, router_terms, sums, experts,
        (counts[0][0], counts[1][0]),
    )
    projections = (w_query, w_key, w_value)
    grads, kept = together((grads, kept))
    gradient_hidden = hidden_gradient(
        grads, projections, hidden_in, gain_one[None], out_grad
    )
    rows_at = []
    for level in range(levels):
        rows_at.append([chain[0].shape[0] for chain in chains])
        received = [
            (chain[0], exchange_pieces(order[level], chain[1:]))
            for chain, order in zip(chains, orders)
        ]
        last = level + 1 == levels
        places = jnp.zeros((2,), jnp.int32) if last else places_at(level + 1)
        cuts = [1 if last else count[level + 1] for count in counts]
        own = received[0][0]
        if level == 0:
            own, gradient_hidden = together((own, gradient_hidden))
        if level == 0:
            block_out = combine(spots, produced, residual)
            own, block_out = together((own, block_out))
        received[0] = (own, received[0][1])
        chains = next_pieces(places, received, cuts)
    lows = [chain[0] for chain in chains]
    for level in reversed(range(1, levels)):
        parts = [
            [low] + exchange_pieces(order[level], [low] * len(order[level][2]))
            for low, order in zip(lows, orders)
        ]
        lows = list(join_pieces(places_at(level), parts, rows_at[level - 1]))
    parts = [
        [low] + exchange_pieces(order[0], [low] * len(order[0][2]))
        for low, order in zip(lows, orders)
    ]
    places = jnp.concatenate([core, places_at(0)])
    parts[0][1], places = together((parts[0][1], places))
    others = [[], [lax.ppermute(piece, "narrow", swap) for piece in parts[1]]]
    parts[0][-1] = together((parts[0][-1], *others[1]))[0]
    others[0] = [lax.ppermute(piece, "narrow", swap) for piece in parts[0]]
    parts = [
        [piece for both in zip(own, other) for piece in both] for own, other in zip(parts, others)
    ]
    (
        gradient_query, gradient_key, gradient_value, gradient_output, gradient_first_gain,
        gradient_second_gain, gradient_router, gradient_table,
    ) = finish(places, parts, projections, gain_one[None], experts, rel_table.shape)
    return (
        block_out,
        gradient_hidden,
        gradient_first_gain,
        gradient_query,
        gradient_key,
        gradient_value,
        gradient_output,
        jnp.transpose(gradient_table),
        gradient_second_gain,
        jnp.transpose(gradient_router),
        gradient_expert_up,
        gradient_expert_down,
    )


def solution(mesh):
    split = ("narrow", "wide")
    rows, experts = P(split, None), P(split, None, None)
    return jax.shard_map(
        on_device,
        mesh=mesh,
        in_specs=(rows,) + (P(),) * 8 + (experts, experts, rows, P(split), rows),
        out_specs=(rows, rows) + (P(),) * 8 + (experts, experts),
        check_vma=False,
    )
```

```python
import functools

import jax
import jax.numpy as jnp
from jax import lax
from jax.experimental import pallas as pl
from jax.experimental.pallas import tpu as pltpu
from jax.sharding import PartitionSpec as P

TILE = 128
STRIP = 256
BACK_STRIP = 512
VMEM_CAP = 60 * 1024 * 1024
eps_norm = 1e-06
bucket_edges = (12, 16, 23, 32, 46, 64, 91)


def bucket_of(offset):
    distance = jnp.abs(offset)
    far_bucket = jnp.full(distance.shape, 8, jnp.int32)
    for edge in bucket_edges:
        far_bucket = far_bucket + (distance >= edge).astype(jnp.int32)
    near_bucket = jnp.where(distance < 8, distance, far_bucket)
    return near_bucket + 16 * (offset > 0).astype(jnp.int32)


def band_buckets():
    rows = lax.broadcasted_iota(jnp.int32, (3 * TILE, TILE), 0)
    lanes = lax.broadcasted_iota(jnp.int32, (3 * TILE, TILE), 1)
    return bucket_of(rows - TILE - lanes)


def times_transposed(left, right):
    return lax.dot_general(
        left, right, (((1,), (1,)), ((), ())), preferred_element_type=jnp.float32
    )


def inner_rows(left, right):
    return lax.dot_general(
        left, right, (((0,), (0,)), ((), ())), preferred_element_type=jnp.float32
    )


def times(left, right):
    return jnp.dot(left, right, preferred_element_type=jnp.float32)


def fill_wide(edge_ref, band_ref, wide):
    length = (wide.shape[1] + TILE) // 2
    pair = pl.program_id(0)
    for side in range(2):
        head = 2 * pair + side
        wide[side, : length - 2 * TILE] = jnp.full(
            (length - 2 * TILE, TILE), edge_ref[head, 0], jnp.float32
        )
        wide[side, length - 2 * TILE : length + TILE] = band_ref[side]
        wide[side, length + TILE :] = jnp.full(
            (length - 2 * TILE, TILE), edge_ref[head, 1], jnp.float32
        )


def strip_bias(wide, side, key_start, keys, query_start):
    length = (wide.shape[1] + TILE) // 2
    parts = []
    for start in range(query_start, query_start + STRIP, TILE):
        first = length - TILE - start + key_start
        parts.append(wide[side, first : first + keys, :])
    return jnp.concatenate(parts, axis=1)


def half_of(rows, side):
    half = rows.shape[1] // 2
    lanes = lax.broadcasted_iota(jnp.int32, rows.shape, 1)
    own = lanes < half if side == 0 else lanes >= half
    return jnp.where(own, rows, jnp.zeros_like(rows))


def attend_kernel(
    edge_ref, q_ref, k_ref, v_ref, band_ref, out_ref, turned_ref, log_ref, wide
):
    length = q_ref.shape[0]
    half = q_ref.shape[1] // 2
    scale = half ** (-0.5)
    fill_wide(edge_ref, band_ref, wide)
    keys = k_ref[...]
    values_t = jnp.transpose(v_ref[...])
    for start in range(0, length, STRIP):
        mixed = []
        for side in range(2):
            query = half_of(q_ref[start : start + STRIP, :] * scale, side)
            scores = times_transposed(keys, query) + strip_bias(wide, side, 0, length, start)
            top = jnp.max(scores, axis=0, keepdims=True)
            powers = jnp.exp(scores - top)
            total = jnp.sum(powers, axis=0, keepdims=True)
            raw = times(values_t[side * half : (side + 1) * half], powers.astype(jnp.bfloat16))
            mixed.append(raw / total)
            log_ref[0, side : side + 1, start : start + STRIP] = top + jnp.log(total)
        both = jnp.concatenate(mixed, axis=0)
        out_ref[start : start + STRIP, :] = jnp.transpose(both).astype(jnp.bfloat16)
        turned_ref[:, start : start + STRIP] = both.astype(jnp.bfloat16)


def attend(queries, keys, values, band, edges):
    length, width = queries.shape
    heads = edges.shape[0]
    pairs = heads // 2
    columns = width // pairs
    part = pl.BlockSpec((length, columns), lambda pair: (0, pair))
    return pl.pallas_call(
        attend_kernel,
        grid=(pairs,),
        in_specs=[
            pl.BlockSpec(memory_space=pltpu.SMEM),
            part,
            part,
            part,
            pl.BlockSpec((2, 3 * TILE, TILE), lambda pair: (pair, 0, 0)),
        ],
        out_specs=[
            part,
            pl.BlockSpec((columns, length), lambda pair: (pair, 0)),
            pl.BlockSpec((1, 2, length), lambda pair: (pair, 0, 0)),
        ],
        out_shape=[
            jax.ShapeDtypeStruct((length, width), jnp.bfloat16),
            jax.ShapeDtypeStruct((width, length), jnp.bfloat16),
            jax.ShapeDtypeStruct((pairs, 2, length), jnp.float32),
        ],
        scratch_shapes=[pltpu.VMEM((2, 2 * length - TILE, TILE), jnp.float32)],
        compiler_params=pltpu.CompilerParams(vmem_limit_bytes=VMEM_CAP),
        cost_estimate=pl.CostEstimate(
            flops=4 * heads * length * length * (width // heads),
            bytes_accessed=8 * length * width,
            transcendentals=heads * length * length,
        ),
        name="attend",
    )(edges, queries, keys, values, band)


def weights_kernel(
    edge_ref, q_ref, k_ref, log_ref, band_ref, normed_ref, weights_ref, turned_ref, wide
):
    length = q_ref.shape[0]
    scale = (q_ref.shape[1] // 2) ** (-0.5)
    head = 2 * pl.program_id(0)
    for side in range(2):
        turned = [
            jnp.transpose(band_ref[side, part : part + TILE, :]) for part in range(0, 3 * TILE, TILE)
        ]
        wide[side, :, : length - 2 * TILE] = jnp.full(
            (TILE, length - 2 * TILE), edge_ref[head + side, 0], jnp.float32
        )
        wide[side, :, length - 2 * TILE : length + TILE] = jnp.concatenate(turned, axis=1)
        wide[side, :, length + TILE :] = jnp.full(
            (TILE, length - 2 * TILE), edge_ref[head + side, 1], jnp.float32
        )
    keys = k_ref[...]
    turned_ref[...] = jnp.transpose(normed_ref[...])
    for start in range(0, length, STRIP):
        strip = slice(start, start + STRIP)
        for side in range(2):
            query = half_of(q_ref[strip, :] * scale, side)
            bias = jnp.concatenate(
                [
                    wide[side, :, length - TILE - first : 2 * length - TILE - first]
                    for first in range(start, start + STRIP, TILE)
                ],
                axis=0,
            )
            logs = jnp.transpose(
                jnp.broadcast_to(log_ref[0, side : side + 1, strip], (TILE, STRIP))
            )[:, :1]
            scores = times_transposed(query, keys) + bias
            weights_ref[side, strip, :] = jnp.exp(scores - logs).astype(jnp.bfloat16)


def attend_weights(queries, keys, logs, band, edges, normed):
    length, width = queries.shape
    heads = edges.shape[0]
    pairs = heads // 2
    columns = width // pairs
    part = pl.BlockSpec((length, columns), lambda pair: (0, pair))
    return pl.pallas_call(
        weights_kernel,
        grid=(pairs,),
        in_specs=[
            pl.BlockSpec(memory_space=pltpu.SMEM),
            part,
            part,
            pl.BlockSpec((1, 2, length), lambda pair: (pair, 0, 0)),
            pl.BlockSpec((2, 3 * TILE, TILE), lambda pair: (pair, 0, 0)),
            part,
        ],
        out_specs=[
            pl.BlockSpec((2, length, length), lambda pair: (pair, 0, 0)),
            pl.BlockSpec((columns, length), lambda pair: (pair, 0)),
        ],
        out_shape=[
            jax.ShapeDtypeStruct((heads, length, length), jnp.bfloat16),
            jax.ShapeDtypeStruct((width, length), jnp.bfloat16),
        ],
        scratch_shapes=[pltpu.VMEM((2, TILE, 2 * length - TILE), jnp.float32)],
        compiler_params=pltpu.CompilerParams(vmem_limit_bytes=VMEM_CAP),
        cost_estimate=pl.CostEstimate(
            flops=2 * heads * length * length * (width // heads),
            bytes_accessed=4 * length * width + 2 * heads * length * length,
            transcendentals=heads * length * length,
        ),
        name="attend_weights",
    )(edges, queries, keys, logs, band, normed)


def diagonal_sums(near_ref, side, beyond):
    span = 4 * TILE
    zeros = jnp.zeros((8, span - TILE), jnp.float32)
    total = jnp.zeros((8, span), jnp.float32)
    for block in range(3):
        for row in range(0, TILE, 8):
            first = block * TILE + row
            wide = jnp.concatenate([near_ref[side, first : first + 8, :], zeros], axis=1)
            total = total + pltpu.roll(wide, (block + 1) * TILE - 1 - row, 1)
    rows = lax.broadcasted_iota(jnp.int32, total.shape, 0)
    for bit in (1, 2, 4):
        total = jnp.where((rows & bit) != 0, pltpu.roll(total, span - bit, 1), total)
    sums = jnp.sum(total, axis=0, keepdims=True)
    lanes = lax.broadcasted_iota(jnp.int32, sums.shape, 1)
    sums = sums + jnp.where(lanes == 0, beyond[0], 0.0)
    return sums + jnp.where(lanes == span - 2, beyond[1], 0.0)


def attend_back_kernel(
    core_ref, q_ref, k_ref, v_ref, grad_ref, out_ref, weights_ref, normed_ref,
    grads_ref, away_ref, kept_ref, sums_ref,
    near_ref, query_total, square,
):
    length = q_ref.shape[0]
    columns = q_ref.shape[1]
    half = columns // 2
    blocks = length // TILE
    scale = half ** (-0.5)
    names = lax.broadcasted_iota(jnp.int32, (2 * blocks, length), 0)
    owners = lax.broadcasted_iota(jnp.int32, (2 * blocks, length), 1) // TILE
    picks = (names == owners).astype(jnp.float32).astype(jnp.bfloat16)
    queries_t = jnp.transpose(q_ref[...] * scale)
    grads_t = jnp.transpose(grad_ref[...])
    near_ref[...] = jnp.zeros_like(near_ref)
    key_parts, value_parts = [], []
    for side in range(2):
        rows = slice(side * half, (side + 1) * half)
        grad = half_of(grad_ref[...], side)
        keys = half_of(k_ref[...], side)
        center = jnp.sum(
            grad.astype(jnp.float32) * out_ref[...].astype(jnp.float32), axis=1, keepdims=True
        )
        left = jnp.concatenate([queries_t[rows], picks], axis=0)
        key_total, value_total = None, None
        for start in range(0, length, BACK_STRIP):
            strip = slice(start, start + BACK_STRIP)
            weights = weights_ref[side, strip, :]
            weight_grad = times_transposed(grad[strip], v_ref[...])
            score_grad = weights.astype(jnp.float32) * (weight_grad - center[strip])
            score_low = score_grad.astype(jnp.bfloat16)
            value_term = times(grads_t[rows, strip], weights)
            value_total = value_term if value_total is None else value_total + value_term
            key_term = times(left[:, strip], score_low)
            key_total = key_term if key_total is None else key_total + key_term
            query_term = times(score_low, keys)
            if side == 0:
                query_total[strip, :] = query_term
            else:
                query_total[strip, :] += query_term
            for row in range(0, BACK_STRIP, TILE):
                for lane in range(0, length, TILE):
                    apart = (lane - start - row) // TILE
                    if abs(apart) <= 1:
                        spot = (apart + 1) * TILE
                        near_ref[side, spot : spot + TILE, :] += score_grad[
                            row : row + TILE, lane : lane + TILE
                        ]
        key_parts.append(key_total[:half])
        value_parts.append(value_total)
        sums = key_total[half:]
        beyond = [
            jnp.sum(jnp.where(keep, sums, 0.0), keepdims=True)
            for keep in (names >= owners + 2, (names <= owners - 2) & (names < blocks))
        ]
        sums_ref[0, side : side + 1, :] = diagonal_sums(near_ref, side, beyond)
    grads_ref[0] = (query_total[...] * scale).astype(jnp.bfloat16)
    grads_ref[1] = jnp.transpose(jnp.concatenate(key_parts, axis=0)).astype(jnp.bfloat16)
    grads_ref[2] = jnp.transpose(jnp.concatenate(value_parts, axis=0)).astype(jnp.bfloat16)
    part = normed_ref.shape[0] // 2
    stacked = jnp.concatenate([grads_ref[index] for index in range(3)], axis=1)
    square[...] = times(normed_ref[...], stacked)
    away = pl.ds(pl.multiple_of((1 - core_ref[0]) * part, 16), part)
    kept = pl.ds(pl.multiple_of(core_ref[0] * part, 16), part)
    for index in range(3):
        span = slice(index * columns, (index + 1) * columns)
        away_ref[index] = square[away, span].astype(jnp.bfloat16)
        kept_ref[index] = square[kept, span].astype(jnp.bfloat16)


def attend_back(core, queries, keys, values, grads, attended, weights, normed_t):
    length, width = queries.shape
    heads = weights.shape[0]
    pairs = heads // 2
    columns = width // pairs
    part = pl.BlockSpec((length, columns), lambda pair: (0, pair))
    square = pl.BlockSpec((3, width // 2, columns), lambda pair: (0, 0, pair))
    return pl.pallas_call(
        attend_back_kernel,
        grid=(pairs,),
        in_specs=[
            pl.BlockSpec(memory_space=pltpu.SMEM),
            part, part, part, part, part,
            pl.BlockSpec((2, length, length), lambda pair: (pair, 0, 0)),
            pl.BlockSpec((width, length), lambda pair: (0, 0)),
        ],
        out_specs=[
            pl.BlockSpec((3, length, columns), lambda pair: (0, 0, pair)),
            square, square,
            pl.BlockSpec((1, 2, 4 * TILE), lambda pair: (pair, 0, 0)),
        ],
        out_shape=[
            jax.ShapeDtypeStruct((3, length, width), jnp.bfloat16),
            jax.ShapeDtypeStruct((3, width // 2, width), jnp.bfloat16),
            jax.ShapeDtypeStruct((3, width // 2, width), jnp.bfloat16),
            jax.ShapeDtypeStruct((pairs, 2, 4 * TILE), jnp.float32),
        ],
        scratch_shapes=[
            pltpu.VMEM((2, 3 * TILE, TILE), jnp.float32),
            pltpu.VMEM((length, columns), jnp.float32),
            pltpu.VMEM((width, 3 * columns), jnp.float32),
        ],
        compiler_params=pltpu.CompilerParams(vmem_limit_bytes=VMEM_CAP),
        cost_estimate=pl.CostEstimate(
            flops=10 * heads * length * length * (width // heads),
            bytes_accessed=16 * length * width + 2 * heads * length * length,
            transcendentals=0,
        ),
        name="attend_back",
    )(core, queries, keys, values, grads, attended, weights, normed_t)


def bias_band(rel_table):
    buckets, heads = rel_table.shape
    labels = band_buckets().reshape(1, -1)
    onehot = (labels == jnp.arange(buckets, dtype=jnp.int32)[:, None]).astype(jnp.bfloat16)
    band = lax.dot_general(
        rel_table, onehot, (((0,), (0,)), ((), ())), preferred_element_type=jnp.float32
    )
    half = buckets // 2
    edges = jnp.stack([rel_table[half - 1], rel_table[buckets - 1]], axis=1).astype(jnp.float32)
    return band.reshape(heads, 3 * TILE, TILE), edges


normal_tail = (
    0.14372023791716726,
    0.14167152280803838,
    0.14027055919455333,
    0.02504245305870889,
    0.1831401332067321,
    -0.1813703123183242,
    0.04752538660588183,
)
tail_pole = 0.36
normal_height = 0.3989422804014327


def gelu_and_slope(values):
    density = jnp.exp(values * values * -0.5)
    inverse = 1.0 / (1.0 + tail_pole * jnp.abs(values))
    series = jnp.full_like(values, normal_tail[-1])
    for coefficient in normal_tail[-2::-1]:
        series = series * inverse + coefficient
    tail = series * inverse * density
    below = jnp.where(values > 0, 1.0 - tail, tail)
    return values * below, below + values * (density * normal_height)


def send_kernel(
    capacity_ref, route_ref, rows_ref, sent_ref, place_ref, spots_ref, scratch, *, experts, slots, chunks
):
    tokens = route_ref.shape[1]
    block = sent_ref.shape[0]
    step = pl.program_id(0)

    @pl.when(step == 0)
    def _():
        route = route_ref[...]
        names = lax.broadcasted_iota(jnp.int32, (experts, tokens), 0)
        chosen = (names == route).astype(jnp.float32)
        early = lax.broadcasted_iota(jnp.int32, (tokens, tokens), 0)
        late = lax.broadcasted_iota(jnp.int32, (tokens, tokens), 1)
        before = (early < late).astype(jnp.float32).astype(jnp.bfloat16)
        earlier = times(chosen.astype(jnp.bfloat16), before)
        slot = jnp.sum(earlier * chosen, axis=0, keepdims=True).astype(jnp.int32)
        kept = slot < capacity_ref[0]
        share = slots // chunks
        chunk = jnp.zeros_like(slot)
        for later in range(1, chunks):
            chunk = chunk + (slot >= later * share).astype(jnp.int32)
        place = chunk * (experts * share) + route * share + (slot - chunk * share)
        place = jnp.where(kept, place, -1)
        ordered = jnp.where(kept, route * slots + slot, -1)
        scratch[...] = ordered
        place_ref[...] = place
        half = spots_ref.shape[1] // 2
        both = jnp.concatenate(
            [jnp.broadcast_to(place, (half, tokens)), jnp.broadcast_to(ordered, (half, tokens))], axis=0
        )
        spots_ref[...] = jnp.transpose(both)

    places = step * block + lax.broadcasted_iota(jnp.int32, (block, tokens), 0)
    onehot = (places == scratch[...]).astype(jnp.float32).astype(jnp.bfloat16)
    sent_ref[...] = times(onehot, rows_ref[...]).astype(jnp.bfloat16)


def send_first(capacity, route_row, rows, experts, slots, chunks):
    tokens, width = rows.shape
    total = experts * slots
    block = 512
    return pl.pallas_call(
        functools.partial(send_kernel, experts=experts, slots=slots, chunks=chunks),
        grid=(total // block,),
        in_specs=[
            pl.BlockSpec(memory_space=pltpu.SMEM),
            pl.BlockSpec((1, tokens), lambda step: (0, 0)),
            pl.BlockSpec((tokens, width), lambda step: (0, 0)),
        ],
        out_specs=[
            pl.BlockSpec((block, width), lambda step: (step, 0)),
            pl.BlockSpec((1, tokens), lambda step: (0, 0)),
            pl.BlockSpec((tokens, TILE), lambda step: (0, 0)),
        ],
        out_shape=[
            jax.ShapeDtypeStruct((total, width), jnp.bfloat16),
            jax.ShapeDtypeStruct((1, tokens), jnp.int32),
            jax.ShapeDtypeStruct((tokens, TILE), jnp.int32),
        ],
        scratch_shapes=[pltpu.VMEM((1, tokens), jnp.int32)],
        compiler_params=pltpu.CompilerParams(vmem_limit_bytes=VMEM_CAP),
        name="route_and_send",
    )(capacity, route_row, rows)


def send_again_kernel(place_ref, rows_ref, sent_ref, *, first):
    block = sent_ref.shape[0]
    tokens = rows_ref.shape[0]
    start = first + pl.program_id(0) * block
    places = start + lax.broadcasted_iota(jnp.int32, (block, tokens), 0)
    onehot = (places == place_ref[...]).astype(jnp.float32).astype(jnp.bfloat16)
    sent_ref[...] = times(onehot, rows_ref[...]).astype(jnp.bfloat16)


def send_again(place, rows, first, count):
    tokens, width = rows.shape
    block = 512
    return pl.pallas_call(
        functools.partial(send_again_kernel, first=first),
        grid=(count // block,),
        in_specs=[
            pl.BlockSpec((1, tokens), lambda step: (0, 0)),
            pl.BlockSpec((tokens, width), lambda step: (0, 0)),
        ],
        out_specs=pl.BlockSpec((block, width), lambda step: (step, 0)),
        out_shape=jax.ShapeDtypeStruct((count, width), jnp.bfloat16),
        compiler_params=pltpu.CompilerParams(vmem_limit_bytes=VMEM_CAP),
        cost_estimate=pl.CostEstimate(
            flops=2 * count * tokens * width,
            bytes_accessed=2 * (count + tokens) * width,
            transcendentals=0,
        ),
        name="send_rows",
    )(place, rows)


def expert_kernel(
    own_ref, rows_ref, ups_ref, up_ref, down_ref, router_ref, *rest, experts, piece
):
    (
        input_grad_ref, router_grad_ref, produced_ref, activated_ref, pre_grad_ref, slot_grad_ref,
        kept_ref,
    ) = rest[-7:]
    rows = rows_ref[...]
    ups = ups_ref[...].astype(jnp.float32).reshape(rows.shape)
    low_ups = ups.astype(jnp.bfloat16)
    router = router_ref[...]
    hidden = up_ref.shape[1]
    logits = times(rows, router)
    lanes = lax.broadcasted_iota(jnp.int32, logits.shape, 1)
    logits = jnp.where(lanes < experts, logits, -jnp.inf)
    powers = jnp.exp(logits - jnp.max(logits, axis=1, keepdims=True))
    chances = powers / jnp.sum(powers, axis=1, keepdims=True)
    mine = (lanes == own_ref[0]).astype(jnp.float32)
    gate = jnp.sum(chances * mine, axis=1, keepdims=True)
    gate_grad = jnp.zeros_like(gate)
    input_grad = jnp.zeros(rows.shape, jnp.float32)
    produced = jnp.zeros(rows.shape, jnp.float32)
    for first in range(0, hidden, piece):
        span = slice(first, first + piece)
        up = up_ref[:, span]
        down = down_ref[span, :]
        activated, slope = gelu_and_slope(times(rows, up))
        activated = activated.astype(jnp.bfloat16)
        back = times_transposed(low_ups, down)
        gate_grad = gate_grad + jnp.sum(
            activated.astype(jnp.float32) * back, axis=1, keepdims=True
        )
        pre_grad = (back * gate * slope).astype(jnp.bfloat16)
        activated_ref[0, :, span] = activated
        pre_grad_ref[0, :, span] = pre_grad
        input_grad = input_grad + times_transposed(pre_grad, up)
        produced = produced + times(activated, down)
    logit_grad = gate_grad * gate * (mine - chances)
    low_logit = logit_grad.astype(jnp.bfloat16)
    input_grad_ref[...] = (input_grad + times_transposed(low_logit, router)).astype(jnp.bfloat16)
    produced_ref[...] = (produced * gate).reshape(produced_ref.shape).astype(jnp.bfloat16)
    slot_grad_ref[0] = (ups * gate).astype(jnp.bfloat16)
    kept_ref[0] = rows

    @pl.when(pl.program_id(0) == 0)
    def _():
        router_grad_ref[...] = jnp.zeros_like(router_grad_ref)

    router_grad_ref[...] += times(jnp.transpose(logit_grad).astype(jnp.bfloat16), rows)


def expert_pass(own, rows, ups, up, down, router, experts, chunk, before):
    count, width = rows.shape
    groups, chunks, half = ups.shape[:3]
    hidden = up.shape[1]
    block = 256
    lanes = router.shape[1]
    row_spec = pl.BlockSpec((block, width), lambda step: (step, 0))
    whole = lambda shape: pl.BlockSpec(shape, lambda step: (0, 0))
    kept = lambda columns: pl.BlockSpec((1, block, columns), lambda step: (chunk, step, 0))
    stacked = lambda columns: jax.ShapeDtypeStruct((chunks, count, columns), jnp.bfloat16)
    slot_spec = pl.BlockSpec((block // half, 1, half, width), lambda step: (step, chunk, 0, 0))
    widths = (hidden, hidden, width, width)
    return pl.pallas_call(
        functools.partial(expert_kernel, experts=experts, piece=1024),
        grid=(count // block,),
        in_specs=[
            pl.BlockSpec(memory_space=pltpu.SMEM),
            row_spec, slot_spec,
            whole(up.shape), whole(down.shape), whole(router.shape),
        ] + [pl.BlockSpec(memory_space=pl.ANY)] * len(before),
        out_specs=[row_spec, whole((lanes, width)), slot_spec]
        + [kept(columns) for columns in widths],
        out_shape=[
            jax.ShapeDtypeStruct((count, width), jnp.bfloat16),
            jax.ShapeDtypeStruct((lanes, width), jnp.float32),
            jax.ShapeDtypeStruct((groups, chunks, half, width), jnp.bfloat16),
        ] + [stacked(columns) for columns in widths],
        input_output_aliases={6 + index: 2 + index for index in range(len(before))},
        compiler_params=pltpu.CompilerParams(vmem_limit_bytes=VMEM_CAP),
        cost_estimate=pl.CostEstimate(
            flops=8 * count * width * hidden,
            bytes_accessed=4 * width * hidden + 4 * count * hidden + 12 * count * width,
            transcendentals=2 * count * hidden,
        ),
        name="experts",
    )(own, rows, ups, up, down, router, *before)


def spread_rows(spots_ref, part_ref, first):
    target = spots_ref[:, :1]
    count = part_ref.shape[0]
    places = first + lax.broadcasted_iota(jnp.int32, (target.shape[0], count), 1)
    onehot = (places == target).astype(jnp.float32).astype(jnp.bfloat16)
    return times(onehot, part_ref[...])


def fetch_first_kernel(spots_ref, part_ref, out_ref):
    out_ref[...] = spread_rows(spots_ref, part_ref, 0).astype(jnp.bfloat16)


def fetch_first(spots, part):
    tokens = spots.shape[0]
    count, width = part.shape
    block = 256
    return pl.pallas_call(
        fetch_first_kernel,
        grid=(tokens // block,),
        in_specs=[
            pl.BlockSpec((block, TILE), lambda step: (step, 0)),
            pl.BlockSpec((count, width), lambda step: (0, 0)),
        ],
        out_specs=pl.BlockSpec((block, width), lambda step: (step, 0)),
        out_shape=jax.ShapeDtypeStruct((tokens, width), jnp.bfloat16),
        compiler_params=pltpu.CompilerParams(vmem_limit_bytes=64 * 1024 * 1024),
        cost_estimate=pl.CostEstimate(
            flops=2 * count * tokens * width,
            bytes_accessed=4 * tokens * width,
            transcendentals=0,
        ),
        name="fetch_first",
    )(spots, part)


def fetch_kernel(
    spots_ref, early_ref, second_ref, residual_ref, gain_ref, upstream_ref, output_ref,
    out_grad_ref, attended_grad_ref, gain_grad_ref,
):
    total = early_ref[...].astype(jnp.float32) + spread_rows(spots_ref, second_ref, second_ref.shape[0])
    residual = residual_ref[...]
    inverse = lax.rsqrt(jnp.mean(residual * residual, axis=1, keepdims=True) + eps_norm)
    scaled = residual * inverse

    @pl.when(pl.program_id(0) == 0)
    def _():
        gain_grad_ref[...] = jnp.zeros_like(gain_grad_ref)

    gain_grad_ref[...] += jnp.sum((total * scaled).reshape(-1, 8, total.shape[1]), axis=0)
    weighted = total * gain_ref[...]
    spread = jnp.mean(weighted * scaled, axis=1, keepdims=True)
    residual_grad = upstream_ref[...].astype(jnp.float32) + inverse * (weighted - scaled * spread)
    low = residual_grad.astype(jnp.bfloat16)
    out_grad_ref[...] = low
    attended_grad_ref[...] = times_transposed(low, output_ref[...]).astype(jnp.bfloat16)


def fetch_grads(spots, early, second, residual, gain_row, upstream, w_output):
    tokens, width = residual.shape
    block = 256
    row_spec = pl.BlockSpec((block, width), lambda step: (step, 0))
    whole = lambda shape: pl.BlockSpec(shape, lambda step: (0, 0))
    return pl.pallas_call(
        fetch_kernel,
        grid=(tokens // block,),
        in_specs=[
            pl.BlockSpec((block, TILE), lambda step: (step, 0)),
            row_spec, whole(second.shape),
            row_spec, whole(gain_row.shape), row_spec, whole(w_output.shape),
        ],
        out_specs=[row_spec, row_spec, whole((8, width))],
        out_shape=[
            jax.ShapeDtypeStruct((tokens, width), jnp.bfloat16),
            jax.ShapeDtypeStruct((tokens, width), jnp.bfloat16),
            jax.ShapeDtypeStruct((8, width), jnp.float32),
        ],
        compiler_params=pltpu.CompilerParams(vmem_limit_bytes=64 * 1024 * 1024),
        name="fetch_grads",
    )(spots, early, second, residual, gain_row, upstream, w_output)


def combine_kernel(spots_ref, parts_ref, residual_ref, out_ref):
    column = spots_ref.shape[1] // 2
    target = spots_ref[:, column : column + 1]
    count = parts_ref.shape[0]
    places = lax.broadcasted_iota(jnp.int32, (target.shape[0], count), 1)
    onehot = (places == target).astype(jnp.float32).astype(jnp.bfloat16)
    out_ref[...] = (residual_ref[...] + times(onehot, parts_ref[...])).astype(jnp.bfloat16)


def combine(spots, parts, residual):
    tokens, width = residual.shape
    block = 512
    row_spec = pl.BlockSpec((block, width), lambda step: (step, 0))
    return pl.pallas_call(
        combine_kernel,
        grid=(tokens // block,),
        in_specs=[
            pl.BlockSpec((block, TILE), lambda step: (step, 0)),
            pl.BlockSpec(parts.shape, lambda step: (0, 0)),
            row_spec,
        ],
        out_specs=row_spec,
        out_shape=jax.ShapeDtypeStruct((tokens, width), jnp.bfloat16),
        compiler_params=pltpu.CompilerParams(vmem_limit_bytes=VMEM_CAP),
        name="combine",
    )(spots, parts, residual)


def swap_groups(axis, size, shift, count):
    return [
        [(index, index ^ (step << shift)) for index in range(size)] for step in range(1, count)
    ]


def sum_stages(axis_sizes):
    stages = []
    for axis, size in axis_sizes:
        shift = 0
        while (1 << shift) < size:
            count = min(4, size >> shift)
            place = (lax.axis_index(axis) >> shift) & (count - 1)
            stages.append((axis, place, swap_groups(axis, size, shift, count)))
            shift += count.bit_length() - 1
    return stages


def weight_kernel(core_ref, left_ref, right_ref, away_ref, kept_ref, square):
    square[...] = times(left_ref[...], right_ref[...])
    part = away_ref.shape[0]
    away = pl.ds(pl.multiple_of((1 - core_ref[0]) * part, 16), part)
    kept = pl.ds(pl.multiple_of(core_ref[0] * part, 16), part)
    away_ref[...] = square[away, :].astype(jnp.bfloat16)
    kept_ref[...] = square[kept, :].astype(jnp.bfloat16)


def weight_terms(core, left_t, right):
    width = left_t.shape[0]
    vmem = pl.BlockSpec(memory_space=pltpu.VMEM)
    half = jax.ShapeDtypeStruct((width // 2, right.shape[1]), jnp.bfloat16)
    return pl.pallas_call(
        weight_kernel,
        in_specs=[pl.BlockSpec(memory_space=pltpu.SMEM), vmem, vmem],
        out_specs=[vmem, vmem],
        out_shape=[half, half],
        scratch_shapes=[pltpu.VMEM((width, right.shape[1]), jnp.float32)],
        compiler_params=pltpu.CompilerParams(vmem_limit_bytes=24 * 1024 * 1024),
        cost_estimate=pl.CostEstimate(
            flops=2 * width * left_t.shape[1] * right.shape[1],
            bytes_accessed=2 * (width + right.shape[1]) * left_t.shape[1],
            transcendentals=0,
        ),
        name="weight_terms",
    )(core, left_t, right)


def cut_pieces(place, source, own_ref, sent_refs):
    rows = own_ref.shape[0]
    for step, ref in enumerate((own_ref, *sent_refs)):
        first = pl.multiple_of((place ^ step) * rows, 16)
        ref[...] = source[pl.ds(first, rows), :].astype(ref.dtype)


def padded_rows(rows, count):
    return -(-rows // (16 * count)) * 16 * count


def piece_shapes(rows, width, count):
    own = jax.ShapeDtypeStruct((rows // count, width), jnp.bfloat16)
    sent = jax.ShapeDtypeStruct((rows // count, width), jnp.bfloat16)
    return [own] + [sent] * (count - 1)


def first_pieces_kernel(
    place_ref, kept_ref, got_ref, kept_out, got_out, gain_ref, router_one, router_two, sums_ref,
    *rest, experts, counts,
):
    outs, outs_two, (small, sums) = rest[: counts[0]], rest[counts[0] : sum(counts)], rest[sum(counts) :]
    small[...] = jnp.zeros_like(small)
    sums[...] = jnp.zeros_like(sums)
    for pair in range(sums_ref.shape[0]):
        sums[2 * pair : 2 * pair + 2, :] = sums_ref[pair]
    small[:8, :] = gain_ref[...]
    small[8 : 8 + experts, :] = router_one[:experts] + router_two[:experts]
    lanes = lax.broadcasted_iota(jnp.int32, (TILE, sums.shape[1]), 1)
    names = lax.broadcasted_iota(jnp.int32, (TILE, sums.shape[1]), 0)
    onehot = (bucket_of(lanes - (2 * TILE - 1)) == names).astype(jnp.float32)
    small[8 + experts : 8 + experts + sums.shape[0], :TILE] = lax.dot_general(
        sums[...], onehot, (((1,), (1,)), ((), ())),
        precision=lax.Precision.HIGHEST, preferred_element_type=jnp.float32,
    )
    matrices, part = kept_ref.shape[:2]
    share = part // len(outs)
    extra = small.shape[0] // len(outs)
    for step, ref in enumerate(outs):
        place = place_ref[0] ^ step
        rows = pl.ds(pl.multiple_of(place * share, 16), share)
        for index in range(matrices):
            ref[index * share : (index + 1) * share, :] = (
                kept_ref[index, rows, :].astype(jnp.float32)
                + got_ref[index, rows, :].astype(jnp.float32)
            ).astype(ref.dtype)
        rows = pl.ds(pl.multiple_of(place * extra, 16), extra)
        ref[matrices * share :, :] = small[rows, :].astype(ref.dtype)
    share = part // len(outs_two)
    for step, ref in enumerate(outs_two):
        rows = pl.ds(pl.multiple_of((place_ref[1] ^ step) * share, 16), share)
        ref[...] = (
            kept_out[rows, :].astype(jnp.float32) + got_out[rows, :].astype(jnp.float32)
        ).astype(ref.dtype)


def first_pieces(
    places, kept, got, kept_out, got_out, gain_terms, router_terms, sums, experts, counts
):
    matrices, part, width = kept.shape
    sum_rows = -(-2 * sums.shape[0] // 8) * 8
    extra = padded_rows(8 + experts + sum_rows, counts[0])
    vmem = pl.BlockSpec(memory_space=pltpu.VMEM)
    shapes = piece_shapes(matrices * part + extra, width, counts[0])
    shapes += piece_shapes(part, width, counts[1])
    outs = pl.pallas_call(
        functools.partial(first_pieces_kernel, experts=experts, counts=counts),
        grid=(1,),
        in_specs=[pl.BlockSpec(memory_space=pltpu.SMEM)]
        + [vmem] * 5
        + [pl.BlockSpec((experts, width), lambda step: (0, 0))] * 2
        + [vmem],
        out_specs=[vmem] * len(shapes),
        out_shape=shapes,
        scratch_shapes=[
            pltpu.VMEM((extra, width), jnp.float32),
            pltpu.VMEM((sum_rows, sums.shape[2]), jnp.float32),
        ],
        compiler_params=pltpu.CompilerParams(vmem_limit_bytes=64 * 1024 * 1024),
        name="first_pieces",
    )(places, kept, got, kept_out, got_out, gain_terms, *router_terms, sums)
    return outs[: counts[0]], outs[counts[0] :]


def next_pieces_kernel(place_ref, *rest, received, counts):
    operands, rest = rest[: sum(received) + len(received)], rest[sum(received) + len(received) :]
    outs, sources = rest[: sum(counts)], rest[sum(counts) :]
    for chain, (count, made) in enumerate(zip(received, counts)):
        parts, operands = operands[: count + 1], operands[count + 1 :]
        cuts, outs = outs[:made], outs[made:]
        total = parts[0][...].astype(jnp.float32)
        for ref in parts[1:]:
            total = total + ref[...].astype(jnp.float32)
        rows = total.shape[0]
        source = sources[chain]
        source[:rows, :] = total
        if source.shape[0] > rows:
            source[rows:, :] = jnp.zeros((source.shape[0] - rows, total.shape[1]), jnp.float32)
        cut_pieces(place_ref[chain], source, cuts[0], cuts[1:])


def next_pieces(places, chains, counts):
    width = chains[0][0].shape[1]
    vmem = pl.BlockSpec(memory_space=pltpu.VMEM)
    shapes, scratch = [], []
    for (own, _), count in zip(chains, counts):
        rows = own.shape[0]
        padded = padded_rows(rows, count)
        scratch.append(pltpu.VMEM((padded, width), jnp.float32))
        if count == 1:
            shapes.append(jax.ShapeDtypeStruct((rows, width), jnp.bfloat16))
        else:
            shapes += piece_shapes(padded, width, count)
    operands = [array for own, got in chains for array in (own, *got)]
    outs = pl.pallas_call(
        functools.partial(
            next_pieces_kernel, received=tuple(len(got) for _, got in chains), counts=tuple(counts)
        ),
        in_specs=[pl.BlockSpec(memory_space=pltpu.SMEM)] + [vmem] * len(operands),
        out_specs=[vmem] * len(shapes),
        out_shape=shapes,
        scratch_shapes=scratch,
        compiler_params=pltpu.CompilerParams(vmem_limit_bytes=20 * 1024 * 1024),
        name="next_pieces",
    )(places, *operands)
    return outs[: counts[0]], outs[counts[0] :]


def join_kernel(place_ref, *rest, counts):
    pieces, rest = rest[: sum(counts)], rest[sum(counts) :]
    outs, joined = rest[: len(counts)], rest[len(counts) :]
    for chain, count in enumerate(counts):
        parts, pieces = pieces[:count], pieces[count:]
        rows = parts[0].shape[0]
        for step, ref in enumerate(parts):
            first = pl.multiple_of((place_ref[chain] ^ step) * rows, 16)
            joined[chain][pl.ds(first, rows), :] = ref[...]
        outs[chain][...] = joined[chain][: outs[chain].shape[0], :]


def join_pieces(places, chains, kept):
    width = chains[0][0].shape[1]
    vmem = pl.BlockSpec(memory_space=pltpu.VMEM)
    operands = [piece for pieces in chains for piece in pieces]
    return pl.pallas_call(
        functools.partial(join_kernel, counts=tuple(len(pieces) for pieces in chains)),
        in_specs=[pl.BlockSpec(memory_space=pltpu.SMEM)] + [vmem] * len(operands),
        out_specs=[vmem] * len(chains),
        out_shape=[jax.ShapeDtypeStruct((rows, width), jnp.bfloat16) for rows in kept],
        scratch_shapes=[
            pltpu.VMEM((len(pieces) * pieces[0].shape[0], width), jnp.bfloat16) for pieces in chains
        ],
        compiler_params=pltpu.CompilerParams(vmem_limit_bytes=20 * 1024 * 1024),
        name="join_pieces",
    )(places, *operands)


def finish_kernel(place_ref, *rest, counts, table):
    ones, twos = rest[: 2 * counts[0]], rest[2 * counts[0] : 2 * sum(counts)]
    rest = rest[2 * sum(counts) :]
    weight_refs, gain_ref, rest = rest[:3], rest[3], rest[4:]
    square_outs, (gain_out, second_out, router_out, table_out), rest = rest[:4], rest[4:8], rest[8:]
    weights, squares, columns, small, load_sems, store_sems = rest
    core = place_ref[0]
    width = weights.shape[2]
    part = width // 2
    share = part // counts[0]
    loads = [
        pltpu.make_async_copy(ref, weights.at[index], load_sems.at[index])
        for index, ref in enumerate(weight_refs)
    ]
    for load in loads:
        load.start()

    def spots(place, count, rows):
        found = []
        for step in range(count):
            for other in range(2):
                half = 1 - core if other else core
                first = half * part + (place ^ step) * rows
                found.append(pl.ds(pl.multiple_of(first, 16), rows))
        return found

    stores = []
    for index in (3, 0, 1, 2):
        if index == 3:
            rows_two = part // counts[1]
            for ref, rows in zip(twos, spots(place_ref[2], counts[1], rows_two)):
                squares[index, rows, :] = ref[:rows_two, :].astype(jnp.float32)
        else:
            loads[index].wait()
            for ref, rows in zip(ones, spots(place_ref[1], counts[0], share)):
                total = ref[index * share : (index + 1) * share, :].astype(jnp.float32)
                squares[index, rows, :] = total
                term = jnp.sum(
                    total * weights[index, rows, :].astype(jnp.float32), axis=1, keepdims=True
                )
                if index == 0:
                    columns[rows, :] = jnp.broadcast_to(term, (share, TILE))
                else:
                    columns[rows, :] += jnp.broadcast_to(term, (share, TILE))
        store = pltpu.make_async_copy(squares.at[index], square_outs[index], store_sems.at[index])
        store.start()
        stores.append(store)
    gain = jnp.transpose(columns[...])[:1] / gain_ref[...]
    gain_out[...] = gain.reshape(width)
    extra = small.shape[0] // counts[0]
    for step in range(counts[0]):
        rows = pl.ds(pl.multiple_of((place_ref[1] ^ step) * extra, 16), extra)
        small[rows, :] = ones[2 * step][3 * share :, :].astype(jnp.float32) + ones[2 * step + 1][
            3 * share :, :
        ].astype(jnp.float32)
    experts = router_out.shape[0]
    buckets, heads = table
    second_out[...] = jnp.sum(small[:8, :], axis=0, keepdims=True).reshape(width)
    router_out[...] = small[8 : 8 + experts, :]
    table_out[...] = small[8 + experts : 8 + experts + heads, :buckets]
    for store in stores:
        store.wait()


def finish(places, chains, weights, gain_row, experts, table):
    width = weights[0].shape[1]
    counts = tuple(len(pieces) // 2 for pieces in chains)
    square = jax.ShapeDtypeStruct((width, width), jnp.float32)
    row = jax.ShapeDtypeStruct((width,), jnp.float32)
    vmem = pl.BlockSpec(memory_space=pltpu.VMEM)
    extra = chains[0][0].shape[0] - 3 * (width // 2 // counts[0])
    pieces = [piece for chain in chains for piece in chain]
    return pl.pallas_call(
        functools.partial(finish_kernel, counts=counts, table=table),
        in_specs=[pl.BlockSpec(memory_space=pltpu.SMEM)]
        + [vmem] * len(pieces)
        + [pl.BlockSpec(memory_space=pl.ANY)] * 3
        + [vmem],
        out_specs=[pl.BlockSpec(memory_space=pl.ANY)] * 4 + [vmem] * 4,
        out_shape=[
            square, square, square, square, row, row,
            jax.ShapeDtypeStruct((experts, width), jnp.float32),
            jax.ShapeDtypeStruct(table[::-1], jnp.float32),
        ],
        scratch_shapes=[
            pltpu.VMEM((3, width, width), jnp.bfloat16),
            pltpu.VMEM((4, width, width), jnp.float32),
            pltpu.VMEM((width, TILE), jnp.float32),
            pltpu.VMEM((counts[0] * extra, width), jnp.float32),
            pltpu.SemaphoreType.DMA((3,)),
            pltpu.SemaphoreType.DMA((4,)),
        ],
        compiler_params=pltpu.CompilerParams(vmem_limit_bytes=40 * 1024 * 1024),
        name="finish",
    )(places, *pieces, *weights, gain_row)


def hidden_kernel(
    grads_ref, query_ref, key_ref, value_ref, hidden_ref, gain_ref, residual_grad_ref, out_ref
):
    total = None
    for index, weight in enumerate((query_ref, key_ref, value_ref)):
        term = times_transposed(grads_ref[index], weight[...])
        total = term if total is None else total + term
    hidden = hidden_ref[...].astype(jnp.float32)
    inverse = lax.rsqrt(jnp.mean(hidden * hidden, axis=1, keepdims=True) + eps_norm)
    scaled = hidden * inverse
    weighted = total * gain_ref[...]
    spread = jnp.mean(weighted * scaled, axis=1, keepdims=True)
    out_ref[...] = (
        residual_grad_ref[...].astype(jnp.float32) + inverse * (weighted - scaled * spread)
    ).astype(jnp.bfloat16)


def hidden_gradient(grads, weights, hidden, gain_row, residual_grad):
    tokens, width = hidden.shape
    block = 256
    row_spec = pl.BlockSpec((block, width), lambda step: (step, 0))
    whole = lambda shape: pl.BlockSpec(shape, lambda step: (0, 0))
    return pl.pallas_call(
        hidden_kernel,
        grid=(tokens // block,),
        in_specs=[pl.BlockSpec((3, block, width), lambda step: (0, step, 0))]
        + [whole(weight.shape) for weight in weights]
        + [row_spec, whole(gain_row.shape), row_spec],
        out_specs=row_spec,
        out_shape=jax.ShapeDtypeStruct((tokens, width), jnp.bfloat16),
        compiler_params=pltpu.CompilerParams(vmem_limit_bytes=VMEM_CAP),
        cost_estimate=pl.CostEstimate(
            flops=6 * tokens * width * width, bytes_accessed=20 * tokens * width, transcendentals=0
        ),
        name="hidden_gradient",
    )(grads, *weights, hidden, gain_row, residual_grad)


def exchange_pieces(stage, pieces):
    axis, _, swaps = stage
    return [lax.ppermute(piece, axis, pairs) for piece, pairs in zip(pieces, swaps)]


def on_device(
    hidden_in,
    first_gain,
    w_query,
    w_key,
    w_value,
    w_output,
    rel_table,
    second_gain,
    router,
    expert_up,
    expert_down,
    routes,
    capacity_factor,
    cotangent,
):
    axes = ("narrow", "wide")
    chunks = 2
    tokens, width = hidden_in.shape
    bucket_count = rel_table.shape[0]
    experts = router.shape[1]
    slots = 2 * tokens // experts
    capacity = capacity_factor * tokens // experts
    devices = lax.axis_size(axes)
    own = lax.axis_index(axes).astype(jnp.int32).reshape(1)
    padded = -(-experts // TILE) * TILE
    router_wide = jnp.pad(router, ((0, 0), (0, padded - experts)))

    def exchange(rows):
        blocks = rows.reshape(experts, -1, width)
        return lax.all_to_all(blocks, axes, split_axis=0, concat_axis=0, tiled=True).reshape(
            -1, width
        )

    together = lax.optimization_barrier
    sent_ups, place, spots = send_first(
        capacity, routes.reshape(1, tokens), cotangent, experts, slots, chunks
    )
    sent_ups, hidden_in = together((sent_ups, hidden_in))
    ups = exchange(sent_ups)

    band, edges = bias_band(rel_table)
    hidden = hidden_in.astype(jnp.float32)
    gain_one = first_gain.astype(jnp.float32)
    gain_two = second_gain.astype(jnp.float32)
    inverse_one = lax.rsqrt(jnp.mean(hidden * hidden, axis=-1, keepdims=True) + eps_norm)
    normed_first = (hidden * inverse_one * gain_one).astype(jnp.bfloat16)
    queries = times(normed_first, w_query).astype(jnp.bfloat16)
    keys = times(normed_first, w_key).astype(jnp.bfloat16)
    values = times(normed_first, w_value).astype(jnp.bfloat16)
    attended, attended_t, logs = attend(queries, keys, values, band, edges)
    residual = hidden + times(attended, w_output)
    inverse_two = lax.rsqrt(jnp.mean(residual * residual, axis=-1, keepdims=True) + eps_norm)
    normed_second = (residual * inverse_two * gain_two).astype(jnp.bfloat16)
    half = experts * slots // chunks
    sent = send_again(place, normed_second, 0, half)
    sent, ups = together((sent, ups))
    rows = [exchange(sent)]
    queries_again, _ = together((queries, ups))
    weights, normed_t = attend_weights(queries_again, keys, logs, band, edges, normed_first)
    sent = send_again(place, normed_second, half, half)
    sent, rows[0], weights, normed_t = together((sent, rows[0], weights, normed_t))
    rows.append(exchange(sent))
    ups = ups.reshape(experts, chunks, slots // chunks, width)

    saved = ()
    input_grads, router_terms = [], []
    for c in range(chunks):
        input_grad, router_term, *saved = expert_pass(
            own, rows[c], ups, expert_up[0], expert_down[0], router_wide, experts, c, saved
        )
        if c + 1 < chunks:
            input_grad, rows[-1] = together((input_grad, rows[-1]))
        if input_grads:
            input_grad, input_grads[-1] = together((input_grad, input_grads[-1]))
        input_grads.append(exchange(input_grad))
        router_terms.append(router_term)
    saved, input_grads[0] = together((saved, input_grads[0]))
    produced = saved[0].reshape(-1, width)
    activated, pre_grad, slot_grad, kept_rows = [
        array.reshape(-1, array.shape[-1]) for array in saved[1:]
    ]
    gradient_expert_down = inner_rows(activated, slot_grad)[None]
    gradient_expert_up = inner_rows(kept_rows, pre_grad)[None]
    fetched = fetch_first(spots, input_grads[0])
    gain_row = gain_two[None]
    input_grads[-1], fetched, gradient_expert_down, gradient_expert_up, produced, gain_row = together(
        (input_grads[-1], fetched, gradient_expert_down, gradient_expert_up, produced, gain_row)
    )
    produced = exchange(produced)
    out_grad, attended_grad, gain_terms = fetch_grads(
        spots, fetched, input_grads[-1], residual, gain_row, cotangent, w_output
    )
    core = lax.axis_index("narrow").astype(jnp.int32).reshape(1)
    swap = [(0, 1), (1, 0)]
    grads, away, kept, sums = attend_back(
        core, queries, keys, values, attended_grad, attended, weights, normed_t
    )
    got = lax.ppermute(away, "narrow", swap)
    out_grad, kept = together((out_grad, kept))
    away_out, kept_out = weight_terms(core, attended_t, out_grad)
    got_out = lax.ppermute(away_out, "narrow", swap)
    stages = sum_stages([("wide", lax.axis_size("wide"))])
    levels = len(stages)
    orders = (stages, stages[1:] + stages[:1])
    counts = [[len(stage[2]) + 1 for stage in order] for order in orders]

    def places_at(level):
        return jnp.stack([order[level][1] for order in orders]).astype(jnp.int32)

    chains = first_pieces(
        places_at(0), kept, got, kept_out, got_out, gain_terms, router_terms, sums, experts,
        (counts[0][0], counts[1][0]),
    )
    projections = (w_query, w_key, w_value)
    grads, kept = together((grads, kept))
    gradient_hidden = hidden_gradient(
        grads, projections, hidden_in, gain_one[None], out_grad
    )
    rows_at = []
    for level in range(levels):
        rows_at.append([chain[0].shape[0] for chain in chains])
        received = [
            (chain[0], exchange_pieces(order[level], chain[1:]))
            for chain, order in zip(chains, orders)
        ]
        last = level + 1 == levels
        places = jnp.zeros((2,), jnp.int32) if last else places_at(level + 1)
        cuts = [1 if last else count[level + 1] for count in counts]
        own = received[0][0]
        if level == 0:
            own, gradient_hidden = together((own, gradient_hidden))
        if level == 0:
            block_out = combine(spots, produced, residual)
            own, block_out = together((own, block_out))
        received[0] = (own, received[0][1])
        chains = next_pieces(places, received, cuts)
    lows = [chain[0] for chain in chains]
    for level in reversed(range(1, levels)):
        parts = [
            [low] + exchange_pieces(order[level], [low] * len(order[level][2]))
            for low, order in zip(lows, orders)
        ]
        lows = list(join_pieces(places_at(level), parts, rows_at[level - 1]))
    parts = [
        [low] + exchange_pieces(order[0], [low] * len(order[0][2]))
        for low, order in zip(lows, orders)
    ]
    places = jnp.concatenate([core, places_at(0)])
    parts[0][1], places = together((parts[0][1], places))
    others = [[], [lax.ppermute(piece, "narrow", swap) for piece in parts[1]]]
    parts[0][-1] = together((parts[0][-1], *others[1]))[0]
    others[0] = [lax.ppermute(piece, "narrow", swap) for piece in parts[0]]
    parts = [
        [piece for both in zip(own, other) for piece in both] for own, other in zip(parts, others)
    ]
    (
        gradient_query, gradient_key, gradient_value, gradient_output, gradient_first_gain,
        gradient_second_gain, gradient_router, gradient_table,
    ) = finish(places, parts, projections, gain_one[None], experts, rel_table.shape)
    return (
        block_out,
        gradient_hidden,
        gradient_first_gain,
        gradient_query,
        gradient_key,
        gradient_value,
        gradient_output,
        jnp.transpose(gradient_table),
        gradient_second_gain,
        jnp.transpose(gradient_router),
        gradient_expert_up,
        gradient_expert_down,
    )


def solution(mesh):
    split = ("narrow", "wide")
    rows, experts = P(split, None), P(split, None, None)
    return jax.shard_map(
        on_device,
        mesh=mesh,
        in_specs=(rows,) + (P(),) * 8 + (experts, experts, rows, P(split), rows),
        out_specs=(rows, rows) + (P(),) * 8 + (experts, experts),
        check_vma=False,
    )
```

```python
import functools

import jax
import jax.numpy as jnp
from jax import lax
from jax.experimental import pallas as pl
from jax.experimental.pallas import tpu as pltpu
from jax.sharding import PartitionSpec as P

TILE = 128
STRIP = 256
BACK_STRIP = 512
VMEM_CAP = 60 * 1024 * 1024
eps_norm = 1e-06
bucket_edges = (12, 16, 23, 32, 46, 64, 91)


def bucket_of(offset):
    distance = jnp.abs(offset)
    far_bucket = jnp.full(distance.shape, 8, jnp.int32)
    for edge in bucket_edges:
        far_bucket = far_bucket + (distance >= edge).astype(jnp.int32)
    near_bucket = jnp.where(distance < 8, distance, far_bucket)
    return near_bucket + 16 * (offset > 0).astype(jnp.int32)


def band_buckets():
    rows = lax.broadcasted_iota(jnp.int32, (3 * TILE, TILE), 0)
    lanes = lax.broadcasted_iota(jnp.int32, (3 * TILE, TILE), 1)
    return bucket_of(rows - TILE - lanes)


def times_transposed(left, right):
    return lax.dot_general(
        left, right, (((1,), (1,)), ((), ())), preferred_element_type=jnp.float32
    )


def inner_rows(left, right):
    return lax.dot_general(
        left, right, (((0,), (0,)), ((), ())), preferred_element_type=jnp.float32
    )


def times(left, right):
    return jnp.dot(left, right, preferred_element_type=jnp.float32)


def fill_wide(edge_ref, band_ref, wide):
    length = (wide.shape[1] + TILE) // 2
    pair = pl.program_id(0)
    for side in range(2):
        head = 2 * pair + side
        wide[side, : length - 2 * TILE] = jnp.full(
            (length - 2 * TILE, TILE), edge_ref[head, 0], jnp.float32
        )
        wide[side, length - 2 * TILE : length + TILE] = band_ref[side]
        wide[side, length + TILE :] = jnp.full(
            (length - 2 * TILE, TILE), edge_ref[head, 1], jnp.float32
        )


def strip_bias(wide, side, key_start, keys, query_start):
    length = (wide.shape[1] + TILE) // 2
    parts = []
    for start in range(query_start, query_start + STRIP, TILE):
        first = length - TILE - start + key_start
        parts.append(wide[side, first : first + keys, :])
    return jnp.concatenate(parts, axis=1)


def half_of(rows, side):
    half = rows.shape[1] // 2
    lanes = lax.broadcasted_iota(jnp.int32, rows.shape, 1)
    own = lanes < half if side == 0 else lanes >= half
    return jnp.where(own, rows, jnp.zeros_like(rows))


def attend_kernel(
    edge_ref, q_ref, k_ref, v_ref, band_ref, out_ref, turned_ref, log_ref, wide
):
    length = q_ref.shape[0]
    half = q_ref.shape[1] // 2
    scale = half ** (-0.5)
    fill_wide(edge_ref, band_ref, wide)
    keys = k_ref[...]
    values_t = jnp.transpose(v_ref[...])
    for start in range(0, length, STRIP):
        mixed = []
        for side in range(2):
            query = half_of(q_ref[start : start + STRIP, :] * scale, side)
            scores = times_transposed(keys, query) + strip_bias(wide, side, 0, length, start)
            top = jnp.max(scores, axis=0, keepdims=True)
            powers = jnp.exp(scores - top)
            total = jnp.sum(powers, axis=0, keepdims=True)
            raw = times(values_t[side * half : (side + 1) * half], powers.astype(jnp.bfloat16))
            mixed.append(raw / total)
            log_ref[0, side : side + 1, start : start + STRIP] = top + jnp.log(total)
        both = jnp.concatenate(mixed, axis=0)
        out_ref[start : start + STRIP, :] = jnp.transpose(both).astype(jnp.bfloat16)
        turned_ref[:, start : start + STRIP] = both.astype(jnp.bfloat16)


def attend(queries, keys, values, band, edges):
    length, width = queries.shape
    heads = edges.shape[0]
    pairs = heads // 2
    columns = width // pairs
    part = pl.BlockSpec((length, columns), lambda pair: (0, pair))
    return pl.pallas_call(
        attend_kernel,
        grid=(pairs,),
        in_specs=[
            pl.BlockSpec(memory_space=pltpu.SMEM),
            part,
            part,
            part,
            pl.BlockSpec((2, 3 * TILE, TILE), lambda pair: (pair, 0, 0)),
        ],
        out_specs=[
            part,
            pl.BlockSpec((columns, length), lambda pair: (pair, 0)),
            pl.BlockSpec((1, 2, length), lambda pair: (pair, 0, 0)),
        ],
        out_shape=[
            jax.ShapeDtypeStruct((length, width), jnp.bfloat16),
            jax.ShapeDtypeStruct((width, length), jnp.bfloat16),
            jax.ShapeDtypeStruct((pairs, 2, length), jnp.float32),
        ],
        scratch_shapes=[pltpu.VMEM((2, 2 * length - TILE, TILE), jnp.float32)],
        compiler_params=pltpu.CompilerParams(vmem_limit_bytes=VMEM_CAP),
        cost_estimate=pl.CostEstimate(
            flops=4 * heads * length * length * (width // heads),
            bytes_accessed=8 * length * width,
            transcendentals=heads * length * length,
        ),
        name="attend",
    )(edges, queries, keys, values, band)


def weights_kernel(
    edge_ref, q_ref, k_ref, log_ref, band_ref, normed_ref, weights_ref, turned_ref, wide
):
    length = q_ref.shape[0]
    scale = (q_ref.shape[1] // 2) ** (-0.5)
    head = 2 * pl.program_id(0)
    for side in range(2):
        turned = [
            jnp.transpose(band_ref[side, part : part + TILE, :]) for part in range(0, 3 * TILE, TILE)
        ]
        wide[side, :, : length - 2 * TILE] = jnp.full(
            (TILE, length - 2 * TILE), edge_ref[head + side, 0], jnp.float32
        )
        wide[side, :, length - 2 * TILE : length + TILE] = jnp.concatenate(turned, axis=1)
        wide[side, :, length + TILE :] = jnp.full(
            (TILE, length - 2 * TILE), edge_ref[head + side, 1], jnp.float32
        )
    keys = k_ref[...]
    turned_ref[...] = jnp.transpose(normed_ref[...])
    for start in range(0, length, STRIP):
        strip = slice(start, start + STRIP)
        for side in range(2):
            query = half_of(q_ref[strip, :] * scale, side)
            bias = jnp.concatenate(
                [
                    wide[side, :, length - TILE - first : 2 * length - TILE - first]
                    for first in range(start, start + STRIP, TILE)
                ],
                axis=0,
            )
            logs = jnp.transpose(
                jnp.broadcast_to(log_ref[0, side : side + 1, strip], (TILE, STRIP))
            )[:, :1]
            scores = times_transposed(query, keys) + bias
            weights_ref[side, strip, :] = jnp.exp(scores - logs).astype(jnp.bfloat16)


def attend_weights(queries, keys, logs, band, edges, normed):
    length, width = queries.shape
    heads = edges.shape[0]
    pairs = heads // 2
    columns = width // pairs
    part = pl.BlockSpec((length, columns), lambda pair: (0, pair))
    return pl.pallas_call(
        weights_kernel,
        grid=(pairs,),
        in_specs=[
            pl.BlockSpec(memory_space=pltpu.SMEM),
            part,
            part,
            pl.BlockSpec((1, 2, length), lambda pair: (pair, 0, 0)),
            pl.BlockSpec((2, 3 * TILE, TILE), lambda pair: (pair, 0, 0)),
            part,
        ],
        out_specs=[
            pl.BlockSpec((2, length, length), lambda pair: (pair, 0, 0)),
            pl.BlockSpec((columns, length), lambda pair: (pair, 0)),
        ],
        out_shape=[
            jax.ShapeDtypeStruct((heads, length, length), jnp.bfloat16),
            jax.ShapeDtypeStruct((width, length), jnp.bfloat16),
        ],
        scratch_shapes=[pltpu.VMEM((2, TILE, 2 * length - TILE), jnp.float32)],
        compiler_params=pltpu.CompilerParams(vmem_limit_bytes=VMEM_CAP),
        cost_estimate=pl.CostEstimate(
            flops=2 * heads * length * length * (width // heads),
            bytes_accessed=4 * length * width + 2 * heads * length * length,
            transcendentals=heads * length * length,
        ),
        name="attend_weights",
    )(edges, queries, keys, logs, band, normed)


def diagonal_sums(near_ref, side, beyond):
    span = 4 * TILE
    zeros = jnp.zeros((8, span - TILE), jnp.float32)
    total = jnp.zeros((8, span), jnp.float32)
    for block in range(3):
        for row in range(0, TILE, 8):
            first = block * TILE + row
            wide = jnp.concatenate([near_ref[side, first : first + 8, :], zeros], axis=1)
            total = total + pltpu.roll(wide, (block + 1) * TILE - 1 - row, 1)
    rows = lax.broadcasted_iota(jnp.int32, total.shape, 0)
    for bit in (1, 2, 4):
        total = jnp.where((rows & bit) != 0, pltpu.roll(total, span - bit, 1), total)
    sums = jnp.sum(total, axis=0, keepdims=True)
    lanes = lax.broadcasted_iota(jnp.int32, sums.shape, 1)
    sums = sums + jnp.where(lanes == 0, beyond[0], 0.0)
    return sums + jnp.where(lanes == span - 2, beyond[1], 0.0)


def attend_back_kernel(
    core_ref, q_ref, k_ref, v_ref, grad_ref, out_ref, weights_ref, normed_ref,
    grads_ref, away_ref, kept_ref, sums_ref,
    near_ref, query_total, square,
):
    length = q_ref.shape[0]
    columns = q_ref.shape[1]
    half = columns // 2
    blocks = length // TILE
    scale = half ** (-0.5)
    names = lax.broadcasted_iota(jnp.int32, (2 * blocks, length), 0)
    owners = lax.broadcasted_iota(jnp.int32, (2 * blocks, length), 1) // TILE
    picks = (names == owners).astype(jnp.float32).astype(jnp.bfloat16)
    queries_t = jnp.transpose(q_ref[...] * scale)
    grads_t = jnp.transpose(grad_ref[...])
    near_ref[...] = jnp.zeros_like(near_ref)
    key_parts, value_parts = [], []
    for side in range(2):
        rows = slice(side * half, (side + 1) * half)
        grad = half_of(grad_ref[...], side)
        keys = half_of(k_ref[...], side)
        center = jnp.sum(
            grad.astype(jnp.float32) * out_ref[...].astype(jnp.float32), axis=1, keepdims=True
        )
        left = jnp.concatenate([queries_t[rows], picks], axis=0)
        key_total, value_total = None, None
        for start in range(0, length, BACK_STRIP):
            strip = slice(start, start + BACK_STRIP)
            weights = weights_ref[side, strip, :]
            weight_grad = times_transposed(grad[strip], v_ref[...])
            score_grad = weights.astype(jnp.float32) * (weight_grad - center[strip])
            score_low = score_grad.astype(jnp.bfloat16)
            value_term = times(grads_t[rows, strip], weights)
            value_total = value_term if value_total is None else value_total + value_term
            key_term = times(left[:, strip], score_low)
            key_total = key_term if key_total is None else key_total + key_term
            query_term = times(score_low, keys)
            if side == 0:
                query_total[strip, :] = query_term
            else:
                query_total[strip, :] += query_term
            for row in range(0, BACK_STRIP, TILE):
                for lane in range(0, length, TILE):
                    apart = (lane - start - row) // TILE
                    if abs(apart) <= 1:
                        spot = (apart + 1) * TILE
                        near_ref[side, spot : spot + TILE, :] += score_grad[
                            row : row + TILE, lane : lane + TILE
                        ]
        key_parts.append(key_total[:half])
        value_parts.append(value_total)
        sums = key_total[half:]
        beyond = [
            jnp.sum(jnp.where(keep, sums, 0.0), keepdims=True)
            for keep in (names >= owners + 2, (names <= owners - 2) & (names < blocks))
        ]
        sums_ref[0, side : side + 1, :] = diagonal_sums(near_ref, side, beyond)
    grads_ref[0] = (query_total[...] * scale).astype(jnp.bfloat16)
    grads_ref[1] = jnp.transpose(jnp.concatenate(key_parts, axis=0)).astype(jnp.bfloat16)
    grads_ref[2] = jnp.transpose(jnp.concatenate(value_parts, axis=0)).astype(jnp.bfloat16)
    part = normed_ref.shape[0] // 2
    stacked = jnp.concatenate([grads_ref[index] for index in range(3)], axis=1)
    square[...] = times(normed_ref[...], stacked)
    away = pl.ds(pl.multiple_of((1 - core_ref[0]) * part, 16), part)
    kept = pl.ds(pl.multiple_of(core_ref[0] * part, 16), part)
    for index in range(3):
        span = slice(index * columns, (index + 1) * columns)
        away_ref[index] = square[away, span].astype(jnp.bfloat16)
        kept_ref[index] = square[kept, span].astype(jnp.bfloat16)


def attend_back(core, queries, keys, values, grads, attended, weights, normed_t):
    length, width = queries.shape
    heads = weights.shape[0]
    pairs = heads // 2
    columns = width // pairs
    part = pl.BlockSpec((length, columns), lambda pair: (0, pair))
    square = pl.BlockSpec((3, width // 2, columns), lambda pair: (0, 0, pair))
    return pl.pallas_call(
        attend_back_kernel,
        grid=(pairs,),
        in_specs=[
            pl.BlockSpec(memory_space=pltpu.SMEM),
            part, part, part, part, part,
            pl.BlockSpec((2, length, length), lambda pair: (pair, 0, 0)),
            pl.BlockSpec((width, length), lambda pair: (0, 0)),
        ],
        out_specs=[
            pl.BlockSpec((3, length, columns), lambda pair: (0, 0, pair)),
            square, square,
            pl.BlockSpec((1, 2, 4 * TILE), lambda pair: (pair, 0, 0)),
        ],
        out_shape=[
            jax.ShapeDtypeStruct((3, length, width), jnp.bfloat16),
            jax.ShapeDtypeStruct((3, width // 2, width), jnp.bfloat16),
            jax.ShapeDtypeStruct((3, width // 2, width), jnp.bfloat16),
            jax.ShapeDtypeStruct((pairs, 2, 4 * TILE), jnp.float32),
        ],
        scratch_shapes=[
            pltpu.VMEM((2, 3 * TILE, TILE), jnp.float32),
            pltpu.VMEM((length, columns), jnp.float32),
            pltpu.VMEM((width, 3 * columns), jnp.float32),
        ],
        compiler_params=pltpu.CompilerParams(vmem_limit_bytes=VMEM_CAP),
        cost_estimate=pl.CostEstimate(
            flops=10 * heads * length * length * (width // heads),
            bytes_accessed=16 * length * width + 2 * heads * length * length,
            transcendentals=0,
        ),
        name="attend_back",
    )(core, queries, keys, values, grads, attended, weights, normed_t)


def bias_band(rel_table):
    buckets, heads = rel_table.shape
    labels = band_buckets().reshape(1, -1)
    onehot = (labels == jnp.arange(buckets, dtype=jnp.int32)[:, None]).astype(jnp.bfloat16)
    band = lax.dot_general(
        rel_table, onehot, (((0,), (0,)), ((), ())), preferred_element_type=jnp.float32
    )
    half = buckets // 2
    edges = jnp.stack([rel_table[half - 1], rel_table[buckets - 1]], axis=1).astype(jnp.float32)
    return band.reshape(heads, 3 * TILE, TILE), edges


normal_tail = (
    0.14372023791716726,
    0.14167152280803838,
    0.14027055919455333,
    0.02504245305870889,
    0.1831401332067321,
    -0.1813703123183242,
    0.04752538660588183,
)
tail_pole = 0.36
normal_height = 0.3989422804014327


def gelu_and_slope(values):
    density = jnp.exp(values * values * -0.5)
    inverse = 1.0 / (1.0 + tail_pole * jnp.abs(values))
    series = jnp.full_like(values, normal_tail[-1])
    for coefficient in normal_tail[-2::-1]:
        series = series * inverse + coefficient
    tail = series * inverse * density
    below = jnp.where(values > 0, 1.0 - tail, tail)
    return values * below, below + values * (density * normal_height)


def send_kernel(
    capacity_ref, route_ref, rows_ref, sent_ref, place_ref, spots_ref, scratch, *, experts, slots, chunks
):
    tokens = route_ref.shape[1]
    block = sent_ref.shape[0]
    step = pl.program_id(0)

    @pl.when(step == 0)
    def _():
        route = route_ref[...]
        names = lax.broadcasted_iota(jnp.int32, (experts, tokens), 0)
        chosen = (names == route).astype(jnp.float32)
        early = lax.broadcasted_iota(jnp.int32, (tokens, tokens), 0)
        late = lax.broadcasted_iota(jnp.int32, (tokens, tokens), 1)
        before = (early < late).astype(jnp.float32).astype(jnp.bfloat16)
        earlier = times(chosen.astype(jnp.bfloat16), before)
        slot = jnp.sum(earlier * chosen, axis=0, keepdims=True).astype(jnp.int32)
        kept = slot < capacity_ref[0]
        share = slots // chunks
        chunk = jnp.zeros_like(slot)
        for later in range(1, chunks):
            chunk = chunk + (slot >= later * share).astype(jnp.int32)
        place = chunk * (experts * share) + route * share + (slot - chunk * share)
        place = jnp.where(kept, place, -1)
        ordered = jnp.where(kept, route * slots + slot, -1)
        scratch[...] = ordered
        place_ref[...] = place
        half = spots_ref.shape[1] // 2
        both = jnp.concatenate(
            [jnp.broadcast_to(place, (half, tokens)), jnp.broadcast_to(ordered, (half, tokens))], axis=0
        )
        spots_ref[...] = jnp.transpose(both)

    places = step * block + lax.broadcasted_iota(jnp.int32, (block, tokens), 0)
    onehot = (places == scratch[...]).astype(jnp.float32).astype(jnp.bfloat16)
    sent_ref[...] = times(onehot, rows_ref[...]).astype(jnp.bfloat16)


def send_first(capacity, route_row, rows, experts, slots, chunks):
    tokens, width = rows.shape
    total = experts * slots
    block = 1024
    return pl.pallas_call(
        functools.partial(send_kernel, experts=experts, slots=slots, chunks=chunks),
        grid=(total // block,),
        in_specs=[
            pl.BlockSpec(memory_space=pltpu.SMEM),
            pl.BlockSpec((1, tokens), lambda step: (0, 0)),
            pl.BlockSpec((tokens, width), lambda step: (0, 0)),
        ],
        out_specs=[
            pl.BlockSpec((block, width), lambda step: (step, 0)),
            pl.BlockSpec((1, tokens), lambda step: (0, 0)),
            pl.BlockSpec((tokens, TILE), lambda step: (0, 0)),
        ],
        out_shape=[
            jax.ShapeDtypeStruct((total, width), jnp.bfloat16),
            jax.ShapeDtypeStruct((1, tokens), jnp.int32),
            jax.ShapeDtypeStruct((tokens, TILE), jnp.int32),
        ],
        scratch_shapes=[pltpu.VMEM((1, tokens), jnp.int32)],
        compiler_params=pltpu.CompilerParams(vmem_limit_bytes=VMEM_CAP),
        name="route_and_send",
    )(capacity, route_row, rows)


def send_again_kernel(place_ref, rows_ref, sent_ref, *, first):
    block = sent_ref.shape[0]
    tokens = rows_ref.shape[0]
    start = first + pl.program_id(0) * block
    places = start + lax.broadcasted_iota(jnp.int32, (block, tokens), 0)
    onehot = (places == place_ref[...]).astype(jnp.float32).astype(jnp.bfloat16)
    sent_ref[...] = times(onehot, rows_ref[...]).astype(jnp.bfloat16)


def send_again(place, rows, first, count):
    tokens, width = rows.shape
    block = 512
    return pl.pallas_call(
        functools.partial(send_again_kernel, first=first),
        grid=(count // block,),
        in_specs=[
            pl.BlockSpec((1, tokens), lambda step: (0, 0)),
            pl.BlockSpec((tokens, width), lambda step: (0, 0)),
        ],
        out_specs=pl.BlockSpec((block, width), lambda step: (step, 0)),
        out_shape=jax.ShapeDtypeStruct((count, width), jnp.bfloat16),
        compiler_params=pltpu.CompilerParams(vmem_limit_bytes=VMEM_CAP),
        cost_estimate=pl.CostEstimate(
            flops=2 * count * tokens * width,
            bytes_accessed=2 * (count + tokens) * width,
            transcendentals=0,
        ),
        name="send_rows",
    )(place, rows)


def expert_kernel(
    own_ref, rows_ref, ups_ref, up_ref, down_ref, router_ref, *rest, experts, piece
):
    (
        input_grad_ref, router_grad_ref, produced_ref, activated_ref, pre_grad_ref, slot_grad_ref,
        kept_ref,
    ) = rest[-7:]
    rows = rows_ref[...]
    ups = ups_ref[...].astype(jnp.float32).reshape(rows.shape)
    low_ups = ups.astype(jnp.bfloat16)
    router = router_ref[...]
    hidden = up_ref.shape[1]
    logits = times(rows, router)
    lanes = lax.broadcasted_iota(jnp.int32, logits.shape, 1)
    logits = jnp.where(lanes < experts, logits, -jnp.inf)
    powers = jnp.exp(logits - jnp.max(logits, axis=1, keepdims=True))
    chances = powers / jnp.sum(powers, axis=1, keepdims=True)
    mine = (lanes == own_ref[0]).astype(jnp.float32)
    gate = jnp.sum(chances * mine, axis=1, keepdims=True)
    gate_grad = jnp.zeros_like(gate)
    input_grad = jnp.zeros(rows.shape, jnp.float32)
    produced = jnp.zeros(rows.shape, jnp.float32)
    for first in range(0, hidden, piece):
        span = slice(first, first + piece)
        up = up_ref[:, span]
        down = down_ref[span, :]
        activated, slope = gelu_and_slope(times(rows, up))
        activated = activated.astype(jnp.bfloat16)
        back = times_transposed(low_ups, down)
        gate_grad = gate_grad + jnp.sum(
            activated.astype(jnp.float32) * back, axis=1, keepdims=True
        )
        pre_grad = (back * gate * slope).astype(jnp.bfloat16)
        activated_ref[0, :, span] = activated
        pre_grad_ref[0, :, span] = pre_grad
        input_grad = input_grad + times_transposed(pre_grad, up)
        produced = produced + times(activated, down)
    logit_grad = gate_grad * gate * (mine - chances)
    low_logit = logit_grad.astype(jnp.bfloat16)
    input_grad_ref[...] = (input_grad + times_transposed(low_logit, router)).astype(jnp.bfloat16)
    produced_ref[...] = (produced * gate).reshape(produced_ref.shape).astype(jnp.bfloat16)
    slot_grad_ref[0] = (ups * gate).astype(jnp.bfloat16)
    kept_ref[0] = rows

    @pl.when(pl.program_id(0) == 0)
    def _():
        router_grad_ref[...] = jnp.zeros_like(router_grad_ref)

    router_grad_ref[...] += times(jnp.transpose(logit_grad).astype(jnp.bfloat16), rows)


def expert_pass(own, rows, ups, up, down, router, experts, chunk, before):
    count, width = rows.shape
    groups, chunks, half = ups.shape[:3]
    hidden = up.shape[1]
    block = 256
    lanes = router.shape[1]
    row_spec = pl.BlockSpec((block, width), lambda step: (step, 0))
    whole = lambda shape: pl.BlockSpec(shape, lambda step: (0, 0))
    kept = lambda columns: pl.BlockSpec((1, block, columns), lambda step: (chunk, step, 0))
    stacked = lambda columns: jax.ShapeDtypeStruct((chunks, count, columns), jnp.bfloat16)
    slot_spec = pl.BlockSpec((block // half, 1, half, width), lambda step: (step, chunk, 0, 0))
    widths = (hidden, hidden, width, width)
    return pl.pallas_call(
        functools.partial(expert_kernel, experts=experts, piece=1024),
        grid=(count // block,),
        in_specs=[
            pl.BlockSpec(memory_space=pltpu.SMEM),
            row_spec, slot_spec,
            whole(up.shape), whole(down.shape), whole(router.shape),
        ] + [pl.BlockSpec(memory_space=pl.ANY)] * len(before),
        out_specs=[row_spec, whole((lanes, width)), slot_spec]
        + [kept(columns) for columns in widths],
        out_shape=[
            jax.ShapeDtypeStruct((count, width), jnp.bfloat16),
            jax.ShapeDtypeStruct((lanes, width), jnp.float32),
            jax.ShapeDtypeStruct((groups, chunks, half, width), jnp.bfloat16),
        ] + [stacked(columns) for columns in widths],
        input_output_aliases={6 + index: 2 + index for index in range(len(before))},
        compiler_params=pltpu.CompilerParams(vmem_limit_bytes=VMEM_CAP),
        cost_estimate=pl.CostEstimate(
            flops=8 * count * width * hidden,
            bytes_accessed=4 * width * hidden + 4 * count * hidden + 12 * count * width,
            transcendentals=2 * count * hidden,
        ),
        name="experts",
    )(own, rows, ups, up, down, router, *before)


def spread_rows(spots_ref, part_ref, first):
    target = spots_ref[:, :1]
    count = part_ref.shape[0]
    places = first + lax.broadcasted_iota(jnp.int32, (target.shape[0], count), 1)
    onehot = (places == target).astype(jnp.float32).astype(jnp.bfloat16)
    return times(onehot, part_ref[...])


def fetch_first_kernel(spots_ref, part_ref, out_ref):
    out_ref[...] = spread_rows(spots_ref, part_ref, 0).astype(jnp.bfloat16)


def fetch_first(spots, part):
    tokens = spots.shape[0]
    count, width = part.shape
    block = 256
    return pl.pallas_call(
        fetch_first_kernel,
        grid=(tokens // block,),
        in_specs=[
            pl.BlockSpec((block, TILE), lambda step: (step, 0)),
            pl.BlockSpec((count, width), lambda step: (0, 0)),
        ],
        out_specs=pl.BlockSpec((block, width), lambda step: (step, 0)),
        out_shape=jax.ShapeDtypeStruct((tokens, width), jnp.bfloat16),
        compiler_params=pltpu.CompilerParams(vmem_limit_bytes=64 * 1024 * 1024),
        cost_estimate=pl.CostEstimate(
            flops=2 * count * tokens * width,
            bytes_accessed=4 * tokens * width,
            transcendentals=0,
        ),
        name="fetch_first",
    )(spots, part)


def fetch_kernel(
    spots_ref, early_ref, second_ref, residual_ref, gain_ref, upstream_ref, output_ref,
    out_grad_ref, attended_grad_ref, gain_grad_ref,
):
    total = early_ref[...].astype(jnp.float32) + spread_rows(spots_ref, second_ref, second_ref.shape[0])
    residual = residual_ref[...]
    inverse = lax.rsqrt(jnp.mean(residual * residual, axis=1, keepdims=True) + eps_norm)
    scaled = residual * inverse

    @pl.when(pl.program_id(0) == 0)
    def _():
        gain_grad_ref[...] = jnp.zeros_like(gain_grad_ref)

    gain_grad_ref[...] += jnp.sum((total * scaled).reshape(-1, 8, total.shape[1]), axis=0)
    weighted = total * gain_ref[...]
    spread = jnp.mean(weighted * scaled, axis=1, keepdims=True)
    residual_grad = upstream_ref[...].astype(jnp.float32) + inverse * (weighted - scaled * spread)
    low = residual_grad.astype(jnp.bfloat16)
    out_grad_ref[...] = low
    attended_grad_ref[...] = times_transposed(low, output_ref[...]).astype(jnp.bfloat16)


def fetch_grads(spots, early, second, residual, gain_row, upstream, w_output):
    tokens, width = residual.shape
    block = 512
    row_spec = pl.BlockSpec((block, width), lambda step: (step, 0))
    whole = lambda shape: pl.BlockSpec(shape, lambda step: (0, 0))
    return pl.pallas_call(
        fetch_kernel,
        grid=(tokens // block,),
        in_specs=[
            pl.BlockSpec((block, TILE), lambda step: (step, 0)),
            row_spec, whole(second.shape),
            row_spec, whole(gain_row.shape), row_spec, whole(w_output.shape),
        ],
        out_specs=[row_spec, row_spec, whole((8, width))],
        out_shape=[
            jax.ShapeDtypeStruct((tokens, width), jnp.bfloat16),
            jax.ShapeDtypeStruct((tokens, width), jnp.bfloat16),
            jax.ShapeDtypeStruct((8, width), jnp.float32),
        ],
        compiler_params=pltpu.CompilerParams(vmem_limit_bytes=64 * 1024 * 1024),
        name="fetch_grads",
    )(spots, early, second, residual, gain_row, upstream, w_output)


def combine_kernel(spots_ref, parts_ref, residual_ref, out_ref):
    column = spots_ref.shape[1] // 2
    target = spots_ref[:, column : column + 1]
    count = parts_ref.shape[0]
    places = lax.broadcasted_iota(jnp.int32, (target.shape[0], count), 1)
    onehot = (places == target).astype(jnp.float32).astype(jnp.bfloat16)
    out_ref[...] = (residual_ref[...] + times(onehot, parts_ref[...])).astype(jnp.bfloat16)


def combine(spots, parts, residual):
    tokens, width = residual.shape
    block = 512
    row_spec = pl.BlockSpec((block, width), lambda step: (step, 0))
    return pl.pallas_call(
        combine_kernel,
        grid=(tokens // block,),
        in_specs=[
            pl.BlockSpec((block, TILE), lambda step: (step, 0)),
            pl.BlockSpec(parts.shape, lambda step: (0, 0)),
            row_spec,
        ],
        out_specs=row_spec,
        out_shape=jax.ShapeDtypeStruct((tokens, width), jnp.bfloat16),
        compiler_params=pltpu.CompilerParams(vmem_limit_bytes=VMEM_CAP),
        name="combine",
    )(spots, parts, residual)


def swap_groups(axis, size, shift, count):
    return [
        [(index, index ^ (step << shift)) for index in range(size)] for step in range(1, count)
    ]


def sum_stages(axis_sizes):
    stages = []
    for axis, size in axis_sizes:
        shift = 0
        while (1 << shift) < size:
            count = min(4, size >> shift)
            place = (lax.axis_index(axis) >> shift) & (count - 1)
            stages.append((axis, place, swap_groups(axis, size, shift, count)))
            shift += count.bit_length() - 1
    return stages


def weight_kernel(core_ref, left_ref, right_ref, away_ref, kept_ref, square):
    square[...] = times(left_ref[...], right_ref[...])
    part = away_ref.shape[0]
    away = pl.ds(pl.multiple_of((1 - core_ref[0]) * part, 16), part)
    kept = pl.ds(pl.multiple_of(core_ref[0] * part, 16), part)
    away_ref[...] = square[away, :].astype(jnp.bfloat16)
    kept_ref[...] = square[kept, :].astype(jnp.bfloat16)


def weight_terms(core, left_t, right):
    width = left_t.shape[0]
    vmem = pl.BlockSpec(memory_space=pltpu.VMEM)
    half = jax.ShapeDtypeStruct((width // 2, right.shape[1]), jnp.bfloat16)
    return pl.pallas_call(
        weight_kernel,
        in_specs=[pl.BlockSpec(memory_space=pltpu.SMEM), vmem, vmem],
        out_specs=[vmem, vmem],
        out_shape=[half, half],
        scratch_shapes=[pltpu.VMEM((width, right.shape[1]), jnp.float32)],
        compiler_params=pltpu.CompilerParams(vmem_limit_bytes=24 * 1024 * 1024),
        cost_estimate=pl.CostEstimate(
            flops=2 * width * left_t.shape[1] * right.shape[1],
            bytes_accessed=2 * (width + right.shape[1]) * left_t.shape[1],
            transcendentals=0,
        ),
        name="weight_terms",
    )(core, left_t, right)


def cut_pieces(place, source, own_ref, sent_refs):
    rows = own_ref.shape[0]
    for step, ref in enumerate((own_ref, *sent_refs)):
        first = pl.multiple_of((place ^ step) * rows, 16)
        ref[...] = source[pl.ds(first, rows), :].astype(ref.dtype)


def padded_rows(rows, count):
    return -(-rows // (16 * count)) * 16 * count


def piece_shapes(rows, width, count):
    own = jax.ShapeDtypeStruct((rows // count, width), jnp.bfloat16)
    sent = jax.ShapeDtypeStruct((rows // count, width), jnp.bfloat16)
    return [own] + [sent] * (count - 1)


def first_pieces_kernel(
    place_ref, kept_ref, got_ref, kept_out, got_out, gain_ref, router_one, router_two, sums_ref,
    *rest, experts, counts,
):
    outs, outs_two, (small, sums) = rest[: counts[0]], rest[counts[0] : sum(counts)], rest[sum(counts) :]
    small[...] = jnp.zeros_like(small)
    sums[...] = jnp.zeros_like(sums)
    for pair in range(sums_ref.shape[0]):
        sums[2 * pair : 2 * pair + 2, :] = sums_ref[pair]
    small[:8, :] = gain_ref[...]
    small[8 : 8 + experts, :] = router_one[:experts] + router_two[:experts]
    lanes = lax.broadcasted_iota(jnp.int32, (TILE, sums.shape[1]), 1)
    names = lax.broadcasted_iota(jnp.int32, (TILE, sums.shape[1]), 0)
    onehot = (bucket_of(lanes - (2 * TILE - 1)) == names).astype(jnp.float32)
    small[8 + experts : 8 + experts + sums.shape[0], :TILE] = lax.dot_general(
        sums[...], onehot, (((1,), (1,)), ((), ())),
        precision=lax.Precision.HIGHEST, preferred_element_type=jnp.float32,
    )
    matrices, part = kept_ref.shape[:2]
    share = part // len(outs)
    extra = small.shape[0] // len(outs)
    for step, ref in enumerate(outs):
        place = place_ref[0] ^ step
        rows = pl.ds(pl.multiple_of(place * share, 16), share)
        for index in range(matrices):
            ref[index * share : (index + 1) * share, :] = (
                kept_ref[index, rows, :].astype(jnp.float32)
                + got_ref[index, rows, :].astype(jnp.float32)
            ).astype(ref.dtype)
        rows = pl.ds(pl.multiple_of(place * extra, 16), extra)
        ref[matrices * share :, :] = small[rows, :].astype(ref.dtype)
    share = part // len(outs_two)
    for step, ref in enumerate(outs_two):
        rows = pl.ds(pl.multiple_of((place_ref[1] ^ step) * share, 16), share)
        ref[...] = (
            kept_out[rows, :].astype(jnp.float32) + got_out[rows, :].astype(jnp.float32)
        ).astype(ref.dtype)


def first_pieces(
    places, kept, got, kept_out, got_out, gain_terms, router_terms, sums, experts, counts
):
    matrices, part, width = kept.shape
    sum_rows = -(-2 * sums.shape[0] // 8) * 8
    extra = padded_rows(8 + experts + sum_rows, counts[0])
    vmem = pl.BlockSpec(memory_space=pltpu.VMEM)
    shapes = piece_shapes(matrices * part + extra, width, counts[0])
    shapes += piece_shapes(part, width, counts[1])
    outs = pl.pallas_call(
        functools.partial(first_pieces_kernel, experts=experts, counts=counts),
        grid=(1,),
        in_specs=[pl.BlockSpec(memory_space=pltpu.SMEM)]
        + [vmem] * 5
        + [pl.BlockSpec((experts, width), lambda step: (0, 0))] * 2
        + [vmem],
        out_specs=[vmem] * len(shapes),
        out_shape=shapes,
        scratch_shapes=[
            pltpu.VMEM((extra, width), jnp.float32),
            pltpu.VMEM((sum_rows, sums.shape[2]), jnp.float32),
        ],
        compiler_params=pltpu.CompilerParams(vmem_limit_bytes=64 * 1024 * 1024),
        name="first_pieces",
    )(places, kept, got, kept_out, got_out, gain_terms, *router_terms, sums)
    return outs[: counts[0]], outs[counts[0] :]


def next_pieces_kernel(place_ref, *rest, received, counts):
    operands, rest = rest[: sum(received) + len(received)], rest[sum(received) + len(received) :]
    outs, sources = rest[: sum(counts)], rest[sum(counts) :]
    for chain, (count, made) in enumerate(zip(received, counts)):
        parts, operands = operands[: count + 1], operands[count + 1 :]
        cuts, outs = outs[:made], outs[made:]
        total = parts[0][...].astype(jnp.float32)
        for ref in parts[1:]:
            total = total + ref[...].astype(jnp.float32)
        rows = total.shape[0]
        source = sources[chain]
        source[:rows, :] = total
        if source.shape[0] > rows:
            source[rows:, :] = jnp.zeros((source.shape[0] - rows, total.shape[1]), jnp.float32)
        cut_pieces(place_ref[chain], source, cuts[0], cuts[1:])


def next_pieces(places, chains, counts):
    width = chains[0][0].shape[1]
    vmem = pl.BlockSpec(memory_space=pltpu.VMEM)
    shapes, scratch = [], []
    for (own, _), count in zip(chains, counts):
        rows = own.shape[0]
        padded = padded_rows(rows, count)
        scratch.append(pltpu.VMEM((padded, width), jnp.float32))
        if count == 1:
            shapes.append(jax.ShapeDtypeStruct((rows, width), jnp.bfloat16))
        else:
            shapes += piece_shapes(padded, width, count)
    operands = [array for own, got in chains for array in (own, *got)]
    outs = pl.pallas_call(
        functools.partial(
            next_pieces_kernel, received=tuple(len(got) for _, got in chains), counts=tuple(counts)
        ),
        in_specs=[pl.BlockSpec(memory_space=pltpu.SMEM)] + [vmem] * len(operands),
        out_specs=[vmem] * len(shapes),
        out_shape=shapes,
        scratch_shapes=scratch,
        compiler_params=pltpu.CompilerParams(vmem_limit_bytes=20 * 1024 * 1024),
        name="next_pieces",
    )(places, *operands)
    return outs[: counts[0]], outs[counts[0] :]


def join_kernel(place_ref, *rest, counts):
    pieces, rest = rest[: sum(counts)], rest[sum(counts) :]
    outs, joined = rest[: len(counts)], rest[len(counts) :]
    for chain, count in enumerate(counts):
        parts, pieces = pieces[:count], pieces[count:]
        rows = parts[0].shape[0]
        for step, ref in enumerate(parts):
            first = pl.multiple_of((place_ref[chain] ^ step) * rows, 16)
            joined[chain][pl.ds(first, rows), :] = ref[...]
        outs[chain][...] = joined[chain][: outs[chain].shape[0], :]


def join_pieces(places, chains, kept):
    width = chains[0][0].shape[1]
    vmem = pl.BlockSpec(memory_space=pltpu.VMEM)
    operands = [piece for pieces in chains for piece in pieces]
    return pl.pallas_call(
        functools.partial(join_kernel, counts=tuple(len(pieces) for pieces in chains)),
        in_specs=[pl.BlockSpec(memory_space=pltpu.SMEM)] + [vmem] * len(operands),
        out_specs=[vmem] * len(chains),
        out_shape=[jax.ShapeDtypeStruct((rows, width), jnp.bfloat16) for rows in kept],
        scratch_shapes=[
            pltpu.VMEM((len(pieces) * pieces[0].shape[0], width), jnp.bfloat16) for pieces in chains
        ],
        compiler_params=pltpu.CompilerParams(vmem_limit_bytes=20 * 1024 * 1024),
        name="join_pieces",
    )(places, *operands)


def finish_kernel(place_ref, *rest, counts, table):
    ones, twos = rest[: 2 * counts[0]], rest[2 * counts[0] : 2 * sum(counts)]
    rest = rest[2 * sum(counts) :]
    weight_refs, gain_ref, rest = rest[:3], rest[3], rest[4:]
    square_outs, (gain_out, second_out, router_out, table_out), rest = rest[:4], rest[4:8], rest[8:]
    weights, squares, columns, small, load_sems, store_sems = rest
    core = place_ref[0]
    width = weights.shape[2]
    part = width // 2
    share = part // counts[0]
    loads = [
        pltpu.make_async_copy(ref, weights.at[index], load_sems.at[index])
        for index, ref in enumerate(weight_refs)
    ]
    for load in loads:
        load.start()

    def spots(place, count, rows):
        found = []
        for step in range(count):
            for other in range(2):
                half = 1 - core if other else core
                first = half * part + (place ^ step) * rows
                found.append(pl.ds(pl.multiple_of(first, 16), rows))
        return found

    stores = []
    for index in (3, 0, 1, 2):
        if index == 3:
            rows_two = part // counts[1]
            for ref, rows in zip(twos, spots(place_ref[2], counts[1], rows_two)):
                squares[index, rows, :] = ref[:rows_two, :].astype(jnp.float32)
        else:
            loads[index].wait()
            for ref, rows in zip(ones, spots(place_ref[1], counts[0], share)):
                total = ref[index * share : (index + 1) * share, :].astype(jnp.float32)
                squares[index, rows, :] = total
                term = jnp.sum(
                    total * weights[index, rows, :].astype(jnp.float32), axis=1, keepdims=True
                )
                if index == 0:
                    columns[rows, :] = jnp.broadcast_to(term, (share, TILE))
                else:
                    columns[rows, :] += jnp.broadcast_to(term, (share, TILE))
        store = pltpu.make_async_copy(squares.at[index], square_outs[index], store_sems.at[index])
        store.start()
        stores.append(store)
    gain = jnp.transpose(columns[...])[:1] / gain_ref[...]
    gain_out[...] = gain.reshape(width)
    extra = small.shape[0] // counts[0]
    for step in range(counts[0]):
        rows = pl.ds(pl.multiple_of((place_ref[1] ^ step) * extra, 16), extra)
        small[rows, :] = ones[2 * step][3 * share :, :].astype(jnp.float32) + ones[2 * step + 1][
            3 * share :, :
        ].astype(jnp.float32)
    experts = router_out.shape[0]
    buckets, heads = table
    second_out[...] = jnp.sum(small[:8, :], axis=0, keepdims=True).reshape(width)
    router_out[...] = small[8 : 8 + experts, :]
    table_out[...] = small[8 + experts : 8 + experts + heads, :buckets]
    for store in stores:
        store.wait()


def finish(places, chains, weights, gain_row, experts, table):
    width = weights[0].shape[1]
    counts = tuple(len(pieces) // 2 for pieces in chains)
    square = jax.ShapeDtypeStruct((width, width), jnp.float32)
    row = jax.ShapeDtypeStruct((width,), jnp.float32)
    vmem = pl.BlockSpec(memory_space=pltpu.VMEM)
    extra = chains[0][0].shape[0] - 3 * (width // 2 // counts[0])
    pieces = [piece for chain in chains for piece in chain]
    return pl.pallas_call(
        functools.partial(finish_kernel, counts=counts, table=table),
        in_specs=[pl.BlockSpec(memory_space=pltpu.SMEM)]
        + [vmem] * len(pieces)
        + [pl.BlockSpec(memory_space=pl.ANY)] * 3
        + [vmem],
        out_specs=[pl.BlockSpec(memory_space=pl.ANY)] * 4 + [vmem] * 4,
        out_shape=[
            square, square, square, square, row, row,
            jax.ShapeDtypeStruct((experts, width), jnp.float32),
            jax.ShapeDtypeStruct(table[::-1], jnp.float32),
        ],
        scratch_shapes=[
            pltpu.VMEM((3, width, width), jnp.bfloat16),
            pltpu.VMEM((4, width, width), jnp.float32),
            pltpu.VMEM((width, TILE), jnp.float32),
            pltpu.VMEM((counts[0] * extra, width), jnp.float32),
            pltpu.SemaphoreType.DMA((3,)),
            pltpu.SemaphoreType.DMA((4,)),
        ],
        compiler_params=pltpu.CompilerParams(vmem_limit_bytes=40 * 1024 * 1024),
        name="finish",
    )(places, *pieces, *weights, gain_row)


def hidden_kernel(
    grads_ref, query_ref, key_ref, value_ref, hidden_ref, gain_ref, residual_grad_ref, out_ref
):
    total = None
    for index, weight in enumerate((query_ref, key_ref, value_ref)):
        term = times_transposed(grads_ref[index], weight[...])
        total = term if total is None else total + term
    hidden = hidden_ref[...].astype(jnp.float32)
    inverse = lax.rsqrt(jnp.mean(hidden * hidden, axis=1, keepdims=True) + eps_norm)
    scaled = hidden * inverse
    weighted = total * gain_ref[...]
    spread = jnp.mean(weighted * scaled, axis=1, keepdims=True)
    out_ref[...] = (
        residual_grad_ref[...].astype(jnp.float32) + inverse * (weighted - scaled * spread)
    ).astype(jnp.bfloat16)


def hidden_gradient(grads, weights, hidden, gain_row, residual_grad):
    tokens, width = hidden.shape
    block = 256
    row_spec = pl.BlockSpec((block, width), lambda step: (step, 0))
    whole = lambda shape: pl.BlockSpec(shape, lambda step: (0, 0))
    return pl.pallas_call(
        hidden_kernel,
        grid=(tokens // block,),
        in_specs=[pl.BlockSpec((3, block, width), lambda step: (0, step, 0))]
        + [whole(weight.shape) for weight in weights]
        + [row_spec, whole(gain_row.shape), row_spec],
        out_specs=row_spec,
        out_shape=jax.ShapeDtypeStruct((tokens, width), jnp.bfloat16),
        compiler_params=pltpu.CompilerParams(vmem_limit_bytes=VMEM_CAP),
        cost_estimate=pl.CostEstimate(
            flops=6 * tokens * width * width, bytes_accessed=20 * tokens * width, transcendentals=0
        ),
        name="hidden_gradient",
    )(grads, *weights, hidden, gain_row, residual_grad)


def exchange_pieces(stage, pieces):
    axis, _, swaps = stage
    return [lax.ppermute(piece, axis, pairs) for piece, pairs in zip(pieces, swaps)]


def on_device(
    hidden_in,
    first_gain,
    w_query,
    w_key,
    w_value,
    w_output,
    rel_table,
    second_gain,
    router,
    expert_up,
    expert_down,
    routes,
    capacity_factor,
    cotangent,
):
    axes = ("narrow", "wide")
    chunks = 2
    tokens, width = hidden_in.shape
    bucket_count = rel_table.shape[0]
    experts = router.shape[1]
    slots = 2 * tokens // experts
    capacity = capacity_factor * tokens // experts
    devices = lax.axis_size(axes)
    own = lax.axis_index(axes).astype(jnp.int32).reshape(1)
    padded = -(-experts // TILE) * TILE
    router_wide = jnp.pad(router, ((0, 0), (0, padded - experts)))

    def exchange(rows):
        blocks = rows.reshape(experts, -1, width)
        return lax.all_to_all(blocks, axes, split_axis=0, concat_axis=0, tiled=True).reshape(
            -1, width
        )

    together = lax.optimization_barrier
    sent_ups, place, spots = send_first(
        capacity, routes.reshape(1, tokens), cotangent, experts, slots, chunks
    )
    sent_ups, hidden_in = together((sent_ups, hidden_in))
    ups = exchange(sent_ups)

    band, edges = bias_band(rel_table)
    hidden = hidden_in.astype(jnp.float32)
    gain_one = first_gain.astype(jnp.float32)
    gain_two = second_gain.astype(jnp.float32)
    inverse_one = lax.rsqrt(jnp.mean(hidden * hidden, axis=-1, keepdims=True) + eps_norm)
    normed_first = (hidden * inverse_one * gain_one).astype(jnp.bfloat16)
    queries = times(normed_first, w_query).astype(jnp.bfloat16)
    keys = times(normed_first, w_key).astype(jnp.bfloat16)
    values = times(normed_first, w_value).astype(jnp.bfloat16)
    attended, attended_t, logs = attend(queries, keys, values, band, edges)
    residual = hidden + times(attended, w_output)
    inverse_two = lax.rsqrt(jnp.mean(residual * residual, axis=-1, keepdims=True) + eps_norm)
    normed_second = (residual * inverse_two * gain_two).astype(jnp.bfloat16)
    half = experts * slots // chunks
    sent = send_again(place, normed_second, 0, half)
    sent, ups = together((sent, ups))
    rows = [exchange(sent)]
    queries_again, _ = together((queries, ups))
    weights, normed_t = attend_weights(queries_again, keys, logs, band, edges, normed_first)
    sent = send_again(place, normed_second, half, half)
    sent, rows[0], weights, normed_t = together((sent, rows[0], weights, normed_t))
    rows.append(exchange(sent))
    ups = ups.reshape(experts, chunks, slots // chunks, width)

    saved = ()
    input_grads, router_terms = [], []
    for c in range(chunks):
        input_grad, router_term, *saved = expert_pass(
            own, rows[c], ups, expert_up[0], expert_down[0], router_wide, experts, c, saved
        )
        if c + 1 < chunks:
            input_grad, rows[-1] = together((input_grad, rows[-1]))
        if input_grads:
            input_grad, input_grads[-1] = together((input_grad, input_grads[-1]))
        input_grads.append(exchange(input_grad))
        router_terms.append(router_term)
    saved, input_grads[0] = together((saved, input_grads[0]))
    produced = saved[0].reshape(-1, width)
    activated, pre_grad, slot_grad, kept_rows = [
        array.reshape(-1, array.shape[-1]) for array in saved[1:]
    ]
    gradient_expert_down = inner_rows(activated, slot_grad)[None]
    gradient_expert_up = inner_rows(kept_rows, pre_grad)[None]
    fetched = fetch_first(spots, input_grads[0])
    gain_row = gain_two[None]
    input_grads[-1], fetched, gradient_expert_down, gradient_expert_up, produced, gain_row = together(
        (input_grads[-1], fetched, gradient_expert_down, gradient_expert_up, produced, gain_row)
    )
    produced = exchange(produced)
    out_grad, attended_grad, gain_terms = fetch_grads(
        spots, fetched, input_grads[-1], residual, gain_row, cotangent, w_output
    )
    core = lax.axis_index("narrow").astype(jnp.int32).reshape(1)
    swap = [(0, 1), (1, 0)]
    grads, away, kept, sums = attend_back(
        core, queries, keys, values, attended_grad, attended, weights, normed_t
    )
    got = lax.ppermute(away, "narrow", swap)
    out_grad, kept = together((out_grad, kept))
    away_out, kept_out = weight_terms(core, attended_t, out_grad)
    got_out = lax.ppermute(away_out, "narrow", swap)
    stages = sum_stages([("wide", lax.axis_size("wide"))])
    levels = len(stages)
    orders = (stages, stages[1:] + stages[:1])
    counts = [[len(stage[2]) + 1 for stage in order] for order in orders]

    def places_at(level):
        return jnp.stack([order[level][1] for order in orders]).astype(jnp.int32)

    chains = first_pieces(
        places_at(0), kept, got, kept_out, got_out, gain_terms, router_terms, sums, experts,
        (counts[0][0], counts[1][0]),
    )
    projections = (w_query, w_key, w_value)
    grads, kept = together((grads, kept))
    gradient_hidden = hidden_gradient(
        grads, projections, hidden_in, gain_one[None], out_grad
    )
    rows_at = []
    for level in range(levels):
        rows_at.append([chain[0].shape[0] for chain in chains])
        received = [
            (chain[0], exchange_pieces(order[level], chain[1:]))
            for chain, order in zip(chains, orders)
        ]
        last = level + 1 == levels
        places = jnp.zeros((2,), jnp.int32) if last else places_at(level + 1)
        cuts = [1 if last else count[level + 1] for count in counts]
        own = received[0][0]
        if level == 0:
            own, gradient_hidden = together((own, gradient_hidden))
        if level == 0:
            block_out = combine(spots, produced, residual)
            own, block_out = together((own, block_out))
        received[0] = (own, received[0][1])
        chains = next_pieces(places, received, cuts)
    lows = [chain[0] for chain in chains]
    for level in reversed(range(1, levels)):
        parts = [
            [low] + exchange_pieces(order[level], [low] * len(order[level][2]))
            for low, order in zip(lows, orders)
        ]
        lows = list(join_pieces(places_at(level), parts, rows_at[level - 1]))
    parts = [
        [low] + exchange_pieces(order[0], [low] * len(order[0][2]))
        for low, order in zip(lows, orders)
    ]
    places = jnp.concatenate([core, places_at(0)])
    parts[0][1], places = together((parts[0][1], places))
    others = [[], [lax.ppermute(piece, "narrow", swap) for piece in parts[1]]]
    parts[0][-1] = together((parts[0][-1], *others[1]))[0]
    others[0] = [lax.ppermute(piece, "narrow", swap) for piece in parts[0]]
    parts = [
        [piece for both in zip(own, other) for piece in both] for own, other in zip(parts, others)
    ]
    (
        gradient_query, gradient_key, gradient_value, gradient_output, gradient_first_gain,
        gradient_second_gain, gradient_router, gradient_table,
    ) = finish(places, parts, projections, gain_one[None], experts, rel_table.shape)
    return (
        block_out,
        gradient_hidden,
        gradient_first_gain,
        gradient_query,
        gradient_key,
        gradient_value,
        gradient_output,
        jnp.transpose(gradient_table),
        gradient_second_gain,
        jnp.transpose(gradient_router),
        gradient_expert_up,
        gradient_expert_down,
    )


def solution(mesh):
    split = ("narrow", "wide")
    rows, experts = P(split, None), P(split, None, None)
    return jax.shard_map(
        on_device,
        mesh=mesh,
        in_specs=(rows,) + (P(),) * 8 + (experts, experts, rows, P(split), rows),
        out_specs=(rows, rows) + (P(),) * 8 + (experts, experts),
        check_vma=False,
    )
```
